32 devices in a mesh: expert: 8 (over y, x, core), tensor: 4 (over z).
Axes of the slice: x: 2, y: 2, z: 4, core: 2. Of those that a mesh axis runs over, the one named last changes fastest.
Arguments:
- tokens: bfloat16 [4096, 768], P('expert'), may hold values from -6 to 6
- segment_ids: int32 [8, 512], P('expert'), may hold values from 0 to 7, never falling along the last dimension, each value on 1 to 128 neighbouring positions
- expert_choice: int32 [4096], P('expert'), may hold values from 0 to 63
- slot_index: int32 [4096], P('expert'), may hold values from -1 to 9, as said below
- first_gain: float32 [768], replicated, may hold values from 0.5 to 1.5
- input_weight: bfloat16 [3, 768, 768], P(None, None, 'tensor'), may hold values from -0.078125 to 0.078125
- bias_table: float32 [32, 12], P(None, 'tensor'), may hold values from -1.5 to 1.5
- output_weight: bfloat16 [768, 768], P('tensor'), may hold values from -3.5 to 3.5
- second_gain: float32 [768], replicated, may hold values from 0.5 to 1.5
- router_weight: float32 [768, 64], replicated, may hold values from -1 to 1
- expert_in: bfloat16 [64, 768, 3072], P('expert', None, 'tensor'), may hold values from -0.21875 to 0.21875
- expert_out: bfloat16 [64, 3072, 768], P('expert', 'tensor'), may hold values from -6 to 6
- cotangent: bfloat16 [4096, 768], P('expert'), may hold values from -6 to 6
Outputs:
- block_output: bfloat16 [4096, 768], P('expert')
- grad_tokens: float32 [4096, 768], P('expert')
- grad_first_gain: float32 [768], replicated
- grad_input_weight: float32 [3, 768, 768], P(None, None, 'tensor')
- grad_bias_table: float32 [32, 12], P(None, 'tensor')
- grad_output_weight: float32 [768, 768], P('tensor')
- grad_second_gain: float32 [768], replicated
- grad_router_weight: float32 [768, 64], replicated
- grad_expert_in: float32 [64, 768, 3072], P('expert', None, 'tensor')
- grad_expert_out: float32 [64, 3072, 768], P('expert', 'tensor')
The draws below stay inside these ranges and needn't reach their ends.
Inputs may be any that keep to these rules, and one draw needn't show every extreme that they name: slot_index[t] is the number of earlier tokens of the same aligned block of 512 tokens (the tokens of one index of expert) with the same expert_choice, or -1 where that number is 10 or more (the token is dropped); so at most 10 tokens of one block are kept by one expert.
All inputs are finite; a program needn't handle non-finite values.
Results may differ from the reference program's by a relative error of at most 0.012.
The reference program's roundings to bfloat16 on the way count: a program that leaves them out, or rounds other values in their place, can miss the bound.
Values may be sent and summed in bfloat16 or wider, within the bound.
No kernel may reach another device: no remote copies, remote signals or barrier semaphores. Data moves between devices by JAX's collectives and lax.ppermute only.
A program may use at most 192 MiB of HBM per device.

```python
import math
import jax
import jax.numpy as jnp
import numpy as np
from jax import lax

D = 768
HEADS = 12
HEAD_DIM = 64
FF = 3072
EXPERTS = 64
BUCKETS = 32
SEQ = 512
SEGS = 8
TOKENS_PER_SHARD = 512
TOKENS = 4096
NSEQ = 8
CAP = 10


def routing_pair(key):
    router_random_key = jax.random.fold_in(key, 41)
    popular_expert_key, uniform_choice_key, surge_random_key = jax.random.split(router_random_key, 3)
    source_indices = TOKENS // TOKENS_PER_SHARD
    hot_expert = jax.random.randint(popular_expert_key, (), 0, EXPERTS, dtype=jnp.int32)
    drawn_choice = jax.random.randint(uniform_choice_key, (source_indices, TOKENS_PER_SHARD), 0, EXPERTS, dtype=jnp.int32)
    permuted_rows = jax.vmap(lambda block_random_key: jax.random.permutation(block_random_key, TOKENS_PER_SHARD))(jax.random.split(surge_random_key, source_indices))
    picked = jnp.where(permuted_rows < CAP + 2, hot_expert, drawn_choice).astype(jnp.int32)
    matches = (picked[:, :, None] == jnp.arange(EXPERTS, dtype=jnp.int32)[None, None, :]).astype(jnp.int32)
    places = jnp.sum((jnp.cumsum(matches, axis=1) - 1) * matches, axis=2)
    slots = jnp.where(places < CAP, places, -1).astype(jnp.int32)
    return (picked.reshape(TOKENS), slots.reshape(TOKENS))


def draw_expert_choice(key, part):
    return routing_pair(key)[0]


def draw_slot_index(key, part):
    return routing_pair(key)[1]


def draw_bias_table(key, part):
    key = jax.random.fold_in(key, 7)
    return jnp.clip(0.5 * jax.random.normal(key, (BUCKETS, HEADS), jnp.float32), -1.5, 1.5)


def draw_router_weight(key, part):
    key = jax.random.fold_in(key, 11)
    base_key, spread_key = jax.random.split(key, 2)
    fan_scale = 1.0 / math.sqrt(D)
    spread = jnp.exp(jax.random.uniform(spread_key, (EXPERTS,), jnp.float32, math.log(0.5), 0.0))
    unit_draw = jnp.clip(jax.random.normal(base_key, (D, EXPERTS), jnp.float32), -4.0, 4.0)
    return unit_draw * spread * fan_scale


def steps_of(key, extent, cuts, smallest, top_value):
    loudness, own = 1.0, jax.random.fold_in(key, 6)
    for position, parts in cuts:
        heights = jnp.exp(jax.random.uniform(jax.random.fold_in(own, position), (parts,), jnp.float32, smallest / len(cuts), top_value / len(cuts)))
        loudness = loudness * jnp.repeat(heights, extent[position] // parts).reshape([-1 if axis == position else 1 for axis in range(len(extent))])
    return loudness


def split_up(number_of, total, most, lean):
    loads = [(1 << 20) // math.isqrt(standing ** lean) + 1 for standing in range(2, number_of + 1)]
    surplus, given = total - most - (number_of - 1), [1] * (number_of - 1)
    while surplus > 0:
        movable = [i for i in range(number_of - 1) if given[i] < most]
        mass, left = sum([loads[i] for i in movable]), surplus
        for i in movable:
            more = min(most - given[i], max(1, left * loads[i] // mass), surplus)
            given[i] = given[i] + more
            surplus = surplus - more
    return np.array([most] + given)


def uneven(key, amount, total, limit, lean):
    if amount == 2:
        one = jax.random.randint(key, (), max(1, total - limit), min(limit, total - 1) + 1)
        return jnp.stack([one, total - one])
    sizes = jnp.asarray(split_up(amount, total, limit, lean), jnp.int32)
    twos = (amount - 1) // 2
    giver, taker = sizes[1:1 + 2 * twos:2], sizes[2:2 + 2 * twos:2]
    slack = jnp.minimum(giver - 1, limit - taker)
    moved = jax.random.randint(jax.random.fold_in(key, 1), (twos,), 0, 1 << 20) % (slack + 1)
    sizes = sizes.at[1:1 + 2 * twos:2].set(giver - moved).at[2:2 + 2 * twos:2].set(taker + moved)
    return sizes[jax.random.permutation(jax.random.fold_in(key, 2), amount)]


def centred(key, extent, width, bound, pieces=(), kind=jnp.bfloat16):
    level = steps_of(key, extent, pieces, -0.22, 0.18) if pieces else 1.0
    values = jax.random.normal(key, extent, jnp.float32) * width * level
    return jnp.minimum(jnp.maximum(values, -bound), bound).astype(kind)


def setup_inputs(seed: int = 0) -> dict:
    splits = jax.random.split(jax.random.key(seed), 14)
    return {
        "tokens": centred(splits[0], (TOKENS, D), 1.0, 6.0, ((0, 8),)),
        "segment_ids": jax.vmap(lambda own: jnp.searchsorted(jnp.cumsum(uneven(own, SEGS, SEQ, SEQ // 4, 1)), jnp.arange(SEQ), side="right"))(jax.random.split(splits[1], NSEQ)).reshape((NSEQ, SEQ)).astype(jnp.int32),
        "expert_choice": draw_expert_choice(jax.random.fold_in(splits[13], 71), 0),
        "slot_index": draw_slot_index(jax.random.fold_in(splits[13], 71), 0),
        "first_gain": jnp.clip(1.0 + 0.1 * jax.random.normal(splits[4], (D,), jnp.float32), 0.5, 1.5),
        "input_weight": centred(splits[5], (3, D, HEADS * HEAD_DIM), 0.0125, 0.078125, ((2, 4),)),
        "bias_table": draw_bias_table(jax.random.fold_in(splits[13], 71), 0),
        "output_weight": centred(splits[7], (HEADS * HEAD_DIM, D), 0.6, 3.5, ((0, 4),)),
        "second_gain": jnp.clip(1.0 + 0.1 * jax.random.normal(splits[8], (D,), jnp.float32), 0.5, 1.5),
        "router_weight": draw_router_weight(jax.random.fold_in(splits[13], 71), 0),
        "expert_in": centred(splits[10], (EXPERTS, D, FF), D ** -0.5, 0.21875, ((0, 8), (2, 4))),
        "expert_out": centred(splits[11], (EXPERTS, FF, D), 1.0, 6.0, ((0, 8), (1, 4))),
        "cotangent": centred(splits[12], (TOKENS, D), 1.0, 6.0, ((0, 8),)),
    }


bucket_edges = (12, 16, 23, 32, 46, 64, 91)
norm_eps = 1e-06
masked_score = -1e+30
gelu_const = math.sqrt(2.0 / math.pi)
gelu_cubic = 0.044715

def gelu_value(pre):
    inner = jnp.tanh(gelu_const * (pre + gelu_cubic * pre * pre * pre))
    return 0.5 * pre * (1.0 + inner)

def gelu_slope(pre):
    inner = jnp.tanh(gelu_const * (pre + gelu_cubic * pre * pre * pre))
    return 0.5 * (1.0 + inner) + 0.5 * pre * (1.0 - inner * inner) * gelu_const * (1.0 + 3.0 * gelu_cubic * pre * pre)

def to_low(array):
    return lax.optimization_barrier(array.astype(jnp.bfloat16))

def bucket_of(relative):
    distance = jnp.abs(relative)
    beyond = jnp.zeros_like(distance)
    for threshold in bucket_edges:
        beyond = beyond + (distance >= threshold).astype(jnp.int32)
    magnitude = jnp.where(distance < 8, distance, 8 + beyond)
    return magnitude + 16 * (relative > 0).astype(jnp.int32)

def sequence_scores(queries, keys_all, segment, bias_table):
    length = queries.shape[0]
    positions = jnp.arange(length, dtype=jnp.int32)
    buckets = bucket_of(positions[None, :] - positions[:, None])
    bias_full = jnp.transpose(bias_table[buckets], (2, 0, 1))
    scores = jnp.einsum('qhc,khc->hqk', queries.astype(jnp.float32), keys_all.astype(jnp.float32)) + bias_full
    same_doc = segment[:, None] == segment[None, :]
    return (jnp.where(same_doc[None], scores, masked_score), buckets)

def sequence_probs(scores):
    highest = lax.optimization_barrier(jnp.max(scores, -1, keepdims=True))
    log_total = highest + jnp.log(lax.optimization_barrier(jnp.sum(jnp.exp(scores - highest), -1, keepdims=True)))
    return jnp.exp(scores - log_total)

def attend_sequence(queries, keys_all, values, segment, bias_table):
    scores, buckets = sequence_scores(queries, keys_all, segment, bias_table)
    weights = to_low(sequence_probs(scores))
    return to_low(jnp.einsum('hqk,khc->qhc', weights.astype(jnp.float32), values.astype(jnp.float32)))

def attend_sequence_grad(queries, keys_all, values, segment, bias_table, grad_rows):
    scores, buckets = sequence_scores(queries, keys_all, segment, bias_table)
    probs_full = sequence_probs(scores)
    weights = to_low(probs_full)
    grad_wide = grad_rows.astype(jnp.float32)
    grad_probs = jnp.einsum('qhc,khc->hqk', grad_wide, values.astype(jnp.float32))
    grad_scores = probs_full * (grad_probs - lax.optimization_barrier(jnp.sum(probs_full * grad_probs, -1, keepdims=True)))
    rounded = to_low(grad_scores).astype(jnp.float32)
    grad_query = jnp.einsum('hqk,khc->qhc', rounded, keys_all.astype(jnp.float32))
    grad_key = jnp.einsum('hqk,qhc->khc', rounded, queries.astype(jnp.float32))
    grad_value = jnp.einsum('hqk,qhc->khc', weights.astype(jnp.float32), grad_wide)
    head_count = bias_table.shape[1]
    grad_table = jax.ops.segment_sum(grad_scores.reshape(head_count, -1).T, buckets.reshape(-1), num_segments=BUCKETS)
    return (to_low(grad_query), to_low(grad_key), to_low(grad_value), grad_table)

def reference(tokens, segment_ids, expert_choice, slot_index, first_gain, input_weight, bias_table, output_weight, second_gain, router_weight, expert_in, expert_out, cotangent):
    highest_prec = lax.Precision.HIGHEST
    token_float = tokens.astype(jnp.float32)
    first_scale = lax.rsqrt(lax.optimization_barrier(jnp.mean(token_float * token_float, -1, keepdims=True)) + norm_eps)
    first_normed = to_low(token_float * first_scale * first_gain)
    projected = to_low(jnp.einsum('td,jdc->jtc', first_normed.astype(jnp.float32), input_weight.astype(jnp.float32)))
    per_head = projected.reshape(3, NSEQ, SEQ, HEADS, HEAD_DIM)

    def forward_sequence(sequence_item):
        return attend_sequence(sequence_item[0], sequence_item[1], sequence_item[2], sequence_item[3], bias_table)
    attended = lax.map(forward_sequence, (per_head[0], per_head[1], per_head[2], segment_ids))
    attended = attended.reshape(TOKENS, HEADS * HEAD_DIM)
    hidden = token_float + jnp.dot(attended, output_weight, preferred_element_type=jnp.float32)
    second_scale = lax.rsqrt(lax.optimization_barrier(jnp.mean(hidden * hidden, -1, keepdims=True)) + norm_eps)
    second_normed = hidden * second_scale * second_gain
    routed_input = to_low(second_normed)
    logits = jnp.dot(second_normed, router_weight, precision=highest_prec)
    router_prob = sequence_probs(logits)
    chosen = (expert_choice[:, None] == jnp.arange(EXPERTS, dtype=jnp.int32)[None, :]).astype(jnp.float32)
    gate_value = lax.optimization_barrier(jnp.sum(router_prob * chosen, -1))
    kept_mask = slot_index >= 0
    source_count = TOKENS // TOKENS_PER_SHARD
    slot_total = EXPERTS * source_count * CAP
    block_of = jnp.arange(TOKENS, dtype=jnp.int32) // TOKENS_PER_SHARD
    dest_row = jnp.where(kept_mask, (expert_choice * source_count + block_of) * CAP + slot_index, slot_total)

    def scatter_rows(token_rows):
        filled = jnp.zeros((slot_total, D), jnp.bfloat16).at[dest_row].set(token_rows, mode='drop')
        return filled.reshape(EXPERTS, source_count * CAP, D)

    def gather_rows(slot_rows):
        flat_rows = slot_rows.reshape(slot_total, D)
        picked = flat_rows[jnp.minimum(dest_row, slot_total - 1)]
        return jnp.where(kept_mask[:, None], picked, jnp.zeros_like(picked))
    expert_rows = scatter_rows(routed_input)

    def expert_forward(expert_item):
        pre_act = jnp.dot(expert_item[0], expert_item[1], preferred_element_type=jnp.float32)
        hidden_act = to_low(gelu_value(pre_act))
        return to_low(jnp.dot(hidden_act, expert_item[2], preferred_element_type=jnp.float32))
    expert_result = gather_rows(lax.map(expert_forward, (expert_rows, expert_in, expert_out))).astype(jnp.float32)
    block_output = (hidden + gate_value[:, None] * expert_result).astype(jnp.bfloat16)
    grad_float = cotangent.astype(jnp.float32)
    grad_gate = lax.optimization_barrier(jnp.sum(grad_float * expert_result, -1))
    grad_result = to_low(gate_value[:, None] * grad_float)
    grad_slots = scatter_rows(grad_result)

    def expert_backward(expert_item):
        slot_input, slot_grad, weight_first, weight_second = expert_item
        pre_act = jnp.dot(slot_input, weight_first, preferred_element_type=jnp.float32)
        hidden_act = to_low(gelu_value(pre_act))
        grad_act = jnp.dot(slot_grad, weight_second.T, preferred_element_type=jnp.float32)
        grad_act = to_low(grad_act * gelu_slope(pre_act))
        grad_second_w = jnp.dot(hidden_act.T, slot_grad, preferred_element_type=jnp.float32)
        grad_first_w = jnp.dot(slot_input.T, grad_act, preferred_element_type=jnp.float32)
        grad_input_rows = to_low(jnp.dot(grad_act, weight_first.T, preferred_element_type=jnp.float32))
        return (grad_first_w, grad_second_w, grad_input_rows)
    grad_expert_in, grad_expert_out, grad_slot_rows = lax.map(expert_backward, (expert_rows, grad_slots, expert_in, expert_out))
    grad_routed = gather_rows(grad_slot_rows).astype(jnp.float32)
    grad_logits = (grad_gate * gate_value)[:, None] * (chosen - router_prob)
    grad_router_weight = jnp.dot(second_normed.T, grad_logits, precision=highest_prec)
    grad_normed = grad_routed + jnp.dot(grad_logits, router_weight.T, precision=highest_prec)
    grad_second_gain = lax.optimization_barrier(jnp.sum(grad_normed * hidden * second_scale, 0))
    scaled_second = grad_normed * second_gain
    grad_hidden = grad_float + second_scale * scaled_second - hidden * (second_scale * second_scale * second_scale) * lax.optimization_barrier(jnp.mean(scaled_second * hidden, -1, keepdims=True))
    grad_hidden_low = to_low(grad_hidden)
    grad_output_weight = jnp.dot(attended.T, grad_hidden_low, preferred_element_type=jnp.float32)
    grad_attended = to_low(jnp.dot(grad_hidden_low, output_weight.T, preferred_element_type=jnp.float32))
    grad_attended = grad_attended.reshape(NSEQ, SEQ, HEADS, HEAD_DIM)

    def backward_sequence(sequence_item):
        return attend_sequence_grad(sequence_item[0], sequence_item[1], sequence_item[2], sequence_item[3], bias_table, sequence_item[4])
    grad_query, grad_key, grad_value, grad_tables = lax.map(backward_sequence, (per_head[0], per_head[1], per_head[2], segment_ids, grad_attended))
    grad_bias_table = lax.optimization_barrier(jnp.sum(grad_tables, 0))
    grad_projected = jnp.stack([grad_query, grad_key, grad_value]).reshape(3, TOKENS, HEADS * HEAD_DIM).astype(jnp.float32)
    grad_input_weight = jnp.einsum('td,jtc->jdc', first_normed.astype(jnp.float32), grad_projected)
    grad_first_normed = jnp.einsum('jtc,jdc->td', grad_projected, input_weight.astype(jnp.float32))
    grad_first_gain = lax.optimization_barrier(jnp.sum(grad_first_normed * token_float * first_scale, 0))
    scaled_first = grad_first_normed * first_gain
    grad_tokens = grad_hidden + first_scale * scaled_first - token_float * (first_scale * first_scale * first_scale) * lax.optimization_barrier(jnp.mean(scaled_first * token_float, -1, keepdims=True))
    return (block_output, grad_tokens, grad_first_gain, grad_input_weight, grad_bias_table, grad_output_weight, grad_second_gain, grad_router_weight, grad_expert_in, grad_expert_out)
```

```python
import math

import jax
import jax.numpy as jnp
from jax import lax
from jax.experimental import pallas as pl
from jax.experimental.pallas import tpu as pltpu
from jax.sharding import PartitionSpec as P

CAP = 10

bucket_edges = (12, 16, 23, 32, 46, 64, 91)
norm_eps = 1e-06
masked_score = -1e30
gelu_const = math.sqrt(2.0 / math.pi)
gelu_cubic = 0.044715

BLOCK = 128
BAND = 3 * BLOCK
ROLL = 4 * BLOCK
HEAD = 64
EXTRA = 16

bf16 = jnp.bfloat16
f32 = jnp.float32
i32 = jnp.int32
highest = lax.Precision.HIGHEST

NN = (((1,), (0,)), ((), ()))
NT = (((1,), (1,)), ((), ()))
TN = (((0,), (0,)), ((), ()))


def dot(left, right, dims=NN, precision=None):
    return lax.dot_general(left, right, dims, precision=precision, preferred_element_type=f32)


def iota(shape, axis):
    return lax.broadcasted_iota(i32, shape, axis)


def call(kernel, outs, args, scratch=(), **extra):
    vmem = pl.BlockSpec(memory_space=pltpu.VMEM)
    return pl.pallas_call(
        kernel,
        out_shape=[jax.ShapeDtypeStruct(shape, dtype) for shape, dtype in outs],
        in_specs=[vmem] * len(args),
        out_specs=[vmem] * len(outs),
        scratch_shapes=list(scratch),
        compiler_params=pltpu.CompilerParams(vmem_limit_bytes=56 * 2**20),
        **extra,
    )(*args)


def split3(value):
    high = value.astype(bf16).astype(f32)
    rest = value - high
    middle = rest.astype(bf16).astype(f32)
    return high, middle, rest - middle


def columns3(value, width):
    high, middle, low = split3(value)
    lane = iota((value.shape[0], width), 1)
    picked = jnp.where(lane == 0, high, jnp.where(lane == 1, middle, jnp.where(lane == 2, low, 0.0)))
    return picked.astype(bf16)


def column_of(row):
    return jnp.transpose(jnp.broadcast_to(row.astype(f32), (128, row.shape[1])))


def wide(column, width):
    return jnp.concatenate([column] * (width // 128), 1)


def bucket_of(relative):
    distance = jnp.abs(relative)
    beyond = jnp.zeros_like(distance)
    for threshold in bucket_edges:
        beyond = beyond + (distance >= threshold).astype(i32)
    magnitude = jnp.where(distance < 8, distance, 8 + beyond)
    return magnitude + 16 * (relative > 0).astype(i32)


def band_onehot(buckets):
    offset = iota((buckets, ROLL), 1)
    relative = jnp.where(offset < BAND, offset, offset - ROLL) - BLOCK
    return bucket_of(relative) == iota((buckets, ROLL), 0)


def bias_tile(onehot, table_column):
    row = jnp.sum(jnp.where(onehot, table_column, 0.0), 0, keepdims=True)
    full = jnp.broadcast_to(row, (BLOCK, ROLL))
    return pltpu.roll(full, 0, 1, stride=1, stride_axis=0)[:, :BAND]


def head_mask(head, width):
    lane = iota((1, width), 1)
    return ((lane >= head * HEAD) & (lane < (head + 1) * HEAD)).astype(f32)


def padded_segments(seg):
    edge = jnp.full((1, BLOCK), -1.0, f32)
    return jnp.concatenate([edge, seg, edge], 1)


def first_norm(tok, gain):
    scale = lax.rsqrt(jnp.mean(tok * tok, -1, keepdims=True) + norm_eps)
    return (tok * scale * gain).astype(bf16), scale


def probabilities(query, keys, bias, same):
    scores = jnp.where(same, dot(query, keys, NT) + bias, masked_score)
    top = jnp.max(scores, -1, keepdims=True)
    weights = jnp.exp(scores - top)
    return weights * (1.0 / jnp.sum(weights, -1, keepdims=True))


def forward_kernel(tok_ref, gain_ref, iw_ref, bt_ref, seg_ref, att_ref, normed_ref, keys, values):
    rows, width = att_ref.shape
    normed, _ = first_norm(tok_ref[...].astype(f32), gain_ref[...])
    normed_ref[...] = normed
    queries = dot(normed, iw_ref[0]).astype(bf16)
    edge = jnp.zeros((BLOCK, width), bf16)
    for ref, j in ((keys, 1), (values, 2)):
        ref[pl.ds(0, BLOCK), :] = edge
        ref[pl.ds(rows + BLOCK, BLOCK), :] = edge
        ref[pl.ds(BLOCK, rows), :] = dot(normed, iw_ref[j]).astype(bf16)
    seg = seg_ref[...].astype(f32)
    seg_keys = padded_segments(seg)
    seg_rows = column_of(seg)
    table = bt_ref[...]
    onehot = band_onehot(table.shape[0])
    heads = table.shape[1]
    tiles = [bias_tile(onehot, table[:, h : h + 1]) for h in range(heads)]
    masks = [head_mask(h, width) for h in range(heads)]
    for block in range(rows // BLOCK):
        at = block * BLOCK
        same = wide(seg_rows[at : at + BLOCK], BAND) == seg_keys[:, at : at + BAND]
        key_band = keys[pl.ds(at, BAND), :]
        value_band = values[pl.ds(at, BAND), :]
        query = queries[at : at + BLOCK]
        total = jnp.zeros((BLOCK, width), f32)
        for h in range(heads):
            weights = probabilities(query * masks[h].astype(bf16), key_band, tiles[h], same)
            total = total + dot(weights.astype(bf16), value_band) * masks[h]
        att_ref[pl.ds(at, BLOCK), :] = total.astype(bf16)


def group_backward(normed, weight, out_weight, table, seg, grad_low, scratch, bias_grads):
    keys, values, grad_keys, grad_values, grad_queries = scratch
    rows = normed.shape[0]
    width = out_weight.shape[0]
    queries = dot(normed, weight[0]).astype(bf16)
    edge = jnp.zeros((BLOCK, width), bf16)
    for ref, j in ((keys, 1), (values, 2)):
        ref[pl.ds(0, BLOCK), :] = edge
        ref[pl.ds(rows + BLOCK, BLOCK), :] = edge
        ref[pl.ds(BLOCK, rows), :] = dot(normed, weight[j]).astype(bf16)
    grad_att = dot(grad_low, out_weight, NT).astype(bf16)
    grad_keys[...] = jnp.zeros(grad_keys.shape, f32)
    grad_values[...] = jnp.zeros(grad_values.shape, f32)
    seg_keys = padded_segments(seg)
    seg_rows = column_of(seg)
    onehot = band_onehot(table.shape[0])
    heads = table.shape[1]
    tiles = [bias_tile(onehot, table[:, h : h + 1]) for h in range(heads)]
    masks = [head_mask(h, width).astype(bf16) for h in range(heads)]
    sums = [None] * heads
    for block in range(rows // BLOCK):
        at = block * BLOCK
        same = wide(seg_rows[at : at + BLOCK], BAND) == seg_keys[:, at : at + BAND]
        key_band = keys[pl.ds(at, BAND), :]
        value_band = values[pl.ds(at, BAND), :]
        query = queries[at : at + BLOCK]
        grad_rows = grad_att[at : at + BLOCK]
        query_total = jnp.zeros((BLOCK, width), f32)
        key_total = jnp.zeros((BAND, width), f32)
        value_total = jnp.zeros((BAND, width), f32)
        for h in range(heads):
            head_query = query * masks[h]
            head_grad = grad_rows * masks[h]
            weights = probabilities(head_query, key_band, tiles[h], same)
            grad_probs = dot(head_grad, value_band, NT)
            scaled = weights * grad_probs
            grad_scores = scaled - weights * jnp.sum(scaled, -1, keepdims=True)
            rounded = grad_scores.astype(bf16)
            query_total = query_total + dot(rounded, key_band * masks[h])
            key_total = key_total + dot(rounded, head_query, TN)
            value_total = value_total + dot(weights.astype(bf16), head_grad, TN)
            if bias_grads:
                sums[h] = grad_scores if sums[h] is None else sums[h] + grad_scores
        grad_queries[pl.ds(at, BLOCK), :] = query_total.astype(bf16)
        grad_keys[pl.ds(at, BAND), :] += key_total
        grad_values[pl.ds(at, BAND), :] += value_total
    parts = (
        grad_queries[...],
        grad_keys[pl.ds(BLOCK, rows), :].astype(bf16),
        grad_values[pl.ds(BLOCK, rows), :].astype(bf16),
    )
    if not bias_grads:
        return parts, None
    lane = iota((table.shape[0], 128), 1)
    table_grad = jnp.zeros((table.shape[0], 128), f32)
    row_index = iota((BLOCK, ROLL), 0)
    for h in range(heads):
        moved = jnp.concatenate([sums[h], jnp.zeros((BLOCK, ROLL - BAND), f32)], 1)
        step = 1
        while step < BLOCK:
            moved = jnp.where((row_index & step) != 0, pltpu.roll(moved, ROLL - step, 1), moved)
            step *= 2
        diagonal = jnp.sum(moved, 0, keepdims=True)
        bucket_sum = jnp.sum(jnp.where(onehot, diagonal, 0.0), 1, keepdims=True)
        table_grad = table_grad + jnp.where(lane == h, bucket_sum, 0.0)
    return parts, table_grad


def own_backward_kernel(normed_ref, iw_ref, ow_ref, bt_ref, seg_ref, low_ref, grad_iw_ref, parts_ref, table_ref, *scratch):
    normed = normed_ref[...]
    parts, table_grad = group_backward(
        normed, iw_ref, ow_ref[...], bt_ref[...], seg_ref[...].astype(f32), low_ref[...], scratch, True
    )
    table_ref[...] = table_grad
    for j in range(3):
        parts_ref[j] = parts[j]
        grad_iw_ref[j] = dot(normed, parts[j], TN).astype(bf16)


def rest_backward_kernel(
    tensor_size,
    normed_ref, iw_ref, ow_ref, bt_ref, seg_ref, low_ref, parts_ref, tok_ref, gain_ref, grad_hidden_ref,
    grad_tok_ref, grad_gain_ref, total, *scratch,
):
    me = lax.axis_index("tensor")
    width = ow_ref.shape[1]
    own = iw_ref.at[me]
    total[...] = sum(dot(parts_ref[j], own[j], NT) for j in range(3))

    def step(shift, carry):
        group = lax.rem(me + shift, tensor_size)
        weight = iw_ref.at[group]
        parts, _ = group_backward(
            normed_ref[...], weight, ow_ref[group], bt_ref[group], seg_ref[...].astype(f32), low_ref[...], scratch, False
        )
        total[...] += sum(dot(parts[j], weight[j], NT) for j in range(3))
        return carry

    lax.fori_loop(1, tensor_size, step, 0)
    tok = tok_ref[...].astype(f32)
    gain = gain_ref[...]
    scale = lax.rsqrt(jnp.mean(tok * tok, -1, keepdims=True) + norm_eps)
    grad_normed = total[...]
    grad_gain_ref[...] = jnp.sum(grad_normed * tok * scale, 0, keepdims=True)
    scaled = grad_normed * gain
    grad_tok_ref[...] = (
        grad_hidden_ref[...]
        + scale * scaled
        - tok * (scale * scale * scale) * jnp.mean(scaled * tok, -1, keepdims=True)
    )


def slot_onehot(choice, slot, slots):
    dest = jnp.where(slot >= 0, choice * CAP + slot, slots)
    return (iota((slots, dest.shape[1]), 0) == dest).astype(f32).astype(bf16)


def cotangent_kernel(cot_ref, choice_ref, slot_ref, out_ref):
    fill = slot_onehot(choice_ref[...], slot_ref[...], out_ref.shape[0])
    out_ref[...] = dot(fill, cot_ref[...]).astype(bf16)


def middle_kernel(
    tensor_size,
    tok_ref, ow_ref, gain_ref, rw_ref, choice_ref, slot_ref, *refs,
):
    att_refs, (hidden_ref, prob_ref, send_ref) = refs[:tensor_size], refs[tensor_size:]
    me = lax.axis_index("tensor")
    hidden = tok_ref[...].astype(f32)
    for shift in range(tensor_size):
        source = lax.rem(me + tensor_size - shift, tensor_size)
        hidden = hidden + dot(att_refs[shift][...], ow_ref[source])
    hidden_ref[...] = hidden
    scale = lax.rsqrt(jnp.mean(hidden * hidden, -1, keepdims=True) + norm_eps)
    normed = hidden * scale * gain_ref[...]
    logits = dot(normed, rw_ref[...], precision=highest)
    top = jnp.max(logits, -1, keepdims=True)
    raised = jnp.exp(logits - top)
    prob = raised * (1.0 / jnp.sum(raised, -1, keepdims=True))
    prob_ref[...] = prob
    gate = jnp.sum(prob * chosen_of(choice_ref[...], prob.shape[1]), -1, keepdims=True)
    width = normed.shape[1]
    fill = slot_onehot(choice_ref[...], slot_ref[...], send_ref.shape[0])
    send_ref[:, :width] = dot(fill, normed.astype(bf16)).astype(bf16)
    send_ref[:, width:] = dot(fill, columns3(gate, 128)).astype(bf16)


def chosen_of(choice, experts):
    column = column_of(choice)[:, :experts]
    return (column == iota(column.shape, 1).astype(f32)).astype(f32)


def expert_kernel(
    tensor_size,
    sources,
    recv_ref, cot_ref, win_ref, wout_ref,
    rows_ref, grads_ref, act_ref, grad_act_ref, dots_ref, *refs,
):
    grad_chunks, result_chunks = refs[:tensor_size], refs[tensor_size : 2 * tensor_size]
    x_all, c_all, g_all, y_all, r_all, d_all = refs[2 * tensor_size :]
    slots = recv_ref.shape[0]
    width = cot_ref.shape[1]
    step = pl.program_id(0)
    local = pl.num_programs(0)
    per = rows_ref.shape[0]
    index = iota((1, slots), 1)

    @pl.when(step == 0)
    def _():
        chunk = slots // sources
        source, rest = lax.div(index, chunk), lax.rem(index, chunk)
        target = lax.div(rest, CAP) * per + source * CAP + lax.rem(rest, CAP)
        order = (iota((slots, slots), 0) == target).astype(f32).astype(bf16)
        x_all[...] = dot(order, recv_ref[:, :width]).astype(bf16)
        gate = jnp.sum(dot(order, recv_ref[:, width:]), -1, keepdims=True)
        cot = dot(order, cot_ref[...])
        c_all[...] = cot.astype(bf16)
        g_all[...] = (gate * cot).astype(bf16)

    at = pl.ds(pl.multiple_of(step * per, 16), per)
    x = x_all[at, :]
    g = g_all[at, :]
    weight_in = win_ref[0]
    weight_out = wout_ref[0]
    pre = dot(x, weight_in)
    inner = jnp.tanh(gelu_const * (pre + gelu_cubic * pre * pre * pre))
    act = (0.5 * pre * (1.0 + inner)).astype(bf16)
    slope = 0.5 * (1.0 + inner) + 0.5 * pre * (1.0 - inner * inner) * gelu_const * (
        1.0 + 3.0 * gelu_cubic * pre * pre
    )
    grad_act = (dot(g, weight_out, NT) * slope).astype(bf16)
    result = dot(act, weight_out)
    r_all[at, :] = dot(grad_act, weight_in, NT).astype(bf16)
    y_all[at, :] = result.astype(bf16)
    d_all[at, :] = columns3(jnp.sum(result * c_all[at, :].astype(f32), -1, keepdims=True), 128)
    rows_ref[...] = x
    grads_ref[...] = g
    act_ref[...] = act
    grad_act_ref[...] = grad_act

    @pl.when(step == local - 1)
    def _():
        expert, rest = lax.div(index, per), lax.rem(index, per)
        target = lax.div(rest, CAP) * (slots // sources) + expert * CAP + lax.rem(rest, CAP)
        order = (iota((slots, slots), 0) == target).astype(f32).astype(bf16)
        dots_ref[...] = dot(order, d_all[...]).astype(bf16)
        me = lax.axis_index("tensor")
        quarter = width // tensor_size
        grad_rows = dot(order, r_all[...]).astype(bf16)
        result_rows = dot(order, y_all[...]).astype(bf16)
        for shift in range(tensor_size):
            first = lax.rem(me + shift, tensor_size) * quarter
            pick = (iota((width, quarter), 0) == iota((width, quarter), 1) + first).astype(f32).astype(bf16)
            grad_chunks[shift][...] = dot(grad_rows, pick).astype(bf16)
            result_chunks[shift][...] = dot(result_rows, pick).astype(bf16)


def back_kernel(recv_ref, choice_ref, slot_ref, out_ref):
    slots = recv_ref.shape[0]
    choice, slot = choice_ref[...], slot_ref[...]
    dest = column_of(jnp.where(slot >= 0, choice * CAP + slot, slots))
    take = (wide(dest, slots) == iota((dest.shape[0], slots), 1).astype(f32)).astype(f32).astype(bf16)
    out_ref[...] = dot(take, recv_ref[...]).astype(bf16)


def spread(refs, me, tensor_size, width):
    quarter = width // tensor_size
    total = None
    for shift in range(tensor_size):
        first = lax.rem(me + tensor_size - shift, tensor_size) * quarter
        part = refs[shift][...]
        shape = (part.shape[1], width)
        row = iota(shape, 0)
        place = ((iota(shape, 1) == row + first) & (row < quarter)).astype(f32).astype(bf16)
        term = dot(part, place)
        total = term if total is None else total + term
    return total


def hidden_backward_kernel(
    tensor_size,
    hidden_ref, prob_ref, cot_ref, gain_ref, rw_ref, choice_ref, att_ref, *refs,
):
    parts = refs[:tensor_size]
    grad_hidden_ref, low_ref, sums_ref = refs[tensor_size:]
    me = lax.axis_index("tensor")
    hidden = hidden_ref[...]
    rows, width = hidden.shape
    quarter = width // tensor_size
    grad_routed = spread(parts, me, tensor_size, width)
    lane = iota((rows, quarter + EXTRA), 1)
    grad_gate = sum(
        jnp.sum(jnp.where(lane >= quarter, part[...].astype(f32), 0.0), -1, keepdims=True) for part in parts
    )
    prob = prob_ref[...]
    chosen = chosen_of(choice_ref[...], prob.shape[1])
    gate = jnp.sum(prob * chosen, -1, keepdims=True)
    grad_logits = (grad_gate * gate) * (chosen - prob)
    grad_normed = grad_routed + dot(grad_logits, rw_ref[...], NT, precision=highest)
    gain = gain_ref[...]
    scale = lax.rsqrt(jnp.mean(hidden * hidden, -1, keepdims=True) + norm_eps)
    scaled = grad_normed * gain
    grad_hidden = (
        cot_ref[...].astype(f32)
        + scale * scaled
        - hidden * (scale * scale * scale) * jnp.mean(scaled * hidden, -1, keepdims=True)
    )
    grad_hidden_ref[...] = grad_hidden
    low = grad_hidden.astype(bf16)
    low_ref[...] = low
    at, experts = att_ref.shape[1], prob.shape[1]
    sums_ref[pl.ds(0, at), :] = dot(att_ref[...], low, TN).astype(bf16)
    sums_ref[pl.ds(at, experts), :] = dot(
        grad_logits, hidden * scale * gain, TN, precision=highest
    ).astype(bf16)
    tail = sums_ref.shape[0] - at - experts
    grad_gain = jnp.sum(grad_normed * hidden * scale, 0, keepdims=True)
    high, middle, low_part = split3(grad_gain)
    row = iota((tail, width), 0)
    sums_ref[pl.ds(at + experts, tail), :] = jnp.where(
        row == 0, high, jnp.where(row == 1, middle, jnp.where(row == 2, low_part, 0.0))
    ).astype(bf16)


def output_kernel(tensor_size, hidden_ref, prob_ref, choice_ref, *refs):
    parts, out_ref = refs[:tensor_size], refs[tensor_size]
    hidden = hidden_ref[...]
    result = spread(parts, lax.axis_index("tensor"), tensor_size, hidden.shape[1])
    prob = prob_ref[...]
    gate = jnp.sum(prob * chosen_of(choice_ref[...], prob.shape[1]), -1, keepdims=True)
    out_ref[...] = (hidden + gate * result).astype(bf16)


def make(mesh):
    tensor_size = mesh.shape["tensor"]
    expert_size = mesh.shape["expert"]

    def shards(
        tokens,
        segment_ids,
        expert_choice,
        slot_index,
        first_gain,
        input_weight,
        bias_table,
        output_weight,
        second_gain,
        router_weight,
        expert_in,
        expert_out,
        cotangent,
    ):
        token_count, width = tokens.shape
        sequences, length = segment_ids.shape
        quarter = output_weight.shape[0]
        experts = router_weight.shape[1]
        local = expert_in.shape[0]
        slots = experts * CAP
        per = slots // local
        chunk = slots // expert_size
        buckets, heads = bias_table.shape
        expert_index = lax.axis_index("expert")
        seg = (segment_ids + 8 * jnp.arange(sequences, dtype=i32)[:, None]).reshape(1, token_count)
        choice = expert_choice.reshape(1, token_count)
        slot = slot_index.reshape(1, token_count)
        gain_first = first_gain.reshape(1, width)
        gain_second = second_gain.reshape(1, width)

        def shift_by(array, shift):
            return lax.ppermute(array, "tensor", [(i, (i + shift) % tensor_size) for i in range(tensor_size)])

        def gather_tensor(array):
            return [array] + [shift_by(array, s) for s in range(1, tensor_size)]

        def gather_weights(part):
            got = lax.all_gather(part, ("expert", "tensor"), axis=0)
            return got.reshape((expert_size, tensor_size) + part.shape)

        ow_rows = quarter // expert_size
        ow_part = lax.dynamic_slice_in_dim(output_weight, expert_index * ow_rows, ow_rows, 0)
        ow_all = jnp.swapaxes(gather_weights(ow_part), 0, 1).reshape(tensor_size, quarter, width)

        attended, first_normed = call(
            forward_kernel,
            [((token_count, quarter), bf16), ((token_count, width), bf16)],
            (tokens, gain_first, input_weight, bias_table, seg),
            [pltpu.VMEM((token_count + 2 * BLOCK, quarter), bf16)] * 2,
        )
        attended_parts = gather_tensor(attended)
        (cot_slots,) = call(cotangent_kernel, [((slots, width), bf16)], (cotangent, choice, slot))
        cot_recv = lax.all_to_all(cot_slots.reshape(expert_size, chunk, width), "expert", 0, 0)

        hidden, prob, send = call(
            lambda *refs: middle_kernel(tensor_size, *refs),
            [((token_count, width), f32), ((token_count, experts), f32), ((slots, width + 128), bf16)],
            (tokens, ow_all, gain_second, router_weight, choice, slot, *attended_parts),
        )
        recv = lax.all_to_all(send.reshape(expert_size, chunk, width + 128), "expert", 0, 0)

        iw_rows = width // expert_size
        iw_part = lax.dynamic_slice_in_dim(input_weight, expert_index * iw_rows, iw_rows, 1)
        bias_parts = jnp.stack(split3(bias_table)).astype(bf16).reshape(-1)
        bias_rows = -(-bias_parts.shape[0] // quarter)
        bias_rows = bias_rows + (-(3 * iw_rows + bias_rows)) % 16
        bias_parts = jnp.pad(bias_parts, (0, bias_rows * quarter - bias_parts.shape[0]))
        iw_got = gather_weights(
            jnp.concatenate([iw_part.reshape(3 * iw_rows, quarter), bias_parts.reshape(bias_rows, quarter)], 0)
        )
        iw_all = (
            iw_got[:, :, : 3 * iw_rows]
            .reshape(expert_size, tensor_size, 3, iw_rows, quarter)
            .transpose(1, 2, 0, 3, 4)
            .reshape(tensor_size, 3, width, quarter)
        )
        bias_all = jnp.sum(
            iw_got[0, :, 3 * iw_rows :]
            .reshape(tensor_size, bias_rows * quarter)[:, : 3 * buckets * heads]
            .reshape(tensor_size, 3, buckets, heads)
            .astype(f32),
            1,
        )

        whole = lambda shape: pl.BlockSpec(shape, lambda j: (0,) * len(shape))
        by_expert = pl.BlockSpec((per, width), lambda j: (j, 0))
        hidden_units = expert_in.shape[2]
        by_hidden = pl.BlockSpec((per, hidden_units), lambda j: (j, 0))
        outs = pl.pallas_call(
            lambda *refs: expert_kernel(tensor_size, expert_size, *refs),
            grid=(local,),
            in_specs=[
                whole((slots, width + 128)),
                whole((slots, width)),
                pl.BlockSpec((1, width, hidden_units), lambda j: (j, 0, 0)),
                pl.BlockSpec((1, hidden_units, width), lambda j: (j, 0, 0)),
            ],
            out_specs=[by_expert, by_expert, by_hidden, by_hidden, whole((slots, 128))]
            + [whole((slots, quarter))] * (2 * tensor_size),
            out_shape=[jax.ShapeDtypeStruct((slots, width), bf16)] * 2
            + [jax.ShapeDtypeStruct((slots, hidden_units), bf16)] * 2
            + [jax.ShapeDtypeStruct((slots, 128), bf16)]
            + [jax.ShapeDtypeStruct((slots, quarter), bf16)] * (2 * tensor_size),
            scratch_shapes=[pltpu.VMEM((slots, width), bf16)] * 5 + [pltpu.VMEM((slots, 128), bf16)],
            compiler_params=pltpu.CompilerParams(vmem_limit_bytes=56 * 2**20),
        )(recv.reshape(slots, width + 128), cot_recv.reshape(slots, width), expert_in, expert_out)
        expert_rows, grad_slots, expert_act, grad_act, dots = outs[:5]
        grad_chunks = outs[5 : 5 + tensor_size]
        result_chunks = outs[5 + tensor_size :]

        def reduce_tensor(chunks):
            total = chunks[0].astype(f32)
            for s in range(1, tensor_size):
                total = total + shift_by(chunks[s], s).astype(f32)
            return total.astype(bf16)

        def return_rows(rows):
            back = lax.all_to_all(rows.reshape(expert_size, chunk, rows.shape[1]), "expert", 0, 0)
            (out,) = call(
                back_kernel,
                [((token_count, rows.shape[1]), bf16)],
                (back.reshape(slots, rows.shape[1]), choice, slot),
            )
            return gather_tensor(out)

        grad_parts = return_rows(jnp.concatenate([reduce_tensor(grad_chunks), dots[:, :EXTRA]], 1))
        by = lambda array: array.reshape(local, per, array.shape[1])
        grad_expert_out = jnp.einsum("erf,erd->efd", by(expert_act), by(grad_slots), preferred_element_type=f32)
        grad_expert_in = jnp.einsum("erd,erf->edf", by(expert_rows), by(grad_act), preferred_element_type=f32)

        sum_rows = quarter + experts + 32
        grad_hidden, grad_low, early_sums = call(
            lambda *refs: hidden_backward_kernel(tensor_size, *refs),
            [((token_count, width), f32), ((token_count, width), bf16), ((sum_rows, width), bf16)],
            (hidden, prob, cotangent, gain_second, router_weight, choice, attended, *grad_parts),
        )
        result_parts = return_rows(reduce_tensor(result_chunks))
        (block_output,) = call(
            lambda *refs: output_kernel(tensor_size, *refs),
            [((token_count, width), bf16)],
            (hidden, prob, choice, *result_parts),
        )

        def expert_scatter(array):
            rows = array.shape[0] // expert_size
            got = lax.all_to_all(array.reshape(expert_size, rows, array.shape[1]), "expert", 0, 0)
            return jnp.sum(got.astype(f32), 0)

        def expert_gather(array):
            return lax.all_gather(array, "expert", axis=0)

        early = expert_gather(expert_scatter(early_sums).astype(bf16)).reshape(sum_rows, width).astype(f32)
        grad_output_weight = early[:quarter]
        grad_router_weight = early[quarter : quarter + experts].T
        grad_second_gain = jnp.sum(early[quarter + experts :], 0)

        padded = token_count + 2 * BLOCK
        scratch = [pltpu.VMEM((padded, quarter), bf16)] * 2 + [pltpu.VMEM((padded, quarter), f32)] * 2
        scratch = scratch + [pltpu.VMEM((token_count, quarter), bf16)]
        grad_iw, own_parts, table_grad = call(
            own_backward_kernel,
            [((3, width, quarter), bf16), ((3, token_count, quarter), bf16), ((buckets, 128), f32)],
            (first_normed, input_weight, output_weight, bias_table, seg, grad_low),
            scratch,
        )
        grad_tokens, gain_grad = call(
            lambda *refs: rest_backward_kernel(tensor_size, *refs),
            [((token_count, width), f32), ((1, width), f32)],
            (
                first_normed, iw_all, ow_all, bias_all, seg, grad_low, own_parts, tokens, gain_first, grad_hidden,
            ),
            [pltpu.VMEM((token_count, width), f32)] + scratch,
        )
        iw_sum = expert_scatter(grad_iw.reshape(3 * width, quarter)).astype(bf16)
        tail = jnp.concatenate([gain_grad.reshape(-1), table_grad[:, :heads].reshape(-1)])
        tail_size = tail.shape[0]
        tail = jnp.stack(split3(tail)).astype(bf16).reshape(-1)
        tail_rows = -(-tail.shape[0] // quarter)
        tail_rows = tail_rows + (-(iw_sum.shape[0] + tail_rows)) % 16
        tail = jnp.pad(tail, (0, tail_rows * quarter - tail.shape[0])).reshape(tail_rows, quarter)
        late = expert_gather(jnp.concatenate([iw_sum, tail], 0))
        grad_input_weight = late[:, : iw_sum.shape[0]].reshape(3, width, quarter).astype(f32)
        tail = late[:, iw_sum.shape[0] :].reshape(expert_size, -1)[:, : 3 * tail_size].astype(f32)
        tail = jnp.sum(tail.reshape(expert_size * 3, tail_size), 0)
        grad_first_gain = tail[:width]
        grad_bias_table = tail[width:].reshape(buckets, heads)
        return (
            block_output,
            grad_tokens,
            grad_first_gain,
            grad_input_weight,
            grad_bias_table,
            grad_output_weight,
            grad_second_gain,
            grad_router_weight,
            grad_expert_in,
            grad_expert_out,
        )

    return shards


def solution(mesh):
    placed = (
        P("expert", None),
        P("expert", None),
        P("expert"),
        P("expert"),
        P(),
        P(None, None, "tensor"),
        P(None, "tensor"),
        P("tensor", None),
        P(),
        P(),
        P("expert", None, "tensor"),
        P("expert", "tensor", None),
        P("expert", None),
    )
    return jax.shard_map(
        make(mesh),
        mesh=mesh,
        in_specs=placed,
        out_specs=(
            P("expert", None),
            P("expert", None),
            P(),
            P(None, None, "tensor"),
            P(None, "tensor"),
            P("tensor", None),
            P(),
            P(),
            P("expert", None, "tensor"),
            P("expert", "tensor", None),
        ),
        check_vma=False,
    )
```

```python
import math

import jax
import jax.numpy as jnp
from jax import lax
from jax.experimental import pallas as pl
from jax.experimental.pallas import tpu as pltpu
from jax.sharding import PartitionSpec as P

CAP = 10

bucket_edges = (12, 16, 23, 32, 46, 64, 91)
norm_eps = 1e-06
masked_score = -1e30
gelu_const = math.sqrt(2.0 / math.pi)
gelu_cubic = 0.044715

BLOCK = 128
BAND = 3 * BLOCK
ROLL = 4 * BLOCK
HEAD = 64
EXTRA = 16

bf16 = jnp.bfloat16
f32 = jnp.float32
i32 = jnp.int32
highest = lax.Precision.HIGHEST

NN = (((1,), (0,)), ((), ()))
NT = (((1,), (1,)), ((), ()))
TN = (((0,), (0,)), ((), ()))


def dot(left, right, dims=NN, precision=None):
    return lax.dot_general(left, right, dims, precision=precision, preferred_element_type=f32)


def iota(shape, axis):
    return lax.broadcasted_iota(i32, shape, axis)


def call(kernel, outs, args, scratch=(), **extra):
    vmem = pl.BlockSpec(memory_space=pltpu.VMEM)
    return pl.pallas_call(
        kernel,
        out_shape=[jax.ShapeDtypeStruct(shape, dtype) for shape, dtype in outs],
        in_specs=[vmem] * len(args),
        out_specs=[vmem] * len(outs),
        scratch_shapes=list(scratch),
        compiler_params=pltpu.CompilerParams(vmem_limit_bytes=56 * 2**20),
        **extra,
    )(*args)


def split3(value):
    high = value.astype(bf16).astype(f32)
    rest = value - high
    middle = rest.astype(bf16).astype(f32)
    return high, middle, rest - middle


def columns3(value, width):
    high, middle, low = split3(value)
    lane = iota((value.shape[0], width), 1)
    picked = jnp.where(lane == 0, high, jnp.where(lane == 1, middle, jnp.where(lane == 2, low, 0.0)))
    return picked.astype(bf16)


def column_of(row):
    return jnp.transpose(jnp.broadcast_to(row.astype(f32), (128, row.shape[1])))


def wide(column, width):
    return jnp.concatenate([column] * (width // 128), 1)


def bucket_of(relative):
    distance = jnp.abs(relative)
    beyond = jnp.zeros_like(distance)
    for threshold in bucket_edges:
        beyond = beyond + (distance >= threshold).astype(i32)
    magnitude = jnp.where(distance < 8, distance, 8 + beyond)
    return magnitude + 16 * (relative > 0).astype(i32)


def band_rows(table):
    buckets = table.shape[1]
    offset = iota((buckets, ROLL), 1)
    relative = jnp.where(offset < BAND, offset, offset - ROLL) - BLOCK
    onehot = (bucket_of(relative) == iota((buckets, ROLL), 0)).astype(f32)
    return dot(table, onehot, precision=highest), onehot


def bias_tiles(table):
    rows, onehot = band_rows(table)
    tiles = []
    for h in range(table.shape[0]):
        full = jnp.broadcast_to(rows[h : h + 1], (BLOCK, ROLL))
        tiles.append(jnp.transpose(pltpu.roll(full, 0, 1, stride=1, stride_axis=0)[:, :BAND]))
    return tiles, onehot


def head_masks(heads):
    lane = iota((1, heads * HEAD), 1)
    return [((lane >= h * HEAD) & (lane < (h + 1) * HEAD)).astype(f32).astype(bf16) for h in range(heads)]


def padded_segments(seg):
    edge = jnp.full((1, BLOCK), -1.0, f32)
    return column_of(jnp.concatenate([edge, seg, edge], 1))


def first_norm(tok, gain):
    scale = lax.rsqrt(jnp.mean(tok * tok, -1, keepdims=True) + norm_eps)
    return (tok * scale * gain).astype(bf16), scale


def probabilities(scores, bias, same):
    scores = jnp.where(same, scores + bias, masked_score)
    weights = jnp.exp(scores - jnp.max(scores, 0, keepdims=True))
    return weights * (1.0 / jnp.sum(weights, 0, keepdims=True))


def stack_heads(rows, masks):
    return jnp.concatenate([rows * mask for mask in masks], 0)


def own_blocks(product, heads):
    return jnp.concatenate(
        [product[h * HEAD : (h + 1) * HEAD, h * BLOCK : (h + 1) * BLOCK] for h in range(heads)], 0
    )


def fill_rows(ref, value):
    rows = value.shape[0]
    edge = jnp.zeros((BLOCK, value.shape[1]), bf16)
    ref[pl.ds(0, BLOCK), :] = edge
    ref[pl.ds(rows + BLOCK, BLOCK), :] = edge
    ref[pl.ds(BLOCK, rows), :] = value


def fill_columns(ref, value):
    rows = value.shape[1]
    edge = jnp.zeros((value.shape[0], BLOCK), bf16)
    ref[:, pl.ds(0, BLOCK)] = edge
    ref[:, pl.ds(rows + BLOCK, BLOCK)] = edge
    ref[:, pl.ds(BLOCK, rows)] = value


def forward_kernel(tok_ref, gain_ref, iw_ref, bt_ref, seg_ref, att_ref, normed_ref, keys, values):
    rows = tok_ref.shape[0]
    normed, _ = first_norm(tok_ref[...].astype(f32), gain_ref[...])
    normed_ref[...] = normed
    queries = dot(normed, iw_ref[0], NT).astype(bf16)
    fill_rows(keys, dot(normed, iw_ref[1], NT).astype(bf16))
    fill_columns(values, dot(iw_ref[2], normed, NT).astype(bf16))
    seg = seg_ref[...].astype(f32)
    seg_keys = padded_segments(seg)
    tiles, _ = bias_tiles(bt_ref[...])
    heads = len(tiles)
    masks = head_masks(heads)
    for block in range(rows // BLOCK):
        at = block * BLOCK
        same = seg_keys[at : at + BAND] == seg[:, at : at + BLOCK]
        scores = dot(keys[pl.ds(at, BAND), :], stack_heads(queries[at : at + BLOCK], masks), NT)
        weights = [
            probabilities(scores[:, h * BLOCK : (h + 1) * BLOCK], tiles[h], same).astype(bf16) for h in range(heads)
        ]
        product = dot(values[:, pl.ds(at, BAND)], jnp.concatenate(weights, 1))
        att_ref[:, pl.ds(at, BLOCK)] = own_blocks(product, heads).astype(bf16)


def group_backward(normed, weight, out_weight, table, seg, grad_low, scratch, bias_grads):
    keys, values, keys_across, grad_keys, grad_values, grad_queries = scratch
    rows = normed.shape[0]
    queries = dot(normed, weight[0], NT).astype(bf16)
    fill_rows(keys, dot(normed, weight[1], NT).astype(bf16))
    fill_columns(keys_across, dot(weight[1], normed, NT).astype(bf16))
    fill_rows(values, dot(normed, weight[2], NT).astype(bf16))
    grad_att = dot(grad_low, out_weight, NT).astype(bf16)
    grad_keys[...] = jnp.zeros(grad_keys.shape, f32)
    grad_values[...] = jnp.zeros(grad_values.shape, f32)
    seg_keys = padded_segments(seg)
    tiles, onehot = bias_tiles(table)
    heads = len(tiles)
    masks = head_masks(heads)
    sums = [None] * heads
    for block in range(rows // BLOCK):
        at = block * BLOCK
        same = seg_keys[at : at + BAND] == seg[:, at : at + BLOCK]
        head_queries = stack_heads(queries[at : at + BLOCK], masks)
        head_grads = stack_heads(grad_att[at : at + BLOCK], masks)
        scores = dot(keys[pl.ds(at, BAND), :], head_queries, NT)
        grad_probs = dot(values[pl.ds(at, BAND), :], head_grads, NT)
        all_weights, all_grads = [], []
        for h in range(heads):
            columns = slice(h * BLOCK, (h + 1) * BLOCK)
            weights = probabilities(scores[:, columns], tiles[h], same)
            scaled = weights * grad_probs[:, columns]
            grad_scores = scaled - weights * jnp.sum(scaled, 0, keepdims=True)
            all_weights.append(weights.astype(bf16))
            all_grads.append(grad_scores.astype(bf16))
            if bias_grads:
                sums[h] = grad_scores if sums[h] is None else sums[h] + grad_scores
        low = jnp.concatenate(all_grads, 1)
        grad_queries[:, pl.ds(at, BLOCK)] = own_blocks(dot(keys_across[:, pl.ds(at, BAND)], low), heads)
        grad_keys[pl.ds(at, BAND), :] += dot(low, head_queries)
        grad_values[pl.ds(at, BAND), :] += dot(jnp.concatenate(all_weights, 1), head_grads)
    parts = (
        jnp.transpose(grad_queries[...]).astype(bf16),
        grad_keys[pl.ds(BLOCK, rows), :].astype(bf16),
        grad_values[pl.ds(BLOCK, rows), :].astype(bf16),
    )
    if not bias_grads:
        return parts, None
    buckets = table.shape[1]
    lane = iota((buckets, 128), 1)
    table_grad = jnp.zeros((buckets, 128), f32)
    row_index = iota((BLOCK, ROLL), 0)
    for h in range(heads):
        moved = jnp.concatenate([jnp.transpose(sums[h]), jnp.zeros((BLOCK, ROLL - BAND), f32)], 1)
        step = 1
        while step < BLOCK:
            moved = jnp.where((row_index & step) != 0, pltpu.roll(moved, ROLL - step, 1), moved)
            step *= 2
        diagonal = jnp.sum(moved, 0, keepdims=True)
        bucket_sum = jnp.sum(onehot * diagonal, 1, keepdims=True)
        table_grad = table_grad + jnp.where(lane == h, bucket_sum, 0.0)
    return parts, table_grad


def own_backward_kernel(normed_ref, iw_ref, ow_ref, bt_ref, seg_ref, low_ref, grad_iw_ref, parts_ref, table_ref, *scratch):
    normed = normed_ref[...]
    parts, table_grad = group_backward(
        normed, iw_ref, ow_ref[...], bt_ref[...], seg_ref[...].astype(f32), low_ref[...], scratch, True
    )
    table_ref[...] = table_grad
    width = ow_ref.shape[0]
    for j in range(3):
        parts_ref[j] = parts[j]
        grad_iw_ref[pl.ds(j * width, width), :] = dot(parts[j], normed, TN).astype(bf16)


def rest_backward_kernel(
    normed_ref, iw_ref, ow_ref, bt_ref, seg_ref, low_ref, parts_ref, tok_ref, gain_ref, grad_hidden_ref,
    grad_tok_ref, grad_gain_ref, total, *scratch,
):
    width = ow_ref.shape[1]

    def add(parts, group):
        return sum(dot(parts[j], iw_ref[group, pl.ds(j * width, width), :]) for j in range(3))

    total[...] = add(parts_ref, 0)

    def step(group, carry):
        weight = [iw_ref[group, pl.ds(j * width, width), :] for j in range(3)]
        parts, _ = group_backward(
            normed_ref[...], weight, ow_ref[group], bt_ref[group], seg_ref[...].astype(f32), low_ref[...], scratch, False
        )
        total[...] += add(parts, group)
        return carry

    lax.fori_loop(1, ow_ref.shape[0], step, 0)
    tok = tok_ref[...].astype(f32)
    gain = gain_ref[...]
    scale = lax.rsqrt(jnp.mean(tok * tok, -1, keepdims=True) + norm_eps)
    grad_normed = total[...]
    grad_gain_ref[...] = jnp.sum(grad_normed * tok * scale, 0, keepdims=True)
    scaled = grad_normed * gain
    grad_tok_ref[...] = (
        grad_hidden_ref[...]
        + scale * scaled
        - tok * (scale * scale * scale) * jnp.mean(scaled * tok, -1, keepdims=True)
    )


def slot_onehot(choice, slot, slots):
    dest = jnp.where(slot >= 0, choice * CAP + slot, slots)
    return (iota((slots, dest.shape[1]), 0) == dest).astype(f32).astype(bf16)


def slot_order(slots, group, across):
    index = iota((1, slots), 1)
    big, small = slots // across, slots // group
    outer, rest = lax.div(index, big), lax.rem(index, big)
    target = lax.div(rest, CAP) * small + outer * CAP + lax.rem(rest, CAP)
    return (iota((slots, slots), 0) == target).astype(f32).astype(bf16)


def cotangent_kernel(cot_ref, choice_ref, slot_ref, out_ref):
    fill = slot_onehot(choice_ref[...], slot_ref[...], out_ref.shape[0])
    out_ref[...] = dot(fill, cot_ref[...]).astype(bf16)


def order_kernel(sources, local, rows_ref, out_ref):
    out_ref[...] = dot(slot_order(rows_ref.shape[0], local, sources), rows_ref[...]).astype(bf16)


def chosen_of(choice, experts):
    column = column_of(choice)[:, :experts]
    return (column == iota(column.shape, 1).astype(f32)).astype(f32)


def middle_kernel(tok_ref, ow_ref, gain_ref, rw_ref, choice_ref, slot_ref, *refs):
    att_refs, (hidden_ref, prob_ref, send_ref) = refs[:-3], refs[-3:]
    hidden = tok_ref[...].astype(f32)
    for shift, att_ref in enumerate(att_refs):
        hidden = hidden + dot(att_ref[...], ow_ref[shift], TN)
    hidden_ref[...] = hidden
    scale = lax.rsqrt(jnp.mean(hidden * hidden, -1, keepdims=True) + norm_eps)
    normed = hidden * scale * gain_ref[...]
    logits = dot(normed, rw_ref[...], NT, precision=highest)
    raised = jnp.exp(logits - jnp.max(logits, -1, keepdims=True))
    prob = raised * (1.0 / jnp.sum(raised, -1, keepdims=True))
    prob_ref[...] = prob
    gate = jnp.sum(prob * chosen_of(choice_ref[...], prob.shape[1]), -1, keepdims=True)
    width = normed.shape[1]
    fill = slot_onehot(choice_ref[...], slot_ref[...], send_ref.shape[0])
    send_ref[:, :width] = dot(fill, normed.astype(bf16)).astype(bf16)
    send_ref[:, width:] = dot(fill, columns3(gate, 128)).astype(bf16)


def expert_kernel(
    tensor_size, sources, unroll,
    recv_ref, cot_ref, win_ref, wout_ref,
    rows_ref, grads_ref, act_ref, grad_act_ref, dots_ref, result_ref, *refs,
):
    chunks = refs[:tensor_size]
    x_all, g_all, r_all, d_all, turned = refs[tensor_size:]
    slots = recv_ref.shape[0]
    width = cot_ref.shape[1]
    step = pl.program_id(0)
    local = pl.num_programs(0) * unroll
    per = rows_ref.shape[0] // unroll

    @pl.when(step == 0)
    def _():
        order = slot_order(slots, win_ref.shape[0] * (slots // rows_ref.shape[0]), sources)
        x_all[...] = dot(order, recv_ref[:, :width]).astype(bf16)
        gate = jnp.sum(dot(order, recv_ref[:, width:]), -1, keepdims=True)
        g_all[...] = (gate * cot_ref[...].astype(f32)).astype(bf16)

    for u in range(unroll):
        here = pl.ds(u * per, per)
        at = pl.ds(pl.multiple_of((step * unroll + u) * per, 16), per)
        x = x_all[at, :]
        g = g_all[at, :]
        weight_in = win_ref[u]
        weight_out = wout_ref[u]
        pre = dot(x, weight_in)
        grad_act = dot(g, weight_out, NT)
        inner = jnp.tanh(gelu_const * (pre + gelu_cubic * pre * pre * pre))
        act = (0.5 * pre * (1.0 + inner)).astype(bf16)
        slope = 0.5 * (1.0 + inner) + 0.5 * pre * (1.0 - inner * inner) * gelu_const * (
            1.0 + 3.0 * gelu_cubic * pre * pre
        )
        grad_act = (grad_act * slope).astype(bf16)
        r_all[at, :] = dot(grad_act, weight_in, NT).astype(bf16)
        result = dot(act, weight_out)
        result_ref[here, :] = result.astype(bf16)
        d_all[at, :] = columns3(jnp.sum(result * cot_ref[at, :].astype(f32), -1, keepdims=True), 128)
        rows_ref[here, :] = x
        grads_ref[here, :] = g
        act_ref[here, :] = act
        grad_act_ref[here, :] = grad_act

    @pl.when(step == pl.num_programs(0) - 1)
    def _():
        order = slot_order(slots, win_ref.shape[0] * (slots // rows_ref.shape[0]), sources)
        dots_ref[...] = dot(d_all[...], order, TN)[:EXTRA].astype(bf16)
        turn_chunks(tensor_size, dot(r_all[...], order, TN).astype(bf16), turned, chunks)


def turn_chunks(tensor_size, rows, turned, chunks):
    turned[...] = rows
    quarter = rows.shape[0] // tensor_size
    me = lax.axis_index("tensor")
    for shift in range(tensor_size):
        first = lax.rem(me + shift, tensor_size) * quarter
        chunks[shift][...] = turned[pl.ds(pl.multiple_of(first, 64), quarter), :]


def result_kernel(tensor_size, sources, local, rows_ref, *refs):
    order = slot_order(rows_ref.shape[0], local, sources)
    turn_chunks(tensor_size, dot(rows_ref[...], order, TN).astype(bf16), refs[tensor_size], refs[:tensor_size])


def sum_kernel(with_dots, *refs):
    *parts, out_ref = refs
    total = sum(ref[...].astype(f32) for ref in (parts[:-1] if with_dots else parts))
    extra = [parts[-1][...].astype(f32)] if with_dots else []
    rows = total.shape[0] + EXTRA * len(extra)
    blank = jnp.zeros((out_ref.shape[1] - rows, total.shape[1]), f32)
    out_ref[...] = jnp.transpose(jnp.concatenate([total] + extra + [blank], 0)).astype(bf16)


def back_kernel(recv_ref, choice_ref, slot_ref, out_ref):
    fill = slot_onehot(choice_ref[...], slot_ref[...], recv_ref.shape[0])
    out_ref[...] = dot(recv_ref[...], fill, TN)[: out_ref.shape[0]].astype(bf16)


def spread(refs, quarter, turned):
    size = len(refs)
    me = lax.axis_index("tensor")
    for shift, ref in enumerate(refs):
        first = lax.rem(me + size - shift, size) * quarter
        turned[pl.ds(pl.multiple_of(first, 64), quarter), :] = ref[pl.ds(0, quarter), :].astype(f32)
    return jnp.transpose(turned[...])


def hidden_backward_kernel(
    hidden_ref, prob_ref, cot_ref, gain_ref, rw_ref, choice_ref, att_ref, *refs,
):
    parts = refs[:-4]
    grad_hidden_ref, low_ref, sums_ref, turned = refs[-4:]
    hidden = hidden_ref[...]
    rows, width = hidden.shape
    quarter = width // len(parts)
    grad_routed = spread(parts, quarter, turned)
    dots = sum(jnp.sum(ref[pl.ds(quarter, EXTRA), :].astype(f32), 0, keepdims=True) for ref in parts)
    prob = prob_ref[...]
    chosen = chosen_of(choice_ref[...], prob.shape[1])
    gate = jnp.sum(prob * chosen, -1, keepdims=True)
    grad_gate = column_of(dots)[:, :1]
    grad_logits = (grad_gate * gate) * (chosen - prob)
    grad_normed = grad_routed + dot(grad_logits, rw_ref[...], precision=highest)
    gain = gain_ref[...]
    scale = lax.rsqrt(jnp.mean(hidden * hidden, -1, keepdims=True) + norm_eps)
    scaled = grad_normed * gain
    grad_hidden = (
        cot_ref[...].astype(f32)
        + scale * scaled
        - hidden * (scale * scale * scale) * jnp.mean(scaled * hidden, -1, keepdims=True)
    )
    grad_hidden_ref[...] = grad_hidden
    low = grad_hidden.astype(bf16)
    low_ref[...] = low
    at, experts = att_ref.shape[0], prob.shape[1]
    sums_ref[pl.ds(0, at), :] = dot(att_ref[...], low).astype(bf16)
    sums_ref[pl.ds(at, experts), :] = dot(
        grad_logits, hidden * scale * gain, TN, precision=highest
    ).astype(bf16)
    tail = sums_ref.shape[0] - at - experts
    high, middle, low_part = split3(jnp.sum(grad_normed * hidden * scale, 0, keepdims=True))
    row = iota((tail, width), 0)
    sums_ref[pl.ds(at + experts, tail), :] = jnp.where(
        row == 0, high, jnp.where(row == 1, middle, jnp.where(row == 2, low_part, 0.0))
    ).astype(bf16)


def output_kernel(hidden_ref, prob_ref, choice_ref, *refs):
    parts, (out_ref, turned) = refs[:-2], refs[-2:]
    hidden = hidden_ref[...]
    result = spread(parts, hidden.shape[1] // len(parts), turned)
    prob = prob_ref[...]
    gate = jnp.sum(prob * chosen_of(choice_ref[...], prob.shape[1]), -1, keepdims=True)
    out_ref[...] = (hidden + gate * result).astype(bf16)


def make(mesh):
    tensor_size = mesh.shape["tensor"]
    expert_size = mesh.shape["expert"]

    def shards(
        tokens,
        segment_ids,
        expert_choice,
        slot_index,
        first_gain,
        input_weight,
        bias_table,
        output_weight,
        second_gain,
        router_weight,
        expert_in,
        expert_out,
        cotangent,
    ):
        token_count, width = tokens.shape
        sequences, length = segment_ids.shape
        quarter = output_weight.shape[0]
        experts = router_weight.shape[1]
        local = expert_in.shape[0]
        hidden_units = expert_in.shape[2]
        slots = experts * CAP
        per = slots // local
        chunk = slots // expert_size
        buckets, heads = bias_table.shape
        expert_index = lax.axis_index("expert")
        seg = (segment_ids + 8 * jnp.arange(sequences, dtype=i32)[:, None]).reshape(1, token_count)
        choice = expert_choice.reshape(1, token_count)
        slot = slot_index.reshape(1, token_count)
        gain_first = first_gain.reshape(1, width)
        gain_second = second_gain.reshape(1, width)
        iw_own = jnp.swapaxes(input_weight, 1, 2)
        table = bias_table.T
        rw = router_weight.T
        after = lax.optimization_barrier

        def gather_tensor(array):
            shifts = [[(i, (i + s) % tensor_size) for i in range(tensor_size)] for s in range(1, tensor_size)]
            return [array] + [lax.ppermute(array, "tensor", pairs) for pairs in shifts]

        def gather_weights(part):
            planes = jnp.stack(gather_tensor(part))
            got = lax.all_gather(planes, "expert", axis=0)
            return got

        def joined(got):
            return jnp.swapaxes(got, 0, 1).reshape(tensor_size, -1, got.shape[-1])

        def exchange(array):
            rows = array.shape[0] // expert_size
            got = lax.all_to_all(array.reshape(expert_size, rows, array.shape[1]), "expert", 0, 0)
            return got.reshape(array.shape)

        ow_rows = quarter // expert_size
        ow_all = joined(gather_weights(lax.dynamic_slice_in_dim(output_weight, expert_index * ow_rows, ow_rows, 0)))

        attended, first_normed = call(
            forward_kernel,
            [((quarter, token_count), bf16), ((token_count, width), bf16)],
            (tokens, gain_first, iw_own, table, seg),
            [
                pltpu.VMEM((token_count + 2 * BLOCK, quarter), bf16),
                pltpu.VMEM((quarter, token_count + 2 * BLOCK), bf16),
            ],
        )
        attended_parts = gather_tensor(attended)
        (cot_slots,) = call(cotangent_kernel, [((slots, width), bf16)], (cotangent, choice, slot))
        (cot_rows,) = call(
            lambda *refs: order_kernel(expert_size, local, *refs), [((slots, width), bf16)], (exchange(cot_slots),)
        )

        hidden, prob, send = call(
            middle_kernel,
            [((token_count, width), f32), ((token_count, experts), f32), ((slots, width + 128), bf16)],
            (tokens, ow_all, gain_second, rw, choice, slot, *attended_parts),
        )
        recv = exchange(send)

        iw_rows = 3 * quarter // expert_size
        iw_part = lax.dynamic_slice_in_dim(iw_own.reshape(3 * quarter, width), expert_index * iw_rows, iw_rows, 0)
        bias_parts = jnp.stack(split3(table)).astype(bf16).reshape(-1)
        bias_parts = jnp.pad(bias_parts, (0, 8 * width - bias_parts.shape[0])).reshape(8, width)
        iw_part, _ = after((jnp.concatenate([iw_part, bias_parts], 0), send))
        iw_got = gather_weights(iw_part)
        iw_all = joined(iw_got[:, :, :iw_rows])
        bias_all = jnp.sum(
            iw_got[0, :, iw_rows:]
            .reshape(tensor_size, -1)[:, : 3 * buckets * heads]
            .reshape(tensor_size, 3, heads, buckets)
            .astype(f32),
            1,
        )

        unroll = 2 if local % 2 == 0 else 1
        whole = lambda shape: pl.BlockSpec(shape, lambda j: (0,) * len(shape))
        by_expert = pl.BlockSpec((unroll * per, width), lambda j: (j, 0))
        by_hidden = pl.BlockSpec((unroll * per, hidden_units), lambda j: (j, 0))
        outs = pl.pallas_call(
            lambda *refs: expert_kernel(tensor_size, expert_size, unroll, *refs),
            grid=(local // unroll,),
            in_specs=[
                whole((slots, width + 128)),
                whole((slots, width)),
                pl.BlockSpec((unroll, width, hidden_units), lambda j: (j, 0, 0)),
                pl.BlockSpec((unroll, hidden_units, width), lambda j: (j, 0, 0)),
            ],
            out_specs=[by_expert, by_expert, by_hidden, by_hidden, whole((EXTRA, slots)), by_expert]
            + [whole((quarter, slots))] * tensor_size,
            out_shape=[jax.ShapeDtypeStruct((slots, width), bf16)] * 2
            + [jax.ShapeDtypeStruct((slots, hidden_units), bf16)] * 2
            + [jax.ShapeDtypeStruct((EXTRA, slots), bf16), jax.ShapeDtypeStruct((slots, width), bf16)]
            + [jax.ShapeDtypeStruct((quarter, slots), bf16)] * tensor_size,
            scratch_shapes=[pltpu.VMEM((slots, width), bf16)] * 3
            + [pltpu.VMEM((slots, 128), bf16), pltpu.VMEM((width, slots), bf16)],
            compiler_params=pltpu.CompilerParams(vmem_limit_bytes=56 * 2**20),
        )(recv, cot_rows, expert_in, expert_out)
        expert_rows, grad_slots, expert_act, grad_act, dots, result_rows = outs[:6]
        grad_chunks = outs[6:]

        def trade_chunks(chunks):
            shifts = [[(i, (i + s) % tensor_size) for i in range(tensor_size)] for s in range(1, tensor_size)]
            return [chunks[0]] + [lax.ppermute(c, "tensor", pairs) for c, pairs in zip(chunks[1:], shifts)]

        def sum_rows(parts, with_dots):
            columns = -(-(quarter + (EXTRA if with_dots else 0)) // 128) * 128
            return call(lambda *refs: sum_kernel(with_dots, *refs), [((slots, columns), bf16)], parts)[0]

        def own_tokens(rows, kept):
            return call(back_kernel, [((kept, token_count), bf16)], (rows, choice, slot))[0]

        by = lambda array: array.reshape(local, per, array.shape[1])
        grad_expert_out = jnp.einsum("erf,erd->efd", by(expert_act), by(grad_slots), preferred_element_type=f32)
        grad_expert_in = jnp.einsum("erd,erf->edf", by(expert_rows), by(grad_act), preferred_element_type=f32)

        summed = sum_rows(trade_chunks(grad_chunks) + [dots], True)
        summed, grad_expert_out = after((summed, grad_expert_out))
        returned = own_tokens(exchange(summed), quarter + EXTRA)
        returned, grad_expert_in = after((returned, grad_expert_in))
        result_rows, _ = after((result_rows, returned))
        result_chunks = call(
            lambda *refs: result_kernel(tensor_size, expert_size, local, *refs),
            [((quarter, slots), bf16)] * tensor_size,
            (result_rows,),
            [pltpu.VMEM((width, slots), bf16)],
        )
        grad_parts = gather_tensor(returned)
        grad_parts, result_chunks, iw_all, bias_all = after((grad_parts, result_chunks, iw_all, bias_all))

        early_rows = quarter + experts + 64
        grad_hidden, grad_low, early_sums = call(
            hidden_backward_kernel,
            [((token_count, width), f32), ((token_count, width), bf16), ((early_rows, width), bf16)],
            (hidden, prob, cotangent, gain_second, rw, choice, attended, *grad_parts),
            [pltpu.VMEM((width, token_count), f32)],
        )
        result_sum = sum_rows(trade_chunks(result_chunks), False)
        result_parts = gather_tensor(own_tokens(exchange(result_sum), quarter))
        (block_output,) = call(
            output_kernel,
            [((token_count, width), bf16)],
            (hidden, prob, choice, *result_parts),
            [pltpu.VMEM((width, token_count), f32)],
        )

        def sum_experts(array):
            return jnp.sum(exchange(array).reshape(expert_size, -1, array.shape[1]).astype(f32), 0).astype(bf16)

        padded = token_count + 2 * BLOCK
        scratch = [pltpu.VMEM((padded, quarter), bf16)] * 2 + [pltpu.VMEM((quarter, padded), bf16)]
        scratch = scratch + [pltpu.VMEM((padded, quarter), f32)] * 2 + [pltpu.VMEM((quarter, token_count), f32)]
        grad_iw, own_parts, table_grad = call(
            own_backward_kernel,
            [((3 * quarter, width), bf16), ((3, token_count, quarter), bf16), ((buckets, 128), f32)],
            (first_normed, iw_own, output_weight, table, seg, grad_low),
            scratch,
        )
        grad_tokens, gain_grad = call(
            rest_backward_kernel,
            [((token_count, width), f32), ((1, width), f32)],
            (first_normed, iw_all, ow_all, bias_all, seg, grad_low, own_parts, tokens, gain_first, grad_hidden),
            [pltpu.VMEM((token_count, width), f32)] + scratch,
        )
        iw_sum = sum_experts(grad_iw)
        early_sum = sum_experts(early_sums)
        tail = jnp.stack(split3(table_grad[:, :heads].T)).reshape(1, -1)
        tail = jnp.pad(tail, ((0, 4), (0, width - tail.shape[1])))
        tail = jnp.concatenate(list(split3(gain_grad)) + [tail], 0).astype(bf16)
        late = lax.all_gather(jnp.concatenate([iw_sum, early_sum, tail], 0), "expert", axis=0)
        cut = iw_sum.shape[0]
        grad_input_weight = late[:, :cut].reshape(3, quarter, width).astype(f32)
        early = late[:, cut : cut + early_sum.shape[0]].reshape(early_rows, width).astype(f32)
        tail = jnp.sum(late[:, cut + early_sum.shape[0] :].astype(f32), 0)
        grad_table = jnp.sum(tail[3, : 3 * buckets * heads].reshape(3, heads, buckets), 0)
        return (
            block_output,
            grad_tokens,
            jnp.sum(tail[:3], 0),
            jnp.swapaxes(grad_input_weight, 1, 2),
            grad_table.T,
            early[:quarter],
            jnp.sum(early[quarter + experts :], 0),
            early[quarter : quarter + experts].T,
            grad_expert_in,
            grad_expert_out,
        )

    return shards


def solution(mesh):
    placed = (
        P("expert", None),
        P("expert", None),
        P("expert"),
        P("expert"),
        P(),
        P(None, None, "tensor"),
        P(None, "tensor"),
        P("tensor", None),
        P(),
        P(),
        P("expert", None, "tensor"),
        P("expert", "tensor", None),
        P("expert", None),
    )
    return jax.shard_map(
        make(mesh),
        mesh=mesh,
        in_specs=placed,
        out_specs=(
            P("expert", None),
            P("expert", None),
            P(),
            P(None, None, "tensor"),
            P(None, "tensor"),
            P("tensor", None),
            P(),
            P(),
            P("expert", None, "tensor"),
            P("expert", "tensor", None),
        ),
        check_vma=False,
    )
```

```python
import math

import jax
import jax.numpy as jnp
from jax import lax
from jax.experimental import pallas as pl
from jax.experimental.pallas import tpu as pltpu
from jax.sharding import PartitionSpec as P

CAP = 10

bucket_edges = (12, 16, 23, 32, 46, 64, 91)
norm_eps = 1e-06
masked_score = -1e30
gelu_const = math.sqrt(2.0 / math.pi)
gelu_cubic = 0.044715

BLOCK = 128
BAND = 3 * BLOCK
ROLL = 4 * BLOCK
HEAD = 64
EXTRA = 16

bf16 = jnp.bfloat16
f32 = jnp.float32
i32 = jnp.int32
highest = lax.Precision.HIGHEST

NN = (((1,), (0,)), ((), ()))
NT = (((1,), (1,)), ((), ()))
TN = (((0,), (0,)), ((), ()))


def dot(left, right, dims=NN, precision=None):
    return lax.dot_general(left, right, dims, precision=precision, preferred_element_type=f32)


def dot3(left, right, dims=NN):
    left_high, right_high = left.astype(bf16), right.astype(bf16)
    left_low = (left - left_high.astype(f32)).astype(bf16)
    right_low = (right - right_high.astype(f32)).astype(bf16)
    return dot(left_high, right_high, dims) + (dot(left_high, right_low, dims) + dot(left_low, right_high, dims))


def flat(ref):
    return ref[...].reshape(1, -1)


def iota(shape, axis):
    return lax.broadcasted_iota(i32, shape, axis)


def call(kernel, outs, args, scratch=(), **extra):
    vmem = pl.BlockSpec(memory_space=pltpu.VMEM)
    return pl.pallas_call(
        kernel,
        out_shape=[jax.ShapeDtypeStruct(shape, dtype) for shape, dtype in outs],
        in_specs=[vmem] * len(args),
        out_specs=[vmem] * len(outs),
        scratch_shapes=list(scratch),
        compiler_params=pltpu.CompilerParams(vmem_limit_bytes=56 * 2**20),
        **extra,
    )(*args)


def split3(value):
    high = value.astype(bf16).astype(f32)
    rest = value - high
    middle = rest.astype(bf16).astype(f32)
    return high, middle, rest - middle


def columns3(value, width):
    high, middle, low = split3(value)
    lane = iota((value.shape[0], width), 1)
    picked = jnp.where(lane == 0, high, jnp.where(lane == 1, middle, jnp.where(lane == 2, low, 0.0)))
    return picked.astype(bf16)


def column_of(row):
    return jnp.transpose(jnp.broadcast_to(row.astype(f32), (128, row.shape[1])))


def wide(column, width):
    return jnp.concatenate([column] * (width // 128), 1)


def bucket_of(relative):
    distance = jnp.abs(relative)
    beyond = jnp.zeros_like(distance)
    for threshold in bucket_edges:
        beyond = beyond + (distance >= threshold).astype(i32)
    magnitude = jnp.where(distance < 8, distance, 8 + beyond)
    return magnitude + 16 * (relative > 0).astype(i32)


def band_rows(table):
    buckets = table.shape[1]
    offset = iota((buckets, ROLL), 1)
    relative = jnp.where(offset < BAND, offset, offset - ROLL) - BLOCK
    onehot = (bucket_of(relative) == iota((buckets, ROLL), 0)).astype(f32)
    return dot(table, onehot, precision=highest), onehot


def bias_tiles(table):
    rows, onehot = band_rows(table)
    tiles = []
    for h in range(table.shape[0]):
        full = jnp.broadcast_to(rows[h : h + 1], (BLOCK, ROLL))
        tiles.append(jnp.transpose(pltpu.roll(full, 0, 1, stride=1, stride_axis=0)[:, :BAND]))
    return tiles, onehot


def head_masks(heads):
    lane = iota((1, heads * HEAD), 1)
    return [((lane >= h * HEAD) & (lane < (h + 1) * HEAD)).astype(f32).astype(bf16) for h in range(heads)]


def padded_segments(seg):
    edge = jnp.full((1, BLOCK), -1.0, f32)
    return column_of(jnp.concatenate([edge, seg, edge], 1))


def first_norm(tok, gain):
    scale = lax.rsqrt(jnp.mean(tok * tok, -1, keepdims=True) + norm_eps)
    return (tok * scale * gain).astype(bf16), scale


def probabilities(scores, bias, same):
    scores = jnp.where(same, scores + bias, masked_score)
    weights = jnp.exp(scores - jnp.max(scores, 0, keepdims=True))
    return weights * (1.0 / jnp.sum(weights, 0, keepdims=True))


def stack_heads(rows, masks):
    return jnp.concatenate([rows * mask for mask in masks], 0)


def own_blocks(product, heads):
    return jnp.concatenate(
        [product[h * HEAD : (h + 1) * HEAD, h * BLOCK : (h + 1) * BLOCK] for h in range(heads)], 0
    )


def fill_rows(ref, value):
    rows = value.shape[0]
    edge = jnp.zeros((BLOCK, value.shape[1]), bf16)
    ref[pl.ds(0, BLOCK), :] = edge
    ref[pl.ds(rows + BLOCK, BLOCK), :] = edge
    ref[pl.ds(BLOCK, rows), :] = value


def fill_columns(ref, value):
    rows = value.shape[1]
    edge = jnp.zeros((value.shape[0], BLOCK), bf16)
    ref[:, pl.ds(0, BLOCK)] = edge
    ref[:, pl.ds(rows + BLOCK, BLOCK)] = edge
    ref[:, pl.ds(BLOCK, rows)] = value


def forward_kernel(tok_ref, gain_ref, iw_ref, bt_ref, seg_ref, att_ref, normed_ref, keys, values):
    rows = tok_ref.shape[0]
    normed, _ = first_norm(tok_ref[...].astype(f32), flat(gain_ref))
    normed_ref[...] = normed
    queries = dot(normed, iw_ref[0], NT).astype(bf16)
    fill_rows(keys, dot(normed, iw_ref[1], NT).astype(bf16))
    fill_columns(values, dot(iw_ref[2], normed, NT).astype(bf16))
    seg = seg_ref[...].astype(f32)
    seg_keys = padded_segments(seg)
    tiles, _ = bias_tiles(bt_ref[...])
    heads = len(tiles)
    masks = head_masks(heads)
    for block in range(rows // BLOCK):
        at = block * BLOCK
        same = seg_keys[at : at + BAND] == seg[:, at : at + BLOCK]
        scores = dot(keys[pl.ds(at, BAND), :], stack_heads(queries[at : at + BLOCK], masks), NT)
        weights = [
            probabilities(scores[:, h * BLOCK : (h + 1) * BLOCK], tiles[h], same).astype(bf16) for h in range(heads)
        ]
        product = dot(values[:, pl.ds(at, BAND)], jnp.concatenate(weights, 1))
        att_ref[:, pl.ds(at, BLOCK)] = own_blocks(product, heads).astype(bf16)


def group_backward(normed, weight, out_weight, table, seg, grad_low, scratch, bias_grads):
    keys, values, keys_across, grad_keys, grad_values, grad_queries = scratch
    rows = normed.shape[0]
    queries = dot(normed, weight[0], NT).astype(bf16)
    fill_rows(keys, dot(normed, weight[1], NT).astype(bf16))
    fill_columns(keys_across, dot(weight[1], normed, NT).astype(bf16))
    fill_rows(values, dot(normed, weight[2], NT).astype(bf16))
    grad_att = dot(grad_low, out_weight, NT).astype(bf16)
    grad_keys[...] = jnp.zeros(grad_keys.shape, f32)
    grad_values[...] = jnp.zeros(grad_values.shape, f32)
    seg_keys = padded_segments(seg)
    tiles, onehot = bias_tiles(table)
    heads = len(tiles)
    masks = head_masks(heads)
    sums = [None] * heads
    for block in range(rows // BLOCK):
        at = block * BLOCK
        same = seg_keys[at : at + BAND] == seg[:, at : at + BLOCK]
        head_queries = stack_heads(queries[at : at + BLOCK], masks)
        head_grads = stack_heads(grad_att[at : at + BLOCK], masks)
        scores = dot(keys[pl.ds(at, BAND), :], head_queries, NT)
        grad_probs = dot(values[pl.ds(at, BAND), :], head_grads, NT)
        all_weights, all_grads = [], []
        for h in range(heads):
            columns = slice(h * BLOCK, (h + 1) * BLOCK)
            weights = probabilities(scores[:, columns], tiles[h], same)
            scaled = weights * grad_probs[:, columns]
            grad_scores = scaled - weights * jnp.sum(scaled, 0, keepdims=True)
            all_weights.append(weights.astype(bf16))
            all_grads.append(grad_scores.astype(bf16))
            if bias_grads:
                sums[h] = grad_scores if sums[h] is None else sums[h] + grad_scores
        low = jnp.concatenate(all_grads, 1)
        grad_queries[:, pl.ds(at, BLOCK)] = own_blocks(dot(keys_across[:, pl.ds(at, BAND)], low), heads)
        grad_keys[pl.ds(at, BAND), :] += dot(low, head_queries)
        grad_values[pl.ds(at, BAND), :] += dot(jnp.concatenate(all_weights, 1), head_grads)
    parts = (
        jnp.transpose(grad_queries[...]).astype(bf16),
        grad_keys[pl.ds(BLOCK, rows), :].astype(bf16),
        grad_values[pl.ds(BLOCK, rows), :].astype(bf16),
    )
    if not bias_grads:
        return parts, None
    diagonals = []
    row_index = iota((BLOCK, ROLL), 0)
    for h in range(heads):
        moved = jnp.concatenate([jnp.transpose(sums[h]), jnp.zeros((BLOCK, ROLL - BAND), f32)], 1)
        step = 1
        while step < BLOCK:
            moved = jnp.where((row_index & step) != 0, pltpu.roll(moved, ROLL - step, 1), moved)
            step *= 2
        diagonals.append(jnp.sum(moved, 0, keepdims=True))
    onehot = jnp.concatenate([onehot, jnp.zeros((128 - onehot.shape[0], ROLL), f32)], 0)
    by_head = dot(jnp.concatenate(diagonals, 0), onehot, NT, precision=highest)
    return parts, jnp.concatenate([by_head[h : h + 1] for h in range(heads)], 1)


def own_backward_kernel(normed_ref, iw_ref, ow_ref, bt_ref, seg_ref, low_ref, grad_iw_ref, parts_ref, table_ref, *scratch):
    normed = normed_ref[...]
    parts, table_grad = group_backward(
        normed, iw_ref, ow_ref[...], bt_ref[...], seg_ref[...].astype(f32), low_ref[...], scratch, True
    )
    table_ref[...] = jnp.concatenate(
        [table_grad, jnp.zeros((1, table_ref.shape[1] - table_grad.shape[1]), f32)], 1
    )
    width = ow_ref.shape[0]
    for j in range(3):
        parts_ref[j] = parts[j]
        grad_iw_ref[pl.ds(j * width, width), :] = dot(parts[j], normed, TN).astype(bf16)


def rest_backward_kernel(
    normed_ref, own_iw_ref, iw_ref, ow_ref, bt_ref, seg_ref, low_ref, parts_ref, tok_ref, gain_ref, grad_hidden_ref,
    table_ref, grad_tok_ref, tail_ref, total, *scratch,
):
    width = ow_ref.shape[1]
    total[...] = sum(dot(parts_ref[j], own_iw_ref[j]) for j in range(3))

    def step(group, carry):
        weight = [iw_ref[group, pl.ds(j * width, width), :] for j in range(3)]
        parts, _ = group_backward(
            normed_ref[...], weight, ow_ref[group], bt_ref[group], seg_ref[...].astype(f32), low_ref[...], scratch, False
        )
        total[...] += sum(dot(parts[j], weight[j]) for j in range(3))
        return carry

    lax.fori_loop(0, ow_ref.shape[0], step, 0)
    tok = tok_ref[...].astype(f32)
    gain = flat(gain_ref)
    scale = lax.rsqrt(jnp.mean(tok * tok, -1, keepdims=True) + norm_eps)
    grad_normed = total[...]
    tail_ref[...] = rows3([jnp.sum(grad_normed * tok * scale, 0, keepdims=True), table_ref[...]], tail_ref.shape[0])
    scaled = grad_normed * gain
    grad_tok_ref[...] = (
        grad_hidden_ref[...]
        + scale * scaled
        - tok * (scale * scale * scale) * jnp.mean(scaled * tok, -1, keepdims=True)
    )


def rows3(values, count):
    parts = [part for value in values for part in split3(value)]
    row = iota((count, values[0].shape[1]), 0)
    total = jnp.zeros(row.shape, f32)
    for index, part in enumerate(parts):
        total = jnp.where(row == index, part, total)
    return total.astype(bf16)


def finish_kernel(late_ref, early_ref, *refs):
    grad_iw_ref, grad_ow_ref, grad_rw_ref, second_ref, first_ref, table_ref = refs
    devices = late_ref.shape[0]
    late_rows = grad_iw_ref.shape[0] // devices
    tail = jnp.zeros((late_ref.shape[1] - late_rows, late_ref.shape[2]), f32)
    for device in range(devices):
        block = late_ref[device].astype(f32)
        grad_iw_ref[pl.ds(device * late_rows, late_rows), :] = block[:late_rows]
        tail = tail + block[late_rows:]
    first_ref[...] = jnp.sum(tail[:3], 0)
    table_ref[...] = jnp.sum(tail[3:6], 0, keepdims=True)
    at, experts = grad_ow_ref.shape[0], grad_rw_ref.shape[0]
    early = early_ref[...]
    grad_ow_ref[...] = early[:at]
    grad_rw_ref[...] = early[at : at + experts]
    second_ref[...] = jnp.sum(early[at + experts : at + experts + 8], 0)


def slot_onehot(choice, slot, slots):
    dest = jnp.where(slot >= 0, choice * CAP + slot, slots)
    return (iota((slots, dest.shape[1]), 0) == dest).astype(f32).astype(bf16)


def slot_order(slots, group, across):
    index = iota((1, slots), 1)
    big, small = slots // across, slots // group
    outer, rest = lax.div(index, big), lax.rem(index, big)
    target = lax.div(rest, CAP) * small + outer * CAP + lax.rem(rest, CAP)
    return (iota((slots, slots), 0) == target).astype(f32).astype(bf16)


def cotangent_kernel(cot_ref, choice_ref, slot_ref, out_ref):
    fill = slot_onehot(flat(choice_ref), flat(slot_ref), out_ref.shape[0])
    out_ref[...] = dot(fill, cot_ref[...]).astype(bf16)


def order_kernel(sources, local, rows_ref, out_ref):
    out_ref[...] = dot(slot_order(rows_ref.shape[0], local, sources), rows_ref[...]).astype(bf16)


def chosen_of(choice, experts):
    column = column_of(choice)[:, :experts]
    return (column == iota(column.shape, 1).astype(f32)).astype(f32)


def middle_kernel(tok_ref, own_ow_ref, ow_ref, gain_ref, rw_ref, choice_ref, slot_ref, *refs):
    att_refs, (hidden_ref, prob_ref, send_ref) = refs[:-3], refs[-3:]
    hidden = tok_ref[...].astype(f32)
    for shift, att_ref in enumerate(att_refs):
        hidden = hidden + dot(att_ref[...], ow_ref[shift - 1] if shift else own_ow_ref[...], TN)
    hidden_ref[...] = hidden
    scale = lax.rsqrt(jnp.mean(hidden * hidden, -1, keepdims=True) + norm_eps)
    normed = hidden * scale * flat(gain_ref)
    logits = dot3(normed, rw_ref[...], NT)
    raised = jnp.exp(logits - jnp.max(logits, -1, keepdims=True))
    prob = raised * (1.0 / jnp.sum(raised, -1, keepdims=True))
    prob_ref[...] = prob
    gate = jnp.sum(prob * chosen_of(flat(choice_ref), prob.shape[1]), -1, keepdims=True)
    width = normed.shape[1]
    fill = slot_onehot(flat(choice_ref), flat(slot_ref), send_ref.shape[0])
    send_ref[:, :width] = dot(fill, normed.astype(bf16)).astype(bf16)
    send_ref[:, width:] = dot(fill, columns3(gate, 128)).astype(bf16)


def expert_kernel(
    tensor_size, sources, unroll,
    recv_ref, cot_ref, win_ref, wout_ref,
    rows_ref, grads_ref, act_ref, grad_act_ref, dots_ref, result_ref, *refs,
):
    chunks = refs[:tensor_size]
    x_all, g_all, r_all, d_all, turned = refs[tensor_size:]
    slots = recv_ref.shape[0]
    width = cot_ref.shape[1]
    step = pl.program_id(0)
    local = pl.num_programs(0) * unroll
    per = rows_ref.shape[0] // unroll

    @pl.when(step == 0)
    def _():
        order = slot_order(slots, win_ref.shape[0] * (slots // rows_ref.shape[0]), sources)
        x_all[...] = dot(order, recv_ref[:, :width]).astype(bf16)
        gate = jnp.sum(dot(order, recv_ref[:, width:]), -1, keepdims=True)
        g_all[...] = (gate * cot_ref[...].astype(f32)).astype(bf16)

    for u in range(unroll):
        here = pl.ds(u * per, per)
        at = pl.ds(pl.multiple_of((step * unroll + u) * per, 16), per)
        x = x_all[at, :]
        g = g_all[at, :]
        weight_in = win_ref[u]
        weight_out = wout_ref[u]
        pre = dot(x, weight_in)
        grad_act = dot(g, weight_out, NT)
        inner = jnp.tanh(gelu_const * (pre + gelu_cubic * pre * pre * pre))
        act = (0.5 * pre * (1.0 + inner)).astype(bf16)
        slope = 0.5 * (1.0 + inner) + 0.5 * pre * (1.0 - inner * inner) * gelu_const * (
            1.0 + 3.0 * gelu_cubic * pre * pre
        )
        grad_act = (grad_act * slope).astype(bf16)
        r_all[at, :] = dot(grad_act, weight_in, NT).astype(bf16)
        result = dot(act, weight_out)
        result_ref[here, :] = result.astype(bf16)
        d_all[at, :] = columns3(jnp.sum(result * cot_ref[at, :].astype(f32), -1, keepdims=True), 128)
        rows_ref[here, :] = x
        grads_ref[here, :] = g
        act_ref[here, :] = act
        grad_act_ref[here, :] = grad_act

    @pl.when(step == pl.num_programs(0) - 1)
    def _():
        order = slot_order(slots, win_ref.shape[0] * (slots // rows_ref.shape[0]), sources)
        dots_ref[...] = dot(d_all[...], order, TN)[:EXTRA].astype(bf16)
        turn_chunks(tensor_size, dot(r_all[...], order, TN).astype(bf16), turned, chunks)


def turn_chunks(tensor_size, rows, turned, chunks):
    turned[...] = rows
    quarter = rows.shape[0] // tensor_size
    me = lax.axis_index("tensor")
    for shift in range(tensor_size):
        first = lax.rem(me + shift, tensor_size) * quarter
        chunks[shift][...] = turned[pl.ds(pl.multiple_of(first, 64), quarter), :]


def result_kernel(tensor_size, sources, local, rows_ref, *refs):
    order = slot_order(rows_ref.shape[0], local, sources)
    turn_chunks(tensor_size, dot(rows_ref[...], order, TN).astype(bf16), refs[tensor_size], refs[:tensor_size])


def sum_kernel(with_dots, *refs):
    *parts, out_ref = refs
    total = sum(ref[...].astype(f32) for ref in (parts[:-1] if with_dots else parts))
    extra = [parts[-1][...].astype(f32)] if with_dots else []
    rows = total.shape[0] + EXTRA * len(extra)
    blank = jnp.zeros((out_ref.shape[1] - rows, total.shape[1]), f32)
    out_ref[...] = jnp.transpose(jnp.concatenate([total] + extra + [blank], 0)).astype(bf16)


def back_kernel(recv_ref, choice_ref, slot_ref, out_ref):
    fill = slot_onehot(flat(choice_ref), flat(slot_ref), recv_ref.shape[0])
    out_ref[...] = dot(recv_ref[...], fill, TN)[: out_ref.shape[0]].astype(bf16)


def spread(refs, quarter, turned):
    size = len(refs)
    me = lax.axis_index("tensor")
    for shift, ref in enumerate(refs):
        first = lax.rem(me + size - shift, size) * quarter
        turned[pl.ds(pl.multiple_of(first, 64), quarter), :] = ref[pl.ds(0, quarter), :].astype(f32)
    return jnp.transpose(turned[...])


def hidden_backward_kernel(
    hidden_ref, prob_ref, cot_ref, gain_ref, rw_ref, choice_ref, att_ref, *refs,
):
    parts = refs[:-4]
    grad_hidden_ref, low_ref, sums_ref, turned = refs[-4:]
    hidden = hidden_ref[...]
    rows, width = hidden.shape
    quarter = width // len(parts)
    grad_routed = spread(parts, quarter, turned)
    dots = sum(jnp.sum(ref[pl.ds(quarter, EXTRA), :].astype(f32), 0, keepdims=True) for ref in parts)
    prob = prob_ref[...]
    chosen = chosen_of(flat(choice_ref), prob.shape[1])
    gate = jnp.sum(prob * chosen, -1, keepdims=True)
    grad_gate = column_of(dots)[:, :1]
    grad_logits = (grad_gate * gate) * (chosen - prob)
    grad_normed = grad_routed + dot3(grad_logits, rw_ref[...])
    gain = flat(gain_ref)
    scale = lax.rsqrt(jnp.mean(hidden * hidden, -1, keepdims=True) + norm_eps)
    scaled = grad_normed * gain
    grad_hidden = (
        cot_ref[...].astype(f32)
        + scale * scaled
        - hidden * (scale * scale * scale) * jnp.mean(scaled * hidden, -1, keepdims=True)
    )
    grad_hidden_ref[...] = grad_hidden
    low = grad_hidden.astype(bf16)
    low_ref[...] = low
    at, experts = att_ref.shape[0], prob.shape[1]
    sums_ref[pl.ds(0, at), :] = dot(att_ref[...], low).astype(bf16)
    sums_ref[pl.ds(at, experts), :] = dot3(grad_logits, hidden * scale * gain, TN).astype(bf16)
    tail = sums_ref.shape[0] - at - experts
    sums_ref[pl.ds(at + experts, tail), :] = rows3([jnp.sum(grad_normed * hidden * scale, 0, keepdims=True)], tail)


def output_kernel(hidden_ref, prob_ref, choice_ref, *refs):
    parts, (out_ref, turned) = refs[:-2], refs[-2:]
    hidden = hidden_ref[...]
    result = spread(parts, hidden.shape[1] // len(parts), turned)
    prob = prob_ref[...]
    gate = jnp.sum(prob * chosen_of(flat(choice_ref), prob.shape[1]), -1, keepdims=True)
    out_ref[...] = (hidden + gate * result).astype(bf16)


def make(mesh):
    tensor_size = mesh.shape["tensor"]
    expert_size = mesh.shape["expert"]

    def shards(
        tokens,
        segment_ids,
        expert_choice,
        slot_index,
        first_gain,
        input_weight,
        bias_table,
        output_weight,
        second_gain,
        router_weight,
        expert_in,
        expert_out,
        cotangent,
    ):
        token_count, width = tokens.shape
        sequences, length = segment_ids.shape
        quarter = output_weight.shape[0]
        experts = router_weight.shape[1]
        local = expert_in.shape[0]
        hidden_units = expert_in.shape[2]
        slots = experts * CAP
        per = slots // local
        chunk = slots // expert_size
        buckets, heads = bias_table.shape
        expert_index = lax.axis_index("expert")
        seg = (segment_ids + 8 * jnp.arange(sequences, dtype=i32)[:, None]).reshape(1, token_count)
        choice, slot = expert_choice, slot_index
        gain_first, gain_second = first_gain, second_gain
        iw_own = jnp.swapaxes(input_weight, 1, 2)
        table = bias_table.T
        rw = router_weight.T
        after = lax.optimization_barrier

        shifts = [[(i, (i + s) % tensor_size) for i in range(tensor_size)] for s in range(1, tensor_size)]

        def from_others(array):
            return [lax.ppermute(array, "tensor", pairs) for pairs in shifts]

        def gather_tensor(array):
            return [array] + from_others(array)

        def joined(planes):
            got = lax.all_gather(planes, "expert", axis=0)
            return jnp.swapaxes(got, 0, 1).reshape(tensor_size - 1, -1, got.shape[-1])

        def exchange(array):
            rows = array.shape[0] // expert_size
            got = lax.all_to_all(array.reshape(expert_size, rows, array.shape[1]), "expert", 0, 0)
            return got.reshape(array.shape)

        ow_rows = quarter // expert_size
        ow_part = lax.dynamic_slice_in_dim(output_weight, expert_index * ow_rows, ow_rows, 0)
        ow_all = joined(jnp.stack(from_others(ow_part)))

        attended, first_normed = call(
            forward_kernel,
            [((quarter, token_count), bf16), ((token_count, width), bf16)],
            (tokens, gain_first, iw_own, table, seg),
            [
                pltpu.VMEM((token_count + 2 * BLOCK, quarter), bf16),
                pltpu.VMEM((quarter, token_count + 2 * BLOCK), bf16),
            ],
        )
        attended_parts = gather_tensor(attended)
        (cot_slots,) = call(cotangent_kernel, [((slots, width), bf16)], (cotangent, choice, slot))
        cot_recv = exchange(cot_slots)
        attended_parts, cot_recv = after((attended_parts, cot_recv))

        hidden, prob, send = call(
            middle_kernel,
            [((token_count, width), f32), ((token_count, experts), f32), ((slots, width + 128), bf16)],
            (tokens, output_weight, ow_all, gain_second, rw, choice, slot, *attended_parts),
        )
        recv = exchange(send)
        cot_recv, _ = after((cot_recv, send))
        (cot_rows,) = call(
            lambda *refs: order_kernel(expert_size, local, *refs), [((slots, width), bf16)], (cot_recv,)
        )

        iw_rows = 3 * quarter // expert_size
        iw_part = lax.dynamic_slice_in_dim(iw_own.reshape(3 * quarter, width), expert_index * iw_rows, iw_rows, 0)
        bias_parts = jnp.stack(split3(table)).astype(bf16).reshape(-1)
        bias_parts = jnp.pad(bias_parts, (0, 8 * width - bias_parts.shape[0])).reshape(8, width)
        iw_part, _ = after((jnp.concatenate([iw_part, bias_parts], 0), send))
        iw_planes = from_others(iw_part)

        unroll = 2 if local % 2 == 0 else 1
        whole = lambda shape: pl.BlockSpec(shape, lambda j: (0,) * len(shape))
        by_expert = pl.BlockSpec((unroll * per, width), lambda j: (j, 0))
        by_hidden = pl.BlockSpec((unroll * per, hidden_units), lambda j: (j, 0))
        outs = pl.pallas_call(
            lambda *refs: expert_kernel(tensor_size, expert_size, unroll, *refs),
            grid=(local // unroll,),
            in_specs=[
                whole((slots, width + 128)),
                whole((slots, width)),
                pl.BlockSpec((unroll, width, hidden_units), lambda j: (j, 0, 0)),
                pl.BlockSpec((unroll, hidden_units, width), lambda j: (j, 0, 0)),
            ],
            out_specs=[by_expert, by_expert, by_hidden, by_hidden, whole((EXTRA, slots)), by_expert]
            + [whole((quarter, slots))] * tensor_size,
            out_shape=[jax.ShapeDtypeStruct((slots, width), bf16)] * 2
            + [jax.ShapeDtypeStruct((slots, hidden_units), bf16)] * 2
            + [jax.ShapeDtypeStruct((EXTRA, slots), bf16), jax.ShapeDtypeStruct((slots, width), bf16)]
            + [jax.ShapeDtypeStruct((quarter, slots), bf16)] * tensor_size,
            scratch_shapes=[pltpu.VMEM((slots, width), bf16)] * 3
            + [pltpu.VMEM((slots, 128), bf16), pltpu.VMEM((width, slots), bf16)],
            compiler_params=pltpu.CompilerParams(vmem_limit_bytes=56 * 2**20),
        )(recv, cot_rows, expert_in, expert_out)
        expert_rows, grad_slots, expert_act, grad_act, dots, result_rows = outs[:6]
        grad_chunks = outs[6:]

        def trade_chunks(chunks):
            return [chunks[0]] + [lax.ppermute(c, "tensor", pairs) for c, pairs in zip(chunks[1:], shifts)]

        def sum_rows(parts, with_dots):
            columns = -(-(quarter + (EXTRA if with_dots else 0)) // 128) * 128
            return call(lambda *refs: sum_kernel(with_dots, *refs), [((slots, columns), bf16)], parts)[0]

        def own_tokens(rows, kept):
            return call(back_kernel, [((kept, token_count), bf16)], (rows, choice, slot))[0]

        by = lambda array: array.reshape(local, per, array.shape[1])
        grad_expert_out = jnp.einsum("erf,erd->efd", by(expert_act), by(grad_slots), preferred_element_type=f32)
        grad_expert_in = jnp.einsum("erd,erf->edf", by(expert_rows), by(grad_act), preferred_element_type=f32)

        iw_planes, _ = after((iw_planes, grad_chunks[0]))
        iw_planes = jnp.stack(iw_planes)
        iw_all = joined(iw_planes[:, :iw_rows])
        bias_all = jnp.sum(
            iw_planes[:, iw_rows:]
            .reshape(tensor_size - 1, -1)[:, : 3 * buckets * heads]
            .reshape(tensor_size - 1, 3, heads, buckets)
            .astype(f32),
            1,
        )
        result_chunks = call(
            lambda *refs: result_kernel(tensor_size, expert_size, local, *refs),
            [((quarter, slots), bf16)] * tensor_size,
            (result_rows,),
            [pltpu.VMEM((width, slots), bf16)],
        )
        traded, result_chunks, grad_expert_out = after((trade_chunks(grad_chunks), result_chunks, grad_expert_out))
        summed = sum_rows(traded + [dots], True)
        result_chunks, _ = after((result_chunks, summed))
        result_traded = trade_chunks(result_chunks)
        returned = own_tokens(exchange(summed), quarter + EXTRA)
        returned, grad_expert_in = after((returned, grad_expert_in))
        grad_parts = gather_tensor(returned)
        result_traded, _ = after((result_traded, returned))
        result_own = own_tokens(exchange(sum_rows(result_traded, False)), quarter)
        grad_parts, result_own, bias_all = after((grad_parts, result_own, bias_all))

        early_rows = quarter + experts + 64
        grad_hidden, grad_low, early_sums = call(
            hidden_backward_kernel,
            [((token_count, width), f32), ((token_count, width), bf16), ((early_rows, width), bf16)],
            (hidden, prob, cotangent, gain_second, rw, choice, attended, *grad_parts),
            [pltpu.VMEM((width, token_count), f32)],
        )
        def sum_experts(array):
            return jnp.sum(exchange(array).reshape(expert_size, -1, array.shape[1]).astype(f32), 0)

        padded = token_count + 2 * BLOCK
        scratch = [pltpu.VMEM((padded, quarter), bf16)] * 2 + [pltpu.VMEM((quarter, padded), bf16)]
        scratch = scratch + [pltpu.VMEM((padded, quarter), f32)] * 2 + [pltpu.VMEM((quarter, token_count), f32)]
        grad_iw, own_parts, table_grad = call(
            own_backward_kernel,
            [((3 * quarter, width), bf16), ((3, token_count, quarter), bf16), ((1, width), f32)],
            (first_normed, iw_own, output_weight, table, seg, grad_low),
            scratch,
        )
        result_own, _ = after((result_own, grad_iw))
        result_parts = gather_tensor(result_own)
        grad_tokens, tail = call(
            rest_backward_kernel,
            [((token_count, width), f32), ((8, width), bf16)],
            (
                first_normed, iw_own, iw_all, ow_all, bias_all, seg, grad_low, own_parts, tokens, gain_first,
                grad_hidden, table_grad,
            ),
            [pltpu.VMEM((token_count, width), f32)] + scratch,
        )
        (block_output,) = call(
            output_kernel,
            [((token_count, width), bf16)],
            (hidden, prob, choice, *result_parts),
            [pltpu.VMEM((width, token_count), f32)],
        )
        early_sum = sum_experts(early_sums).astype(f32)
        early = lax.all_gather(jnp.pad(early_sum, ((0, 8), (0, 0))), "expert", axis=0)
        early = early[:, : early_sum.shape[0]].reshape(early_rows, width)
        late = lax.all_gather(jnp.concatenate([sum_experts(grad_iw).astype(bf16), tail], 0), "expert", axis=0)
        grad_iw, grad_ow, grad_rw, grad_second, grad_first, grad_table = call(
            finish_kernel,
            [
                ((3 * quarter, width), f32),
                ((quarter, width), f32),
                ((experts, width), f32),
                ((width,), f32),
                ((width,), f32),
                ((1, width), f32),
            ],
            (late, early),
        )
        return (
            block_output,
            grad_tokens,
            grad_first,
            jnp.swapaxes(grad_iw.reshape(3, quarter, width), 1, 2),
            grad_table.reshape(width // 128, 128)[:heads, :buckets].T,
            grad_ow,
            grad_second,
            grad_rw.T,
            grad_expert_in,
            grad_expert_out,
        )

    return shards


def solution(mesh):
    placed = (
        P("expert", None),
        P("expert", None),
        P("expert"),
        P("expert"),
        P(),
        P(None, None, "tensor"),
        P(None, "tensor"),
        P("tensor", None),
        P(),
        P(),
        P("expert", None, "tensor"),
        P("expert", "tensor", None),
        P("expert", None),
    )
    return jax.shard_map(
        make(mesh),
        mesh=mesh,
        in_specs=placed,
        out_specs=(
            P("expert", None),
            P("expert", None),
            P(),
            P(None, None, "tensor"),
            P(None, "tensor"),
            P("tensor", None),
            P(),
            P(),
            P("expert", None, "tensor"),
            P("expert", "tensor", None),
        ),
        check_vma=False,
    )
```

```python
import math

import jax
import jax.numpy as jnp
from jax import lax
from jax.experimental import pallas as pl
from jax.experimental.pallas import tpu as pltpu
from jax.sharding import PartitionSpec as P

CAP = 10

bucket_edges = (12, 16, 23, 32, 46, 64, 91)
norm_eps = 1e-06
masked_score = -1e30
gelu_const = math.sqrt(2.0 / math.pi)
gelu_cubic = 0.044715

BLOCK = 128
BAND = 3 * BLOCK
ROLL = 4 * BLOCK
HEAD = 64
EXTRA = 16

bf16 = jnp.bfloat16
f32 = jnp.float32
i32 = jnp.int32
highest = lax.Precision.HIGHEST

NN = (((1,), (0,)), ((), ()))
NT = (((1,), (1,)), ((), ()))
TN = (((0,), (0,)), ((), ()))


def dot(left, right, dims=NN, precision=None):
    return lax.dot_general(left, right, dims, precision=precision, preferred_element_type=f32)


def dot3(left, right, dims=NN):
    left_high, right_high = left.astype(bf16), right.astype(bf16)
    left_low = (left - left_high.astype(f32)).astype(bf16)
    right_low = (right - right_high.astype(f32)).astype(bf16)
    return dot(left_high, right_high, dims) + (dot(left_high, right_low, dims) + dot(left_low, right_high, dims))


def flat(ref):
    return ref[...].reshape(1, -1)


def iota(shape, axis):
    return lax.broadcasted_iota(i32, shape, axis)


def call(kernel, outs, args, scratch=(), **extra):
    vmem = pl.BlockSpec(memory_space=pltpu.VMEM)
    return pl.pallas_call(
        kernel,
        out_shape=[jax.ShapeDtypeStruct(shape, dtype) for shape, dtype in outs],
        in_specs=[vmem] * len(args),
        out_specs=[vmem] * len(outs),
        scratch_shapes=list(scratch),
        compiler_params=pltpu.CompilerParams(vmem_limit_bytes=56 * 2**20),
        **extra,
    )(*args)


def split3(value):
    high = value.astype(bf16).astype(f32)
    rest = value - high
    middle = rest.astype(bf16).astype(f32)
    return high, middle, rest - middle


def columns3(value, width):
    high, middle, low = split3(value)
    lane = iota((value.shape[0], width), 1)
    picked = jnp.where(lane == 0, high, jnp.where(lane == 1, middle, jnp.where(lane == 2, low, 0.0)))
    return picked.astype(bf16)


def column_of(row):
    return jnp.transpose(jnp.broadcast_to(row.astype(f32), (128, row.shape[1])))


def wide(column, width):
    return jnp.concatenate([column] * (width // 128), 1)


def bucket_of(relative):
    distance = jnp.abs(relative)
    beyond = jnp.zeros_like(distance)
    for threshold in bucket_edges:
        beyond = beyond + (distance >= threshold).astype(i32)
    magnitude = jnp.where(distance < 8, distance, 8 + beyond)
    return magnitude + 16 * (relative > 0).astype(i32)


def band_rows(table):
    buckets = table.shape[1]
    offset = iota((buckets, ROLL), 1)
    relative = jnp.where(offset < BAND, offset, offset - ROLL) - BLOCK
    onehot = (bucket_of(relative) == iota((buckets, ROLL), 0)).astype(f32)
    return dot(table, onehot, precision=highest), onehot


def bias_tiles(table):
    rows, onehot = band_rows(table)
    tiles = []
    for h in range(table.shape[0]):
        full = jnp.broadcast_to(rows[h : h + 1], (BLOCK, ROLL))
        tiles.append(jnp.transpose(pltpu.roll(full, 0, 1, stride=1, stride_axis=0)[:, :BAND]))
    return tiles, onehot


def head_masks(heads):
    lane = iota((1, heads * HEAD), 1)
    return [((lane >= h * HEAD) & (lane < (h + 1) * HEAD)).astype(f32).astype(bf16) for h in range(heads)]


def padded_segments(seg):
    edge = jnp.full((1, BLOCK), -1.0, f32)
    return column_of(jnp.concatenate([edge, seg, edge], 1))


def first_norm(tok, gain):
    scale = lax.rsqrt(jnp.mean(tok * tok, -1, keepdims=True) + norm_eps)
    return (tok * scale * gain).astype(bf16), scale


def probabilities(scores, bias, same):
    scores = jnp.where(same, scores + bias, masked_score)
    weights = jnp.exp(scores - jnp.max(scores, 0, keepdims=True))
    return weights * (1.0 / jnp.sum(weights, 0, keepdims=True))


def stack_heads(rows, masks):
    return jnp.concatenate([rows * mask for mask in masks], 0)


def own_blocks(product, heads):
    return jnp.concatenate(
        [product[h * HEAD : (h + 1) * HEAD, h * BLOCK : (h + 1) * BLOCK] for h in range(heads)], 0
    )


def fill_rows(ref, value):
    rows = value.shape[0]
    edge = jnp.zeros((BLOCK, value.shape[1]), bf16)
    ref[pl.ds(0, BLOCK), :] = edge
    ref[pl.ds(rows + BLOCK, BLOCK), :] = edge
    ref[pl.ds(BLOCK, rows), :] = value


def fill_columns(ref, value):
    rows = value.shape[1]
    edge = jnp.zeros((value.shape[0], BLOCK), bf16)
    ref[:, pl.ds(0, BLOCK)] = edge
    ref[:, pl.ds(rows + BLOCK, BLOCK)] = edge
    ref[:, pl.ds(BLOCK, rows)] = value


def forward_kernel(tok_ref, gain_ref, iw_ref, bt_ref, seg_ref, att_ref, normed_ref, keys, values):
    rows = tok_ref.shape[0]
    normed, _ = first_norm(tok_ref[...].astype(f32), flat(gain_ref))
    normed_ref[...] = normed
    queries = dot(normed, iw_ref[0], NT).astype(bf16)
    fill_rows(keys, dot(normed, iw_ref[1], NT).astype(bf16))
    fill_columns(values, dot(iw_ref[2], normed, NT).astype(bf16))
    seg = seg_ref[...].astype(f32)
    seg_keys = padded_segments(seg)
    tiles, _ = bias_tiles(bt_ref[...])
    heads = len(tiles)
    masks = head_masks(heads)
    for block in range(rows // BLOCK):
        at = block * BLOCK
        same = seg_keys[at : at + BAND] == seg[:, at : at + BLOCK]
        scores = dot(keys[pl.ds(at, BAND), :], stack_heads(queries[at : at + BLOCK], masks), NT)
        weights = [
            probabilities(scores[:, h * BLOCK : (h + 1) * BLOCK], tiles[h], same).astype(bf16) for h in range(heads)
        ]
        product = dot(values[:, pl.ds(at, BAND)], jnp.concatenate(weights, 1))
        att_ref[:, pl.ds(at, BLOCK)] = own_blocks(product, heads).astype(bf16)


def group_backward(normed, weight, out_weight, table, seg, grad_low, scratch, bias_grads):
    keys, values, keys_across, grad_keys, grad_values, grad_queries = scratch
    rows = normed.shape[0]
    queries = dot(normed, weight[0], NT).astype(bf16)
    fill_rows(keys, dot(normed, weight[1], NT).astype(bf16))
    fill_columns(keys_across, dot(weight[1], normed, NT).astype(bf16))
    fill_rows(values, dot(normed, weight[2], NT).astype(bf16))
    grad_att = dot(grad_low, out_weight, NT).astype(bf16)
    grad_keys[...] = jnp.zeros(grad_keys.shape, f32)
    grad_values[...] = jnp.zeros(grad_values.shape, f32)
    seg_keys = padded_segments(seg)
    tiles, onehot = bias_tiles(table)
    heads = len(tiles)
    masks = head_masks(heads)
    sums = [None] * heads
    for block in range(rows // BLOCK):
        at = block * BLOCK
        same = seg_keys[at : at + BAND] == seg[:, at : at + BLOCK]
        head_queries = stack_heads(queries[at : at + BLOCK], masks)
        head_grads = stack_heads(grad_att[at : at + BLOCK], masks)
        scores = dot(keys[pl.ds(at, BAND), :], head_queries, NT)
        grad_probs = dot(values[pl.ds(at, BAND), :], head_grads, NT)
        all_weights, all_grads = [], []
        for h in range(heads):
            columns = slice(h * BLOCK, (h + 1) * BLOCK)
            weights = probabilities(scores[:, columns], tiles[h], same)
            scaled = weights * grad_probs[:, columns]
            grad_scores = scaled - weights * jnp.sum(scaled, 0, keepdims=True)
            all_weights.append(weights.astype(bf16))
            all_grads.append(grad_scores.astype(bf16))
            if bias_grads:
                sums[h] = grad_scores if sums[h] is None else sums[h] + grad_scores
        low = jnp.concatenate(all_grads, 1)
        grad_queries[:, pl.ds(at, BLOCK)] = own_blocks(dot(keys_across[:, pl.ds(at, BAND)], low), heads)
        grad_keys[pl.ds(at, BAND), :] += dot(low, head_queries)
        grad_values[pl.ds(at, BAND), :] += dot(jnp.concatenate(all_weights, 1), head_grads)
    parts = (
        jnp.transpose(grad_queries[...]).astype(bf16),
        grad_keys[pl.ds(BLOCK, rows), :].astype(bf16),
        grad_values[pl.ds(BLOCK, rows), :].astype(bf16),
    )
    if not bias_grads:
        return parts, None
    diagonals = []
    row_index = iota((BLOCK, ROLL), 0)
    for h in range(heads):
        moved = jnp.concatenate([jnp.transpose(sums[h]), jnp.zeros((BLOCK, ROLL - BAND), f32)], 1)
        step = 1
        while step < BLOCK:
            moved = jnp.where((row_index & step) != 0, pltpu.roll(moved, ROLL - step, 1), moved)
            step *= 2
        diagonals.append(jnp.sum(moved, 0, keepdims=True))
    onehot = jnp.concatenate([onehot, jnp.zeros((128 - onehot.shape[0], ROLL), f32)], 0)
    by_head = dot(jnp.concatenate(diagonals, 0), onehot, NT, precision=highest)
    return parts, jnp.concatenate([by_head[h : h + 1] for h in range(heads)], 1)


def own_backward_kernel(normed_ref, iw_ref, ow_ref, bt_ref, seg_ref, low_ref, grad_iw_ref, parts_ref, table_ref, *scratch):
    normed = normed_ref[...]
    parts, table_grad = group_backward(
        normed, iw_ref, ow_ref[...], bt_ref[...], seg_ref[...].astype(f32), low_ref[...], scratch, True
    )
    table_ref[...] = jnp.concatenate(
        [table_grad, jnp.zeros((1, table_ref.shape[1] - table_grad.shape[1]), f32)], 1
    )
    width = ow_ref.shape[0]
    for j in range(3):
        parts_ref[j] = parts[j]
        grad_iw_ref[pl.ds(j * width, width), :] = dot(parts[j], normed, TN).astype(bf16)


def group_kernel(first, last, normed_ref, iw_ref, ow_ref, bt_ref, seg_ref, low_ref, *refs):
    refs, scratch = refs[:-6], refs[-6:]
    width = ow_ref.shape[1]
    if first:
        parts_ref, own_iw_ref, *refs = refs
        total = sum(dot(parts_ref[j], own_iw_ref[j]) for j in range(3))
    else:
        total_ref, *refs = refs
        total = total_ref[...]
    weight = [iw_ref[0, pl.ds(j * width, width), :] for j in range(3)]
    parts, _ = group_backward(
        normed_ref[...], weight, ow_ref[0], bt_ref[0], seg_ref[...].astype(f32), low_ref[...], scratch, False
    )
    total = total + sum(dot(parts[j], weight[j]) for j in range(3))
    if not last:
        refs[0][...] = total
        return
    tok_ref, gain_ref, grad_hidden_ref, table_ref, grad_tok_ref, tail_ref = refs
    tok = tok_ref[...].astype(f32)
    gain = flat(gain_ref)
    scale = lax.rsqrt(jnp.mean(tok * tok, -1, keepdims=True) + norm_eps)
    tail_ref[...] = rows3([jnp.sum(total * tok * scale, 0, keepdims=True), table_ref[...]], tail_ref.shape[0])
    scaled = total * gain
    grad_tok_ref[...] = (
        grad_hidden_ref[...]
        + scale * scaled
        - tok * (scale * scale * scale) * jnp.mean(scaled * tok, -1, keepdims=True)
    )


def rows3(values, count):
    parts = [part for value in values for part in split3(value)]
    row = iota((count, values[0].shape[1]), 0)
    total = jnp.zeros(row.shape, f32)
    for index, part in enumerate(parts):
        total = jnp.where(row == index, part, total)
    return total.astype(bf16)


def finish_kernel(late_ref, early_ref, *refs):
    grad_iw_ref, grad_ow_ref, grad_rw_ref, second_ref, first_ref, table_ref = refs
    devices = late_ref.shape[0]
    late_rows = grad_iw_ref.shape[0] // devices
    tail = jnp.zeros((late_ref.shape[1] - late_rows, late_ref.shape[2]), f32)
    for device in range(devices):
        block = late_ref[device].astype(f32)
        grad_iw_ref[pl.ds(device * late_rows, late_rows), :] = block[:late_rows]
        tail = tail + block[late_rows:]
    first_ref[...] = jnp.sum(tail[:3], 0)
    table_ref[...] = jnp.sum(tail[3:6], 0, keepdims=True)
    at, experts = grad_ow_ref.shape[0], grad_rw_ref.shape[0]
    early = early_ref[...]
    grad_ow_ref[...] = early[:at]
    grad_rw_ref[...] = early[at : at + experts]
    second_ref[...] = jnp.sum(early[at + experts : at + experts + 8], 0)


def slot_onehot(choice, slot, slots):
    dest = jnp.where(slot >= 0, choice * CAP + slot, slots)
    return (iota((slots, dest.shape[1]), 0) == dest).astype(f32).astype(bf16)


def slot_order(slots, group, across):
    index = iota((1, slots), 1)
    big, small = slots // across, slots // group
    outer, rest = lax.div(index, big), lax.rem(index, big)
    target = lax.div(rest, CAP) * small + outer * CAP + lax.rem(rest, CAP)
    return (iota((slots, slots), 0) == target).astype(f32).astype(bf16)


def cotangent_kernel(cot_ref, choice_ref, slot_ref, out_ref):
    fill = slot_onehot(flat(choice_ref), flat(slot_ref), out_ref.shape[0])
    out_ref[...] = dot(fill, cot_ref[...]).astype(bf16)


def order_kernel(sources, local, rows_ref, out_ref):
    out_ref[...] = dot(slot_order(rows_ref.shape[0], local, sources), rows_ref[...]).astype(bf16)


def chosen_of(choice, experts):
    column = column_of(choice)[:, :experts]
    return (column == iota(column.shape, 1).astype(f32)).astype(f32)


def middle_kernel(tok_ref, own_ow_ref, ow_ref, gain_ref, rw_ref, choice_ref, slot_ref, *refs):
    att_refs, (hidden_ref, prob_ref, send_ref) = refs[:-3], refs[-3:]
    hidden = tok_ref[...].astype(f32)
    for shift, att_ref in enumerate(att_refs):
        hidden = hidden + dot(att_ref[...], ow_ref[shift - 1] if shift else own_ow_ref[...], TN)
    hidden_ref[...] = hidden
    scale = lax.rsqrt(jnp.mean(hidden * hidden, -1, keepdims=True) + norm_eps)
    normed = hidden * scale * flat(gain_ref)
    logits = dot3(normed, rw_ref[...], NT)
    raised = jnp.exp(logits - jnp.max(logits, -1, keepdims=True))
    prob = raised * (1.0 / jnp.sum(raised, -1, keepdims=True))
    prob_ref[...] = prob
    gate = jnp.sum(prob * chosen_of(flat(choice_ref), prob.shape[1]), -1, keepdims=True)
    width = normed.shape[1]
    fill = slot_onehot(flat(choice_ref), flat(slot_ref), send_ref.shape[0])
    send_ref[:, :width] = dot(fill, normed.astype(bf16)).astype(bf16)
    send_ref[:, width:] = dot(fill, columns3(gate, 128)).astype(bf16)


def expert_kernel(
    tensor_size, sources, unroll,
    recv_ref, cot_ref, win_ref, wout_ref,
    rows_ref, grads_ref, act_ref, grad_act_ref, dots_ref, result_ref, *refs,
):
    chunks = refs[:tensor_size]
    x_all, g_all, r_all, d_all, turned = refs[tensor_size:]
    slots = recv_ref.shape[0]
    width = cot_ref.shape[1]
    step = pl.program_id(0)
    local = pl.num_programs(0) * unroll
    per = rows_ref.shape[0] // unroll

    @pl.when(step == 0)
    def _():
        order = slot_order(slots, win_ref.shape[0] * (slots // rows_ref.shape[0]), sources)
        x_all[...] = dot(order, recv_ref[:, :width]).astype(bf16)
        gate = jnp.sum(dot(order, recv_ref[:, width:]), -1, keepdims=True)
        g_all[...] = (gate * cot_ref[...].astype(f32)).astype(bf16)

    for u in range(unroll):
        here = pl.ds(u * per, per)
        at = pl.ds(pl.multiple_of((step * unroll + u) * per, 16), per)
        x = x_all[at, :]
        g = g_all[at, :]
        weight_in = win_ref[u]
        weight_out = wout_ref[u]
        pre = dot(x, weight_in)
        grad_act = dot(g, weight_out, NT)
        inner = jnp.tanh(gelu_const * (pre + gelu_cubic * pre * pre * pre))
        act = (0.5 * pre * (1.0 + inner)).astype(bf16)
        slope = 0.5 * (1.0 + inner) + 0.5 * pre * (1.0 - inner * inner) * gelu_const * (
            1.0 + 3.0 * gelu_cubic * pre * pre
        )
        grad_act = (grad_act * slope).astype(bf16)
        r_all[at, :] = dot(grad_act, weight_in, NT).astype(bf16)
        result = dot(act, weight_out)
        result_ref[here, :] = result.astype(bf16)
        d_all[at, :] = columns3(jnp.sum(result * cot_ref[at, :].astype(f32), -1, keepdims=True), 128)
        rows_ref[here, :] = x
        grads_ref[here, :] = g
        act_ref[here, :] = act
        grad_act_ref[here, :] = grad_act

    @pl.when(step == pl.num_programs(0) - 1)
    def _():
        order = slot_order(slots, win_ref.shape[0] * (slots // rows_ref.shape[0]), sources)
        dots_ref[...] = dot(d_all[...], order, TN)[:EXTRA].astype(bf16)
        turn_chunks(tensor_size, dot(r_all[...], order, TN).astype(bf16), turned, chunks)


def turn_chunks(tensor_size, rows, turned, chunks):
    turned[...] = rows
    quarter = rows.shape[0] // tensor_size
    me = lax.axis_index("tensor")
    for shift in range(tensor_size):
        first = lax.rem(me + shift, tensor_size) * quarter
        chunks[shift][...] = turned[pl.ds(pl.multiple_of(first, 64), quarter), :]


def result_kernel(tensor_size, sources, local, rows_ref, *refs):
    order = slot_order(rows_ref.shape[0], local, sources)
    turn_chunks(tensor_size, dot(rows_ref[...], order, TN).astype(bf16), refs[tensor_size], refs[:tensor_size])


def sum_kernel(with_dots, *refs):
    *parts, out_ref = refs
    total = sum(ref[...].astype(f32) for ref in (parts[:-1] if with_dots else parts))
    extra = [parts[-1][...].astype(f32)] if with_dots else []
    rows = total.shape[0] + EXTRA * len(extra)
    blank = jnp.zeros((out_ref.shape[1] - rows, total.shape[1]), f32)
    out_ref[...] = jnp.transpose(jnp.concatenate([total] + extra + [blank], 0)).astype(bf16)


def back_kernel(recv_ref, choice_ref, slot_ref, out_ref):
    fill = slot_onehot(flat(choice_ref), flat(slot_ref), recv_ref.shape[0])
    out_ref[...] = dot(recv_ref[...], fill, TN)[: out_ref.shape[0]].astype(bf16)


def spread(refs, quarter, turned):
    size = len(refs)
    me = lax.axis_index("tensor")
    for shift, ref in enumerate(refs):
        first = lax.rem(me + size - shift, size) * quarter
        turned[pl.ds(pl.multiple_of(first, 64), quarter), :] = ref[pl.ds(0, quarter), :].astype(f32)
    return jnp.transpose(turned[...])


def hidden_backward_kernel(
    hidden_ref, prob_ref, cot_ref, gain_ref, rw_ref, choice_ref, att_ref, *refs,
):
    parts = refs[:-4]
    grad_hidden_ref, low_ref, sums_ref, turned = refs[-4:]
    hidden = hidden_ref[...]
    rows, width = hidden.shape
    quarter = width // len(parts)
    grad_routed = spread(parts, quarter, turned)
    dots = sum(jnp.sum(ref[pl.ds(quarter, EXTRA), :].astype(f32), 0, keepdims=True) for ref in parts)
    prob = prob_ref[...]
    chosen = chosen_of(flat(choice_ref), prob.shape[1])
    gate = jnp.sum(prob * chosen, -1, keepdims=True)
    grad_gate = column_of(dots)[:, :1]
    grad_logits = (grad_gate * gate) * (chosen - prob)
    grad_normed = grad_routed + dot3(grad_logits, rw_ref[...])
    gain = flat(gain_ref)
    scale = lax.rsqrt(jnp.mean(hidden * hidden, -1, keepdims=True) + norm_eps)
    scaled = grad_normed * gain
    grad_hidden = (
        cot_ref[...].astype(f32)
        + scale * scaled
        - hidden * (scale * scale * scale) * jnp.mean(scaled * hidden, -1, keepdims=True)
    )
    grad_hidden_ref[...] = grad_hidden
    low = grad_hidden.astype(bf16)
    low_ref[...] = low
    at, experts = att_ref.shape[0], prob.shape[1]
    sums_ref[pl.ds(0, at), :] = dot(att_ref[...], low).astype(bf16)
    sums_ref[pl.ds(at, experts), :] = dot3(grad_logits, hidden * scale * gain, TN).astype(bf16)
    tail = sums_ref.shape[0] - at - experts
    sums_ref[pl.ds(at + experts, tail), :] = rows3([jnp.sum(grad_normed * hidden * scale, 0, keepdims=True)], tail)


def output_kernel(hidden_ref, prob_ref, choice_ref, *refs):
    parts, (out_ref, turned) = refs[:-2], refs[-2:]
    hidden = hidden_ref[...]
    result = spread(parts, hidden.shape[1] // len(parts), turned)
    prob = prob_ref[...]
    gate = jnp.sum(prob * chosen_of(flat(choice_ref), prob.shape[1]), -1, keepdims=True)
    out_ref[...] = (hidden + gate * result).astype(bf16)


def make(mesh):
    tensor_size = mesh.shape["tensor"]
    expert_size = mesh.shape["expert"]

    def shards(
        tokens,
        segment_ids,
        expert_choice,
        slot_index,
        first_gain,
        input_weight,
        bias_table,
        output_weight,
        second_gain,
        router_weight,
        expert_in,
        expert_out,
        cotangent,
    ):
        token_count, width = tokens.shape
        sequences, length = segment_ids.shape
        quarter = output_weight.shape[0]
        experts = router_weight.shape[1]
        local = expert_in.shape[0]
        hidden_units = expert_in.shape[2]
        slots = experts * CAP
        per = slots // local
        chunk = slots // expert_size
        buckets, heads = bias_table.shape
        expert_index = lax.axis_index("expert")
        seg = (segment_ids + 8 * jnp.arange(sequences, dtype=i32)[:, None]).reshape(1, token_count)
        choice, slot = expert_choice, slot_index
        gain_first, gain_second = first_gain, second_gain
        iw_own = jnp.swapaxes(input_weight, 1, 2)
        table = bias_table.T
        rw = router_weight.T
        after = lax.optimization_barrier

        shifts = [[(i, (i + s) % tensor_size) for i in range(tensor_size)] for s in range(1, tensor_size)]

        def from_others(array):
            return [lax.ppermute(array, "tensor", pairs) for pairs in shifts]

        def gather_tensor(array):
            return [array] + from_others(array)

        def joined(planes):
            got = lax.all_gather(planes, "expert", axis=0)
            return jnp.swapaxes(got, 0, 1).reshape(tensor_size - 1, -1, got.shape[-1])

        def exchange(array):
            rows = array.shape[0] // expert_size
            got = lax.all_to_all(array.reshape(expert_size, rows, array.shape[1]), "expert", 0, 0)
            return got.reshape(array.shape)

        ow_rows = quarter // expert_size
        ow_part = lax.dynamic_slice_in_dim(output_weight, expert_index * ow_rows, ow_rows, 0)
        ow_all = joined(jnp.stack(from_others(ow_part)))

        attended, first_normed = call(
            forward_kernel,
            [((quarter, token_count), bf16), ((token_count, width), bf16)],
            (tokens, gain_first, iw_own, table, seg),
            [
                pltpu.VMEM((token_count + 2 * BLOCK, quarter), bf16),
                pltpu.VMEM((quarter, token_count + 2 * BLOCK), bf16),
            ],
        )
        attended_parts = gather_tensor(attended)
        (cot_slots,) = call(cotangent_kernel, [((slots, width), bf16)], (cotangent, choice, slot))
        cot_recv = exchange(cot_slots)
        attended_parts, cot_recv = after((attended_parts, cot_recv))

        hidden, prob, send = call(
            middle_kernel,
            [((token_count, width), f32), ((token_count, experts), f32), ((slots, width + 128), bf16)],
            (tokens, output_weight, ow_all, gain_second, rw, choice, slot, *attended_parts),
        )
        recv = exchange(send)
        cot_recv, _ = after((cot_recv, send))
        (cot_rows,) = call(
            lambda *refs: order_kernel(expert_size, local, *refs), [((slots, width), bf16)], (cot_recv,)
        )

        iw_rows = 3 * quarter // expert_size
        iw_part = lax.dynamic_slice_in_dim(iw_own.reshape(3 * quarter, width), expert_index * iw_rows, iw_rows, 0)
        bias_parts = jnp.stack(split3(table)).astype(bf16).reshape(-1)
        bias_parts = jnp.pad(bias_parts, (0, 8 * width - bias_parts.shape[0])).reshape(8, width)
        iw_part, _ = after((jnp.concatenate([iw_part, bias_parts], 0), send))
        iw_planes = from_others(iw_part)

        unroll = 2 if local % 2 == 0 else 1
        whole = lambda shape: pl.BlockSpec(shape, lambda j: (0,) * len(shape))
        by_expert = pl.BlockSpec((unroll * per, width), lambda j: (j, 0))
        by_hidden = pl.BlockSpec((unroll * per, hidden_units), lambda j: (j, 0))
        outs = pl.pallas_call(
            lambda *refs: expert_kernel(tensor_size, expert_size, unroll, *refs),
            grid=(local // unroll,),
            in_specs=[
                whole((slots, width + 128)),
                whole((slots, width)),
                pl.BlockSpec((unroll, width, hidden_units), lambda j: (j, 0, 0)),
                pl.BlockSpec((unroll, hidden_units, width), lambda j: (j, 0, 0)),
            ],
            out_specs=[by_expert, by_expert, by_hidden, by_hidden, whole((EXTRA, slots)), by_expert]
            + [whole((quarter, slots))] * tensor_size,
            out_shape=[jax.ShapeDtypeStruct((slots, width), bf16)] * 2
            + [jax.ShapeDtypeStruct((slots, hidden_units), bf16)] * 2
            + [jax.ShapeDtypeStruct((EXTRA, slots), bf16), jax.ShapeDtypeStruct((slots, width), bf16)]
            + [jax.ShapeDtypeStruct((quarter, slots), bf16)] * tensor_size,
            scratch_shapes=[pltpu.VMEM((slots, width), bf16)] * 3
            + [pltpu.VMEM((slots, 128), bf16), pltpu.VMEM((width, slots), bf16)],
            compiler_params=pltpu.CompilerParams(vmem_limit_bytes=56 * 2**20),
        )(recv, cot_rows, expert_in, expert_out)
        expert_rows, grad_slots, expert_act, grad_act, dots, result_rows = outs[:6]
        grad_chunks = outs[6:]

        def trade_chunks(chunks):
            return [chunks[0]] + [lax.ppermute(c, "tensor", pairs) for c, pairs in zip(chunks[1:], shifts)]

        def sum_rows(parts, with_dots):
            columns = -(-(quarter + (EXTRA if with_dots else 0)) // 128) * 128
            return call(lambda *refs: sum_kernel(with_dots, *refs), [((slots, columns), bf16)], parts)[0]

        def own_tokens(rows, kept):
            return call(back_kernel, [((kept, token_count), bf16)], (rows, choice, slot))[0]

        by = lambda array: array.reshape(local, per, array.shape[1])
        grad_expert_out = jnp.einsum("erf,erd->efd", by(expert_act), by(grad_slots), preferred_element_type=f32)
        grad_expert_in = jnp.einsum("erd,erf->edf", by(expert_rows), by(grad_act), preferred_element_type=f32)

        iw_planes, _ = after((iw_planes, grad_chunks[0]))
        iw_planes = jnp.stack(iw_planes)
        iw_all = joined(iw_planes[:, :iw_rows])
        bias_all = jnp.sum(
            iw_planes[:, iw_rows:]
            .reshape(tensor_size - 1, -1)[:, : 3 * buckets * heads]
            .reshape(tensor_size - 1, 3, heads, buckets)
            .astype(f32),
            1,
        )
        result_chunks = call(
            lambda *refs: result_kernel(tensor_size, expert_size, local, *refs),
            [((quarter, slots), bf16)] * tensor_size,
            (result_rows,),
            [pltpu.VMEM((width, slots), bf16)],
        )
        traded, result_chunks, grad_expert_out = after((trade_chunks(grad_chunks), result_chunks, grad_expert_out))
        summed = sum_rows(traded + [dots], True)
        result_chunks, _ = after((result_chunks, summed))
        result_traded = trade_chunks(result_chunks)
        returned = own_tokens(exchange(summed), quarter + EXTRA)
        returned, grad_expert_in = after((returned, grad_expert_in))
        grad_parts = gather_tensor(returned)
        result_traded, _ = after((result_traded, grad_parts[1]))
        result_own = own_tokens(exchange(sum_rows(result_traded, False)), quarter)
        grad_parts, iw_all, bias_all = after((grad_parts, iw_all, bias_all))

        early_rows = quarter + experts + 64
        grad_hidden, grad_low, early_sums = call(
            hidden_backward_kernel,
            [((token_count, width), f32), ((token_count, width), bf16), ((early_rows, width), bf16)],
            (hidden, prob, cotangent, gain_second, rw, choice, attended, *grad_parts),
            [pltpu.VMEM((width, token_count), f32)],
        )
        def sum_experts(array):
            return jnp.sum(exchange(array).reshape(expert_size, -1, array.shape[1]).astype(f32), 0)

        padded = token_count + 2 * BLOCK
        scratch = [pltpu.VMEM((padded, quarter), bf16)] * 2 + [pltpu.VMEM((quarter, padded), bf16)]
        scratch = scratch + [pltpu.VMEM((padded, quarter), f32)] * 2 + [pltpu.VMEM((quarter, token_count), f32)]
        grad_low, result_own = after((grad_low, result_own))
        grad_iw, own_parts, table_grad = call(
            own_backward_kernel,
            [((3 * quarter, width), bf16), ((3, token_count, quarter), bf16), ((1, width), f32)],
            (first_normed, iw_own, output_weight, table, seg, grad_low),
            scratch,
        )
        result_own, _ = after((result_own, grad_iw))
        result_parts = gather_tensor(result_own)
        early_sums, _ = after((early_sums, grad_iw))
        others = tensor_size - 1
        total = None
        for group in range(others):
            last = group == others - 1
            args = [first_normed, iw_all, ow_all, bias_all, seg, grad_low]
            specs = [pl.BlockSpec(array.shape, lambda j, n=array.ndim: (0,) * n) for array in args]
            for place in (1, 2, 3):
                array = args[place]
                specs[place] = pl.BlockSpec((1,) + array.shape[1:], lambda j, g=group: (g, 0, 0))
            more = [total] if group else [own_parts, iw_own]
            more += [tokens, gain_first, grad_hidden, table_grad] if last else []
            specs += [pl.BlockSpec(array.shape, lambda j, n=array.ndim: (0,) * n) for array in more]
            shapes = [jax.ShapeDtypeStruct((token_count, width), f32)]
            shapes += [jax.ShapeDtypeStruct((8, width), bf16)] if last else []
            outs = pl.pallas_call(
                lambda *refs, first=group == 0, last=last: group_kernel(first, last, *refs),
                grid=(1,),
                in_specs=specs,
                out_specs=[pl.BlockSpec(shape.shape, lambda j: (0, 0)) for shape in shapes],
                out_shape=shapes,
                scratch_shapes=scratch,
                compiler_params=pltpu.CompilerParams(vmem_limit_bytes=56 * 2**20),
            )(*args, *more)
            total = outs[0]
        grad_tokens, tail = outs
        (block_output,) = call(
            output_kernel,
            [((token_count, width), bf16)],
            (hidden, prob, choice, *result_parts),
            [pltpu.VMEM((width, token_count), f32)],
        )
        early_sum = sum_experts(early_sums).astype(f32)
        early = lax.all_gather(jnp.pad(early_sum, ((0, 8), (0, 0))), "expert", axis=0)
        early = early[:, : early_sum.shape[0]].reshape(early_rows, width)
        late = lax.all_gather(jnp.concatenate([sum_experts(grad_iw).astype(bf16), tail], 0), "expert", axis=0)
        grad_iw, grad_ow, grad_rw, grad_second, grad_first, grad_table = call(
            finish_kernel,
            [
                ((3 * quarter, width), f32),
                ((quarter, width), f32),
                ((experts, width), f32),
                ((width,), f32),
                ((width,), f32),
                ((1, width), f32),
            ],
            (late, early),
        )
        return (
            block_output,
            grad_tokens,
            grad_first,
            jnp.swapaxes(grad_iw.reshape(3, quarter, width), 1, 2),
            grad_table.reshape(width // 128, 128)[:heads, :buckets].T,
            grad_ow,
            grad_second,
            grad_rw.T,
            grad_expert_in,
            grad_expert_out,
        )

    return shards


def solution(mesh):
    placed = (
        P("expert", None),
        P("expert", None),
        P("expert"),
        P("expert"),
        P(),
        P(None, None, "tensor"),
        P(None, "tensor"),
        P("tensor", None),
        P(),
        P(),
        P("expert", None, "tensor"),
        P("expert", "tensor", None),
        P("expert", None),
    )
    return jax.shard_map(
        make(mesh),
        mesh=mesh,
        in_specs=placed,
        out_specs=(
            P("expert", None),
            P("expert", None),
            P(),
            P(None, None, "tensor"),
            P(None, "tensor"),
            P("tensor", None),
            P(),
            P(),
            P("expert", None, "tensor"),
            P("expert", "tensor", None),
        ),
        check_vma=False,
    )
```

```python
import math

import jax
import jax.numpy as jnp
from jax import lax
from jax.experimental import pallas as pl
from jax.experimental.pallas import tpu as pltpu
from jax.sharding import PartitionSpec as P

CAP = 10

bucket_edges = (12, 16, 23, 32, 46, 64, 91)
norm_eps = 1e-06
masked_score = -1e30
gelu_const = math.sqrt(2.0 / math.pi)
gelu_cubic = 0.044715

BLOCK = 128
BAND = 3 * BLOCK
ROLL = 4 * BLOCK
HEAD = 64
EXTRA = 16

bf16 = jnp.bfloat16
f32 = jnp.float32
i32 = jnp.int32
highest = lax.Precision.HIGHEST

NN = (((1,), (0,)), ((), ()))
NT = (((1,), (1,)), ((), ()))
TN = (((0,), (0,)), ((), ()))


def dot(left, right, dims=NN, precision=None):
    return lax.dot_general(left, right, dims, precision=precision, preferred_element_type=f32)


def dot3(left, right, dims=NN):
    left_high, right_high = left.astype(bf16), right.astype(bf16)
    left_low = (left - left_high.astype(f32)).astype(bf16)
    right_low = (right - right_high.astype(f32)).astype(bf16)
    return dot(left_high, right_high, dims) + (dot(left_high, right_low, dims) + dot(left_low, right_high, dims))


def flat(ref):
    return ref[...].reshape(1, -1)


def iota(shape, axis):
    return lax.broadcasted_iota(i32, shape, axis)


def call(kernel, outs, args, scratch=(), **extra):
    vmem = pl.BlockSpec(memory_space=pltpu.VMEM)
    return pl.pallas_call(
        kernel,
        out_shape=[jax.ShapeDtypeStruct(shape, dtype) for shape, dtype in outs],
        in_specs=[vmem] * len(args),
        out_specs=[vmem] * len(outs),
        scratch_shapes=list(scratch),
        compiler_params=pltpu.CompilerParams(vmem_limit_bytes=56 * 2**20),
        **extra,
    )(*args)


def split3(value):
    high = value.astype(bf16).astype(f32)
    rest = value - high
    middle = rest.astype(bf16).astype(f32)
    return high, middle, rest - middle


def columns3(value, width):
    high, middle, low = split3(value)
    lane = iota((value.shape[0], width), 1)
    picked = jnp.where(lane == 0, high, jnp.where(lane == 1, middle, jnp.where(lane == 2, low, 0.0)))
    return picked.astype(bf16)


def column_of(row):
    return jnp.transpose(jnp.broadcast_to(row.astype(f32), (128, row.shape[1])))


def wide(column, width):
    return jnp.concatenate([column] * (width // 128), 1)


def bucket_of(relative):
    distance = jnp.abs(relative)
    beyond = jnp.zeros_like(distance)
    for threshold in bucket_edges:
        beyond = beyond + (distance >= threshold).astype(i32)
    magnitude = jnp.where(distance < 8, distance, 8 + beyond)
    return magnitude + 16 * (relative > 0).astype(i32)


def band_rows(table):
    buckets = table.shape[1]
    offset = iota((buckets, ROLL), 1)
    relative = jnp.where(offset < BAND, offset, offset - ROLL) - BLOCK
    onehot = (bucket_of(relative) == iota((buckets, ROLL), 0)).astype(f32)
    return dot(table, onehot, precision=highest), onehot


def bias_tiles(table):
    rows, onehot = band_rows(table)
    tiles = []
    for h in range(table.shape[0]):
        full = jnp.broadcast_to(rows[h : h + 1], (BLOCK, ROLL))
        tiles.append(jnp.transpose(pltpu.roll(full, 0, 1, stride=1, stride_axis=0)[:, :BAND]))
    return tiles, onehot


def head_masks(heads):
    lane = iota((1, heads * HEAD), 1)
    return [((lane >= h * HEAD) & (lane < (h + 1) * HEAD)).astype(f32).astype(bf16) for h in range(heads)]


def padded_segments(seg):
    edge = jnp.full((1, BLOCK), -1.0, f32)
    return column_of(jnp.concatenate([edge, seg, edge], 1))


def first_norm(tok, gain):
    scale = lax.rsqrt(jnp.mean(tok * tok, -1, keepdims=True) + norm_eps)
    return (tok * scale * gain).astype(bf16), scale


def probabilities(scores, bias, same):
    scores = jnp.where(same, scores + bias, masked_score)
    weights = jnp.exp(scores - jnp.max(scores, 0, keepdims=True))
    return weights * (1.0 / jnp.sum(weights, 0, keepdims=True))


def stack_heads(rows, masks):
    return jnp.concatenate([rows * mask for mask in masks], 0)


def own_blocks(product, heads):
    return jnp.concatenate(
        [product[h * HEAD : (h + 1) * HEAD, h * BLOCK : (h + 1) * BLOCK] for h in range(heads)], 0
    )


def fill_rows(ref, value):
    rows = value.shape[0]
    edge = jnp.zeros((BLOCK, value.shape[1]), bf16)
    ref[pl.ds(0, BLOCK), :] = edge
    ref[pl.ds(rows + BLOCK, BLOCK), :] = edge
    ref[pl.ds(BLOCK, rows), :] = value


def fill_columns(ref, value):
    rows = value.shape[1]
    edge = jnp.zeros((value.shape[0], BLOCK), bf16)
    ref[:, pl.ds(0, BLOCK)] = edge
    ref[:, pl.ds(rows + BLOCK, BLOCK)] = edge
    ref[:, pl.ds(BLOCK, rows)] = value


def forward_kernel(tok_ref, gain_ref, iw_ref, bt_ref, seg_ref, att_ref, normed_ref, keys, values):
    rows = tok_ref.shape[0]
    normed, _ = first_norm(tok_ref[...].astype(f32), flat(gain_ref))
    normed_ref[...] = normed
    queries = dot(normed, iw_ref[0], NT).astype(bf16)
    fill_rows(keys, dot(normed, iw_ref[1], NT).astype(bf16))
    fill_columns(values, dot(iw_ref[2], normed, NT).astype(bf16))
    seg = seg_ref[...].astype(f32)
    seg_keys = padded_segments(seg)
    tiles, _ = bias_tiles(bt_ref[...])
    heads = len(tiles)
    masks = head_masks(heads)
    for block in range(rows // BLOCK):
        at = block * BLOCK
        same = seg_keys[at : at + BAND] == seg[:, at : at + BLOCK]
        scores = dot(keys[pl.ds(at, BAND), :], stack_heads(queries[at : at + BLOCK], masks), NT)
        weights = [
            probabilities(scores[:, h * BLOCK : (h + 1) * BLOCK], tiles[h], same).astype(bf16) for h in range(heads)
        ]
        product = dot(values[:, pl.ds(at, BAND)], jnp.concatenate(weights, 1))
        att_ref[:, pl.ds(at, BLOCK)] = own_blocks(product, heads).astype(bf16)


def group_backward(normed, weight, out_weight, table, seg, grad_low, scratch, bias_grads):
    keys, values, keys_across, grad_keys, grad_values, grad_queries = scratch
    rows = normed.shape[0]
    queries = dot(normed, weight[0], NT).astype(bf16)
    fill_rows(keys, dot(normed, weight[1], NT).astype(bf16))
    fill_columns(keys_across, dot(weight[1], normed, NT).astype(bf16))
    fill_rows(values, dot(normed, weight[2], NT).astype(bf16))
    grad_att = dot(grad_low, out_weight, NT).astype(bf16)
    grad_keys[...] = jnp.zeros(grad_keys.shape, f32)
    grad_values[...] = jnp.zeros(grad_values.shape, f32)
    seg_keys = padded_segments(seg)
    tiles, onehot = bias_tiles(table)
    heads = len(tiles)
    masks = head_masks(heads)
    sums = [None] * heads
    for block in range(rows // BLOCK):
        at = block * BLOCK
        same = seg_keys[at : at + BAND] == seg[:, at : at + BLOCK]
        head_queries = stack_heads(queries[at : at + BLOCK], masks)
        head_grads = stack_heads(grad_att[at : at + BLOCK], masks)
        scores = dot(keys[pl.ds(at, BAND), :], head_queries, NT)
        grad_probs = dot(values[pl.ds(at, BAND), :], head_grads, NT)
        all_weights, all_grads = [], []
        for h in range(heads):
            columns = slice(h * BLOCK, (h + 1) * BLOCK)
            weights = probabilities(scores[:, columns], tiles[h], same)
            scaled = weights * grad_probs[:, columns]
            grad_scores = scaled - weights * jnp.sum(scaled, 0, keepdims=True)
            all_weights.append(weights.astype(bf16))
            all_grads.append(grad_scores.astype(bf16))
            if bias_grads:
                sums[h] = grad_scores if sums[h] is None else sums[h] + grad_scores
        low = jnp.concatenate(all_grads, 1)
        grad_queries[:, pl.ds(at, BLOCK)] = own_blocks(dot(keys_across[:, pl.ds(at, BAND)], low), heads)
        grad_keys[pl.ds(at, BAND), :] += dot(low, head_queries)
        grad_values[pl.ds(at, BAND), :] += dot(jnp.concatenate(all_weights, 1), head_grads)
    parts = (
        jnp.transpose(grad_queries[...]).astype(bf16),
        grad_keys[pl.ds(BLOCK, rows), :].astype(bf16),
        grad_values[pl.ds(BLOCK, rows), :].astype(bf16),
    )
    if not bias_grads:
        return parts, None
    diagonals = []
    row_index = iota((BLOCK, ROLL), 0)
    for h in range(heads):
        moved = jnp.concatenate([jnp.transpose(sums[h]), jnp.zeros((BLOCK, ROLL - BAND), f32)], 1)
        step = 1
        while step < BLOCK:
            moved = jnp.where((row_index & step) != 0, pltpu.roll(moved, ROLL - step, 1), moved)
            step *= 2
        diagonals.append(jnp.sum(moved, 0, keepdims=True))
    onehot = jnp.concatenate([onehot, jnp.zeros((128 - onehot.shape[0], ROLL), f32)], 0)
    by_head = dot(jnp.concatenate(diagonals, 0), onehot, NT, precision=highest)
    return parts, jnp.concatenate([by_head[h : h + 1] for h in range(heads)], 1)


def own_backward_kernel(normed_ref, iw_ref, ow_ref, bt_ref, seg_ref, low_ref, grad_iw_ref, parts_ref, table_ref, *scratch):
    normed = normed_ref[...]
    parts, table_grad = group_backward(
        normed, iw_ref, ow_ref[...], bt_ref[...], seg_ref[...].astype(f32), low_ref[...], scratch, True
    )
    table_ref[...] = jnp.concatenate(
        [table_grad, jnp.zeros((1, table_ref.shape[1] - table_grad.shape[1]), f32)], 1
    )
    width = ow_ref.shape[0]
    for j in range(3):
        parts_ref[j] = parts[j]
        grad_iw_ref[pl.ds(j * width, width), :] = dot(parts[j], normed, TN).astype(bf16)


def rest_backward_kernel(
    normed_ref, own_iw_ref, iw_ref, ow_ref, bt_ref, seg_ref, low_ref, parts_ref, tok_ref, gain_ref, grad_hidden_ref,
    table_ref, grad_tok_ref, tail_ref, total, *scratch,
):
    width = ow_ref.shape[1]
    total[...] = sum(dot(parts_ref[j], own_iw_ref[j]) for j in range(3))

    def step(group, carry):
        weight = [iw_ref[group, pl.ds(j * width, width), :] for j in range(3)]
        parts, _ = group_backward(
            normed_ref[...], weight, ow_ref[group], bt_ref[group], seg_ref[...].astype(f32), low_ref[...], scratch, False
        )
        total[...] += sum(dot(parts[j], weight[j]) for j in range(3))
        return carry

    lax.fori_loop(0, ow_ref.shape[0], step, 0)
    tok = tok_ref[...].astype(f32)
    gain = flat(gain_ref)
    scale = lax.rsqrt(jnp.mean(tok * tok, -1, keepdims=True) + norm_eps)
    grad_normed = total[...]
    tail_ref[...] = rows3([jnp.sum(grad_normed * tok * scale, 0, keepdims=True), table_ref[...]], tail_ref.shape[0])
    scaled = grad_normed * gain
    grad_tok_ref[...] = (
        grad_hidden_ref[...]
        + scale * scaled
        - tok * (scale * scale * scale) * jnp.mean(scaled * tok, -1, keepdims=True)
    )


def rows3(values, count):
    parts = [part for value in values for part in split3(value)]
    row = iota((count, values[0].shape[1]), 0)
    total = jnp.zeros(row.shape, f32)
    for index, part in enumerate(parts):
        total = jnp.where(row == index, part, total)
    return total.astype(bf16)


def finish_kernel(late_ref, early_ref, *refs):
    grad_iw_ref, grad_ow_ref, grad_rw_ref, second_ref, first_ref, table_ref = refs
    devices = late_ref.shape[0]
    late_rows = grad_iw_ref.shape[0] // devices
    tail = jnp.zeros((late_ref.shape[1] - late_rows, late_ref.shape[2]), f32)
    for device in range(devices):
        block = late_ref[device].astype(f32)
        grad_iw_ref[pl.ds(device * late_rows, late_rows), :] = block[:late_rows]
        tail = tail + block[late_rows:]
    first_ref[...] = jnp.sum(tail[:3], 0)
    table_ref[...] = jnp.sum(tail[3:6], 0, keepdims=True)
    at, experts = grad_ow_ref.shape[0], grad_rw_ref.shape[0]
    early = early_ref[...]
    grad_ow_ref[...] = early[:at]
    grad_rw_ref[...] = early[at : at + experts]
    second_ref[...] = jnp.sum(early[at + experts : at + experts + 8], 0)


def slot_onehot(choice, slot, slots):
    dest = jnp.where(slot >= 0, choice * CAP + slot, slots)
    return (iota((slots, dest.shape[1]), 0) == dest).astype(f32).astype(bf16)


def slot_order(slots, group, across):
    index = iota((1, slots), 1)
    big, small = slots // across, slots // group
    outer, rest = lax.div(index, big), lax.rem(index, big)
    target = lax.div(rest, CAP) * small + outer * CAP + lax.rem(rest, CAP)
    return (iota((slots, slots), 0) == target).astype(f32).astype(bf16)


def cotangent_kernel(cot_ref, choice_ref, slot_ref, out_ref):
    fill = slot_onehot(flat(choice_ref), flat(slot_ref), out_ref.shape[0])
    out_ref[...] = dot(fill, cot_ref[...]).astype(bf16)


def order_kernel(sources, local, rows_ref, out_ref):
    out_ref[...] = dot(slot_order(rows_ref.shape[0], local, sources), rows_ref[...]).astype(bf16)


def chosen_of(choice, experts):
    column = column_of(choice)[:, :experts]
    return (column == iota(column.shape, 1).astype(f32)).astype(f32)


def middle_kernel(tok_ref, own_ow_ref, ow_ref, gain_ref, rw_ref, choice_ref, slot_ref, *refs):
    att_refs, (hidden_ref, prob_ref, send_ref) = refs[:-3], refs[-3:]
    hidden = tok_ref[...].astype(f32)
    for shift, att_ref in enumerate(att_refs):
        hidden = hidden + dot(att_ref[...], ow_ref[shift - 1] if shift else own_ow_ref[...], TN)
    hidden_ref[...] = hidden
    scale = lax.rsqrt(jnp.mean(hidden * hidden, -1, keepdims=True) + norm_eps)
    normed = hidden * scale * flat(gain_ref)
    logits = dot3(normed, rw_ref[...], NT)
    raised = jnp.exp(logits - jnp.max(logits, -1, keepdims=True))
    prob = raised * (1.0 / jnp.sum(raised, -1, keepdims=True))
    prob_ref[...] = prob
    gate = jnp.sum(prob * chosen_of(flat(choice_ref), prob.shape[1]), -1, keepdims=True)
    width = normed.shape[1]
    fill = slot_onehot(flat(choice_ref), flat(slot_ref), send_ref.shape[0])
    send_ref[:, :width] = dot(fill, normed.astype(bf16)).astype(bf16)
    send_ref[:, width:] = dot(fill, columns3(gate, 128)).astype(bf16)


def expert_kernel(
    tensor_size, sources, unroll,
    recv_ref, cot_ref, win_ref, wout_ref,
    rows_ref, grads_ref, act_ref, grad_act_ref, dots_ref, result_ref, *refs,
):
    chunks = refs[:tensor_size]
    x_all, g_all, r_all, d_all, turned = refs[tensor_size:]
    slots = recv_ref.shape[0]
    width = cot_ref.shape[1]
    step = pl.program_id(0)
    local = pl.num_programs(0) * unroll
    per = rows_ref.shape[0] // unroll

    @pl.when(step == 0)
    def _():
        order = slot_order(slots, win_ref.shape[0] * (slots // rows_ref.shape[0]), sources)
        x_all[...] = dot(order, recv_ref[:, :width]).astype(bf16)
        gate = jnp.sum(dot(order, recv_ref[:, width:]), -1, keepdims=True)
        g_all[...] = (gate * cot_ref[...].astype(f32)).astype(bf16)

    for u in range(unroll):
        here = pl.ds(u * per, per)
        at = pl.ds(pl.multiple_of((step * unroll + u) * per, 16), per)
        x = x_all[at, :]
        g = g_all[at, :]
        weight_in = win_ref[u]
        weight_out = wout_ref[u]
        pre = dot(x, weight_in)
        grad_act = dot(g, weight_out, NT)
        inner = jnp.tanh(gelu_const * (pre + gelu_cubic * pre * pre * pre))
        act = (0.5 * pre * (1.0 + inner)).astype(bf16)
        slope = 0.5 * (1.0 + inner) + 0.5 * pre * (1.0 - inner * inner) * gelu_const * (
            1.0 + 3.0 * gelu_cubic * pre * pre
        )
        grad_act = (grad_act * slope).astype(bf16)
        r_all[at, :] = dot(grad_act, weight_in, NT).astype(bf16)
        result = dot(act, weight_out)
        result_ref[here, :] = result.astype(bf16)
        d_all[at, :] = columns3(jnp.sum(result * cot_ref[at, :].astype(f32), -1, keepdims=True), 128)
        rows_ref[here, :] = x
        grads_ref[here, :] = g
        act_ref[here, :] = act
        grad_act_ref[here, :] = grad_act

    @pl.when(step == pl.num_programs(0) - 1)
    def _():
        order = slot_order(slots, win_ref.shape[0] * (slots // rows_ref.shape[0]), sources)
        dots_ref[...] = dot(d_all[...], order, TN)[:EXTRA].astype(bf16)
        turn_chunks(tensor_size, dot(r_all[...], order, TN).astype(bf16), turned, chunks)


def turn_chunks(tensor_size, rows, turned, chunks):
    turned[...] = rows
    quarter = rows.shape[0] // tensor_size
    me = lax.axis_index("tensor")
    for shift in range(tensor_size):
        first = lax.rem(me + shift, tensor_size) * quarter
        chunks[shift][...] = turned[pl.ds(pl.multiple_of(first, 64), quarter), :]


def result_kernel(sources, local, rows_ref, out_ref):
    out_ref[...] = dot(slot_order(rows_ref.shape[0], local, sources), rows_ref[...], TN).astype(bf16)


def result_back_kernel(recv_ref, choice_ref, slot_ref, out_ref):
    fill = slot_onehot(flat(choice_ref), flat(slot_ref), recv_ref.shape[0])
    out_ref[...] = dot(fill, recv_ref[...], TN).astype(bf16)


def sum_kernel(*refs):
    *parts, dots_ref, out_ref = refs
    total = sum(ref[...].astype(f32) for ref in parts)
    blank = jnp.zeros((out_ref.shape[1] - total.shape[0] - EXTRA, total.shape[1]), f32)
    out_ref[...] = jnp.transpose(jnp.concatenate([total, dots_ref[...].astype(f32), blank], 0)).astype(bf16)


def back_kernel(recv_ref, choice_ref, slot_ref, out_ref):
    fill = slot_onehot(flat(choice_ref), flat(slot_ref), recv_ref.shape[0])
    out_ref[...] = dot(recv_ref[...], fill, TN)[: out_ref.shape[0]].astype(bf16)


def spread(refs, quarter, turned):
    size = len(refs)
    me = lax.axis_index("tensor")
    for shift, ref in enumerate(refs):
        first = lax.rem(me + size - shift, size) * quarter
        turned[pl.ds(pl.multiple_of(first, 64), quarter), :] = ref[pl.ds(0, quarter), :].astype(f32)
    return jnp.transpose(turned[...])


def hidden_backward_kernel(
    hidden_ref, prob_ref, cot_ref, gain_ref, rw_ref, choice_ref, att_ref, *refs,
):
    parts = refs[:-4]
    grad_hidden_ref, low_ref, sums_ref, turned = refs[-4:]
    hidden = hidden_ref[...]
    rows, width = hidden.shape
    quarter = width // len(parts)
    grad_routed = spread(parts, quarter, turned)
    dots = sum(jnp.sum(ref[pl.ds(quarter, EXTRA), :].astype(f32), 0, keepdims=True) for ref in parts)
    prob = prob_ref[...]
    chosen = chosen_of(flat(choice_ref), prob.shape[1])
    gate = jnp.sum(prob * chosen, -1, keepdims=True)
    grad_gate = column_of(dots)[:, :1]
    grad_logits = (grad_gate * gate) * (chosen - prob)
    grad_normed = grad_routed + dot3(grad_logits, rw_ref[...])
    gain = flat(gain_ref)
    scale = lax.rsqrt(jnp.mean(hidden * hidden, -1, keepdims=True) + norm_eps)
    scaled = grad_normed * gain
    grad_hidden = (
        cot_ref[...].astype(f32)
        + scale * scaled
        - hidden * (scale * scale * scale) * jnp.mean(scaled * hidden, -1, keepdims=True)
    )
    grad_hidden_ref[...] = grad_hidden
    low = grad_hidden.astype(bf16)
    low_ref[...] = low
    at, experts = att_ref.shape[0], prob.shape[1]
    sums_ref[pl.ds(0, at), :] = dot(att_ref[...], low)
    sums_ref[pl.ds(at, experts), :] = dot3(grad_logits, hidden * scale * gain, TN)
    tail = sums_ref.shape[0] - at - experts
    sums_ref[pl.ds(at + experts, tail), :] = jnp.sum((grad_normed * hidden * scale).reshape(-1, tail, width), 0)


def output_kernel(hidden_ref, prob_ref, choice_ref, result_ref, out_ref):
    prob = prob_ref[...]
    gate = jnp.sum(prob * chosen_of(flat(choice_ref), prob.shape[1]), -1, keepdims=True)
    out_ref[...] = (hidden_ref[...] + gate * result_ref[...].astype(f32)).astype(bf16)


def make(mesh):
    tensor_size = mesh.shape["tensor"]
    expert_size = mesh.shape["expert"]

    def shards(
        tokens,
        segment_ids,
        expert_choice,
        slot_index,
        first_gain,
        input_weight,
        bias_table,
        output_weight,
        second_gain,
        router_weight,
        expert_in,
        expert_out,
        cotangent,
    ):
        token_count, width = tokens.shape
        sequences, length = segment_ids.shape
        quarter = output_weight.shape[0]
        experts = router_weight.shape[1]
        local = expert_in.shape[0]
        hidden_units = expert_in.shape[2]
        slots = experts * CAP
        per = slots // local
        chunk = slots // expert_size
        buckets, heads = bias_table.shape
        expert_index = lax.axis_index("expert")
        seg = (segment_ids + 8 * jnp.arange(sequences, dtype=i32)[:, None]).reshape(1, token_count)
        choice, slot = expert_choice, slot_index
        gain_first, gain_second = first_gain, second_gain
        iw_own = jnp.swapaxes(input_weight, 1, 2)
        table = bias_table.T
        rw = router_weight.T
        after = lax.optimization_barrier

        shifts = [[(i, (i + s) % tensor_size) for i in range(tensor_size)] for s in range(1, tensor_size)]

        def from_others(array):
            return [lax.ppermute(array, "tensor", pairs) for pairs in shifts]

        def gather_tensor(array):
            return [array] + from_others(array)

        def joined(planes):
            got = lax.all_gather(planes, "expert", axis=0)
            return jnp.swapaxes(got, 0, 1).reshape(tensor_size - 1, -1, got.shape[-1])

        def exchange(array):
            rows = array.shape[0] // expert_size
            got = lax.all_to_all(array.reshape(expert_size, rows, array.shape[1]), "expert", 0, 0)
            return got.reshape(array.shape)

        ow_rows = quarter // expert_size
        ow_part = lax.dynamic_slice_in_dim(output_weight, expert_index * ow_rows, ow_rows, 0)
        ow_all = joined(jnp.stack(from_others(ow_part)))

        attended, first_normed = call(
            forward_kernel,
            [((quarter, token_count), bf16), ((token_count, width), bf16)],
            (tokens, gain_first, iw_own, table, seg),
            [
                pltpu.VMEM((token_count + 2 * BLOCK, quarter), bf16),
                pltpu.VMEM((quarter, token_count + 2 * BLOCK), bf16),
            ],
        )
        attended_parts = gather_tensor(attended)
        (cot_slots,) = call(cotangent_kernel, [((slots, width), bf16)], (cotangent, choice, slot))
        cot_recv = exchange(cot_slots)
        attended_parts, cot_recv = after((attended_parts, cot_recv))

        hidden, prob, send = call(
            middle_kernel,
            [((token_count, width), f32), ((token_count, experts), f32), ((slots, width + 128), bf16)],
            (tokens, output_weight, ow_all, gain_second, rw, choice, slot, *attended_parts),
        )
        recv = exchange(send)
        cot_recv, _ = after((cot_recv, send))
        (cot_rows,) = call(
            lambda *refs: order_kernel(expert_size, local, *refs), [((slots, width), bf16)], (cot_recv,)
        )

        iw_rows = 3 * quarter // expert_size
        iw_part = lax.dynamic_slice_in_dim(iw_own.reshape(3 * quarter, width), expert_index * iw_rows, iw_rows, 0)
        bias_parts = jnp.stack(split3(table)).astype(bf16).reshape(-1)
        bias_parts = jnp.pad(bias_parts, (0, 8 * width - bias_parts.shape[0])).reshape(8, width)
        iw_part, _ = after((jnp.concatenate([iw_part, bias_parts], 0), send))
        iw_planes = from_others(iw_part)

        unroll = 2 if local % 2 == 0 else 1
        whole = lambda shape: pl.BlockSpec(shape, lambda j: (0,) * len(shape))
        by_expert = pl.BlockSpec((unroll * per, width), lambda j: (j, 0))
        by_hidden = pl.BlockSpec((unroll * per, hidden_units), lambda j: (j, 0))
        outs = pl.pallas_call(
            lambda *refs: expert_kernel(tensor_size, expert_size, unroll, *refs),
            grid=(local // unroll,),
            in_specs=[
                whole((slots, width + 128)),
                whole((slots, width)),
                pl.BlockSpec((unroll, width, hidden_units), lambda j: (j, 0, 0)),
                pl.BlockSpec((unroll, hidden_units, width), lambda j: (j, 0, 0)),
            ],
            out_specs=[by_expert, by_expert, by_hidden, by_hidden, whole((EXTRA, slots)), by_expert]
            + [whole((quarter, slots))] * tensor_size,
            out_shape=[jax.ShapeDtypeStruct((slots, width), bf16)] * 2
            + [jax.ShapeDtypeStruct((slots, hidden_units), bf16)] * 2
            + [jax.ShapeDtypeStruct((EXTRA, slots), bf16), jax.ShapeDtypeStruct((slots, width), bf16)]
            + [jax.ShapeDtypeStruct((quarter, slots), bf16)] * tensor_size,
            scratch_shapes=[pltpu.VMEM((slots, width), bf16)] * 3
            + [pltpu.VMEM((slots, 128), bf16), pltpu.VMEM((width, slots), bf16)],
            compiler_params=pltpu.CompilerParams(vmem_limit_bytes=56 * 2**20),
        )(recv, cot_rows, expert_in, expert_out)
        expert_rows, grad_slots, expert_act, grad_act, dots, result_rows = outs[:6]
        grad_chunks = outs[6:]

        def trade_chunks(chunks):
            return [chunks[0]] + [lax.ppermute(c, "tensor", pairs) for c, pairs in zip(chunks[1:], shifts)]

        def sum_rows(parts):
            columns = -(-(quarter + EXTRA) // 128) * 128
            return call(sum_kernel, [((slots, columns), bf16)], parts)[0]

        def own_tokens(rows, kept):
            return call(back_kernel, [((kept, token_count), bf16)], (rows, choice, slot))[0]

        by = lambda array: array.reshape(local, per, array.shape[1])
        grad_expert_out = jnp.einsum("erf,erd->efd", by(expert_act), by(grad_slots), preferred_element_type=f32)
        grad_expert_in = jnp.einsum("erd,erf->edf", by(expert_rows), by(grad_act), preferred_element_type=f32)

        iw_planes, _ = after((iw_planes, grad_chunks[0]))
        iw_planes = jnp.stack(iw_planes)
        iw_all = joined(iw_planes[:, :iw_rows])
        bias_all = jnp.sum(
            iw_planes[:, iw_rows:]
            .reshape(tensor_size - 1, -1)[:, : 3 * buckets * heads]
            .reshape(tensor_size - 1, 3, heads, buckets)
            .astype(f32),
            1,
        )
        (result_rows,) = call(
            lambda *refs: result_kernel(expert_size, local, *refs), [((slots, width), bf16)], (result_rows,)
        )
        traded, grad_expert_out = after((trade_chunks(grad_chunks), grad_expert_out))
        summed = sum_rows(traded + [dots])
        (result_part,) = call(
            result_back_kernel, [((token_count, width), bf16)], (exchange(result_rows), choice, slot)
        )
        returned = own_tokens(exchange(summed), quarter + EXTRA)
        returned, grad_expert_in, result_part = after((returned, grad_expert_in, result_part))
        grad_parts = gather_tensor(returned)
        grad_parts, iw_all, bias_all, result_part = after((grad_parts, iw_all, bias_all, result_part))
        result = lax.psum(result_part, "tensor")

        early_rows = quarter + experts + 8
        grad_hidden, grad_low, early_sums = call(
            hidden_backward_kernel,
            [((token_count, width), f32), ((token_count, width), bf16), ((early_rows, width), f32)],
            (hidden, prob, cotangent, gain_second, rw, choice, attended, *grad_parts),
            [pltpu.VMEM((width, token_count), f32)],
        )
        def sum_experts(array):
            return jnp.sum(exchange(array).reshape(expert_size, -1, array.shape[1]).astype(f32), 0)

        padded = token_count + 2 * BLOCK
        scratch = [pltpu.VMEM((padded, quarter), bf16)] * 2 + [pltpu.VMEM((quarter, padded), bf16)]
        scratch = scratch + [pltpu.VMEM((padded, quarter), f32)] * 2 + [pltpu.VMEM((quarter, token_count), f32)]
        grad_iw, own_parts, table_grad = call(
            own_backward_kernel,
            [((3 * quarter, width), bf16), ((3, token_count, quarter), bf16), ((1, width), f32)],
            (first_normed, iw_own, output_weight, table, seg, grad_low),
            scratch,
        )
        grad_tokens, tail = call(
            rest_backward_kernel,
            [((token_count, width), f32), ((8, width), bf16)],
            (
                first_normed, iw_own, iw_all, ow_all, bias_all, seg, grad_low, own_parts, tokens, gain_first,
                grad_hidden, table_grad,
            ),
            [pltpu.VMEM((token_count, width), f32)] + scratch,
        )
        (block_output,) = call(
            output_kernel,
            [((token_count, width), bf16)],
            (hidden, prob, choice, result),
        )
        early = lax.psum(early_sums, "expert")
        late = lax.all_gather(jnp.concatenate([sum_experts(grad_iw).astype(bf16), tail], 0), "expert", axis=0)
        grad_iw, grad_ow, grad_rw, grad_second, grad_first, grad_table = call(
            finish_kernel,
            [
                ((3 * quarter, width), f32),
                ((quarter, width), f32),
                ((experts, width), f32),
                ((width,), f32),
                ((width,), f32),
                ((1, width), f32),
            ],
            (late, early),
        )
        return (
            block_output,
            grad_tokens,
            grad_first,
            jnp.swapaxes(grad_iw.reshape(3, quarter, width), 1, 2),
            grad_table.reshape(width // 128, 128)[:heads, :buckets].T,
            grad_ow,
            grad_second,
            grad_rw.T,
            grad_expert_in,
            grad_expert_out,
        )

    return shards


def solution(mesh):
    placed = (
        P("expert", None),
        P("expert", None),
        P("expert"),
        P("expert"),
        P(),
        P(None, None, "tensor"),
        P(None, "tensor"),
        P("tensor", None),
        P(),
        P(),
        P("expert", None, "tensor"),
        P("expert", "tensor", None),
        P("expert", None),
    )
    return jax.shard_map(
        make(mesh),
        mesh=mesh,
        in_specs=placed,
        out_specs=(
            P("expert", None),
            P("expert", None),
            P(),
            P(None, None, "tensor"),
            P(None, "tensor"),
            P("tensor", None),
            P(),
            P(),
            P("expert", None, "tensor"),
            P("expert", "tensor", None),
        ),
        check_vma=False,
    )
```

```python
import math

import jax
import jax.numpy as jnp
from jax import lax
from jax.experimental import pallas as pl
from jax.experimental.pallas import tpu as pltpu
from jax.sharding import PartitionSpec as P

CAP = 10

bucket_edges = (12, 16, 23, 32, 46, 64, 91)
norm_eps = 1e-06
masked_score = -1e30
gelu_const = math.sqrt(2.0 / math.pi)
gelu_cubic = 0.044715

BLOCK = 128
BAND = 3 * BLOCK
ROLL = 4 * BLOCK
HEAD = 64
EXTRA = 16

bf16 = jnp.bfloat16
f32 = jnp.float32
i32 = jnp.int32
highest = lax.Precision.HIGHEST

NN = (((1,), (0,)), ((), ()))
NT = (((1,), (1,)), ((), ()))
TN = (((0,), (0,)), ((), ()))


def dot(left, right, dims=NN, precision=None):
    return lax.dot_general(left, right, dims, precision=precision, preferred_element_type=f32)


def dot3(left, right, dims=NN):
    left_high, right_high = left.astype(bf16), right.astype(bf16)
    left_low = (left - left_high.astype(f32)).astype(bf16)
    right_low = (right - right_high.astype(f32)).astype(bf16)
    return dot(left_high, right_high, dims) + (dot(left_high, right_low, dims) + dot(left_low, right_high, dims))


def flat(ref):
    return ref[...].reshape(1, -1)


def iota(shape, axis):
    return lax.broadcasted_iota(i32, shape, axis)


def call(kernel, outs, args, scratch=(), **extra):
    vmem = pl.BlockSpec(memory_space=pltpu.VMEM)
    return pl.pallas_call(
        kernel,
        out_shape=[jax.ShapeDtypeStruct(shape, dtype) for shape, dtype in outs],
        in_specs=[vmem] * len(args),
        out_specs=[vmem] * len(outs),
        scratch_shapes=list(scratch),
        compiler_params=pltpu.CompilerParams(vmem_limit_bytes=56 * 2**20),
        **extra,
    )(*args)


def split3(value):
    high = value.astype(bf16).astype(f32)
    rest = value - high
    middle = rest.astype(bf16).astype(f32)
    return high, middle, rest - middle


def columns3(value, width):
    high, middle, low = split3(value)
    lane = iota((value.shape[0], width), 1)
    picked = jnp.where(lane == 0, high, jnp.where(lane == 1, middle, jnp.where(lane == 2, low, 0.0)))
    return picked.astype(bf16)


def column_of(row):
    return jnp.transpose(jnp.broadcast_to(row.astype(f32), (128, row.shape[1])))


def wide(column, width):
    return jnp.concatenate([column] * (width // 128), 1)


def bucket_of(relative):
    distance = jnp.abs(relative)
    beyond = jnp.zeros_like(distance)
    for threshold in bucket_edges:
        beyond = beyond + (distance >= threshold).astype(i32)
    magnitude = jnp.where(distance < 8, distance, 8 + beyond)
    return magnitude + 16 * (relative > 0).astype(i32)


def band_rows(table):
    buckets = table.shape[1]
    offset = iota((buckets, ROLL), 1)
    relative = jnp.where(offset < BAND, offset, offset - ROLL) - BLOCK
    onehot = (bucket_of(relative) == iota((buckets, ROLL), 0)).astype(f32)
    return dot(table, onehot, precision=highest), onehot


def bias_tiles(table):
    rows, onehot = band_rows(table)
    tiles = []
    for h in range(table.shape[0]):
        full = jnp.broadcast_to(rows[h : h + 1], (BLOCK, ROLL))
        tiles.append(jnp.transpose(pltpu.roll(full, 0, 1, stride=1, stride_axis=0)[:, :BAND]))
    return tiles, onehot


def head_masks(heads):
    lane = iota((1, heads * HEAD), 1)
    return [((lane >= h * HEAD) & (lane < (h + 1) * HEAD)).astype(f32).astype(bf16) for h in range(heads)]


def padded_segments(seg):
    edge = jnp.full((1, BLOCK), -1.0, f32)
    return column_of(jnp.concatenate([edge, seg, edge], 1))


def first_norm(tok, gain):
    scale = lax.rsqrt(jnp.mean(tok * tok, -1, keepdims=True) + norm_eps)
    return (tok * scale * gain).astype(bf16), scale


def probabilities(scores, bias, same):
    scores = jnp.where(same, scores + bias, masked_score)
    weights = jnp.exp(scores - jnp.max(scores, 0, keepdims=True))
    return weights * (1.0 / jnp.sum(weights, 0, keepdims=True))


def stack_heads(rows, masks):
    return jnp.concatenate([rows * mask for mask in masks], 0)


def own_blocks(product, heads):
    return jnp.concatenate(
        [product[h * HEAD : (h + 1) * HEAD, h * BLOCK : (h + 1) * BLOCK] for h in range(heads)], 0
    )


def fill_rows(ref, value):
    rows = value.shape[0]
    edge = jnp.zeros((BLOCK, value.shape[1]), bf16)
    ref[pl.ds(0, BLOCK), :] = edge
    ref[pl.ds(rows + BLOCK, BLOCK), :] = edge
    ref[pl.ds(BLOCK, rows), :] = value


def fill_columns(ref, value):
    rows = value.shape[1]
    edge = jnp.zeros((value.shape[0], BLOCK), bf16)
    ref[:, pl.ds(0, BLOCK)] = edge
    ref[:, pl.ds(rows + BLOCK, BLOCK)] = edge
    ref[:, pl.ds(BLOCK, rows)] = value


def forward_kernel(tok_ref, gain_ref, iw_ref, bt_ref, seg_ref, att_ref, normed_ref, keys, values):
    rows = tok_ref.shape[0]
    normed, _ = first_norm(tok_ref[...].astype(f32), flat(gain_ref))
    normed_ref[...] = normed
    queries = dot(normed, iw_ref[0], NT).astype(bf16)
    fill_rows(keys, dot(normed, iw_ref[1], NT).astype(bf16))
    fill_columns(values, dot(iw_ref[2], normed, NT).astype(bf16))
    seg = seg_ref[...].astype(f32)
    seg_keys = padded_segments(seg)
    tiles, _ = bias_tiles(bt_ref[...])
    heads = len(tiles)
    masks = head_masks(heads)
    for block in range(rows // BLOCK):
        at = block * BLOCK
        same = seg_keys[at : at + BAND] == seg[:, at : at + BLOCK]
        scores = dot(keys[pl.ds(at, BAND), :], stack_heads(queries[at : at + BLOCK], masks), NT)
        weights = [
            probabilities(scores[:, h * BLOCK : (h + 1) * BLOCK], tiles[h], same).astype(bf16) for h in range(heads)
        ]
        product = dot(values[:, pl.ds(at, BAND)], jnp.concatenate(weights, 1))
        att_ref[:, pl.ds(at, BLOCK)] = own_blocks(product, heads).astype(bf16)


def group_backward(normed, weight, out_weight, table, seg, grad_low, scratch, bias_grads):
    keys, values, keys_across, grad_keys, grad_values, grad_queries = scratch
    rows = normed.shape[0]
    queries = dot(normed, weight[0], NT).astype(bf16)
    fill_rows(keys, dot(normed, weight[1], NT).astype(bf16))
    fill_columns(keys_across, dot(weight[1], normed, NT).astype(bf16))
    fill_rows(values, dot(normed, weight[2], NT).astype(bf16))
    grad_att = dot(grad_low, out_weight, NT).astype(bf16)
    grad_keys[...] = jnp.zeros(grad_keys.shape, f32)
    grad_values[...] = jnp.zeros(grad_values.shape, f32)
    seg_keys = padded_segments(seg)
    tiles, onehot = bias_tiles(table)
    heads = len(tiles)
    masks = head_masks(heads)
    sums = [None] * heads
    for block in range(rows // BLOCK):
        at = block * BLOCK
        same = seg_keys[at : at + BAND] == seg[:, at : at + BLOCK]
        head_queries = stack_heads(queries[at : at + BLOCK], masks)
        head_grads = stack_heads(grad_att[at : at + BLOCK], masks)
        scores = dot(keys[pl.ds(at, BAND), :], head_queries, NT)
        grad_probs = dot(values[pl.ds(at, BAND), :], head_grads, NT)
        all_weights, all_grads = [], []
        for h in range(heads):
            columns = slice(h * BLOCK, (h + 1) * BLOCK)
            weights = probabilities(scores[:, columns], tiles[h], same)
            scaled = weights * grad_probs[:, columns]
            grad_scores = scaled - weights * jnp.sum(scaled, 0, keepdims=True)
            all_weights.append(weights.astype(bf16))
            all_grads.append(grad_scores.astype(bf16))
            if bias_grads:
                sums[h] = grad_scores if sums[h] is None else sums[h] + grad_scores
        low = jnp.concatenate(all_grads, 1)
        grad_queries[:, pl.ds(at, BLOCK)] = own_blocks(dot(keys_across[:, pl.ds(at, BAND)], low), heads)
        grad_keys[pl.ds(at, BAND), :] += dot(low, head_queries)
        grad_values[pl.ds(at, BAND), :] += dot(jnp.concatenate(all_weights, 1), head_grads)
    parts = (
        jnp.transpose(grad_queries[...]).astype(bf16),
        grad_keys[pl.ds(BLOCK, rows), :].astype(bf16),
        grad_values[pl.ds(BLOCK, rows), :].astype(bf16),
    )
    if not bias_grads:
        return parts, None
    diagonals = []
    row_index = iota((BLOCK, ROLL), 0)
    for h in range(heads):
        moved = jnp.concatenate([jnp.transpose(sums[h]), jnp.zeros((BLOCK, ROLL - BAND), f32)], 1)
        step = 1
        while step < BLOCK:
            moved = jnp.where((row_index & step) != 0, pltpu.roll(moved, ROLL - step, 1), moved)
            step *= 2
        diagonals.append(jnp.sum(moved, 0, keepdims=True))
    onehot = jnp.concatenate([onehot, jnp.zeros((128 - onehot.shape[0], ROLL), f32)], 0)
    by_head = dot(jnp.concatenate(diagonals, 0), onehot, NT, precision=highest)
    return parts, jnp.concatenate([by_head[h : h + 1] for h in range(heads)], 1)


def own_backward_kernel(normed_ref, iw_ref, ow_ref, bt_ref, seg_ref, low_ref, grad_iw_ref, parts_ref, table_ref, *scratch):
    normed = normed_ref[...]
    parts, table_grad = group_backward(
        normed, iw_ref, ow_ref[...], bt_ref[...], seg_ref[...].astype(f32), low_ref[...], scratch, True
    )
    table_ref[...] = jnp.concatenate(
        [table_grad, jnp.zeros((1, table_ref.shape[1] - table_grad.shape[1]), f32)], 1
    )
    width = ow_ref.shape[0]
    for j in range(3):
        parts_ref[j] = parts[j]
        grad_iw_ref[pl.ds(j * width, width), :] = dot(parts[j], normed, TN).astype(bf16)


def rest_backward_kernel(
    normed_ref, own_iw_ref, iw_ref, ow_ref, bt_ref, seg_ref, low_ref, parts_ref, tok_ref, gain_ref, grad_hidden_ref,
    table_ref, grad_tok_ref, tail_ref, total, *scratch,
):
    width = ow_ref.shape[1]
    total[...] = sum(dot(parts_ref[j], own_iw_ref[j]) for j in range(3))

    def step(group, carry):
        weight = [iw_ref[group, pl.ds(j * width, width), :] for j in range(3)]
        parts, _ = group_backward(
            normed_ref[...], weight, ow_ref[group], bt_ref[group], seg_ref[...].astype(f32), low_ref[...], scratch, False
        )
        total[...] += sum(dot(parts[j], weight[j]) for j in range(3))
        return carry

    lax.fori_loop(0, ow_ref.shape[0], step, 0)
    tok = tok_ref[...].astype(f32)
    gain = flat(gain_ref)
    scale = lax.rsqrt(jnp.mean(tok * tok, -1, keepdims=True) + norm_eps)
    grad_normed = total[...]
    tail_ref[...] = rows3([jnp.sum(grad_normed * tok * scale, 0, keepdims=True), table_ref[...]], tail_ref.shape[0])
    scaled = grad_normed * gain
    grad_tok_ref[...] = (
        grad_hidden_ref[...]
        + scale * scaled
        - tok * (scale * scale * scale) * jnp.mean(scaled * tok, -1, keepdims=True)
    )


def rows3(values, count):
    parts = [part for value in values for part in split3(value)]
    row = iota((count, values[0].shape[1]), 0)
    total = jnp.zeros(row.shape, f32)
    for index, part in enumerate(parts):
        total = jnp.where(row == index, part, total)
    return total.astype(bf16)


def finish_kernel(late_ref, early_ref, *refs):
    grad_iw_ref, grad_ow_ref, grad_rw_ref, second_ref, first_ref, table_ref = refs
    devices = late_ref.shape[0]
    late_rows = grad_iw_ref.shape[0] // devices
    tail = jnp.zeros((late_ref.shape[1] - late_rows, late_ref.shape[2]), f32)
    for device in range(devices):
        block = late_ref[device].astype(f32)
        grad_iw_ref[pl.ds(device * late_rows, late_rows), :] = block[:late_rows]
        tail = tail + block[late_rows:]
    first_ref[...] = jnp.sum(tail[:3], 0)
    table_ref[...] = jnp.sum(tail[3:6], 0, keepdims=True)
    at, experts = grad_ow_ref.shape[0], grad_rw_ref.shape[0]
    early_rows = early_ref.shape[1] - 8
    early = jnp.concatenate([early_ref[device][:early_rows] for device in range(devices)], 0)
    grad_ow_ref[...] = early[:at]
    grad_rw_ref[...] = early[at : at + experts]
    second_ref[...] = jnp.sum(early[at + experts : at + experts + 8], 0)


def slot_onehot(choice, slot, slots):
    dest = jnp.where(slot >= 0, choice * CAP + slot, slots)
    return (iota((slots, dest.shape[1]), 0) == dest).astype(f32).astype(bf16)


def slot_order(slots, group, across):
    index = iota((1, slots), 1)
    big, small = slots // across, slots // group
    outer, rest = lax.div(index, big), lax.rem(index, big)
    target = lax.div(rest, CAP) * small + outer * CAP + lax.rem(rest, CAP)
    return (iota((slots, slots), 0) == target).astype(f32).astype(bf16)


def cotangent_kernel(cot_ref, choice_ref, slot_ref, out_ref):
    fill = slot_onehot(flat(choice_ref), flat(slot_ref), out_ref.shape[0])
    out_ref[...] = dot(fill, cot_ref[...]).astype(bf16)


def order_kernel(sources, local, rows_ref, out_ref):
    out_ref[...] = dot(slot_order(rows_ref.shape[0], local, sources), rows_ref[...]).astype(bf16)


def chosen_of(choice, experts):
    column = column_of(choice)[:, :experts]
    return (column == iota(column.shape, 1).astype(f32)).astype(f32)


def middle_kernel(tok_ref, own_ow_ref, ow_ref, gain_ref, rw_ref, choice_ref, slot_ref, *refs):
    att_refs, (hidden_ref, prob_ref, send_ref) = refs[:-3], refs[-3:]
    hidden = tok_ref[...].astype(f32)
    for shift, att_ref in enumerate(att_refs):
        hidden = hidden + dot(att_ref[...], ow_ref[shift - 1] if shift else own_ow_ref[...], TN)
    hidden_ref[...] = hidden
    scale = lax.rsqrt(jnp.mean(hidden * hidden, -1, keepdims=True) + norm_eps)
    normed = hidden * scale * flat(gain_ref)
    logits = dot3(normed, rw_ref[...], NT)
    raised = jnp.exp(logits - jnp.max(logits, -1, keepdims=True))
    prob = raised * (1.0 / jnp.sum(raised, -1, keepdims=True))
    prob_ref[...] = prob
    gate = jnp.sum(prob * chosen_of(flat(choice_ref), prob.shape[1]), -1, keepdims=True)
    width = normed.shape[1]
    fill = slot_onehot(flat(choice_ref), flat(slot_ref), send_ref.shape[0])
    send_ref[:, :width] = dot(fill, normed.astype(bf16)).astype(bf16)
    send_ref[:, width:] = dot(fill, columns3(gate, 128)).astype(bf16)


def expert_kernel(
    tensor_size, sources, unroll,
    recv_ref, cot_ref, win_ref, wout_ref,
    rows_ref, grads_ref, act_ref, grad_act_ref, dots_ref, result_ref, *refs,
):
    chunks = refs[:tensor_size]
    x_all, g_all, r_all, d_all, turned = refs[tensor_size:]
    slots = recv_ref.shape[0]
    width = cot_ref.shape[1]
    step = pl.program_id(0)
    local = pl.num_programs(0) * unroll
    per = rows_ref.shape[0] // unroll

    @pl.when(step == 0)
    def _():
        order = slot_order(slots, win_ref.shape[0] * (slots // rows_ref.shape[0]), sources)
        x_all[...] = dot(order, recv_ref[:, :width]).astype(bf16)
        gate = jnp.sum(dot(order, recv_ref[:, width:]), -1, keepdims=True)
        g_all[...] = (gate * cot_ref[...].astype(f32)).astype(bf16)

    for u in range(unroll):
        here = pl.ds(u * per, per)
        at = pl.ds(pl.multiple_of((step * unroll + u) * per, 16), per)
        x = x_all[at, :]
        g = g_all[at, :]
        weight_in = win_ref[u]
        weight_out = wout_ref[u]
        pre = dot(x, weight_in)
        grad_act = dot(g, weight_out, NT)
        inner = jnp.tanh(gelu_const * (pre + gelu_cubic * pre * pre * pre))
        act = (0.5 * pre * (1.0 + inner)).astype(bf16)
        slope = 0.5 * (1.0 + inner) + 0.5 * pre * (1.0 - inner * inner) * gelu_const * (
            1.0 + 3.0 * gelu_cubic * pre * pre
        )
        grad_act = (grad_act * slope).astype(bf16)
        r_all[at, :] = dot(grad_act, weight_in, NT).astype(bf16)
        result = dot(act, weight_out)
        result_ref[here, :] = result.astype(bf16)
        d_all[at, :] = columns3(jnp.sum(result * cot_ref[at, :].astype(f32), -1, keepdims=True), 128)
        rows_ref[here, :] = x
        grads_ref[here, :] = g
        act_ref[here, :] = act
        grad_act_ref[here, :] = grad_act

    @pl.when(step == pl.num_programs(0) - 1)
    def _():
        order = slot_order(slots, win_ref.shape[0] * (slots // rows_ref.shape[0]), sources)
        dots_ref[...] = dot(d_all[...], order, TN)[:EXTRA].astype(bf16)
        turn_chunks(tensor_size, dot(r_all[...], order, TN).astype(bf16), turned, chunks)


def turn_chunks(tensor_size, rows, turned, chunks):
    turned[...] = rows
    quarter = rows.shape[0] // tensor_size
    me = lax.axis_index("tensor")
    for shift in range(tensor_size):
        first = lax.rem(me + shift, tensor_size) * quarter
        chunks[shift][...] = turned[pl.ds(pl.multiple_of(first, 64), quarter), :]


def result_kernel(sources, local, rows_ref, out_ref):
    out_ref[...] = dot(slot_order(rows_ref.shape[0], local, sources), rows_ref[...], TN).astype(bf16)


def result_back_kernel(recv_ref, choice_ref, slot_ref, out_ref):
    fill = slot_onehot(flat(choice_ref), flat(slot_ref), recv_ref.shape[0])
    out_ref[...] = dot(fill, recv_ref[...], TN).astype(bf16)


def sum_kernel(*refs):
    *parts, dots_ref, out_ref = refs
    total = sum(ref[...].astype(f32) for ref in parts)
    blank = jnp.zeros((out_ref.shape[1] - total.shape[0] - EXTRA, total.shape[1]), f32)
    out_ref[...] = jnp.transpose(jnp.concatenate([total, dots_ref[...].astype(f32), blank], 0)).astype(bf16)


def back_kernel(recv_ref, choice_ref, slot_ref, out_ref):
    fill = slot_onehot(flat(choice_ref), flat(slot_ref), recv_ref.shape[0])
    out_ref[...] = dot(recv_ref[...], fill, TN)[: out_ref.shape[0]].astype(bf16)


def spread(refs, quarter, turned):
    size = len(refs)
    me = lax.axis_index("tensor")
    for shift, ref in enumerate(refs):
        first = lax.rem(me + size - shift, size) * quarter
        turned[pl.ds(pl.multiple_of(first, 64), quarter), :] = ref[pl.ds(0, quarter), :].astype(f32)
    return jnp.transpose(turned[...])


def hidden_backward_kernel(
    hidden_ref, prob_ref, cot_ref, gain_ref, rw_ref, choice_ref, att_ref, *refs,
):
    parts = refs[:-4]
    grad_hidden_ref, low_ref, sums_ref, turned = refs[-4:]
    hidden = hidden_ref[...]
    rows, width = hidden.shape
    quarter = width // len(parts)
    grad_routed = spread(parts, quarter, turned)
    dots = sum(jnp.sum(ref[pl.ds(quarter, EXTRA), :].astype(f32), 0, keepdims=True) for ref in parts)
    prob = prob_ref[...]
    chosen = chosen_of(flat(choice_ref), prob.shape[1])
    gate = jnp.sum(prob * chosen, -1, keepdims=True)
    grad_gate = column_of(dots)[:, :1]
    grad_logits = (grad_gate * gate) * (chosen - prob)
    grad_normed = grad_routed + dot3(grad_logits, rw_ref[...])
    gain = flat(gain_ref)
    scale = lax.rsqrt(jnp.mean(hidden * hidden, -1, keepdims=True) + norm_eps)
    scaled = grad_normed * gain
    grad_hidden = (
        cot_ref[...].astype(f32)
        + scale * scaled
        - hidden * (scale * scale * scale) * jnp.mean(scaled * hidden, -1, keepdims=True)
    )
    grad_hidden_ref[...] = grad_hidden
    low = grad_hidden.astype(bf16)
    low_ref[...] = low
    at, experts = att_ref.shape[0], prob.shape[1]
    sums_ref[pl.ds(0, at), :] = dot(att_ref[...], low).astype(bf16)
    sums_ref[pl.ds(at, experts), :] = dot3(grad_logits, hidden * scale * gain, TN).astype(bf16)
    tail = sums_ref.shape[0] - at - experts
    sums_ref[pl.ds(at + experts, tail), :] = rows3([jnp.sum(grad_normed * hidden * scale, 0, keepdims=True)], tail)


def output_kernel(hidden_ref, prob_ref, choice_ref, result_ref, out_ref):
    prob = prob_ref[...]
    gate = jnp.sum(prob * chosen_of(flat(choice_ref), prob.shape[1]), -1, keepdims=True)
    out_ref[...] = (hidden_ref[...] + gate * result_ref[...].astype(f32)).astype(bf16)


def make(mesh):
    tensor_size = mesh.shape["tensor"]
    expert_size = mesh.shape["expert"]

    def shards(
        tokens,
        segment_ids,
        expert_choice,
        slot_index,
        first_gain,
        input_weight,
        bias_table,
        output_weight,
        second_gain,
        router_weight,
        expert_in,
        expert_out,
        cotangent,
    ):
        token_count, width = tokens.shape
        sequences, length = segment_ids.shape
        quarter = output_weight.shape[0]
        experts = router_weight.shape[1]
        local = expert_in.shape[0]
        hidden_units = expert_in.shape[2]
        slots = experts * CAP
        per = slots // local
        chunk = slots // expert_size
        buckets, heads = bias_table.shape
        expert_index = lax.axis_index("expert")
        seg = (segment_ids + 8 * jnp.arange(sequences, dtype=i32)[:, None]).reshape(1, token_count)
        choice, slot = expert_choice, slot_index
        gain_first, gain_second = first_gain, second_gain
        iw_own = jnp.swapaxes(input_weight, 1, 2)
        table = bias_table.T
        rw = router_weight.T
        after = lax.optimization_barrier

        shifts = [[(i, (i + s) % tensor_size) for i in range(tensor_size)] for s in range(1, tensor_size)]

        def from_others(array):
            return [lax.ppermute(array, "tensor", pairs) for pairs in shifts]

        def gather_tensor(array):
            return [array] + from_others(array)

        def joined(planes):
            got = lax.all_gather(planes, "expert", axis=0)
            return jnp.swapaxes(got, 0, 1).reshape(tensor_size - 1, -1, got.shape[-1])

        def exchange(array):
            rows = array.shape[0] // expert_size
            got = lax.all_to_all(array.reshape(expert_size, rows, array.shape[1]), "expert", 0, 0)
            return got.reshape(array.shape)

        ow_rows = quarter // expert_size
        ow_part = lax.dynamic_slice_in_dim(output_weight, expert_index * ow_rows, ow_rows, 0)
        ow_all = joined(jnp.stack(from_others(ow_part)))

        attended, first_normed = call(
            forward_kernel,
            [((quarter, token_count), bf16), ((token_count, width), bf16)],
            (tokens, gain_first, iw_own, table, seg),
            [
                pltpu.VMEM((token_count + 2 * BLOCK, quarter), bf16),
                pltpu.VMEM((quarter, token_count + 2 * BLOCK), bf16),
            ],
        )
        attended_parts = gather_tensor(attended)
        (cot_slots,) = call(cotangent_kernel, [((slots, width), bf16)], (cotangent, choice, slot))
        cot_recv = exchange(cot_slots)
        attended_parts, cot_recv = after((attended_parts, cot_recv))

        hidden, prob, send = call(
            middle_kernel,
            [((token_count, width), f32), ((token_count, experts), f32), ((slots, width + 128), bf16)],
            (tokens, output_weight, ow_all, gain_second, rw, choice, slot, *attended_parts),
        )
        recv = exchange(send)
        cot_recv, _ = after((cot_recv, send))
        (cot_rows,) = call(
            lambda *refs: order_kernel(expert_size, local, *refs), [((slots, width), bf16)], (cot_recv,)
        )

        iw_rows = 3 * quarter // expert_size
        iw_part = lax.dynamic_slice_in_dim(iw_own.reshape(3 * quarter, width), expert_index * iw_rows, iw_rows, 0)
        bias_parts = jnp.stack(split3(table)).astype(bf16).reshape(-1)
        bias_parts = jnp.pad(bias_parts, (0, 8 * width - bias_parts.shape[0])).reshape(8, width)
        iw_part, _ = after((jnp.concatenate([iw_part, bias_parts], 0), send))
        iw_planes = from_others(iw_part)

        iw_planes, recv = after((iw_planes, recv))
        iw_planes = jnp.stack(iw_planes)
        iw_all = joined(iw_planes[:, :iw_rows])
        bias_all = jnp.sum(
            iw_planes[:, iw_rows:]
            .reshape(tensor_size - 1, -1)[:, : 3 * buckets * heads]
            .reshape(tensor_size - 1, 3, heads, buckets)
            .astype(f32),
            1,
        )

        unroll = 2 if local % 2 == 0 else 1
        whole = lambda shape: pl.BlockSpec(shape, lambda j: (0,) * len(shape))
        by_expert = pl.BlockSpec((unroll * per, width), lambda j: (j, 0))
        by_hidden = pl.BlockSpec((unroll * per, hidden_units), lambda j: (j, 0))
        outs = pl.pallas_call(
            lambda *refs: expert_kernel(tensor_size, expert_size, unroll, *refs),
            grid=(local // unroll,),
            in_specs=[
                whole((slots, width + 128)),
                whole((slots, width)),
                pl.BlockSpec((unroll, width, hidden_units), lambda j: (j, 0, 0)),
                pl.BlockSpec((unroll, hidden_units, width), lambda j: (j, 0, 0)),
            ],
            out_specs=[by_expert, by_expert, by_hidden, by_hidden, whole((EXTRA, slots)), by_expert]
            + [whole((quarter, slots))] * tensor_size,
            out_shape=[jax.ShapeDtypeStruct((slots, width), bf16)] * 2
            + [jax.ShapeDtypeStruct((slots, hidden_units), bf16)] * 2
            + [jax.ShapeDtypeStruct((EXTRA, slots), bf16), jax.ShapeDtypeStruct((slots, width), bf16)]
            + [jax.ShapeDtypeStruct((quarter, slots), bf16)] * tensor_size,
            scratch_shapes=[pltpu.VMEM((slots, width), bf16)] * 3
            + [pltpu.VMEM((slots, 128), bf16), pltpu.VMEM((width, slots), bf16)],
            compiler_params=pltpu.CompilerParams(vmem_limit_bytes=56 * 2**20),
        )(recv, cot_rows, expert_in, expert_out)
        expert_rows, grad_slots, expert_act, grad_act, dots, result_rows = outs[:6]
        grad_chunks = outs[6:]

        def trade_chunks(chunks):
            return [chunks[0]] + [lax.ppermute(c, "tensor", pairs) for c, pairs in zip(chunks[1:], shifts)]

        def sum_rows(parts):
            columns = -(-(quarter + EXTRA) // 128) * 128
            return call(sum_kernel, [((slots, columns), bf16)], parts)[0]

        def own_tokens(rows, kept):
            return call(back_kernel, [((kept, token_count), bf16)], (rows, choice, slot))[0]

        by = lambda array: array.reshape(local, per, array.shape[1])
        grad_expert_out = jnp.einsum("erf,erd->efd", by(expert_act), by(grad_slots), preferred_element_type=f32)
        grad_expert_in = jnp.einsum("erd,erf->edf", by(expert_rows), by(grad_act), preferred_element_type=f32)

        (result_rows,) = call(
            lambda *refs: result_kernel(expert_size, local, *refs), [((slots, width), bf16)], (result_rows,)
        )
        traded, grad_expert_out, result_rows = after(
            (trade_chunks(grad_chunks), grad_expert_out, exchange(result_rows))
        )
        summed = sum_rows(traded + [dots])
        (result_part,) = call(
            result_back_kernel, [((token_count, width), bf16)], (result_rows, choice, slot)
        )
        returned = own_tokens(exchange(summed), quarter + EXTRA)
        returned, grad_expert_in, result_part = after((returned, grad_expert_in, result_part))
        result = lax.psum(result_part, "tensor")
        grad_parts = gather_tensor(returned)
        grad_parts, iw_all, bias_all = after((grad_parts, iw_all, bias_all))

        early_rows = quarter + experts + 64
        grad_hidden, grad_low, early_sums = call(
            hidden_backward_kernel,
            [((token_count, width), f32), ((token_count, width), bf16), ((early_rows, width), bf16)],
            (hidden, prob, cotangent, gain_second, rw, choice, attended, *grad_parts),
            [pltpu.VMEM((width, token_count), f32)],
        )
        def sum_chunks(array):
            return jnp.sum(array.reshape(expert_size, -1, array.shape[1]).astype(f32), 0)

        padded = token_count + 2 * BLOCK
        scratch = [pltpu.VMEM((padded, quarter), bf16)] * 2 + [pltpu.VMEM((quarter, padded), bf16)]
        scratch = scratch + [pltpu.VMEM((padded, quarter), f32)] * 2 + [pltpu.VMEM((quarter, token_count), f32)]
        grad_iw, own_parts, table_grad = call(
            own_backward_kernel,
            [((3 * quarter, width), bf16), ((3, token_count, quarter), bf16), ((1, width), f32)],
            (first_normed, iw_own, output_weight, table, seg, grad_low),
            scratch,
        )
        grad_tokens, tail = call(
            rest_backward_kernel,
            [((token_count, width), f32), ((8, width), bf16)],
            (
                first_normed, iw_own, iw_all, ow_all, bias_all, seg, grad_low, own_parts, tokens, gain_first,
                grad_hidden, table_grad,
            ),
            [pltpu.VMEM((token_count, width), f32)] + scratch,
        )
        (block_output,) = call(
            output_kernel,
            [((token_count, width), bf16)],
            (hidden, prob, choice, result),
        )
        early_got, grad_iw = after((exchange(early_sums), grad_iw))
        early_sum = sum_chunks(early_got)
        early = lax.all_gather(jnp.pad(early_sum, ((0, 8), (0, 0))), "expert", axis=0)
        late = lax.all_gather(jnp.concatenate([sum_chunks(exchange(grad_iw)).astype(bf16), tail], 0), "expert", axis=0)
        grad_iw, grad_ow, grad_rw, grad_second, grad_first, grad_table = call(
            finish_kernel,
            [
                ((3 * quarter, width), f32),
                ((quarter, width), f32),
                ((experts, width), f32),
                ((width,), f32),
                ((width,), f32),
                ((1, width), f32),
            ],
            (late, early),
        )
        return (
            block_output,
            grad_tokens,
            grad_first,
            jnp.swapaxes(grad_iw.reshape(3, quarter, width), 1, 2),
            grad_table.reshape(width // 128, 128)[:heads, :buckets].T,
            grad_ow,
            grad_second,
            grad_rw.T,
            grad_expert_in,
            grad_expert_out,
        )

    return shards


def solution(mesh):
    placed = (
        P("expert", None),
        P("expert", None),
        P("expert"),
        P("expert"),
        P(),
        P(None, None, "tensor"),
        P(None, "tensor"),
        P("tensor", None),
        P(),
        P(),
        P("expert", None, "tensor"),
        P("expert", "tensor", None),
        P("expert", None),
    )
    return jax.shard_map(
        make(mesh),
        mesh=mesh,
        in_specs=placed,
        out_specs=(
            P("expert", None),
            P("expert", None),
            P(),
            P(None, None, "tensor"),
            P(None, "tensor"),
            P("tensor", None),
            P(),
            P(),
            P("expert", None, "tensor"),
            P("expert", "tensor", None),
        ),
        check_vma=False,
    )
```

```python
import math

import jax
import jax.numpy as jnp
from jax import lax
from jax.experimental import pallas as pl
from jax.experimental.pallas import tpu as pltpu
from jax.sharding import PartitionSpec as P

CAP = 10

bucket_edges = (12, 16, 23, 32, 46, 64, 91)
norm_eps = 1e-06
masked_score = -1e30
gelu_const = math.sqrt(2.0 / math.pi)
gelu_cubic = 0.044715

BLOCK = 128
BAND = 3 * BLOCK
ROLL = 4 * BLOCK
HEAD = 64
EXTRA = 16

bf16 = jnp.bfloat16
f32 = jnp.float32
i32 = jnp.int32
highest = lax.Precision.HIGHEST

NN = (((1,), (0,)), ((), ()))
NT = (((1,), (1,)), ((), ()))
TN = (((0,), (0,)), ((), ()))


def dot(left, right, dims=NN, precision=None):
    return lax.dot_general(left, right, dims, precision=precision, preferred_element_type=f32)


def dot3(left, right, dims=NN):
    left_high, right_high = left.astype(bf16), right.astype(bf16)
    left_low = (left - left_high.astype(f32)).astype(bf16)
    right_low = (right - right_high.astype(f32)).astype(bf16)
    return dot(left_high, right_high, dims) + (dot(left_high, right_low, dims) + dot(left_low, right_high, dims))


def flat(ref):
    return ref[...].reshape(1, -1)


def iota(shape, axis):
    return lax.broadcasted_iota(i32, shape, axis)


def call(kernel, outs, args, scratch=(), **extra):
    vmem = pl.BlockSpec(memory_space=pltpu.VMEM)
    return pl.pallas_call(
        kernel,
        out_shape=[jax.ShapeDtypeStruct(shape, dtype) for shape, dtype in outs],
        in_specs=[vmem] * len(args),
        out_specs=[vmem] * len(outs),
        scratch_shapes=list(scratch),
        compiler_params=pltpu.CompilerParams(vmem_limit_bytes=56 * 2**20),
        **extra,
    )(*args)


def split3(value):
    high = value.astype(bf16).astype(f32)
    rest = value - high
    middle = rest.astype(bf16).astype(f32)
    return high, middle, rest - middle


def columns3(value, width):
    high, middle, low = split3(value)
    lane = iota((value.shape[0], width), 1)
    picked = jnp.where(lane == 0, high, jnp.where(lane == 1, middle, jnp.where(lane == 2, low, 0.0)))
    return picked.astype(bf16)


def column_of(row):
    return jnp.transpose(jnp.broadcast_to(row.astype(f32), (128, row.shape[1])))


def wide(column, width):
    return jnp.concatenate([column] * (width // 128), 1)


def bucket_of(relative):
    distance = jnp.abs(relative)
    beyond = jnp.zeros_like(distance)
    for threshold in bucket_edges:
        beyond = beyond + (distance >= threshold).astype(i32)
    magnitude = jnp.where(distance < 8, distance, 8 + beyond)
    return magnitude + 16 * (relative > 0).astype(i32)


def band_rows(table):
    buckets = table.shape[1]
    offset = iota((buckets, ROLL), 1)
    relative = jnp.where(offset < BAND, offset, offset - ROLL) - BLOCK
    onehot = (bucket_of(relative) == iota((buckets, ROLL), 0)).astype(f32)
    return dot(table, onehot, precision=highest), onehot


def bias_tiles(table):
    rows, onehot = band_rows(table)
    tiles = []
    for h in range(table.shape[0]):
        full = jnp.broadcast_to(rows[h : h + 1], (BLOCK, ROLL))
        tiles.append(jnp.transpose(pltpu.roll(full, 0, 1, stride=1, stride_axis=0)[:, :BAND]))
    return tiles, onehot


def head_masks(heads):
    lane = iota((1, heads * HEAD), 1)
    return [((lane >= h * HEAD) & (lane < (h + 1) * HEAD)).astype(f32).astype(bf16) for h in range(heads)]


def padded_segments(seg):
    edge = jnp.full((1, BLOCK), -1.0, f32)
    return column_of(jnp.concatenate([edge, seg, edge], 1))


def first_norm(tok, gain):
    scale = lax.rsqrt(jnp.mean(tok * tok, -1, keepdims=True) + norm_eps)
    return (tok * scale * gain).astype(bf16), scale


def probabilities(scores, bias, same):
    scores = jnp.where(same, scores + bias, masked_score)
    weights = jnp.exp(scores - jnp.max(scores, 0, keepdims=True))
    return weights * (1.0 / jnp.sum(weights, 0, keepdims=True))


def stack_heads(rows, masks):
    return jnp.concatenate([rows * mask for mask in masks], 0)


def own_blocks(product, heads):
    return jnp.concatenate(
        [product[h * HEAD : (h + 1) * HEAD, h * BLOCK : (h + 1) * BLOCK] for h in range(heads)], 0
    )


def fill_rows(ref, value):
    rows = value.shape[0]
    edge = jnp.zeros((BLOCK, value.shape[1]), bf16)
    ref[pl.ds(0, BLOCK), :] = edge
    ref[pl.ds(rows + BLOCK, BLOCK), :] = edge
    ref[pl.ds(BLOCK, rows), :] = value


def fill_columns(ref, value):
    rows = value.shape[1]
    edge = jnp.zeros((value.shape[0], BLOCK), bf16)
    ref[:, pl.ds(0, BLOCK)] = edge
    ref[:, pl.ds(rows + BLOCK, BLOCK)] = edge
    ref[:, pl.ds(BLOCK, rows)] = value


def forward_kernel(tok_ref, gain_ref, iw_ref, bt_ref, seg_ref, att_ref, normed_ref, keys, values):
    rows = tok_ref.shape[0]
    normed, _ = first_norm(tok_ref[...].astype(f32), flat(gain_ref))
    normed_ref[...] = normed
    queries = dot(normed, iw_ref[0], NT).astype(bf16)
    fill_rows(keys, dot(normed, iw_ref[1], NT).astype(bf16))
    fill_columns(values, dot(iw_ref[2], normed, NT).astype(bf16))
    seg = seg_ref[...].astype(f32)
    seg_keys = padded_segments(seg)
    tiles, _ = bias_tiles(bt_ref[...])
    heads = len(tiles)
    masks = head_masks(heads)
    for block in range(rows // BLOCK):
        at = block * BLOCK
        same = seg_keys[at : at + BAND] == seg[:, at : at + BLOCK]
        scores = dot(keys[pl.ds(at, BAND), :], stack_heads(queries[at : at + BLOCK], masks), NT)
        weights = [
            probabilities(scores[:, h * BLOCK : (h + 1) * BLOCK], tiles[h], same).astype(bf16) for h in range(heads)
        ]
        product = dot(values[:, pl.ds(at, BAND)], jnp.concatenate(weights, 1))
        att_ref[:, pl.ds(at, BLOCK)] = own_blocks(product, heads).astype(bf16)


def group_backward(normed, weight, out_weight, table, seg, grad_low, scratch, bias_grads):
    keys, values, keys_across, grad_keys, grad_values, grad_queries = scratch
    rows = normed.shape[0]
    queries = dot(normed, weight[0], NT).astype(bf16)
    fill_rows(keys, dot(normed, weight[1], NT).astype(bf16))
    fill_columns(keys_across, dot(weight[1], normed, NT).astype(bf16))
    fill_rows(values, dot(normed, weight[2], NT).astype(bf16))
    grad_att = dot(grad_low, out_weight, NT).astype(bf16)
    grad_keys[...] = jnp.zeros(grad_keys.shape, f32)
    grad_values[...] = jnp.zeros(grad_values.shape, f32)
    seg_keys = padded_segments(seg)
    tiles, onehot = bias_tiles(table)
    heads = len(tiles)
    masks = head_masks(heads)
    sums = [None] * heads
    for block in range(rows // BLOCK):
        at = block * BLOCK
        same = seg_keys[at : at + BAND] == seg[:, at : at + BLOCK]
        head_queries = stack_heads(queries[at : at + BLOCK], masks)
        head_grads = stack_heads(grad_att[at : at + BLOCK], masks)
        scores = dot(keys[pl.ds(at, BAND), :], head_queries, NT)
        grad_probs = dot(values[pl.ds(at, BAND), :], head_grads, NT)
        all_weights, all_grads = [], []
        for h in range(heads):
            columns = slice(h * BLOCK, (h + 1) * BLOCK)
            weights = probabilities(scores[:, columns], tiles[h], same)
            scaled = weights * grad_probs[:, columns]
            grad_scores = scaled - weights * jnp.sum(scaled, 0, keepdims=True)
            all_weights.append(weights.astype(bf16))
            all_grads.append(grad_scores.astype(bf16))
            if bias_grads:
                sums[h] = grad_scores if sums[h] is None else sums[h] + grad_scores
        low = jnp.concatenate(all_grads, 1)
        grad_queries[:, pl.ds(at, BLOCK)] = own_blocks(dot(keys_across[:, pl.ds(at, BAND)], low), heads)
        grad_keys[pl.ds(at, BAND), :] += dot(low, head_queries)
        grad_values[pl.ds(at, BAND), :] += dot(jnp.concatenate(all_weights, 1), head_grads)
    parts = (
        jnp.transpose(grad_queries[...]).astype(bf16),
        grad_keys[pl.ds(BLOCK, rows), :].astype(bf16),
        grad_values[pl.ds(BLOCK, rows), :].astype(bf16),
    )
    if not bias_grads:
        return parts, None
    diagonals = []
    row_index = iota((BLOCK, ROLL), 0)
    for h in range(heads):
        moved = jnp.concatenate([jnp.transpose(sums[h]), jnp.zeros((BLOCK, ROLL - BAND), f32)], 1)
        step = 1
        while step < BLOCK:
            moved = jnp.where((row_index & step) != 0, pltpu.roll(moved, ROLL - step, 1), moved)
            step *= 2
        diagonals.append(jnp.sum(moved, 0, keepdims=True))
    onehot = jnp.concatenate([onehot, jnp.zeros((128 - onehot.shape[0], ROLL), f32)], 0)
    by_head = dot(jnp.concatenate(diagonals, 0), onehot, NT, precision=highest)
    return parts, jnp.concatenate([by_head[h : h + 1] for h in range(heads)], 1)


def own_backward_kernel(normed_ref, iw_ref, ow_ref, bt_ref, seg_ref, low_ref, grad_iw_ref, parts_ref, table_ref, *scratch):
    normed = normed_ref[...]
    parts, table_grad = group_backward(
        normed, iw_ref, ow_ref[...], bt_ref[...], seg_ref[...].astype(f32), low_ref[...], scratch, True
    )
    table_ref[...] = jnp.concatenate(
        [table_grad, jnp.zeros((1, table_ref.shape[1] - table_grad.shape[1]), f32)], 1
    )
    width = ow_ref.shape[0]
    for j in range(3):
        parts_ref[j] = parts[j]
        grad_iw_ref[pl.ds(j * width, width), :] = dot(parts[j], normed, TN).astype(bf16)


def rest_backward_kernel(
    normed_ref, own_iw_ref, iw_ref, ow_ref, bt_ref, seg_ref, low_ref, parts_ref, tok_ref, gain_ref, grad_hidden_ref,
    table_ref, grad_tok_ref, tail_ref, total, *scratch,
):
    width = ow_ref.shape[1]
    total[...] = sum(dot(parts_ref[j], own_iw_ref[j]) for j in range(3))

    def step(group, carry):
        weight = [iw_ref[group, pl.ds(j * width, width), :] for j in range(3)]
        parts, _ = group_backward(
            normed_ref[...], weight, ow_ref[group], bt_ref[group], seg_ref[...].astype(f32), low_ref[...], scratch, False
        )
        total[...] += sum(dot(parts[j], weight[j]) for j in range(3))
        return carry

    lax.fori_loop(0, ow_ref.shape[0], step, 0)
    tok = tok_ref[...].astype(f32)
    gain = flat(gain_ref)
    scale = lax.rsqrt(jnp.mean(tok * tok, -1, keepdims=True) + norm_eps)
    grad_normed = total[...]
    tail_ref[...] = rows3([jnp.sum(grad_normed * tok * scale, 0, keepdims=True), table_ref[...]], tail_ref.shape[0])
    scaled = grad_normed * gain
    grad_tok_ref[...] = (
        grad_hidden_ref[...]
        + scale * scaled
        - tok * (scale * scale * scale) * jnp.mean(scaled * tok, -1, keepdims=True)
    )


def rows3(values, count):
    parts = [part for value in values for part in split3(value)]
    row = iota((count, values[0].shape[1]), 0)
    total = jnp.zeros(row.shape, f32)
    for index, part in enumerate(parts):
        total = jnp.where(row == index, part, total)
    return total.astype(bf16)


def finish_kernel(late_ref, early_ref, *refs):
    grad_iw_ref, grad_ow_ref, grad_rw_ref, second_ref, first_ref, table_ref = refs
    devices = late_ref.shape[0]
    late_rows = grad_iw_ref.shape[0] // devices
    tail = jnp.zeros((late_ref.shape[1] - late_rows, late_ref.shape[2]), f32)
    for device in range(devices):
        block = late_ref[device].astype(f32)
        grad_iw_ref[pl.ds(device * late_rows, late_rows), :] = block[:late_rows]
        tail = tail + block[late_rows:]
    first_ref[...] = jnp.sum(tail[:3], 0)
    table_ref[...] = jnp.sum(tail[3:6], 0, keepdims=True)
    at, experts = grad_ow_ref.shape[0], grad_rw_ref.shape[0]
    early_rows = early_ref.shape[1] - 8
    early = jnp.concatenate([early_ref[device][:early_rows] for device in range(devices)], 0)
    grad_ow_ref[...] = early[:at]
    grad_rw_ref[...] = early[at : at + experts]
    second_ref[...] = jnp.sum(early[at + experts : at + experts + 8], 0)


def slot_onehot(choice, slot, slots):
    dest = jnp.where(slot >= 0, choice * CAP + slot, slots)
    return (iota((slots, dest.shape[1]), 0) == dest).astype(f32).astype(bf16)


def slot_order(slots, group, across):
    index = iota((1, slots), 1)
    big, small = slots // across, slots // group
    outer, rest = lax.div(index, big), lax.rem(index, big)
    target = lax.div(rest, CAP) * small + outer * CAP + lax.rem(rest, CAP)
    return (iota((slots, slots), 0) == target).astype(f32).astype(bf16)


def cotangent_kernel(cot_ref, choice_ref, slot_ref, out_ref):
    fill = slot_onehot(flat(choice_ref), flat(slot_ref), out_ref.shape[0])
    out_ref[...] = dot(fill, cot_ref[...]).astype(bf16)


def order_kernel(sources, local, rows_ref, out_ref):
    out_ref[...] = dot(slot_order(rows_ref.shape[0], local, sources), rows_ref[...]).astype(bf16)


def chosen_of(choice, experts):
    column = column_of(choice)[:, :experts]
    return (column == iota(column.shape, 1).astype(f32)).astype(f32)


def middle_kernel(tok_ref, own_ow_ref, ow_ref, gain_ref, rw_ref, choice_ref, slot_ref, *refs):
    att_refs, (hidden_ref, prob_ref, send_ref) = refs[:-3], refs[-3:]
    hidden = tok_ref[...].astype(f32)
    for shift, att_ref in enumerate(att_refs):
        hidden = hidden + dot(att_ref[...], ow_ref[shift - 1] if shift else own_ow_ref[...], TN)
    hidden_ref[...] = hidden
    scale = lax.rsqrt(jnp.mean(hidden * hidden, -1, keepdims=True) + norm_eps)
    normed = hidden * scale * flat(gain_ref)
    logits = dot3(normed, rw_ref[...], NT)
    raised = jnp.exp(logits - jnp.max(logits, -1, keepdims=True))
    prob = raised * (1.0 / jnp.sum(raised, -1, keepdims=True))
    prob_ref[...] = prob
    gate = jnp.sum(prob * chosen_of(flat(choice_ref), prob.shape[1]), -1, keepdims=True)
    width = normed.shape[1]
    fill = slot_onehot(flat(choice_ref), flat(slot_ref), send_ref.shape[0])
    send_ref[:, :width] = dot(fill, normed.astype(bf16)).astype(bf16)
    send_ref[:, width:] = dot(fill, columns3(gate, 128)).astype(bf16)


def expert_kernel(
    tensor_size, sources, unroll,
    recv_ref, cot_ref, win_ref, wout_ref,
    rows_ref, grads_ref, act_ref, grad_act_ref, dots_ref, result_ref, *refs,
):
    chunks = refs[:tensor_size]
    x_all, g_all, r_all, y_all, d_all, turned = refs[tensor_size:]
    slots = recv_ref.shape[0]
    width = cot_ref.shape[1]
    step = pl.program_id(0)
    local = pl.num_programs(0) * unroll
    per = rows_ref.shape[0] // unroll

    @pl.when(step == 0)
    def _():
        order = slot_order(slots, win_ref.shape[0] * (slots // rows_ref.shape[0]), sources)
        x_all[...] = dot(order, recv_ref[:, :width]).astype(bf16)
        gate = jnp.sum(dot(order, recv_ref[:, width:]), -1, keepdims=True)
        g_all[...] = (gate * cot_ref[...].astype(f32)).astype(bf16)

    for u in range(unroll):
        here = pl.ds(u * per, per)
        at = pl.ds(pl.multiple_of((step * unroll + u) * per, 16), per)
        x = x_all[at, :]
        g = g_all[at, :]
        weight_in = win_ref[u]
        weight_out = wout_ref[u]
        pre = dot(x, weight_in)
        grad_act = dot(g, weight_out, NT)
        inner = jnp.tanh(gelu_const * (pre + gelu_cubic * pre * pre * pre))
        act = (0.5 * pre * (1.0 + inner)).astype(bf16)
        slope = 0.5 * (1.0 + inner) + 0.5 * pre * (1.0 - inner * inner) * gelu_const * (
            1.0 + 3.0 * gelu_cubic * pre * pre
        )
        grad_act = (grad_act * slope).astype(bf16)
        r_all[at, :] = dot(grad_act, weight_in, NT).astype(bf16)
        result = dot(act, weight_out)
        y_all[at, :] = result.astype(bf16)
        d_all[at, :] = columns3(jnp.sum(result * cot_ref[at, :].astype(f32), -1, keepdims=True), 128)
        rows_ref[here, :] = x
        grads_ref[here, :] = g
        act_ref[here, :] = act
        grad_act_ref[here, :] = grad_act

    @pl.when(step == pl.num_programs(0) - 1)
    def _():
        order = slot_order(slots, win_ref.shape[0] * (slots // rows_ref.shape[0]), sources)
        dots_ref[...] = dot(d_all[...], order, TN)[:EXTRA].astype(bf16)
        turn_chunks(tensor_size, dot(r_all[...], order, TN).astype(bf16), turned, chunks)
        result_ref[...] = dot(slot_order(slots, sources, win_ref.shape[0] * (slots // rows_ref.shape[0])), y_all[...]).astype(bf16)


def turn_chunks(tensor_size, rows, turned, chunks):
    turned[...] = rows
    quarter = rows.shape[0] // tensor_size
    me = lax.axis_index("tensor")
    for shift in range(tensor_size):
        first = lax.rem(me + shift, tensor_size) * quarter
        chunks[shift][...] = turned[pl.ds(pl.multiple_of(first, 64), quarter), :]


def result_back_kernel(recv_ref, choice_ref, slot_ref, out_ref):
    fill = slot_onehot(flat(choice_ref), flat(slot_ref), recv_ref.shape[0])
    out_ref[...] = dot(fill, recv_ref[...], TN).astype(bf16)


def sum_kernel(*refs):
    *parts, dots_ref, out_ref = refs
    total = sum(ref[...].astype(f32) for ref in parts)
    blank = jnp.zeros((out_ref.shape[1] - total.shape[0] - EXTRA, total.shape[1]), f32)
    out_ref[...] = jnp.transpose(jnp.concatenate([total, dots_ref[...].astype(f32), blank], 0)).astype(bf16)


def back_kernel(recv_ref, choice_ref, slot_ref, out_ref):
    fill = slot_onehot(flat(choice_ref), flat(slot_ref), recv_ref.shape[0])
    out_ref[...] = dot(recv_ref[...], fill, TN)[: out_ref.shape[0]].astype(bf16)


def spread(refs, quarter, turned):
    size = len(refs)
    me = lax.axis_index("tensor")
    for shift, ref in enumerate(refs):
        first = lax.rem(me + size - shift, size) * quarter
        turned[pl.ds(pl.multiple_of(first, 64), quarter), :] = ref[pl.ds(0, quarter), :].astype(f32)
    return jnp.transpose(turned[...])


def hidden_backward_kernel(
    hidden_ref, prob_ref, cot_ref, gain_ref, rw_ref, choice_ref, att_ref, *refs,
):
    parts = refs[:-4]
    grad_hidden_ref, low_ref, sums_ref, turned = refs[-4:]
    hidden = hidden_ref[...]
    rows, width = hidden.shape
    quarter = width // len(parts)
    grad_routed = spread(parts, quarter, turned)
    dots = sum(jnp.sum(ref[pl.ds(quarter, EXTRA), :].astype(f32), 0, keepdims=True) for ref in parts)
    prob = prob_ref[...]
    chosen = chosen_of(flat(choice_ref), prob.shape[1])
    gate = jnp.sum(prob * chosen, -1, keepdims=True)
    grad_gate = column_of(dots)[:, :1]
    grad_logits = (grad_gate * gate) * (chosen - prob)
    grad_normed = grad_routed + dot3(grad_logits, rw_ref[...])
    gain = flat(gain_ref)
    scale = lax.rsqrt(jnp.mean(hidden * hidden, -1, keepdims=True) + norm_eps)
    scaled = grad_normed * gain
    grad_hidden = (
        cot_ref[...].astype(f32)
        + scale * scaled
        - hidden * (scale * scale * scale) * jnp.mean(scaled * hidden, -1, keepdims=True)
    )
    grad_hidden_ref[...] = grad_hidden
    low = grad_hidden.astype(bf16)
    low_ref[...] = low
    at, experts = att_ref.shape[0], prob.shape[1]
    sums_ref[pl.ds(0, at), :] = dot(att_ref[...], low).astype(bf16)
    sums_ref[pl.ds(at, experts), :] = dot3(grad_logits, hidden * scale * gain, TN).astype(bf16)
    tail = sums_ref.shape[0] - at - experts
    sums_ref[pl.ds(at + experts, tail), :] = rows3([jnp.sum(grad_normed * hidden * scale, 0, keepdims=True)], tail)


def output_kernel(hidden_ref, prob_ref, choice_ref, result_ref, out_ref):
    prob = prob_ref[...]
    gate = jnp.sum(prob * chosen_of(flat(choice_ref), prob.shape[1]), -1, keepdims=True)
    share = hidden_ref.shape[0] // result_ref.shape[0]
    result = jnp.concatenate([result_ref[part][:share] for part in range(result_ref.shape[0])], 0)
    out_ref[...] = (hidden_ref[...] + gate * result.astype(f32)).astype(bf16)


def make(mesh):
    tensor_size = mesh.shape["tensor"]
    expert_size = mesh.shape["expert"]

    def shards(
        tokens,
        segment_ids,
        expert_choice,
        slot_index,
        first_gain,
        input_weight,
        bias_table,
        output_weight,
        second_gain,
        router_weight,
        expert_in,
        expert_out,
        cotangent,
    ):
        token_count, width = tokens.shape
        sequences, length = segment_ids.shape
        quarter = output_weight.shape[0]
        experts = router_weight.shape[1]
        local = expert_in.shape[0]
        hidden_units = expert_in.shape[2]
        slots = experts * CAP
        per = slots // local
        chunk = slots // expert_size
        buckets, heads = bias_table.shape
        expert_index = lax.axis_index("expert")
        seg = (segment_ids + 8 * jnp.arange(sequences, dtype=i32)[:, None]).reshape(1, token_count)
        choice, slot = expert_choice, slot_index
        gain_first, gain_second = first_gain, second_gain
        iw_own = jnp.swapaxes(input_weight, 1, 2)
        table = bias_table.T
        rw = router_weight.T
        after = lax.optimization_barrier

        shifts = [[(i, (i + s) % tensor_size) for i in range(tensor_size)] for s in range(1, tensor_size)]

        def from_others(array):
            return [lax.ppermute(array, "tensor", pairs) for pairs in shifts]

        def gather_tensor(array):
            return [array] + from_others(array)

        def joined(planes):
            got = lax.all_gather(planes, "expert", axis=0)
            return jnp.swapaxes(got, 0, 1).reshape(tensor_size - 1, -1, got.shape[-1])

        def exchange(array):
            rows = array.shape[0] // expert_size
            got = lax.all_to_all(array.reshape(expert_size, rows, array.shape[1]), "expert", 0, 0)
            return got.reshape(array.shape)

        ow_rows = quarter // expert_size
        ow_part = lax.dynamic_slice_in_dim(output_weight, expert_index * ow_rows, ow_rows, 0)
        ow_all = joined(jnp.stack(from_others(ow_part)))

        attended, first_normed = call(
            forward_kernel,
            [((quarter, token_count), bf16), ((token_count, width), bf16)],
            (tokens, gain_first, iw_own, table, seg),
            [
                pltpu.VMEM((token_count + 2 * BLOCK, quarter), bf16),
                pltpu.VMEM((quarter, token_count + 2 * BLOCK), bf16),
            ],
        )
        attended_parts = gather_tensor(attended)
        cot_early, _ = after((cotangent, attended))
        (cot_slots,) = call(cotangent_kernel, [((slots, width), bf16)], (cot_early, choice, slot))
        (cot_rows,) = call(
            lambda *refs: order_kernel(expert_size, local, *refs), [((slots, width), bf16)], (exchange(cot_slots),)
        )
        attended_parts, cot_rows = after((attended_parts, cot_rows))

        hidden, prob, send = call(
            middle_kernel,
            [((token_count, width), f32), ((token_count, experts), f32), ((slots, width + 128), bf16)],
            (tokens, output_weight, ow_all, gain_second, rw, choice, slot, *attended_parts),
        )
        recv = exchange(send)

        iw_rows = 3 * quarter // expert_size
        iw_part = lax.dynamic_slice_in_dim(iw_own.reshape(3 * quarter, width), expert_index * iw_rows, iw_rows, 0)
        bias_parts = jnp.stack(split3(table)).astype(bf16).reshape(-1)
        bias_parts = jnp.pad(bias_parts, (0, 8 * width - bias_parts.shape[0])).reshape(8, width)
        iw_part, _ = after((jnp.concatenate([iw_part, bias_parts], 0), send))
        iw_planes = from_others(iw_part)

        iw_planes, recv = after((iw_planes, recv))
        iw_planes = jnp.stack(iw_planes)
        iw_all = joined(iw_planes[:, :iw_rows])
        bias_all = jnp.sum(
            iw_planes[:, iw_rows:]
            .reshape(tensor_size - 1, -1)[:, : 3 * buckets * heads]
            .reshape(tensor_size - 1, 3, heads, buckets)
            .astype(f32),
            1,
        )

        unroll = 2 if local % 2 == 0 else 1
        whole = lambda shape: pl.BlockSpec(shape, lambda j: (0,) * len(shape))
        by_expert = pl.BlockSpec((unroll * per, width), lambda j: (j, 0))
        by_hidden = pl.BlockSpec((unroll * per, hidden_units), lambda j: (j, 0))
        outs = pl.pallas_call(
            lambda *refs: expert_kernel(tensor_size, expert_size, unroll, *refs),
            grid=(local // unroll,),
            in_specs=[
                whole((slots, width + 128)),
                whole((slots, width)),
                pl.BlockSpec((unroll, width, hidden_units), lambda j: (j, 0, 0)),
                pl.BlockSpec((unroll, hidden_units, width), lambda j: (j, 0, 0)),
            ],
            out_specs=[by_expert, by_expert, by_hidden, by_hidden, whole((EXTRA, slots)), whole((slots, width))]
            + [whole((quarter, slots))] * tensor_size,
            out_shape=[jax.ShapeDtypeStruct((slots, width), bf16)] * 2
            + [jax.ShapeDtypeStruct((slots, hidden_units), bf16)] * 2
            + [jax.ShapeDtypeStruct((EXTRA, slots), bf16), jax.ShapeDtypeStruct((slots, width), bf16)]
            + [jax.ShapeDtypeStruct((quarter, slots), bf16)] * tensor_size,
            scratch_shapes=[pltpu.VMEM((slots, width), bf16)] * 4
            + [pltpu.VMEM((slots, 128), bf16), pltpu.VMEM((width, slots), bf16)],
            compiler_params=pltpu.CompilerParams(vmem_limit_bytes=56 * 2**20),
        )(recv, cot_rows, expert_in, expert_out)
        expert_rows, grad_slots, expert_act, grad_act, dots, result_rows = outs[:6]
        grad_chunks = outs[6:]

        def trade_chunks(chunks):
            return [chunks[0]] + [lax.ppermute(c, "tensor", pairs) for c, pairs in zip(chunks[1:], shifts)]

        def sum_rows(parts):
            columns = -(-(quarter + EXTRA) // 128) * 128
            return call(sum_kernel, [((slots, columns), bf16)], parts)[0]

        def own_tokens(rows, kept):
            return call(back_kernel, [((kept, token_count), bf16)], (rows, choice, slot))[0]

        by = lambda array: array.reshape(local, per, array.shape[1])
        grad_expert_out = jnp.einsum("erf,erd->efd", by(expert_act), by(grad_slots), preferred_element_type=f32)
        grad_expert_in = jnp.einsum("erd,erf->edf", by(expert_rows), by(grad_act), preferred_element_type=f32)

        traded, grad_expert_out, result_rows = after(
            (trade_chunks(grad_chunks), grad_expert_out, exchange(result_rows))
        )
        summed = sum_rows(traded + [dots])
        (result_part,) = call(
            result_back_kernel, [((token_count, width), bf16)], (result_rows, choice, slot)
        )
        returned = own_tokens(exchange(summed), quarter + EXTRA)
        returned, grad_expert_in, result_part = after((returned, grad_expert_in, result_part))
        result_share = lax.psum_scatter(result_part, "tensor", scatter_dimension=0, tiled=True)
        grad_parts = gather_tensor(returned)
        grad_parts, iw_all, bias_all, result_share = after((grad_parts, iw_all, bias_all, result_share))
        result = lax.all_gather(jnp.pad(result_share, ((0, 48), (0, 0))), "tensor", axis=0)

        early_rows = quarter + experts + 64
        grad_hidden, grad_low, early_sums = call(
            hidden_backward_kernel,
            [((token_count, width), f32), ((token_count, width), bf16), ((early_rows, width), bf16)],
            (hidden, prob, cotangent, gain_second, rw, choice, attended, *grad_parts),
            [pltpu.VMEM((width, token_count), f32)],
        )
        def sum_chunks(array):
            return jnp.sum(array.reshape(expert_size, -1, array.shape[1]).astype(f32), 0)

        padded = token_count + 2 * BLOCK
        scratch = [pltpu.VMEM((padded, quarter), bf16)] * 2 + [pltpu.VMEM((quarter, padded), bf16)]
        scratch = scratch + [pltpu.VMEM((padded, quarter), f32)] * 2 + [pltpu.VMEM((quarter, token_count), f32)]
        grad_iw, own_parts, table_grad = call(
            own_backward_kernel,
            [((3 * quarter, width), bf16), ((3, token_count, quarter), bf16), ((1, width), f32)],
            (first_normed, iw_own, output_weight, table, seg, grad_low),
            scratch,
        )
        grad_tokens, tail = call(
            rest_backward_kernel,
            [((token_count, width), f32), ((8, width), bf16)],
            (
                first_normed, iw_own, iw_all, ow_all, bias_all, seg, grad_low, own_parts, tokens, gain_first,
                grad_hidden, table_grad,
            ),
            [pltpu.VMEM((token_count, width), f32)] + scratch,
        )
        (block_output,) = call(
            output_kernel,
            [((token_count, width), bf16)],
            (hidden, prob, choice, result),
        )
        early_got, grad_iw = after((exchange(early_sums), grad_iw))
        early_sum = sum_chunks(early_got)
        early = lax.all_gather(jnp.pad(early_sum, ((0, 8), (0, 0))), "expert", axis=0)
        late = lax.all_gather(jnp.concatenate([sum_chunks(exchange(grad_iw)).astype(bf16), tail], 0), "expert", axis=0)
        grad_iw, grad_ow, grad_rw, grad_second, grad_first, grad_table = call(
            finish_kernel,
            [
                ((3 * quarter, width), f32),
                ((quarter, width), f32),
                ((experts, width), f32),
                ((width,), f32),
                ((width,), f32),
                ((1, width), f32),
            ],
            (late, early),
        )
        return (
            block_output,
            grad_tokens,
            grad_first,
            jnp.swapaxes(grad_iw.reshape(3, quarter, width), 1, 2),
            grad_table.reshape(width // 128, 128)[:heads, :buckets].T,
            grad_ow,
            grad_second,
            grad_rw.T,
            grad_expert_in,
            grad_expert_out,
        )

    return shards


def solution(mesh):
    placed = (
        P("expert", None),
        P("expert", None),
        P("expert"),
        P("expert"),
        P(),
        P(None, None, "tensor"),
        P(None, "tensor"),
        P("tensor", None),
        P(),
        P(),
        P("expert", None, "tensor"),
        P("expert", "tensor", None),
        P("expert", None),
    )
    return jax.shard_map(
        make(mesh),
        mesh=mesh,
        in_specs=placed,
        out_specs=(
            P("expert", None),
            P("expert", None),
            P(),
            P(None, None, "tensor"),
            P(None, "tensor"),
            P("tensor", None),
            P(),
            P(),
            P("expert", None, "tensor"),
            P("expert", "tensor", None),
        ),
        check_vma=False,
    )
```

```python
import math

import jax
import jax.numpy as jnp
from jax import lax
from jax.experimental import pallas as pl
from jax.experimental.pallas import tpu as pltpu
from jax.sharding import PartitionSpec as P

CAP = 10

bucket_edges = (12, 16, 23, 32, 46, 64, 91)
norm_eps = 1e-06
masked_score = -1e30
gelu_const = math.sqrt(2.0 / math.pi)
gelu_cubic = 0.044715

BLOCK = 128
BAND = 3 * BLOCK
ROLL = 4 * BLOCK
HEAD = 64
EXTRA = 16

bf16 = jnp.bfloat16
f32 = jnp.float32
i32 = jnp.int32
highest = lax.Precision.HIGHEST

NN = (((1,), (0,)), ((), ()))
NT = (((1,), (1,)), ((), ()))
TN = (((0,), (0,)), ((), ()))


def dot(left, right, dims=NN, precision=None):
    return lax.dot_general(left, right, dims, precision=precision, preferred_element_type=f32)


def dot3(left, right, dims=NN):
    left_high, right_high = left.astype(bf16), right.astype(bf16)
    left_low = (left - left_high.astype(f32)).astype(bf16)
    right_low = (right - right_high.astype(f32)).astype(bf16)
    return dot(left_high, right_high, dims) + (dot(left_high, right_low, dims) + dot(left_low, right_high, dims))


def flat(ref):
    return ref[...].reshape(1, -1)


def iota(shape, axis):
    return lax.broadcasted_iota(i32, shape, axis)


def call(kernel, outs, args, scratch=(), **extra):
    vmem = pl.BlockSpec(memory_space=pltpu.VMEM)
    return pl.pallas_call(
        kernel,
        out_shape=[jax.ShapeDtypeStruct(shape, dtype) for shape, dtype in outs],
        in_specs=[vmem] * len(args),
        out_specs=[vmem] * len(outs),
        scratch_shapes=list(scratch),
        compiler_params=pltpu.CompilerParams(vmem_limit_bytes=56 * 2**20),
        **extra,
    )(*args)


def split3(value):
    high = value.astype(bf16).astype(f32)
    rest = value - high
    middle = rest.astype(bf16).astype(f32)
    return high, middle, rest - middle


def columns3(value, width):
    high, middle, low = split3(value)
    lane = iota((value.shape[0], width), 1)
    picked = jnp.where(lane == 0, high, jnp.where(lane == 1, middle, jnp.where(lane == 2, low, 0.0)))
    return picked.astype(bf16)


def column_of(row):
    return jnp.transpose(jnp.broadcast_to(row.astype(f32), (128, row.shape[1])))


def wide(column, width):
    return jnp.concatenate([column] * (width // 128), 1)


def bucket_of(relative):
    distance = jnp.abs(relative)
    beyond = jnp.zeros_like(distance)
    for threshold in bucket_edges:
        beyond = beyond + (distance >= threshold).astype(i32)
    magnitude = jnp.where(distance < 8, distance, 8 + beyond)
    return magnitude + 16 * (relative > 0).astype(i32)


def band_rows(table):
    buckets = table.shape[1]
    offset = iota((buckets, ROLL), 1)
    relative = jnp.where(offset < BAND, offset, offset - ROLL) - BLOCK
    onehot = (bucket_of(relative) == iota((buckets, ROLL), 0)).astype(f32)
    return dot(table, onehot, precision=highest), onehot


def bias_tiles(table):
    rows, onehot = band_rows(table)
    tiles = []
    for h in range(table.shape[0]):
        full = jnp.broadcast_to(rows[h : h + 1], (BLOCK, ROLL))
        tiles.append(jnp.transpose(pltpu.roll(full, 0, 1, stride=1, stride_axis=0)[:, :BAND]))
    return tiles, onehot


def head_masks(heads):
    lane = iota((1, heads * HEAD), 1)
    return [((lane >= h * HEAD) & (lane < (h + 1) * HEAD)).astype(f32).astype(bf16) for h in range(heads)]


def padded_segments(seg):
    edge = jnp.full((1, BLOCK), -1.0, f32)
    return column_of(jnp.concatenate([edge, seg, edge], 1))


def first_norm(tok, gain):
    scale = lax.rsqrt(jnp.mean(tok * tok, -1, keepdims=True) + norm_eps)
    return (tok * scale * gain).astype(bf16), scale


def probabilities(scores, bias, same):
    scores = jnp.where(same, scores + bias, masked_score)
    weights = jnp.exp(scores - jnp.max(scores, 0, keepdims=True))
    return weights * (1.0 / jnp.sum(weights, 0, keepdims=True))


def stack_heads(rows, masks):
    return jnp.concatenate([rows * mask for mask in masks], 0)


def own_blocks(product, heads):
    return jnp.concatenate(
        [product[h * HEAD : (h + 1) * HEAD, h * BLOCK : (h + 1) * BLOCK] for h in range(heads)], 0
    )


def fill_rows(ref, value):
    rows = value.shape[0]
    edge = jnp.zeros((BLOCK, value.shape[1]), bf16)
    ref[pl.ds(0, BLOCK), :] = edge
    ref[pl.ds(rows + BLOCK, BLOCK), :] = edge
    ref[pl.ds(BLOCK, rows), :] = value


def fill_columns(ref, value):
    rows = value.shape[1]
    edge = jnp.zeros((value.shape[0], BLOCK), bf16)
    ref[:, pl.ds(0, BLOCK)] = edge
    ref[:, pl.ds(rows + BLOCK, BLOCK)] = edge
    ref[:, pl.ds(BLOCK, rows)] = value


def forward_kernel(tok_ref, gain_ref, iw_ref, bt_ref, seg_ref, att_ref, normed_ref, keys, values):
    rows = tok_ref.shape[0]
    normed, _ = first_norm(tok_ref[...].astype(f32), flat(gain_ref))
    normed_ref[...] = normed
    queries = dot(normed, iw_ref[0], NT).astype(bf16)
    fill_rows(keys, dot(normed, iw_ref[1], NT).astype(bf16))
    fill_columns(values, dot(iw_ref[2], normed, NT).astype(bf16))
    seg = seg_ref[...].astype(f32)
    seg_keys = padded_segments(seg)
    tiles, _ = bias_tiles(bt_ref[...])
    heads = len(tiles)
    masks = head_masks(heads)
    for block in range(rows // BLOCK):
        at = block * BLOCK
        same = seg_keys[at : at + BAND] == seg[:, at : at + BLOCK]
        scores = dot(keys[pl.ds(at, BAND), :], stack_heads(queries[at : at + BLOCK], masks), NT)
        weights = [
            probabilities(scores[:, h * BLOCK : (h + 1) * BLOCK], tiles[h], same).astype(bf16) for h in range(heads)
        ]
        product = dot(values[:, pl.ds(at, BAND)], jnp.concatenate(weights, 1))
        att_ref[:, pl.ds(at, BLOCK)] = own_blocks(product, heads).astype(bf16)


def group_backward(normed, weight, out_weight, table, seg, grad_low, scratch, bias_grads):
    keys, values, keys_across, grad_keys, grad_values, grad_queries = scratch
    rows = normed.shape[0]
    queries = dot(normed, weight[0], NT).astype(bf16)
    fill_rows(keys, dot(normed, weight[1], NT).astype(bf16))
    fill_columns(keys_across, dot(weight[1], normed, NT).astype(bf16))
    fill_rows(values, dot(normed, weight[2], NT).astype(bf16))
    grad_att = dot(grad_low, out_weight, NT).astype(bf16)
    grad_keys[...] = jnp.zeros(grad_keys.shape, f32)
    grad_values[...] = jnp.zeros(grad_values.shape, f32)
    seg_keys = padded_segments(seg)
    tiles, onehot = bias_tiles(table)
    heads = len(tiles)
    masks = head_masks(heads)
    sums = [None] * heads
    for block in range(rows // BLOCK):
        at = block * BLOCK
        same = seg_keys[at : at + BAND] == seg[:, at : at + BLOCK]
        head_queries = stack_heads(queries[at : at + BLOCK], masks)
        head_grads = stack_heads(grad_att[at : at + BLOCK], masks)
        scores = dot(keys[pl.ds(at, BAND), :], head_queries, NT)
        grad_probs = dot(values[pl.ds(at, BAND), :], head_grads, NT)
        all_weights, all_grads = [], []
        for h in range(heads):
            columns = slice(h * BLOCK, (h + 1) * BLOCK)
            weights = probabilities(scores[:, columns], tiles[h], same)
            scaled = weights * grad_probs[:, columns]
            grad_scores = scaled - weights * jnp.sum(scaled, 0, keepdims=True)
            all_weights.append(weights.astype(bf16))
            all_grads.append(grad_scores.astype(bf16))
            if bias_grads:
                sums[h] = grad_scores if sums[h] is None else sums[h] + grad_scores
        low = jnp.concatenate(all_grads, 1)
        grad_queries[:, pl.ds(at, BLOCK)] = own_blocks(dot(keys_across[:, pl.ds(at, BAND)], low), heads)
        grad_keys[pl.ds(at, BAND), :] += dot(low, head_queries)
        grad_values[pl.ds(at, BAND), :] += dot(jnp.concatenate(all_weights, 1), head_grads)
    parts = (
        jnp.transpose(grad_queries[...]).astype(bf16),
        grad_keys[pl.ds(BLOCK, rows), :].astype(bf16),
        grad_values[pl.ds(BLOCK, rows), :].astype(bf16),
    )
    if not bias_grads:
        return parts, None
    diagonals = []
    row_index = iota((BLOCK, ROLL), 0)
    for h in range(heads):
        moved = jnp.concatenate([jnp.transpose(sums[h]), jnp.zeros((BLOCK, ROLL - BAND), f32)], 1)
        step = 1
        while step < BLOCK:
            moved = jnp.where((row_index & step) != 0, pltpu.roll(moved, ROLL - step, 1), moved)
            step *= 2
        diagonals.append(jnp.sum(moved, 0, keepdims=True))
    onehot = jnp.concatenate([onehot, jnp.zeros((128 - onehot.shape[0], ROLL), f32)], 0)
    by_head = dot(jnp.concatenate(diagonals, 0), onehot, NT, precision=highest)
    return parts, jnp.concatenate([by_head[h : h + 1] for h in range(heads)], 1)


def own_backward_kernel(normed_ref, iw_ref, ow_ref, bt_ref, seg_ref, low_ref, grad_iw_ref, parts_ref, table_ref, *scratch):
    normed = normed_ref[...]
    parts, table_grad = group_backward(
        normed, iw_ref, ow_ref[...], bt_ref[...], seg_ref[...].astype(f32), low_ref[...], scratch, True
    )
    table_ref[...] = jnp.concatenate(
        [table_grad, jnp.zeros((1, table_ref.shape[1] - table_grad.shape[1]), f32)], 1
    )
    width = ow_ref.shape[0]
    for j in range(3):
        parts_ref[j] = parts[j]
        grad_iw_ref[pl.ds(j * width, width), :] = dot(parts[j], normed, TN).astype(bf16)


def rest_backward_kernel(
    normed_ref, own_iw_ref, iw_ref, ow_ref, bt_ref, seg_ref, low_ref, parts_ref, tok_ref, gain_ref, grad_hidden_ref,
    table_ref, grad_tok_ref, tail_ref, total, *scratch,
):
    width = ow_ref.shape[1]
    total[...] = sum(dot(parts_ref[j], own_iw_ref[j]) for j in range(3))

    def step(group, carry):
        weight = [iw_ref[group, pl.ds(j * width, width), :] for j in range(3)]
        parts, _ = group_backward(
            normed_ref[...], weight, ow_ref[group], bt_ref[group], seg_ref[...].astype(f32), low_ref[...], scratch, False
        )
        total[...] += sum(dot(parts[j], weight[j]) for j in range(3))
        return carry

    lax.fori_loop(0, ow_ref.shape[0], step, 0)
    tok = tok_ref[...].astype(f32)
    gain = flat(gain_ref)
    scale = lax.rsqrt(jnp.mean(tok * tok, -1, keepdims=True) + norm_eps)
    grad_normed = total[...]
    tail_ref[...] = rows3([jnp.sum(grad_normed * tok * scale, 0, keepdims=True), table_ref[...]], tail_ref.shape[0])
    scaled = grad_normed * gain
    grad_tok_ref[...] = (
        grad_hidden_ref[...]
        + scale * scaled
        - tok * (scale * scale * scale) * jnp.mean(scaled * tok, -1, keepdims=True)
    )


def rows3(values, count):
    parts = [part for value in values for part in split3(value)]
    row = iota((count, values[0].shape[1]), 0)
    total = jnp.zeros(row.shape, f32)
    for index, part in enumerate(parts):
        total = jnp.where(row == index, part, total)
    return total.astype(bf16)


def finish_kernel(late_ref, early_ref, *refs):
    grad_iw_ref, grad_ow_ref, grad_rw_ref, second_ref, first_ref, table_ref = refs
    devices = late_ref.shape[0]
    late_rows = grad_iw_ref.shape[0] // devices
    tail = jnp.zeros((late_ref.shape[1] - late_rows, late_ref.shape[2]), f32)
    for device in range(devices):
        block = late_ref[device].astype(f32)
        grad_iw_ref[pl.ds(device * late_rows, late_rows), :] = block[:late_rows]
        tail = tail + block[late_rows:]
    first_ref[...] = jnp.sum(tail[:3], 0)
    table_ref[...] = jnp.sum(tail[3:6], 0, keepdims=True)
    at, experts = grad_ow_ref.shape[0], grad_rw_ref.shape[0]
    early_rows = early_ref.shape[1] - 8
    early = jnp.concatenate([early_ref[device][:early_rows] for device in range(devices)], 0)
    grad_ow_ref[...] = early[:at]
    grad_rw_ref[...] = early[at : at + experts]
    second_ref[...] = jnp.sum(early[at + experts : at + experts + 8], 0)


def slot_onehot(choice, slot, slots):
    dest = jnp.where(slot >= 0, choice * CAP + slot, slots)
    return (iota((slots, dest.shape[1]), 0) == dest).astype(f32).astype(bf16)


def slot_order(slots, group, across):
    index = iota((1, slots), 1)
    big, small = slots // across, slots // group
    outer, rest = lax.div(index, big), lax.rem(index, big)
    target = lax.div(rest, CAP) * small + outer * CAP + lax.rem(rest, CAP)
    return (iota((slots, slots), 0) == target).astype(f32).astype(bf16)


def cotangent_kernel(cot_ref, choice_ref, slot_ref, out_ref):
    fill = slot_onehot(flat(choice_ref), flat(slot_ref), out_ref.shape[0])
    out_ref[...] = dot(fill, cot_ref[...]).astype(bf16)


def chosen_of(choice, experts):
    column = column_of(choice)[:, :experts]
    return (column == iota(column.shape, 1).astype(f32)).astype(f32)


def middle_kernel(tok_ref, own_ow_ref, ow_ref, gain_ref, rw_ref, choice_ref, slot_ref, *refs):
    att_refs, (hidden_ref, prob_ref, send_ref) = refs[:-3], refs[-3:]
    hidden = tok_ref[...].astype(f32)
    for shift, att_ref in enumerate(att_refs):
        hidden = hidden + dot(att_ref[...], ow_ref[shift - 1] if shift else own_ow_ref[...], TN)
    hidden_ref[...] = hidden
    scale = lax.rsqrt(jnp.mean(hidden * hidden, -1, keepdims=True) + norm_eps)
    normed = hidden * scale * flat(gain_ref)
    logits = dot3(normed, rw_ref[...], NT)
    raised = jnp.exp(logits - jnp.max(logits, -1, keepdims=True))
    prob = raised * (1.0 / jnp.sum(raised, -1, keepdims=True))
    prob_ref[...] = prob
    gate = jnp.sum(prob * chosen_of(flat(choice_ref), prob.shape[1]), -1, keepdims=True)
    width = normed.shape[1]
    fill = slot_onehot(flat(choice_ref), flat(slot_ref), send_ref.shape[0])
    send_ref[:, :width] = dot(fill, normed.astype(bf16)).astype(bf16)
    send_ref[:, width:] = dot(fill, columns3(gate, 128)).astype(bf16)


def expert_kernel(
    tensor_size, sources, unroll,
    recv_ref, cot_ref, win_ref, wout_ref,
    rows_ref, grads_ref, act_ref, grad_act_ref, dots_ref, result_ref, *refs,
):
    chunks = refs[:tensor_size]
    x_all, c_all, g_all, r_all, y_all, d_all, turned = refs[tensor_size:]
    slots = recv_ref.shape[0]
    width = cot_ref.shape[1]
    step = pl.program_id(0)
    local = pl.num_programs(0) * unroll
    per = rows_ref.shape[0] // unroll

    @pl.when(step == 0)
    def _():
        order = slot_order(slots, win_ref.shape[0] * (slots // rows_ref.shape[0]), sources)
        x_all[...] = dot(order, recv_ref[:, :width]).astype(bf16)
        gate = jnp.sum(dot(order, recv_ref[:, width:]), -1, keepdims=True)
        cot = dot(order, cot_ref[...])
        c_all[...] = cot.astype(bf16)
        g_all[...] = (gate * cot).astype(bf16)

    for u in range(unroll):
        here = pl.ds(u * per, per)
        at = pl.ds(pl.multiple_of((step * unroll + u) * per, 16), per)
        x = x_all[at, :]
        g = g_all[at, :]
        weight_in = win_ref[u]
        weight_out = wout_ref[u]
        pre = dot(x, weight_in)
        grad_act = dot(g, weight_out, NT)
        inner = jnp.tanh(gelu_const * (pre + gelu_cubic * pre * pre * pre))
        act = (0.5 * pre * (1.0 + inner)).astype(bf16)
        slope = 0.5 * (1.0 + inner) + 0.5 * pre * (1.0 - inner * inner) * gelu_const * (
            1.0 + 3.0 * gelu_cubic * pre * pre
        )
        grad_act = (grad_act * slope).astype(bf16)
        r_all[at, :] = dot(grad_act, weight_in, NT).astype(bf16)
        result = dot(act, weight_out)
        y_all[at, :] = result.astype(bf16)
        d_all[at, :] = columns3(jnp.sum(result * c_all[at, :].astype(f32), -1, keepdims=True), 128)
        rows_ref[here, :] = x
        grads_ref[here, :] = g
        act_ref[here, :] = act
        grad_act_ref[here, :] = grad_act

    @pl.when(step == pl.num_programs(0) - 1)
    def _():
        order = slot_order(slots, win_ref.shape[0] * (slots // rows_ref.shape[0]), sources)
        dots_ref[...] = dot(d_all[...], order, TN)[:EXTRA].astype(bf16)
        turn_chunks(tensor_size, dot(r_all[...], order, TN).astype(bf16), turned, chunks)
        result_ref[...] = dot(slot_order(slots, sources, win_ref.shape[0] * (slots // rows_ref.shape[0])), y_all[...]).astype(bf16)


def turn_chunks(tensor_size, rows, turned, chunks):
    turned[...] = rows
    quarter = rows.shape[0] // tensor_size
    me = lax.axis_index("tensor")
    for shift in range(tensor_size):
        first = lax.rem(me + shift, tensor_size) * quarter
        chunks[shift][...] = turned[pl.ds(pl.multiple_of(first, 64), quarter), :]


def result_back_kernel(recv_ref, choice_ref, slot_ref, out_ref):
    fill = slot_onehot(flat(choice_ref), flat(slot_ref), recv_ref.shape[0])
    out_ref[...] = dot(fill, recv_ref[...], TN).astype(bf16)


def sum_kernel(*refs):
    *parts, dots_ref, out_ref = refs
    total = sum(ref[...].astype(f32) for ref in parts)
    blank = jnp.zeros((out_ref.shape[1] - total.shape[0] - EXTRA, total.shape[1]), f32)
    out_ref[...] = jnp.transpose(jnp.concatenate([total, dots_ref[...].astype(f32), blank], 0)).astype(bf16)


def back_kernel(recv_ref, choice_ref, slot_ref, out_ref):
    fill = slot_onehot(flat(choice_ref), flat(slot_ref), recv_ref.shape[0])
    out_ref[...] = dot(recv_ref[...], fill, TN)[: out_ref.shape[0]].astype(bf16)


def spread(refs, quarter, turned):
    size = len(refs)
    me = lax.axis_index("tensor")
    for shift, ref in enumerate(refs):
        first = lax.rem(me + size - shift, size) * quarter
        turned[pl.ds(pl.multiple_of(first, 64), quarter), :] = ref[pl.ds(0, quarter), :].astype(f32)
    return jnp.transpose(turned[...])


def hidden_backward_kernel(
    hidden_ref, prob_ref, cot_ref, gain_ref, rw_ref, choice_ref, att_ref, *refs,
):
    parts = refs[:-4]
    grad_hidden_ref, low_ref, sums_ref, turned = refs[-4:]
    hidden = hidden_ref[...]
    rows, width = hidden.shape
    quarter = width // len(parts)
    grad_routed = spread(parts, quarter, turned)
    dots = sum(jnp.sum(ref[pl.ds(quarter, EXTRA), :].astype(f32), 0, keepdims=True) for ref in parts)
    prob = prob_ref[...]
    chosen = chosen_of(flat(choice_ref), prob.shape[1])
    gate = jnp.sum(prob * chosen, -1, keepdims=True)
    grad_gate = column_of(dots)[:, :1]
    grad_logits = (grad_gate * gate) * (chosen - prob)
    grad_normed = grad_routed + dot3(grad_logits, rw_ref[...])
    gain = flat(gain_ref)
    scale = lax.rsqrt(jnp.mean(hidden * hidden, -1, keepdims=True) + norm_eps)
    scaled = grad_normed * gain
    grad_hidden = (
        cot_ref[...].astype(f32)
        + scale * scaled
        - hidden * (scale * scale * scale) * jnp.mean(scaled * hidden, -1, keepdims=True)
    )
    grad_hidden_ref[...] = grad_hidden
    low = grad_hidden.astype(bf16)
    low_ref[...] = low
    at, experts = att_ref.shape[0], prob.shape[1]
    sums_ref[pl.ds(0, at), :] = dot(att_ref[...], low).astype(bf16)
    sums_ref[pl.ds(at, experts), :] = dot3(grad_logits, hidden * scale * gain, TN).astype(bf16)
    tail = sums_ref.shape[0] - at - experts
    sums_ref[pl.ds(at + experts, tail), :] = rows3([jnp.sum(grad_normed * hidden * scale, 0, keepdims=True)], tail)


def output_kernel(hidden_ref, prob_ref, choice_ref, result_ref, out_ref):
    prob = prob_ref[...]
    gate = jnp.sum(prob * chosen_of(flat(choice_ref), prob.shape[1]), -1, keepdims=True)
    share = hidden_ref.shape[0] // result_ref.shape[0]
    result = jnp.concatenate([result_ref[part][:share] for part in range(result_ref.shape[0])], 0)
    out_ref[...] = (hidden_ref[...] + gate * result.astype(f32)).astype(bf16)


def make(mesh):
    tensor_size = mesh.shape["tensor"]
    expert_size = mesh.shape["expert"]

    def shards(
        tokens,
        segment_ids,
        expert_choice,
        slot_index,
        first_gain,
        input_weight,
        bias_table,
        output_weight,
        second_gain,
        router_weight,
        expert_in,
        expert_out,
        cotangent,
    ):
        token_count, width = tokens.shape
        sequences, length = segment_ids.shape
        quarter = output_weight.shape[0]
        experts = router_weight.shape[1]
        local = expert_in.shape[0]
        hidden_units = expert_in.shape[2]
        slots = experts * CAP
        per = slots // local
        chunk = slots // expert_size
        buckets, heads = bias_table.shape
        expert_index = lax.axis_index("expert")
        seg = (segment_ids + 8 * jnp.arange(sequences, dtype=i32)[:, None]).reshape(1, token_count)
        choice, slot = expert_choice, slot_index
        gain_first, gain_second = first_gain, second_gain
        iw_own = jnp.swapaxes(input_weight, 1, 2)
        table = bias_table.T
        rw = router_weight.T
        after = lax.optimization_barrier

        shifts = [[(i, (i + s) % tensor_size) for i in range(tensor_size)] for s in range(1, tensor_size)]

        def from_others(array):
            return [lax.ppermute(array, "tensor", pairs) for pairs in shifts]

        def gather_tensor(array):
            return [array] + from_others(array)

        def joined(planes):
            got = lax.all_gather(planes, "expert", axis=0)
            return jnp.swapaxes(got, 0, 1).reshape(tensor_size - 1, -1, got.shape[-1])

        def exchange(array):
            rows = array.shape[0] // expert_size
            got = lax.all_to_all(array.reshape(expert_size, rows, array.shape[1]), "expert", 0, 0)
            return got.reshape(array.shape)

        ow_rows = quarter // expert_size
        ow_part = lax.dynamic_slice_in_dim(output_weight, expert_index * ow_rows, ow_rows, 0)
        ow_all = joined(jnp.stack(from_others(ow_part)))

        attended, first_normed = call(
            forward_kernel,
            [((quarter, token_count), bf16), ((token_count, width), bf16)],
            (tokens, gain_first, iw_own, table, seg),
            [
                pltpu.VMEM((token_count + 2 * BLOCK, quarter), bf16),
                pltpu.VMEM((quarter, token_count + 2 * BLOCK), bf16),
            ],
        )
        attended_parts = gather_tensor(attended)
        cot_early, _ = after((cotangent, attended))
        (cot_slots,) = call(cotangent_kernel, [((slots, width), bf16)], (cot_early, choice, slot))
        cot_recv = exchange(cot_slots)
        attended_parts, cot_recv = after((attended_parts, cot_recv))

        hidden, prob, send = call(
            middle_kernel,
            [((token_count, width), f32), ((token_count, experts), f32), ((slots, width + 128), bf16)],
            (tokens, output_weight, ow_all, gain_second, rw, choice, slot, *attended_parts),
        )
        recv = exchange(send)

        iw_rows = 3 * quarter // expert_size
        iw_part = lax.dynamic_slice_in_dim(iw_own.reshape(3 * quarter, width), expert_index * iw_rows, iw_rows, 0)
        bias_parts = jnp.stack(split3(table)).astype(bf16).reshape(-1)
        bias_parts = jnp.pad(bias_parts, (0, 8 * width - bias_parts.shape[0])).reshape(8, width)
        iw_part, _ = after((jnp.concatenate([iw_part, bias_parts], 0), send))
        iw_planes = from_others(iw_part)

        iw_planes, recv = after((iw_planes, recv))
        iw_planes = jnp.stack(iw_planes)
        iw_all = joined(iw_planes[:, :iw_rows])
        bias_all = jnp.sum(
            iw_planes[:, iw_rows:]
            .reshape(tensor_size - 1, -1)[:, : 3 * buckets * heads]
            .reshape(tensor_size - 1, 3, heads, buckets)
            .astype(f32),
            1,
        )

        unroll = 2 if local % 2 == 0 else 1
        whole = lambda shape: pl.BlockSpec(shape, lambda j: (0,) * len(shape))
        by_expert = pl.BlockSpec((unroll * per, width), lambda j: (j, 0))
        by_hidden = pl.BlockSpec((unroll * per, hidden_units), lambda j: (j, 0))
        outs = pl.pallas_call(
            lambda *refs: expert_kernel(tensor_size, expert_size, unroll, *refs),
            grid=(local // unroll,),
            in_specs=[
                whole((slots, width + 128)),
                whole((slots, width)),
                pl.BlockSpec((unroll, width, hidden_units), lambda j: (j, 0, 0)),
                pl.BlockSpec((unroll, hidden_units, width), lambda j: (j, 0, 0)),
            ],
            out_specs=[by_expert, by_expert, by_hidden, by_hidden, whole((EXTRA, slots)), whole((slots, width))]
            + [whole((quarter, slots))] * tensor_size,
            out_shape=[jax.ShapeDtypeStruct((slots, width), bf16)] * 2
            + [jax.ShapeDtypeStruct((slots, hidden_units), bf16)] * 2
            + [jax.ShapeDtypeStruct((EXTRA, slots), bf16), jax.ShapeDtypeStruct((slots, width), bf16)]
            + [jax.ShapeDtypeStruct((quarter, slots), bf16)] * tensor_size,
            scratch_shapes=[pltpu.VMEM((slots, width), bf16)] * 5
            + [pltpu.VMEM((slots, 128), bf16), pltpu.VMEM((width, slots), bf16)],
            compiler_params=pltpu.CompilerParams(vmem_limit_bytes=56 * 2**20),
        )(recv, cot_recv, expert_in, expert_out)
        expert_rows, grad_slots, expert_act, grad_act, dots, result_rows = outs[:6]
        grad_chunks = outs[6:]

        def trade_chunks(chunks):
            return [chunks[0]] + [lax.ppermute(c, "tensor", pairs) for c, pairs in zip(chunks[1:], shifts)]

        def sum_rows(parts):
            columns = -(-(quarter + EXTRA) // 128) * 128
            return call(sum_kernel, [((slots, columns), bf16)], parts)[0]

        def own_tokens(rows, kept):
            return call(back_kernel, [((kept, token_count), bf16)], (rows, choice, slot))[0]

        by = lambda array: array.reshape(local, per, array.shape[1])
        grad_expert_out = jnp.einsum("erf,erd->efd", by(expert_act), by(grad_slots), preferred_element_type=f32)
        grad_expert_in = jnp.einsum("erd,erf->edf", by(expert_rows), by(grad_act), preferred_element_type=f32)

        (result_part,) = call(
            result_back_kernel, [((token_count, width), bf16)], (exchange(result_rows), choice, slot)
        )
        traded, grad_expert_out, result_part = after((trade_chunks(grad_chunks), grad_expert_out, result_part))
        summed = sum_rows(traded + [dots])
        returned = own_tokens(exchange(summed), quarter + EXTRA)
        returned, grad_expert_in = after((returned, grad_expert_in))
        result_share = lax.psum_scatter(result_part, "tensor", scatter_dimension=0, tiled=True)
        grad_parts = gather_tensor(returned)
        grad_parts, iw_all, bias_all = after((grad_parts, iw_all, bias_all))

        early_rows = quarter + experts + 64
        grad_hidden, grad_low, early_sums = call(
            hidden_backward_kernel,
            [((token_count, width), f32), ((token_count, width), bf16), ((early_rows, width), bf16)],
            (hidden, prob, cotangent, gain_second, rw, choice, attended, *grad_parts),
            [pltpu.VMEM((width, token_count), f32)],
        )
        result_share, _ = after((result_share, grad_low))
        result = lax.all_gather(jnp.pad(result_share, ((0, 48), (0, 0))), "tensor", axis=0)

        def sum_chunks(array):
            return jnp.sum(array.reshape(expert_size, -1, array.shape[1]).astype(f32), 0)

        padded = token_count + 2 * BLOCK
        scratch = [pltpu.VMEM((padded, quarter), bf16)] * 2 + [pltpu.VMEM((quarter, padded), bf16)]
        scratch = scratch + [pltpu.VMEM((padded, quarter), f32)] * 2 + [pltpu.VMEM((quarter, token_count), f32)]
        grad_iw, own_parts, table_grad = call(
            own_backward_kernel,
            [((3 * quarter, width), bf16), ((3, token_count, quarter), bf16), ((1, width), f32)],
            (first_normed, iw_own, output_weight, table, seg, grad_low),
            scratch,
        )
        grad_tokens, tail = call(
            rest_backward_kernel,
            [((token_count, width), f32), ((8, width), bf16)],
            (
                first_normed, iw_own, iw_all, ow_all, bias_all, seg, grad_low, own_parts, tokens, gain_first,
                grad_hidden, table_grad,
            ),
            [pltpu.VMEM((token_count, width), f32)] + scratch,
        )
        (block_output,) = call(
            output_kernel,
            [((token_count, width), bf16)],
            (hidden, prob, choice, result),
        )
        early_got, grad_iw = after((exchange(early_sums), grad_iw))
        early_sum = sum_chunks(early_got)
        early = lax.all_gather(jnp.pad(early_sum, ((0, 8), (0, 0))), "expert", axis=0)
        late = lax.all_gather(jnp.concatenate([sum_chunks(exchange(grad_iw)).astype(bf16), tail], 0), "expert", axis=0)
        grad_iw, grad_ow, grad_rw, grad_second, grad_first, grad_table = call(
            finish_kernel,
            [
                ((3 * quarter, width), f32),
                ((quarter, width), f32),
                ((experts, width), f32),
                ((width,), f32),
                ((width,), f32),
                ((1, width), f32),
            ],
            (late, early),
        )
        return (
            block_output,
            grad_tokens,
            grad_first,
            jnp.swapaxes(grad_iw.reshape(3, quarter, width), 1, 2),
            grad_table.reshape(width // 128, 128)[:heads, :buckets].T,
            grad_ow,
            grad_second,
            grad_rw.T,
            grad_expert_in,
            grad_expert_out,
        )

    return shards


def solution(mesh):
    placed = (
        P("expert", None),
        P("expert", None),
        P("expert"),
        P("expert"),
        P(),
        P(None, None, "tensor"),
        P(None, "tensor"),
        P("tensor", None),
        P(),
        P(),
        P("expert", None, "tensor"),
        P("expert", "tensor", None),
        P("expert", None),
    )
    return jax.shard_map(
        make(mesh),
        mesh=mesh,
        in_specs=placed,
        out_specs=(
            P("expert", None),
            P("expert", None),
            P(),
            P(None, None, "tensor"),
            P(None, "tensor"),
            P("tensor", None),
            P(),
            P(),
            P("expert", None, "tensor"),
            P("expert", "tensor", None),
        ),
        check_vma=False,
    )
```

```python
import math

import jax
import jax.numpy as jnp
from jax import lax
from jax.experimental import pallas as pl
from jax.experimental.pallas import tpu as pltpu
from jax.sharding import PartitionSpec as P

CAP = 10

bucket_edges = (12, 16, 23, 32, 46, 64, 91)
norm_eps = 1e-06
masked_score = -1e30
gelu_const = math.sqrt(2.0 / math.pi)
gelu_cubic = 0.044715

BLOCK = 128
BAND = 3 * BLOCK
ROLL = 4 * BLOCK
HEAD = 64
EXTRA = 16

bf16 = jnp.bfloat16
f32 = jnp.float32
i32 = jnp.int32
highest = lax.Precision.HIGHEST

NN = (((1,), (0,)), ((), ()))
NT = (((1,), (1,)), ((), ()))
TN = (((0,), (0,)), ((), ()))


def dot(left, right, dims=NN, precision=None):
    return lax.dot_general(left, right, dims, precision=precision, preferred_element_type=f32)


def dot3(left, right, dims=NN):
    left_high, right_high = left.astype(bf16), right.astype(bf16)
    left_low = (left - left_high.astype(f32)).astype(bf16)
    right_low = (right - right_high.astype(f32)).astype(bf16)
    return dot(left_high, right_high, dims) + (dot(left_high, right_low, dims) + dot(left_low, right_high, dims))


def flat(ref):
    return ref[...].reshape(1, -1)


def iota(shape, axis):
    return lax.broadcasted_iota(i32, shape, axis)


def call(kernel, outs, args, scratch=(), room=16):
    vmem = pl.BlockSpec(memory_space=pltpu.VMEM)
    return pl.pallas_call(
        kernel,
        out_shape=[jax.ShapeDtypeStruct(shape, dtype) for shape, dtype in outs],
        in_specs=[vmem] * len(args),
        out_specs=[vmem] * len(outs),
        scratch_shapes=list(scratch),
        compiler_params=pltpu.CompilerParams(vmem_limit_bytes=room * 2**20),
    )(*args)


def split3(value):
    high = value.astype(bf16).astype(f32)
    rest = value - high
    middle = rest.astype(bf16).astype(f32)
    return high, middle, rest - middle


def columns3(value, width):
    high, middle, low = split3(value)
    lane = iota((value.shape[0], width), 1)
    picked = jnp.where(lane == 0, high, jnp.where(lane == 1, middle, jnp.where(lane == 2, low, 0.0)))
    return picked.astype(bf16)


def column_of(row):
    return jnp.transpose(jnp.broadcast_to(row.astype(f32), (128, row.shape[1])))


def wide(column, width):
    return jnp.concatenate([column] * (width // 128), 1)


def bucket_of(relative):
    distance = jnp.abs(relative)
    beyond = jnp.zeros_like(distance)
    for threshold in bucket_edges:
        beyond = beyond + (distance >= threshold).astype(i32)
    magnitude = jnp.where(distance < 8, distance, 8 + beyond)
    return magnitude + 16 * (relative > 0).astype(i32)


def band_rows(table):
    buckets = table.shape[1]
    offset = iota((buckets, ROLL), 1)
    relative = jnp.where(offset < BAND, offset, offset - ROLL) - BLOCK
    onehot = (bucket_of(relative) == iota((buckets, ROLL), 0)).astype(f32)
    return dot(table, onehot, precision=highest), onehot


def bias_tiles(table):
    rows, onehot = band_rows(table)
    tiles = []
    for h in range(table.shape[0]):
        full = jnp.broadcast_to(rows[h : h + 1], (BLOCK, ROLL))
        tiles.append(jnp.transpose(pltpu.roll(full, 0, 1, stride=1, stride_axis=0)[:, :BAND]))
    return tiles, onehot


def head_masks(heads):
    lane = iota((1, heads * HEAD), 1)
    return [((lane >= h * HEAD) & (lane < (h + 1) * HEAD)).astype(f32).astype(bf16) for h in range(heads)]


def padded_segments(seg):
    edge = jnp.full((1, BLOCK), -1.0, f32)
    return column_of(jnp.concatenate([edge, seg, edge], 1))


def first_norm(tok, gain):
    scale = lax.rsqrt(jnp.mean(tok * tok, -1, keepdims=True) + norm_eps)
    return (tok * scale * gain).astype(bf16), scale


def probabilities(scores, bias, same):
    scores = jnp.where(same, scores + bias, masked_score)
    weights = jnp.exp(scores - jnp.max(scores, 0, keepdims=True))
    return weights * (1.0 / jnp.sum(weights, 0, keepdims=True))


def stack_heads(rows, masks):
    return jnp.concatenate([rows * mask for mask in masks], 0)


def own_blocks(product, heads):
    return jnp.concatenate(
        [product[h * HEAD : (h + 1) * HEAD, h * BLOCK : (h + 1) * BLOCK] for h in range(heads)], 0
    )


def fill_rows(ref, value):
    rows = value.shape[0]
    edge = jnp.zeros((BLOCK, value.shape[1]), bf16)
    ref[pl.ds(0, BLOCK), :] = edge
    ref[pl.ds(rows + BLOCK, BLOCK), :] = edge
    ref[pl.ds(BLOCK, rows), :] = value


def fill_columns(ref, value):
    rows = value.shape[1]
    edge = jnp.zeros((value.shape[0], BLOCK), bf16)
    ref[:, pl.ds(0, BLOCK)] = edge
    ref[:, pl.ds(rows + BLOCK, BLOCK)] = edge
    ref[:, pl.ds(BLOCK, rows)] = value


def forward_kernel(tok_ref, gain_ref, iw_ref, bt_ref, seg_ref, att_ref, normed_ref, keys, values):
    rows = tok_ref.shape[0]
    normed, _ = first_norm(tok_ref[...].astype(f32), flat(gain_ref))
    normed_ref[...] = normed
    queries = dot(normed, iw_ref[0], NT).astype(bf16)
    fill_rows(keys, dot(normed, iw_ref[1], NT).astype(bf16))
    fill_columns(values, dot(iw_ref[2], normed, NT).astype(bf16))
    seg = seg_ref[...].astype(f32)
    seg_keys = padded_segments(seg)
    tiles, _ = bias_tiles(bt_ref[...])
    heads = len(tiles)
    masks = head_masks(heads)
    for block in range(rows // BLOCK):
        at = block * BLOCK
        same = seg_keys[at : at + BAND] == seg[:, at : at + BLOCK]
        scores = dot(keys[pl.ds(at, BAND), :], stack_heads(queries[at : at + BLOCK], masks), NT)
        weights = [
            probabilities(scores[:, h * BLOCK : (h + 1) * BLOCK], tiles[h], same).astype(bf16) for h in range(heads)
        ]
        product = dot(values[:, pl.ds(at, BAND)], jnp.concatenate(weights, 1))
        att_ref[:, pl.ds(at, BLOCK)] = own_blocks(product, heads).astype(bf16)


def group_backward(normed, weight, out_weight, table, seg, grad_low, scratch, bias_grads):
    keys, values, keys_across, grad_keys, grad_values, grad_queries = scratch
    rows = normed.shape[0]
    queries = dot(normed, weight[0], NT).astype(bf16)
    fill_rows(keys, dot(normed, weight[1], NT).astype(bf16))
    fill_columns(keys_across, dot(weight[1], normed, NT).astype(bf16))
    fill_rows(values, dot(normed, weight[2], NT).astype(bf16))
    grad_att = dot(grad_low, out_weight, NT).astype(bf16)
    grad_keys[...] = jnp.zeros(grad_keys.shape, f32)
    grad_values[...] = jnp.zeros(grad_values.shape, f32)
    seg_keys = padded_segments(seg)
    tiles, onehot = bias_tiles(table)
    heads = len(tiles)
    masks = head_masks(heads)
    sums = [None] * heads
    for block in range(rows // BLOCK):
        at = block * BLOCK
        same = seg_keys[at : at + BAND] == seg[:, at : at + BLOCK]
        head_queries = stack_heads(queries[at : at + BLOCK], masks)
        head_grads = stack_heads(grad_att[at : at + BLOCK], masks)
        scores = dot(keys[pl.ds(at, BAND), :], head_queries, NT)
        grad_probs = dot(values[pl.ds(at, BAND), :], head_grads, NT)
        all_weights, all_grads = [], []
        for h in range(heads):
            columns = slice(h * BLOCK, (h + 1) * BLOCK)
            weights = probabilities(scores[:, columns], tiles[h], same)
            scaled = weights * grad_probs[:, columns]
            grad_scores = scaled - weights * jnp.sum(scaled, 0, keepdims=True)
            all_weights.append(weights.astype(bf16))
            all_grads.append(grad_scores.astype(bf16))
            if bias_grads:
                sums[h] = grad_scores if sums[h] is None else sums[h] + grad_scores
        low = jnp.concatenate(all_grads, 1)
        grad_queries[:, pl.ds(at, BLOCK)] = own_blocks(dot(keys_across[:, pl.ds(at, BAND)], low), heads)
        grad_keys[pl.ds(at, BAND), :] += dot(low, head_queries)
        grad_values[pl.ds(at, BAND), :] += dot(jnp.concatenate(all_weights, 1), head_grads)
    parts = (
        jnp.transpose(grad_queries[...]).astype(bf16),
        grad_keys[pl.ds(BLOCK, rows), :].astype(bf16),
        grad_values[pl.ds(BLOCK, rows), :].astype(bf16),
    )
    if not bias_grads:
        return parts, None
    diagonals = []
    row_index = iota((BLOCK, ROLL), 0)
    for h in range(heads):
        moved = jnp.concatenate([jnp.transpose(sums[h]), jnp.zeros((BLOCK, ROLL - BAND), f32)], 1)
        step = 1
        while step < BLOCK:
            moved = jnp.where((row_index & step) != 0, pltpu.roll(moved, ROLL - step, 1), moved)
            step *= 2
        diagonals.append(jnp.sum(moved, 0, keepdims=True))
    onehot = jnp.concatenate([onehot, jnp.zeros((128 - onehot.shape[0], ROLL), f32)], 0)
    by_head = dot(jnp.concatenate(diagonals, 0), onehot, NT, precision=highest)
    return parts, jnp.concatenate([by_head[h : h + 1] for h in range(heads)], 1)


def own_backward_kernel(normed_ref, iw_ref, ow_ref, bt_ref, seg_ref, low_ref, grad_iw_ref, parts_ref, table_ref, *scratch):
    normed = normed_ref[...]
    parts, table_grad = group_backward(
        normed, iw_ref, ow_ref[...], bt_ref[...], seg_ref[...].astype(f32), low_ref[...], scratch, True
    )
    table_ref[...] = jnp.concatenate(
        [table_grad, jnp.zeros((1, table_ref.shape[1] - table_grad.shape[1]), f32)], 1
    )
    width = ow_ref.shape[0]
    for j in range(3):
        parts_ref[j] = parts[j]
        grad_iw_ref[pl.ds(j * width, width), :] = dot(parts[j], normed, TN).astype(bf16)


def rest_backward_kernel(
    normed_ref, own_iw_ref, iw_ref, ow_ref, bt_ref, seg_ref, low_ref, parts_ref, tok_ref, gain_ref, grad_hidden_ref,
    table_ref, grad_tok_ref, tail_ref, total, *scratch,
):
    width = ow_ref.shape[1]
    total[...] = sum(dot(parts_ref[j], own_iw_ref[j]) for j in range(3))

    def step(group, carry):
        weight = [iw_ref[group, pl.ds(j * width, width), :] for j in range(3)]
        parts, _ = group_backward(
            normed_ref[...], weight, ow_ref[group], bt_ref[group], seg_ref[...].astype(f32), low_ref[...], scratch, False
        )
        total[...] += sum(dot(parts[j], weight[j]) for j in range(3))
        return carry

    lax.fori_loop(0, ow_ref.shape[0], step, 0)
    tok = tok_ref[...].astype(f32)
    gain = flat(gain_ref)
    scale = lax.rsqrt(jnp.mean(tok * tok, -1, keepdims=True) + norm_eps)
    grad_normed = total[...]
    tail_ref[...] = rows3([jnp.sum(grad_normed * tok * scale, 0, keepdims=True), table_ref[...]], tail_ref.shape[0])
    scaled = grad_normed * gain
    grad_tok_ref[...] = (
        grad_hidden_ref[...]
        + scale * scaled
        - tok * (scale * scale * scale) * jnp.mean(scaled * tok, -1, keepdims=True)
    )


def rows3(values, count):
    parts = [part for value in values for part in split3(value)]
    row = iota((count, values[0].shape[1]), 0)
    total = jnp.zeros(row.shape, f32)
    for index, part in enumerate(parts):
        total = jnp.where(row == index, part, total)
    return total.astype(bf16)


def finish_kernel(late_ref, early_ref, *refs):
    grad_iw_ref, grad_ow_ref, grad_rw_ref, second_ref, first_ref, table_ref = refs
    devices = late_ref.shape[0]
    late_rows = grad_iw_ref.shape[0] // devices
    tail = jnp.zeros((late_ref.shape[1] - late_rows, late_ref.shape[2]), f32)
    for device in range(devices):
        block = late_ref[device].astype(f32)
        grad_iw_ref[pl.ds(device * late_rows, late_rows), :] = block[:late_rows]
        tail = tail + block[late_rows:]
    first_ref[...] = jnp.sum(tail[:3], 0)
    table_ref[...] = jnp.sum(tail[3:6], 0, keepdims=True)
    at, experts = grad_ow_ref.shape[0], grad_rw_ref.shape[0]
    early_rows = early_ref.shape[1] - 8
    early = jnp.concatenate([early_ref[device][:early_rows] for device in range(devices)], 0)
    grad_ow_ref[...] = early[:at]
    grad_rw_ref[...] = early[at : at + experts]
    second_ref[...] = jnp.sum(early[at + experts : at + experts + 8], 0)


def slot_onehot(choice, slot, slots):
    dest = jnp.where(slot >= 0, choice * CAP + slot, slots)
    return (iota((slots, dest.shape[1]), 0) == dest).astype(f32).astype(bf16)


def slot_order(slots, group, across):
    index = iota((1, slots), 1)
    big, small = slots // across, slots // group
    outer, rest = lax.div(index, big), lax.rem(index, big)
    target = lax.div(rest, CAP) * small + outer * CAP + lax.rem(rest, CAP)
    return (iota((slots, slots), 0) == target).astype(f32).astype(bf16)


def cotangent_kernel(cot_ref, choice_ref, slot_ref, out_ref):
    fill = slot_onehot(flat(choice_ref), flat(slot_ref), out_ref.shape[0])
    out_ref[...] = dot(fill, cot_ref[...]).astype(bf16)


def chosen_of(choice, experts):
    column = column_of(choice)[:, :experts]
    return (column == iota(column.shape, 1).astype(f32)).astype(f32)


def middle_kernel(tok_ref, own_ow_ref, ow_ref, gain_ref, rw_ref, choice_ref, slot_ref, *refs):
    att_refs, (hidden_ref, prob_ref, send_ref) = refs[:-3], refs[-3:]
    hidden = tok_ref[...].astype(f32)
    for shift, att_ref in enumerate(att_refs):
        hidden = hidden + dot(att_ref[...], ow_ref[shift - 1] if shift else own_ow_ref[...], TN)
    hidden_ref[...] = hidden
    scale = lax.rsqrt(jnp.mean(hidden * hidden, -1, keepdims=True) + norm_eps)
    normed = hidden * scale * flat(gain_ref)
    logits = dot3(normed, rw_ref[...], NT)
    raised = jnp.exp(logits - jnp.max(logits, -1, keepdims=True))
    prob = raised * (1.0 / jnp.sum(raised, -1, keepdims=True))
    prob_ref[...] = prob
    gate = jnp.sum(prob * chosen_of(flat(choice_ref), prob.shape[1]), -1, keepdims=True)
    width = normed.shape[1]
    fill = slot_onehot(flat(choice_ref), flat(slot_ref), send_ref.shape[0])
    send_ref[:, :width] = dot(fill, normed.astype(bf16)).astype(bf16)
    send_ref[:, width:] = dot(fill, columns3(gate, 128)).astype(bf16)


def expert_kernel(
    tensor_size, sources, unroll,
    recv_ref, cot_ref, win_ref, wout_ref,
    rows_ref, grads_ref, act_ref, grad_act_ref, dots_ref, result_ref, *refs,
):
    chunks = refs[:tensor_size]
    x_all, c_all, g_all, r_all, y_all, d_all, turned = refs[tensor_size:]
    slots = recv_ref.shape[0]
    width = cot_ref.shape[1]
    step = pl.program_id(0)
    local = pl.num_programs(0) * unroll
    per = rows_ref.shape[0] // unroll

    @pl.when(step == 0)
    def _():
        order = slot_order(slots, win_ref.shape[0] * (slots // rows_ref.shape[0]), sources)
        x_all[...] = dot(order, recv_ref[:, :width]).astype(bf16)
        gate = jnp.sum(dot(order, recv_ref[:, width:]), -1, keepdims=True)
        cot = dot(order, cot_ref[...])
        c_all[...] = cot.astype(bf16)
        g_all[...] = (gate * cot).astype(bf16)

    for u in range(unroll):
        here = pl.ds(u * per, per)
        at = pl.ds(pl.multiple_of((step * unroll + u) * per, 16), per)
        x = x_all[at, :]
        g = g_all[at, :]
        weight_in = win_ref[u]
        weight_out = wout_ref[u]
        pre = dot(x, weight_in)
        grad_act = dot(g, weight_out, NT)
        inner = jnp.tanh(gelu_const * (pre + gelu_cubic * pre * pre * pre))
        act = (0.5 * pre * (1.0 + inner)).astype(bf16)
        slope = 0.5 * (1.0 + inner) + 0.5 * pre * (1.0 - inner * inner) * gelu_const * (
            1.0 + 3.0 * gelu_cubic * pre * pre
        )
        grad_act = (grad_act * slope).astype(bf16)
        r_all[at, :] = dot(grad_act, weight_in, NT).astype(bf16)
        result = dot(act, weight_out)
        y_all[at, :] = result.astype(bf16)
        d_all[at, :] = columns3(jnp.sum(result * c_all[at, :].astype(f32), -1, keepdims=True), 128)
        rows_ref[here, :] = x
        grads_ref[here, :] = g
        act_ref[here, :] = act
        grad_act_ref[here, :] = grad_act

    @pl.when(step == pl.num_programs(0) - 1)
    def _():
        order = slot_order(slots, win_ref.shape[0] * (slots // rows_ref.shape[0]), sources)
        dots_ref[...] = dot(d_all[...], order, TN)[:EXTRA].astype(bf16)
        turn_chunks(tensor_size, dot(r_all[...], order, TN).astype(bf16), turned, chunks)
        result_ref[...] = dot(slot_order(slots, sources, win_ref.shape[0] * (slots // rows_ref.shape[0])), y_all[...]).astype(bf16)


def turn_chunks(tensor_size, rows, turned, chunks):
    turned[...] = rows
    quarter = rows.shape[0] // tensor_size
    me = lax.axis_index("tensor")
    for shift in range(tensor_size):
        first = lax.rem(me + shift, tensor_size) * quarter
        chunks[shift][...] = turned[pl.ds(pl.multiple_of(first, 64), quarter), :]


def result_back_kernel(recv_ref, choice_ref, slot_ref, out_ref):
    fill = slot_onehot(flat(choice_ref), flat(slot_ref), recv_ref.shape[0])
    out_ref[...] = dot(fill, recv_ref[...], TN).astype(bf16)


def sum_kernel(*refs):
    *parts, dots_ref, out_ref = refs
    total = sum(ref[...].astype(f32) for ref in parts)
    blank = jnp.zeros((out_ref.shape[1] - total.shape[0] - EXTRA, total.shape[1]), f32)
    out_ref[...] = jnp.transpose(jnp.concatenate([total, dots_ref[...].astype(f32), blank], 0)).astype(bf16)


def back_kernel(recv_ref, choice_ref, slot_ref, out_ref):
    fill = slot_onehot(flat(choice_ref), flat(slot_ref), recv_ref.shape[0])
    out_ref[...] = dot(recv_ref[...], fill, TN)[: out_ref.shape[0]].astype(bf16)


def spread(refs, quarter, turned):
    size = len(refs)
    me = lax.axis_index("tensor")
    for shift, ref in enumerate(refs):
        first = lax.rem(me + size - shift, size) * quarter
        turned[pl.ds(pl.multiple_of(first, 64), quarter), :] = ref[pl.ds(0, quarter), :].astype(f32)
    return jnp.transpose(turned[...])


def hidden_backward_kernel(
    hidden_ref, prob_ref, cot_ref, gain_ref, rw_ref, choice_ref, att_ref, *refs,
):
    parts = refs[:-4]
    grad_hidden_ref, low_ref, sums_ref, turned = refs[-4:]
    hidden = hidden_ref[...]
    rows, width = hidden.shape
    quarter = width // len(parts)
    grad_routed = spread(parts, quarter, turned)
    dots = sum(jnp.sum(ref[pl.ds(quarter, EXTRA), :].astype(f32), 0, keepdims=True) for ref in parts)
    prob = prob_ref[...]
    chosen = chosen_of(flat(choice_ref), prob.shape[1])
    gate = jnp.sum(prob * chosen, -1, keepdims=True)
    grad_gate = column_of(dots)[:, :1]
    grad_logits = (grad_gate * gate) * (chosen - prob)
    grad_normed = grad_routed + dot3(grad_logits, rw_ref[...])
    gain = flat(gain_ref)
    scale = lax.rsqrt(jnp.mean(hidden * hidden, -1, keepdims=True) + norm_eps)
    scaled = grad_normed * gain
    grad_hidden = (
        cot_ref[...].astype(f32)
        + scale * scaled
        - hidden * (scale * scale * scale) * jnp.mean(scaled * hidden, -1, keepdims=True)
    )
    grad_hidden_ref[...] = grad_hidden
    low = grad_hidden.astype(bf16)
    low_ref[...] = low
    at, experts = att_ref.shape[0], prob.shape[1]
    sums_ref[pl.ds(0, at), :] = dot(att_ref[...], low).astype(bf16)
    sums_ref[pl.ds(at, experts), :] = dot3(grad_logits, hidden * scale * gain, TN).astype(bf16)
    tail = sums_ref.shape[0] - at - experts
    sums_ref[pl.ds(at + experts, tail), :] = rows3([jnp.sum(grad_normed * hidden * scale, 0, keepdims=True)], tail)


def output_kernel(hidden_ref, prob_ref, choice_ref, result_ref, out_ref):
    prob = prob_ref[...]
    gate = jnp.sum(prob * chosen_of(flat(choice_ref), prob.shape[1]), -1, keepdims=True)
    share = hidden_ref.shape[0] // result_ref.shape[0]
    result = jnp.concatenate([result_ref[part][:share] for part in range(result_ref.shape[0])], 0)
    out_ref[...] = (hidden_ref[...] + gate * result.astype(f32)).astype(bf16)


def make(mesh):
    tensor_size = mesh.shape["tensor"]
    expert_size = mesh.shape["expert"]

    def shards(
        tokens,
        segment_ids,
        expert_choice,
        slot_index,
        first_gain,
        input_weight,
        bias_table,
        output_weight,
        second_gain,
        router_weight,
        expert_in,
        expert_out,
        cotangent,
    ):
        token_count, width = tokens.shape
        sequences, length = segment_ids.shape
        quarter = output_weight.shape[0]
        experts = router_weight.shape[1]
        local = expert_in.shape[0]
        hidden_units = expert_in.shape[2]
        slots = experts * CAP
        per = slots // local
        chunk = slots // expert_size
        buckets, heads = bias_table.shape
        expert_index = lax.axis_index("expert")
        seg = (segment_ids + 8 * jnp.arange(sequences, dtype=i32)[:, None]).reshape(1, token_count)
        choice, slot = expert_choice, slot_index
        gain_first, gain_second = first_gain, second_gain
        iw_own = jnp.swapaxes(input_weight, 1, 2)
        table = bias_table.T
        rw = router_weight.T
        after = lax.optimization_barrier

        shifts = [[(i, (i + s) % tensor_size) for i in range(tensor_size)] for s in range(1, tensor_size)]

        def from_others(array):
            return [lax.ppermute(array, "tensor", pairs) for pairs in shifts]

        def gather_tensor(array):
            return [array] + from_others(array)

        def joined(planes):
            got = lax.all_gather(planes, "expert", axis=0)
            return jnp.swapaxes(got, 0, 1).reshape(tensor_size - 1, -1, got.shape[-1])

        def exchange(array):
            rows = array.shape[0] // expert_size
            got = lax.all_to_all(array.reshape(expert_size, rows, array.shape[1]), "expert", 0, 0)
            return got.reshape(array.shape)

        ow_rows = quarter // expert_size
        ow_part = lax.dynamic_slice_in_dim(output_weight, expert_index * ow_rows, ow_rows, 0)
        ow_all = joined(jnp.stack(from_others(ow_part)))

        attended, first_normed = call(
            forward_kernel,
            [((quarter, token_count), bf16), ((token_count, width), bf16)],
            (tokens, gain_first, iw_own, table, seg),
            [
                pltpu.VMEM((token_count + 2 * BLOCK, quarter), bf16),
                pltpu.VMEM((quarter, token_count + 2 * BLOCK), bf16),
            ],
        )
        attended_parts = gather_tensor(attended)
        cot_early, _ = after((cotangent, attended))
        (cot_slots,) = call(cotangent_kernel, [((slots, width), bf16)], (cot_early, choice, slot))
        cot_recv = exchange(cot_slots)
        attended_parts, cot_recv = after((attended_parts, cot_recv))

        hidden, prob, send = call(
            middle_kernel,
            [((token_count, width), f32), ((token_count, experts), f32), ((slots, width + 128), bf16)],
            (tokens, output_weight, ow_all, gain_second, rw, choice, slot, *attended_parts),
            room=20,
        )
        recv = exchange(send)

        iw_rows = 3 * quarter // expert_size
        iw_part = lax.dynamic_slice_in_dim(iw_own.reshape(3 * quarter, width), expert_index * iw_rows, iw_rows, 0)
        bias_parts = jnp.stack(split3(table)).astype(bf16).reshape(-1)
        bias_parts = jnp.pad(bias_parts, (0, 8 * width - bias_parts.shape[0])).reshape(8, width)
        iw_part, _ = after((jnp.concatenate([iw_part, bias_parts], 0), send))
        iw_planes = from_others(iw_part)

        iw_planes, recv = after((iw_planes, recv))
        iw_planes = jnp.stack(iw_planes)
        iw_all = joined(iw_planes[:, :iw_rows])
        bias_all = jnp.sum(
            iw_planes[:, iw_rows:]
            .reshape(tensor_size - 1, -1)[:, : 3 * buckets * heads]
            .reshape(tensor_size - 1, 3, heads, buckets)
            .astype(f32),
            1,
        )

        unroll = 2 if local % 2 == 0 else 1
        whole = lambda shape: pl.BlockSpec(shape, lambda j: (0,) * len(shape))
        by_expert = pl.BlockSpec((unroll * per, width), lambda j: (j, 0))
        by_hidden = pl.BlockSpec((unroll * per, hidden_units), lambda j: (j, 0))
        outs = pl.pallas_call(
            lambda *refs: expert_kernel(tensor_size, expert_size, unroll, *refs),
            grid=(local // unroll,),
            in_specs=[
                whole((slots, width + 128)),
                whole((slots, width)),
                pl.BlockSpec((unroll, width, hidden_units), lambda j: (j, 0, 0)),
                pl.BlockSpec((unroll, hidden_units, width), lambda j: (j, 0, 0)),
            ],
            out_specs=[by_expert, by_expert, by_hidden, by_hidden, whole((EXTRA, slots)), whole((slots, width))]
            + [whole((quarter, slots))] * tensor_size,
            out_shape=[jax.ShapeDtypeStruct((slots, width), bf16)] * 2
            + [jax.ShapeDtypeStruct((slots, hidden_units), bf16)] * 2
            + [jax.ShapeDtypeStruct((EXTRA, slots), bf16), jax.ShapeDtypeStruct((slots, width), bf16)]
            + [jax.ShapeDtypeStruct((quarter, slots), bf16)] * tensor_size,
            scratch_shapes=[pltpu.VMEM((slots, width), bf16)] * 5
            + [pltpu.VMEM((slots, 128), bf16), pltpu.VMEM((width, slots), bf16)],
            compiler_params=pltpu.CompilerParams(vmem_limit_bytes=36 * 2**20),
        )(recv, cot_recv, expert_in, expert_out)
        expert_rows, grad_slots, expert_act, grad_act, dots, result_rows = outs[:6]
        grad_chunks = outs[6:]

        def trade_chunks(chunks):
            return [chunks[0]] + [lax.ppermute(c, "tensor", pairs) for c, pairs in zip(chunks[1:], shifts)]

        def sum_rows(parts):
            columns = -(-(quarter + EXTRA) // 128) * 128
            return call(sum_kernel, [((slots, columns), bf16)], parts)[0]

        def own_tokens(rows, kept):
            return call(back_kernel, [((kept, token_count), bf16)], (rows, choice, slot))[0]

        by = lambda array: array.reshape(local, per, array.shape[1])
        grad_expert_out = jnp.einsum("erf,erd->efd", by(expert_act), by(grad_slots), preferred_element_type=f32)
        grad_expert_in = jnp.einsum("erd,erf->edf", by(expert_rows), by(grad_act), preferred_element_type=f32)

        (result_part,) = call(
            result_back_kernel, [((token_count, width), bf16)], (exchange(result_rows), choice, slot)
        )
        traded, grad_expert_out, result_part = after((trade_chunks(grad_chunks), grad_expert_out, result_part))
        summed = sum_rows(traded + [dots])
        returned = own_tokens(exchange(summed), quarter + EXTRA)
        returned, grad_expert_in = after((returned, grad_expert_in))
        result_share = lax.psum_scatter(result_part, "tensor", scatter_dimension=0, tiled=True)
        grad_parts = gather_tensor(returned)
        grad_parts, iw_all, bias_all = after((grad_parts, iw_all, bias_all))

        early_rows = quarter + experts + 64
        grad_hidden, grad_low, early_sums = call(
            hidden_backward_kernel,
            [((token_count, width), f32), ((token_count, width), bf16), ((early_rows, width), bf16)],
            (hidden, prob, cotangent, gain_second, rw, choice, attended, *grad_parts),
            [pltpu.VMEM((width, token_count), f32)],
            room=20,
        )
        result_share, _ = after((result_share, grad_low))
        result = lax.all_gather(jnp.pad(result_share, ((0, 48), (0, 0))), "tensor", axis=0)

        def sum_chunks(array):
            return jnp.sum(array.reshape(expert_size, -1, array.shape[1]).astype(f32), 0)

        padded = token_count + 2 * BLOCK
        scratch = [pltpu.VMEM((padded, quarter), bf16)] * 2 + [pltpu.VMEM((quarter, padded), bf16)]
        scratch = scratch + [pltpu.VMEM((padded, quarter), f32)] * 2 + [pltpu.VMEM((quarter, token_count), f32)]
        grad_iw, own_parts, table_grad = call(
            own_backward_kernel,
            [((3 * quarter, width), bf16), ((3, token_count, quarter), bf16), ((1, width), f32)],
            (first_normed, iw_own, output_weight, table, seg, grad_low),
            scratch,
        )
        grad_tokens, tail = call(
            rest_backward_kernel,
            [((token_count, width), f32), ((8, width), bf16)],
            (
                first_normed, iw_own, iw_all, ow_all, bias_all, seg, grad_low, own_parts, tokens, gain_first,
                grad_hidden, table_grad,
            ),
            [pltpu.VMEM((token_count, width), f32)] + scratch,
            room=24,
        )
        (block_output,) = call(
            output_kernel,
            [((token_count, width), bf16)],
            (hidden, prob, choice, result),
        )
        early_got, grad_iw = after((exchange(early_sums), grad_iw))
        early_sum = sum_chunks(early_got)
        early = lax.all_gather(jnp.pad(early_sum, ((0, 8), (0, 0))), "expert", axis=0)
        late = lax.all_gather(jnp.concatenate([sum_chunks(exchange(grad_iw)).astype(bf16), tail], 0), "expert", axis=0)
        grad_iw, grad_ow, grad_rw, grad_second, grad_first, grad_table = call(
            finish_kernel,
            [
                ((3 * quarter, width), f32),
                ((quarter, width), f32),
                ((experts, width), f32),
                ((width,), f32),
                ((width,), f32),
                ((1, width), f32),
            ],
            (late, early),
        )
        return (
            block_output,
            grad_tokens,
            grad_first,
            jnp.swapaxes(grad_iw.reshape(3, quarter, width), 1, 2),
            grad_table.reshape(width // 128, 128)[:heads, :buckets].T,
            grad_ow,
            grad_second,
            grad_rw.T,
            grad_expert_in,
            grad_expert_out,
        )

    return shards


def solution(mesh):
    placed = (
        P("expert", None),
        P("expert", None),
        P("expert"),
        P("expert"),
        P(),
        P(None, None, "tensor"),
        P(None, "tensor"),
        P("tensor", None),
        P(),
        P(),
        P("expert", None, "tensor"),
        P("expert", "tensor", None),
        P("expert", None),
    )
    return jax.shard_map(
        make(mesh),
        mesh=mesh,
        in_specs=placed,
        out_specs=(
            P("expert", None),
            P("expert", None),
            P(),
            P(None, None, "tensor"),
            P(None, "tensor"),
            P("tensor", None),
            P(),
            P(),
            P("expert", None, "tensor"),
            P("expert", "tensor", None),
        ),
        check_vma=False,
    )
```

```python
import math

import jax
import jax.numpy as jnp
from jax import lax
from jax.experimental import pallas as pl
from jax.experimental.pallas import tpu as pltpu
from jax.sharding import PartitionSpec as P

CAP = 10

bucket_edges = (12, 16, 23, 32, 46, 64, 91)
norm_eps = 1e-06
masked_score = -1e30
gelu_const = math.sqrt(2.0 / math.pi)
gelu_cubic = 0.044715

BLOCK = 128
BAND = 3 * BLOCK
ROLL = 4 * BLOCK
HEAD = 64
EXTRA = 16

bf16 = jnp.bfloat16
f32 = jnp.float32
i32 = jnp.int32
highest = lax.Precision.HIGHEST

NN = (((1,), (0,)), ((), ()))
NT = (((1,), (1,)), ((), ()))
TN = (((0,), (0,)), ((), ()))


def dot(left, right, dims=NN, precision=None):
    return lax.dot_general(left, right, dims, precision=precision, preferred_element_type=f32)


def dot3(left, right, dims=NN):
    left_high, right_high = left.astype(bf16), right.astype(bf16)
    left_low = (left - left_high.astype(f32)).astype(bf16)
    right_low = (right - right_high.astype(f32)).astype(bf16)
    return dot(left_high, right_high, dims) + (dot(left_high, right_low, dims) + dot(left_low, right_high, dims))


def flat(ref):
    return ref[...].reshape(1, -1)


def iota(shape, axis):
    return lax.broadcasted_iota(i32, shape, axis)


def call(kernel, outs, args, scratch=(), **extra):
    vmem = pl.BlockSpec(memory_space=pltpu.VMEM)
    return pl.pallas_call(
        kernel,
        out_shape=[jax.ShapeDtypeStruct(shape, dtype) for shape, dtype in outs],
        in_specs=[vmem] * len(args),
        out_specs=[vmem] * len(outs),
        scratch_shapes=list(scratch),
        compiler_params=pltpu.CompilerParams(vmem_limit_bytes=56 * 2**20),
        **extra,
    )(*args)


def split3(value):
    high = value.astype(bf16).astype(f32)
    rest = value - high
    middle = rest.astype(bf16).astype(f32)
    return high, middle, rest - middle


def columns3(value, width):
    high, middle, low = split3(value)
    lane = iota((value.shape[0], width), 1)
    picked = jnp.where(lane == 0, high, jnp.where(lane == 1, middle, jnp.where(lane == 2, low, 0.0)))
    return picked.astype(bf16)


def column_of(row):
    return jnp.transpose(jnp.broadcast_to(row.astype(f32), (128, row.shape[1])))


def wide(column, width):
    return jnp.concatenate([column] * (width // 128), 1)


def bucket_of(relative):
    distance = jnp.abs(relative)
    beyond = jnp.zeros_like(distance)
    for threshold in bucket_edges:
        beyond = beyond + (distance >= threshold).astype(i32)
    magnitude = jnp.where(distance < 8, distance, 8 + beyond)
    return magnitude + 16 * (relative > 0).astype(i32)


def band_rows(table):
    buckets = table.shape[1]
    offset = iota((buckets, ROLL), 1)
    relative = jnp.where(offset < BAND, offset, offset - ROLL) - BLOCK
    onehot = (bucket_of(relative) == iota((buckets, ROLL), 0)).astype(f32)
    return dot(table, onehot, precision=highest), onehot


def bias_tiles(table):
    rows, onehot = band_rows(table)
    tiles = []
    for h in range(table.shape[0]):
        full = jnp.broadcast_to(rows[h : h + 1], (BLOCK, ROLL))
        tiles.append(jnp.transpose(pltpu.roll(full, 0, 1, stride=1, stride_axis=0)[:, :BAND]))
    return tiles, onehot


def head_masks(heads):
    lane = iota((1, heads * HEAD), 1)
    return [((lane >= h * HEAD) & (lane < (h + 1) * HEAD)).astype(f32).astype(bf16) for h in range(heads)]


def padded_segments(seg):
    edge = jnp.full((1, BLOCK), -1.0, f32)
    return column_of(jnp.concatenate([edge, seg, edge], 1))


def first_norm(tok, gain):
    scale = lax.rsqrt(jnp.mean(tok * tok, -1, keepdims=True) + norm_eps)
    return (tok * scale * gain).astype(bf16), scale


def probabilities(scores, bias, same):
    scores = jnp.where(same, scores + bias, masked_score)
    weights = jnp.exp(scores - jnp.max(scores, 0, keepdims=True))
    return weights * (1.0 / jnp.sum(weights, 0, keepdims=True))


def stack_heads(rows, masks):
    return jnp.concatenate([rows * mask for mask in masks], 0)


def own_blocks(product, heads):
    return jnp.concatenate(
        [product[h * HEAD : (h + 1) * HEAD, h * BLOCK : (h + 1) * BLOCK] for h in range(heads)], 0
    )


def fill_rows(ref, value):
    rows = value.shape[0]
    edge = jnp.zeros((BLOCK, value.shape[1]), bf16)
    ref[pl.ds(0, BLOCK), :] = edge
    ref[pl.ds(rows + BLOCK, BLOCK), :] = edge
    ref[pl.ds(BLOCK, rows), :] = value


def fill_columns(ref, value):
    rows = value.shape[1]
    edge = jnp.zeros((value.shape[0], BLOCK), bf16)
    ref[:, pl.ds(0, BLOCK)] = edge
    ref[:, pl.ds(rows + BLOCK, BLOCK)] = edge
    ref[:, pl.ds(BLOCK, rows)] = value


def forward_kernel(tok_ref, gain_ref, iw_ref, bt_ref, seg_ref, att_ref, normed_ref, keys, values):
    rows = tok_ref.shape[0]
    normed, _ = first_norm(tok_ref[...].astype(f32), flat(gain_ref))
    normed_ref[...] = normed
    queries = dot(normed, iw_ref[0], NT).astype(bf16)
    fill_rows(keys, dot(normed, iw_ref[1], NT).astype(bf16))
    fill_columns(values, dot(iw_ref[2], normed, NT).astype(bf16))
    seg = seg_ref[...].astype(f32)
    seg_keys = padded_segments(seg)
    tiles, _ = bias_tiles(bt_ref[...])
    heads = len(tiles)
    masks = head_masks(heads)
    for block in range(rows // BLOCK):
        at = block * BLOCK
        same = seg_keys[at : at + BAND] == seg[:, at : at + BLOCK]
        scores = dot(keys[pl.ds(at, BAND), :], stack_heads(queries[at : at + BLOCK], masks), NT)
        weights = [
            probabilities(scores[:, h * BLOCK : (h + 1) * BLOCK], tiles[h], same).astype(bf16) for h in range(heads)
        ]
        product = dot(values[:, pl.ds(at, BAND)], jnp.concatenate(weights, 1))
        att_ref[:, pl.ds(at, BLOCK)] = own_blocks(product, heads).astype(bf16)


def group_backward(normed, weight, out_weight, table, seg, grad_low, scratch, bias_grads):
    keys, values, keys_across, grad_keys, grad_values, grad_queries = scratch
    rows = normed.shape[0]
    queries = dot(normed, weight[0], NT).astype(bf16)
    fill_rows(keys, dot(normed, weight[1], NT).astype(bf16))
    fill_columns(keys_across, dot(weight[1], normed, NT).astype(bf16))
    fill_rows(values, dot(normed, weight[2], NT).astype(bf16))
    grad_att = dot(grad_low, out_weight, NT).astype(bf16)
    grad_keys[...] = jnp.zeros(grad_keys.shape, f32)
    grad_values[...] = jnp.zeros(grad_values.shape, f32)
    seg_keys = padded_segments(seg)
    tiles, onehot = bias_tiles(table)
    heads = len(tiles)
    masks = head_masks(heads)
    sums = [None] * heads
    for block in range(rows // BLOCK):
        at = block * BLOCK
        same = seg_keys[at : at + BAND] == seg[:, at : at + BLOCK]
        head_queries = stack_heads(queries[at : at + BLOCK], masks)
        head_grads = stack_heads(grad_att[at : at + BLOCK], masks)
        scores = dot(keys[pl.ds(at, BAND), :], head_queries, NT)
        grad_probs = dot(values[pl.ds(at, BAND), :], head_grads, NT)
        all_weights, all_grads = [], []
        for h in range(heads):
            columns = slice(h * BLOCK, (h + 1) * BLOCK)
            weights = probabilities(scores[:, columns], tiles[h], same)
            scaled = weights * grad_probs[:, columns]
            grad_scores = scaled - weights * jnp.sum(scaled, 0, keepdims=True)
            all_weights.append(weights.astype(bf16))
            all_grads.append(grad_scores.astype(bf16))
            if bias_grads:
                sums[h] = grad_scores if sums[h] is None else sums[h] + grad_scores
        low = jnp.concatenate(all_grads, 1)
        grad_queries[:, pl.ds(at, BLOCK)] = own_blocks(dot(keys_across[:, pl.ds(at, BAND)], low), heads)
        grad_keys[pl.ds(at, BAND), :] += dot(low, head_queries)
        grad_values[pl.ds(at, BAND), :] += dot(jnp.concatenate(all_weights, 1), head_grads)
    parts = (
        jnp.transpose(grad_queries[...]).astype(bf16),
        grad_keys[pl.ds(BLOCK, rows), :].astype(bf16),
        grad_values[pl.ds(BLOCK, rows), :].astype(bf16),
    )
    if not bias_grads:
        return parts, None
    diagonals = []
    row_index = iota((BLOCK, ROLL), 0)
    for h in range(heads):
        moved = jnp.concatenate([jnp.transpose(sums[h]), jnp.zeros((BLOCK, ROLL - BAND), f32)], 1)
        step = 1
        while step < BLOCK:
            moved = jnp.where((row_index & step) != 0, pltpu.roll(moved, ROLL - step, 1), moved)
            step *= 2
        diagonals.append(jnp.sum(moved, 0, keepdims=True))
    onehot = jnp.concatenate([onehot, jnp.zeros((128 - onehot.shape[0], ROLL), f32)], 0)
    by_head = dot(jnp.concatenate(diagonals, 0), onehot, NT, precision=highest)
    return parts, jnp.concatenate([by_head[h : h + 1] for h in range(heads)], 1)


def own_backward_kernel(normed_ref, iw_ref, ow_ref, bt_ref, seg_ref, low_ref, grad_iw_ref, parts_ref, table_ref, *scratch):
    normed = normed_ref[...]
    parts, table_grad = group_backward(
        normed, iw_ref, ow_ref[...], bt_ref[...], seg_ref[...].astype(f32), low_ref[...], scratch, True
    )
    table_ref[...] = jnp.concatenate(
        [table_grad, jnp.zeros((1, table_ref.shape[1] - table_grad.shape[1]), f32)], 1
    )
    width = ow_ref.shape[0]
    for j in range(3):
        parts_ref[j] = parts[j]
        grad_iw_ref[pl.ds(j * width, width), :] = dot(parts[j], normed, TN).astype(bf16)


def rest_backward_kernel(
    normed_ref, own_iw_ref, iw_ref, ow_ref, bt_ref, seg_ref, low_ref, parts_ref, tok_ref, gain_ref, grad_hidden_ref,
    table_ref, grad_tok_ref, tail_ref, total, *scratch,
):
    width = ow_ref.shape[1]
    total[...] = sum(dot(parts_ref[j], own_iw_ref[j]) for j in range(3))

    def step(group, carry):
        weight = [iw_ref[group, pl.ds(j * width, width), :] for j in range(3)]
        parts, _ = group_backward(
            normed_ref[...], weight, ow_ref[group], bt_ref[group], seg_ref[...].astype(f32), low_ref[...], scratch, False
        )
        total[...] += sum(dot(parts[j], weight[j]) for j in range(3))
        return carry

    lax.fori_loop(0, ow_ref.shape[0], step, 0)
    tok = tok_ref[...].astype(f32)
    gain = flat(gain_ref)
    scale = lax.rsqrt(jnp.mean(tok * tok, -1, keepdims=True) + norm_eps)
    grad_normed = total[...]
    tail_ref[...] = rows3([jnp.sum(grad_normed * tok * scale, 0, keepdims=True), table_ref[...]], tail_ref.shape[0])
    scaled = grad_normed * gain
    grad_tok_ref[...] = (
        grad_hidden_ref[...]
        + scale * scaled
        - tok * (scale * scale * scale) * jnp.mean(scaled * tok, -1, keepdims=True)
    )


def rows3(values, count):
    parts = [part for value in values for part in split3(value)]
    row = iota((count, values[0].shape[1]), 0)
    total = jnp.zeros(row.shape, f32)
    for index, part in enumerate(parts):
        total = jnp.where(row == index, part, total)
    return total.astype(bf16)


def finish_kernel(late_ref, early_ref, hidden_ref, prob_ref, choice_ref, result_ref, *refs):
    out_ref, grad_iw_ref, grad_ow_ref, grad_rw_ref, second_ref, first_ref, table_ref = refs
    output_kernel(hidden_ref, prob_ref, choice_ref, result_ref, out_ref)
    devices = late_ref.shape[0]
    late_rows = grad_iw_ref.shape[0] // devices
    tail = jnp.zeros((late_ref.shape[1] - late_rows, late_ref.shape[2]), f32)
    for device in range(devices):
        block = late_ref[device].astype(f32)
        grad_iw_ref[pl.ds(device * late_rows, late_rows), :] = block[:late_rows]
        tail = tail + block[late_rows:]
    first_ref[...] = jnp.sum(tail[:3], 0)
    table = jnp.sum(tail[3:6], 0, keepdims=True)
    heads, buckets = table_ref.shape
    table_ref[...] = jnp.concatenate([table[:, h * 128 : h * 128 + buckets] for h in range(heads)], 0)
    at, experts = grad_ow_ref.shape[0], grad_rw_ref.shape[0]
    early_rows = early_ref.shape[1] - 8
    early = jnp.concatenate([early_ref[device][:early_rows] for device in range(devices)], 0)
    grad_ow_ref[...] = early[:at]
    grad_rw_ref[...] = early[at : at + experts]
    second_ref[...] = jnp.sum(early[at + experts : at + experts + 8], 0)


def slot_onehot(choice, slot, slots):
    dest = jnp.where(slot >= 0, choice * CAP + slot, slots)
    return (iota((slots, dest.shape[1]), 0) == dest).astype(f32).astype(bf16)


def slot_order(slots, group, across):
    index = iota((1, slots), 1)
    big, small = slots // across, slots // group
    outer, rest = lax.div(index, big), lax.rem(index, big)
    target = lax.div(rest, CAP) * small + outer * CAP + lax.rem(rest, CAP)
    return (iota((slots, slots), 0) == target).astype(f32).astype(bf16)


def cotangent_kernel(cot_ref, choice_ref, slot_ref, out_ref):
    fill = slot_onehot(flat(choice_ref), flat(slot_ref), out_ref.shape[0])
    out_ref[...] = dot(fill, cot_ref[...]).astype(bf16)


def chosen_of(choice, experts):
    column = column_of(choice)[:, :experts]
    return (column == iota(column.shape, 1).astype(f32)).astype(f32)


def middle_kernel(tok_ref, own_ow_ref, ow_ref, gain_ref, rw_ref, choice_ref, slot_ref, *refs):
    att_refs, (hidden_ref, prob_ref, send_ref) = refs[:-3], refs[-3:]
    hidden = tok_ref[...].astype(f32)
    for shift, att_ref in enumerate(att_refs):
        hidden = hidden + dot(att_ref[...], ow_ref[shift - 1] if shift else own_ow_ref[...], TN)
    hidden_ref[...] = hidden
    scale = lax.rsqrt(jnp.mean(hidden * hidden, -1, keepdims=True) + norm_eps)
    normed = hidden * scale * flat(gain_ref)
    logits = dot3(normed, rw_ref[...], NT)
    raised = jnp.exp(logits - jnp.max(logits, -1, keepdims=True))
    prob = raised * (1.0 / jnp.sum(raised, -1, keepdims=True))
    prob_ref[...] = prob
    gate = jnp.sum(prob * chosen_of(flat(choice_ref), prob.shape[1]), -1, keepdims=True)
    width = normed.shape[1]
    fill = slot_onehot(flat(choice_ref), flat(slot_ref), send_ref.shape[0])
    send_ref[:, :width] = dot(fill, normed.astype(bf16)).astype(bf16)
    send_ref[:, width:] = dot(fill, columns3(gate, 128)).astype(bf16)


def expert_kernel(
    tensor_size, sources, local,
    recv_ref, cot_ref, win_ref, wout_ref,
    rows_ref, grads_ref, act_ref, grad_act_ref, dots_ref, result_ref, *refs,
):
    chunks = refs[:tensor_size]
    c_all, r_all, y_all, x_all, g_all, h_all, s_all, d_all, turned, win_slots, wout_slots, arrived, left = refs[tensor_size:]
    leaving = []

    def leave(source, target):
        leaving.append(pltpu.make_async_copy(source, target, left.at[len(leaving)]))
        leaving[-1].start()

    slots, width = cot_ref.shape
    per = slots // local
    depth = win_slots.shape[0]

    def fetch(expert):
        slot = expert % depth
        copies = [
            pltpu.make_async_copy(win_ref.at[expert], win_slots.at[slot], arrived.at[0, slot]),
            pltpu.make_async_copy(wout_ref.at[expert], wout_slots.at[slot], arrived.at[1, slot]),
        ]
        for copy in copies:
            copy.start()
        return copies

    coming = [fetch(expert) for expert in range(min(depth, local))]
    order = slot_order(slots, local, sources)
    x_all[...] = dot(order, recv_ref[:, :width]).astype(bf16)
    gate = jnp.sum(dot(order, recv_ref[:, width:]), -1, keepdims=True)
    cot = dot(order, cot_ref[...])
    c_all[...] = cot.astype(bf16)
    g_all[...] = (gate * cot).astype(bf16)
    leave(x_all, rows_ref)
    leave(g_all, grads_ref)

    for expert in range(local):
        at = pl.ds(expert * per, per)
        for copy in coming[expert]:
            copy.wait()
        x = x_all[at, :]
        g = g_all[at, :]
        weight_in = win_slots[expert % depth]
        weight_out = wout_slots[expert % depth]
        pre = dot(x, weight_in)
        grad_act = dot(g, weight_out, NT)
        inner = jnp.tanh(gelu_const * (pre + gelu_cubic * pre * pre * pre))
        act = (0.5 * pre * (1.0 + inner)).astype(bf16)
        slope = 0.5 * (1.0 + inner) + 0.5 * pre * (1.0 - inner * inner) * gelu_const * (
            1.0 + 3.0 * gelu_cubic * pre * pre
        )
        grad_act = (grad_act * slope).astype(bf16)
        r_all[at, :] = dot(grad_act, weight_in, NT).astype(bf16)
        result = dot(act, weight_out)
        y_all[at, :] = result.astype(bf16)
        d_all[at, :] = columns3(jnp.sum(result * c_all[at, :].astype(f32), -1, keepdims=True), 128)
        h_all[at, :] = act
        s_all[at, :] = grad_act
        leave(h_all.at[at], act_ref.at[at])
        leave(s_all.at[at], grad_act_ref.at[at])
        if expert + depth < local:
            coming.append(fetch(expert + depth))

    dots_ref[...] = dot(d_all[...], order, TN)[:EXTRA].astype(bf16)
    turn_chunks(tensor_size, dot(r_all[...], order, TN).astype(bf16), turned, chunks)
    result_ref[...] = dot(slot_order(slots, sources, local), y_all[...]).astype(bf16)
    for copy in leaving:
        copy.wait()


def turn_chunks(tensor_size, rows, turned, chunks):
    turned[...] = rows
    quarter = rows.shape[0] // tensor_size
    me = lax.axis_index("tensor")
    for shift in range(tensor_size):
        first = lax.rem(me + shift, tensor_size) * quarter
        chunks[shift][...] = turned[pl.ds(pl.multiple_of(first, 64), quarter), :]


def result_back_kernel(recv_ref, choice_ref, slot_ref, out_ref):
    fill = slot_onehot(flat(choice_ref), flat(slot_ref), recv_ref.shape[0])
    out_ref[...] = dot(fill, recv_ref[...], TN).astype(bf16)


def sum_kernel(*refs):
    *parts, dots_ref, out_ref = refs
    total = sum(ref[...].astype(f32) for ref in parts)
    blank = jnp.zeros((out_ref.shape[1] - total.shape[0] - EXTRA, total.shape[1]), f32)
    out_ref[...] = jnp.transpose(jnp.concatenate([total, dots_ref[...].astype(f32), blank], 0)).astype(bf16)


def back_kernel(recv_ref, choice_ref, slot_ref, out_ref):
    fill = slot_onehot(flat(choice_ref), flat(slot_ref), recv_ref.shape[0])
    out_ref[...] = dot(recv_ref[...], fill, TN)[: out_ref.shape[0]].astype(bf16)


def spread(refs, quarter, turned):
    size = len(refs)
    me = lax.axis_index("tensor")
    for shift, ref in enumerate(refs):
        first = lax.rem(me + size - shift, size) * quarter
        turned[pl.ds(pl.multiple_of(first, 64), quarter), :] = ref[pl.ds(0, quarter), :].astype(f32)
    return jnp.transpose(turned[...])


def hidden_backward_kernel(
    hidden_ref, prob_ref, cot_ref, gain_ref, rw_ref, choice_ref, att_ref, *refs,
):
    parts = refs[:-4]
    grad_hidden_ref, low_ref, sums_ref, turned = refs[-4:]
    hidden = hidden_ref[...]
    rows, width = hidden.shape
    quarter = width // len(parts)
    grad_routed = spread(parts, quarter, turned)
    dots = sum(jnp.sum(ref[pl.ds(quarter, EXTRA), :].astype(f32), 0, keepdims=True) for ref in parts)
    prob = prob_ref[...]
    chosen = chosen_of(flat(choice_ref), prob.shape[1])
    gate = jnp.sum(prob * chosen, -1, keepdims=True)
    grad_gate = column_of(dots)[:, :1]
    grad_logits = (grad_gate * gate) * (chosen - prob)
    grad_normed = grad_routed + dot3(grad_logits, rw_ref[...])
    gain = flat(gain_ref)
    scale = lax.rsqrt(jnp.mean(hidden * hidden, -1, keepdims=True) + norm_eps)
    scaled = grad_normed * gain
    grad_hidden = (
        cot_ref[...].astype(f32)
        + scale * scaled
        - hidden * (scale * scale * scale) * jnp.mean(scaled * hidden, -1, keepdims=True)
    )
    grad_hidden_ref[...] = grad_hidden
    low = grad_hidden.astype(bf16)
    low_ref[...] = low
    at, experts = att_ref.shape[0], prob.shape[1]
    sums_ref[pl.ds(0, at), :] = dot(att_ref[...], low).astype(bf16)
    sums_ref[pl.ds(at, experts), :] = dot3(grad_logits, hidden * scale * gain, TN).astype(bf16)
    tail = sums_ref.shape[0] - at - experts
    sums_ref[pl.ds(at + experts, tail), :] = rows3([jnp.sum(grad_normed * hidden * scale, 0, keepdims=True)], tail)


def output_kernel(hidden_ref, prob_ref, choice_ref, result_ref, out_ref):
    prob = prob_ref[...]
    gate = jnp.sum(prob * chosen_of(flat(choice_ref), prob.shape[1]), -1, keepdims=True)
    share = hidden_ref.shape[0] // result_ref.shape[0]
    result = jnp.concatenate([result_ref[part][:share] for part in range(result_ref.shape[0])], 0)
    out_ref[...] = (hidden_ref[...] + gate * result.astype(f32)).astype(bf16)


def make(mesh):
    tensor_size = mesh.shape["tensor"]
    expert_size = mesh.shape["expert"]

    def shards(
        tokens,
        segment_ids,
        expert_choice,
        slot_index,
        first_gain,
        input_weight,
        bias_table,
        output_weight,
        second_gain,
        router_weight,
        expert_in,
        expert_out,
        cotangent,
    ):
        token_count, width = tokens.shape
        sequences, length = segment_ids.shape
        quarter = output_weight.shape[0]
        experts = router_weight.shape[1]
        local = expert_in.shape[0]
        hidden_units = expert_in.shape[2]
        slots = experts * CAP
        per = slots // local
        chunk = slots // expert_size
        buckets, heads = bias_table.shape
        expert_index = lax.axis_index("expert")
        seg = (segment_ids + 8 * jnp.arange(sequences, dtype=i32)[:, None]).reshape(1, token_count)
        choice, slot = expert_choice, slot_index
        gain_first, gain_second = first_gain, second_gain
        iw_own = jnp.swapaxes(input_weight, 1, 2)
        table = bias_table.T
        rw = router_weight.T
        after = lax.optimization_barrier

        shifts = [[(i, (i + s) % tensor_size) for i in range(tensor_size)] for s in range(1, tensor_size)]

        def from_others(array):
            return [lax.ppermute(array, "tensor", pairs) for pairs in shifts]

        def gather_tensor(array):
            return [array] + from_others(array)

        def joined(planes):
            got = lax.all_gather(planes, "expert", axis=0)
            return jnp.swapaxes(got, 0, 1).reshape(tensor_size - 1, -1, got.shape[-1])

        def exchange(array):
            rows = array.shape[0] // expert_size
            got = lax.all_to_all(array.reshape(expert_size, rows, array.shape[1]), "expert", 0, 0)
            return got.reshape(array.shape)

        ow_rows = quarter // expert_size
        ow_part = lax.dynamic_slice_in_dim(output_weight, expert_index * ow_rows, ow_rows, 0)
        ow_all = joined(jnp.stack(from_others(ow_part)))

        attended, first_normed = call(
            forward_kernel,
            [((quarter, token_count), bf16), ((token_count, width), bf16)],
            (tokens, gain_first, iw_own, table, seg),
            [
                pltpu.VMEM((token_count + 2 * BLOCK, quarter), bf16),
                pltpu.VMEM((quarter, token_count + 2 * BLOCK), bf16),
            ],
        )
        attended_parts = gather_tensor(attended)
        cot_early, _ = after((cotangent, attended))
        (cot_slots,) = call(cotangent_kernel, [((slots, width), bf16)], (cot_early, choice, slot))
        cot_recv = exchange(cot_slots)
        attended_parts, cot_recv = after((attended_parts, cot_recv))

        hidden, prob, send = call(
            middle_kernel,
            [((token_count, width), f32), ((token_count, experts), f32), ((slots, width + 128), bf16)],
            (tokens, output_weight, ow_all, gain_second, rw, choice, slot, *attended_parts),
        )
        recv = exchange(send)

        iw_rows = 3 * quarter // expert_size
        iw_part = lax.dynamic_slice_in_dim(iw_own.reshape(3 * quarter, width), expert_index * iw_rows, iw_rows, 0)
        bias_parts = jnp.stack(split3(table)).astype(bf16).reshape(-1)
        bias_parts = jnp.pad(bias_parts, (0, 8 * width - bias_parts.shape[0])).reshape(8, width)
        iw_part, _ = after((jnp.concatenate([iw_part, bias_parts], 0), send))
        iw_planes = from_others(iw_part)

        iw_planes, recv = after((iw_planes, recv))
        iw_planes = jnp.stack(iw_planes)
        iw_all = joined(iw_planes[:, :iw_rows])
        bias_all = jnp.sum(
            iw_planes[:, iw_rows:]
            .reshape(tensor_size - 1, -1)[:, : 3 * buckets * heads]
            .reshape(tensor_size - 1, 3, heads, buckets)
            .astype(f32),
            1,
        )

        vmem = pl.BlockSpec(memory_space=pltpu.VMEM)
        left = pl.BlockSpec(memory_space=pl.ANY)
        shapes = [(slots, width)] * 2 + [(slots, hidden_units)] * 2 + [(EXTRA, slots), (slots, width)]
        shapes = shapes + [(quarter, slots)] * tensor_size
        depth = min(4, local)
        outs = pl.pallas_call(
            lambda *refs: expert_kernel(tensor_size, expert_size, local, *refs),
            in_specs=[vmem, vmem, left, left],
            out_specs=[left] * 4 + [vmem] * (len(shapes) - 4),
            out_shape=[jax.ShapeDtypeStruct(shape, bf16) for shape in shapes],
            scratch_shapes=[pltpu.VMEM((slots, width), bf16)] * 5
            + [pltpu.VMEM((slots, hidden_units), bf16)] * 2
            + [
                pltpu.VMEM((slots, 128), bf16),
                pltpu.VMEM((width, slots), bf16),
                pltpu.VMEM((depth, width, hidden_units), bf16),
                pltpu.VMEM((depth, hidden_units, width), bf16),
                pltpu.SemaphoreType.DMA((2, depth)),
                pltpu.SemaphoreType.DMA((2 + 2 * local,)),
            ],
            compiler_params=pltpu.CompilerParams(vmem_limit_bytes=56 * 2**20),
        )(recv, cot_recv, expert_in, expert_out)
        expert_rows, grad_slots, expert_act, grad_act, dots, result_rows = outs[:6]
        grad_chunks = outs[6:]

        def trade_chunks(chunks):
            return [chunks[0]] + [lax.ppermute(c, "tensor", pairs) for c, pairs in zip(chunks[1:], shifts)]

        def sum_rows(parts):
            columns = -(-(quarter + EXTRA) // 128) * 128
            return call(sum_kernel, [((slots, columns), bf16)], parts)[0]

        def own_tokens(rows, kept):
            return call(back_kernel, [((kept, token_count), bf16)], (rows, choice, slot))[0]

        by = lambda array: array.reshape(local, per, array.shape[1])
        grad_expert_out = jnp.einsum("erf,erd->efd", by(expert_act), by(grad_slots), preferred_element_type=f32)
        grad_expert_in = jnp.einsum("erd,erf->edf", by(expert_rows), by(grad_act), preferred_element_type=f32)

        (result_part,) = call(
            result_back_kernel, [((token_count, width), bf16)], (exchange(result_rows), choice, slot)
        )
        traded, grad_expert_out, result_part = after((trade_chunks(grad_chunks), grad_expert_out, result_part))
        summed = sum_rows(traded + [dots])
        returned = own_tokens(exchange(summed), quarter + EXTRA)
        returned, grad_expert_in = after((returned, grad_expert_in))
        result_share = lax.psum_scatter(result_part, "tensor", scatter_dimension=0, tiled=True)
        grad_parts = gather_tensor(returned)
        grad_parts, iw_all, bias_all = after((grad_parts, iw_all, bias_all))

        early_rows = quarter + experts + 64
        grad_hidden, grad_low, early_sums = call(
            hidden_backward_kernel,
            [((token_count, width), f32), ((token_count, width), bf16), ((early_rows, width), bf16)],
            (hidden, prob, cotangent, gain_second, rw, choice, attended, *grad_parts),
            [pltpu.VMEM((width, token_count), f32)],
        )
        result_share, _ = after((result_share, grad_low))
        result = lax.all_gather(jnp.pad(result_share, ((0, 48), (0, 0))), "tensor", axis=0)

        def sum_chunks(array):
            return jnp.sum(array.reshape(expert_size, -1, array.shape[1]).astype(f32), 0)

        padded = token_count + 2 * BLOCK
        scratch = [pltpu.VMEM((padded, quarter), bf16)] * 2 + [pltpu.VMEM((quarter, padded), bf16)]
        scratch = scratch + [pltpu.VMEM((padded, quarter), f32)] * 2 + [pltpu.VMEM((quarter, token_count), f32)]
        grad_iw, own_parts, table_grad = call(
            own_backward_kernel,
            [((3 * quarter, width), bf16), ((3, token_count, quarter), bf16), ((1, width), f32)],
            (first_normed, iw_own, output_weight, table, seg, grad_low),
            scratch,
        )
        grad_tokens, tail = call(
            rest_backward_kernel,
            [((token_count, width), f32), ((8, width), bf16)],
            (
                first_normed, iw_own, iw_all, ow_all, bias_all, seg, grad_low, own_parts, tokens, gain_first,
                grad_hidden, table_grad,
            ),
            [pltpu.VMEM((token_count, width), f32)] + scratch,
        )
        early_got, grad_iw = after((exchange(early_sums), grad_iw))
        early_sum = sum_chunks(early_got)
        early = lax.all_gather(jnp.pad(early_sum, ((0, 8), (0, 0))), "expert", axis=0)
        late = lax.all_gather(jnp.concatenate([sum_chunks(exchange(grad_iw)).astype(bf16), tail], 0), "expert", axis=0)
        block_output, grad_iw, grad_ow, grad_rw, grad_second, grad_first, grad_table = call(
            finish_kernel,
            [
                ((token_count, width), bf16),
                ((3 * quarter, width), f32),
                ((quarter, width), f32),
                ((experts, width), f32),
                ((width,), f32),
                ((width,), f32),
                ((heads, buckets), f32),
            ],
            (late, early, hidden, prob, choice, result),
        )
        return (
            block_output,
            grad_tokens,
            grad_first,
            jnp.swapaxes(grad_iw.reshape(3, quarter, width), 1, 2),
            grad_table.T,
            grad_ow,
            grad_second,
            grad_rw.T,
            grad_expert_in,
            grad_expert_out,
        )

    return shards


def solution(mesh):
    placed = (
        P("expert", None),
        P("expert", None),
        P("expert"),
        P("expert"),
        P(),
        P(None, None, "tensor"),
        P(None, "tensor"),
        P("tensor", None),
        P(),
        P(),
        P("expert", None, "tensor"),
        P("expert", "tensor", None),
        P("expert", None),
    )
    return jax.shard_map(
        make(mesh),
        mesh=mesh,
        in_specs=placed,
        out_specs=(
            P("expert", None),
            P("expert", None),
            P(),
            P(None, None, "tensor"),
            P(None, "tensor"),
            P("tensor", None),
            P(),
            P(),
            P("expert", None, "tensor"),
            P("expert", "tensor", None),
        ),
        check_vma=False,
    )
```

```python
import math

import jax
import jax.numpy as jnp
from jax import lax
from jax.experimental import pallas as pl
from jax.experimental.pallas import tpu as pltpu
from jax.sharding import PartitionSpec as P

CAP = 10

bucket_edges = (12, 16, 23, 32, 46, 64, 91)
norm_eps = 1e-06
masked_score = -1e30
gelu_const = math.sqrt(2.0 / math.pi)
gelu_cubic = 0.044715

BLOCK = 128
BAND = 3 * BLOCK
ROLL = 4 * BLOCK
HEAD = 64
EXTRA = 16

bf16 = jnp.bfloat16
f32 = jnp.float32
i32 = jnp.int32
highest = lax.Precision.HIGHEST

NN = (((1,), (0,)), ((), ()))
NT = (((1,), (1,)), ((), ()))
TN = (((0,), (0,)), ((), ()))


def dot(left, right, dims=NN, precision=None):
    return lax.dot_general(left, right, dims, precision=precision, preferred_element_type=f32)


def dot3(left, right, dims=NN):
    left_high, right_high = left.astype(bf16), right.astype(bf16)
    left_low = (left - left_high.astype(f32)).astype(bf16)
    right_low = (right - right_high.astype(f32)).astype(bf16)
    return dot(left_high, right_high, dims) + (dot(left_high, right_low, dims) + dot(left_low, right_high, dims))


def flat(ref):
    return ref[...].reshape(1, -1)


def iota(shape, axis):
    return lax.broadcasted_iota(i32, shape, axis)


def call(kernel, outs, args, scratch=(), **extra):
    vmem = pl.BlockSpec(memory_space=pltpu.VMEM)
    return pl.pallas_call(
        kernel,
        out_shape=[jax.ShapeDtypeStruct(shape, dtype) for shape, dtype in outs],
        in_specs=[vmem] * len(args),
        out_specs=[vmem] * len(outs),
        scratch_shapes=list(scratch),
        compiler_params=pltpu.CompilerParams(vmem_limit_bytes=56 * 2**20),
        **extra,
    )(*args)


def split3(value):
    high = value.astype(bf16).astype(f32)
    rest = value - high
    middle = rest.astype(bf16).astype(f32)
    return high, middle, rest - middle


def columns3(value, width):
    high, middle, low = split3(value)
    lane = iota((value.shape[0], width), 1)
    picked = jnp.where(lane == 0, high, jnp.where(lane == 1, middle, jnp.where(lane == 2, low, 0.0)))
    return picked.astype(bf16)


def column_of(row):
    return jnp.transpose(jnp.broadcast_to(row.astype(f32), (128, row.shape[1])))


def wide(column, width):
    return jnp.concatenate([column] * (width // 128), 1)


def bucket_of(relative):
    distance = jnp.abs(relative)
    beyond = jnp.zeros_like(distance)
    for threshold in bucket_edges:
        beyond = beyond + (distance >= threshold).astype(i32)
    magnitude = jnp.where(distance < 8, distance, 8 + beyond)
    return magnitude + 16 * (relative > 0).astype(i32)


def band_rows(table):
    buckets = table.shape[1]
    offset = iota((buckets, ROLL), 1)
    relative = jnp.where(offset < BAND, offset, offset - ROLL) - BLOCK
    onehot = (bucket_of(relative) == iota((buckets, ROLL), 0)).astype(f32)
    return dot(table, onehot, precision=highest), onehot


def bias_tiles(table):
    rows, onehot = band_rows(table)
    tiles = []
    for h in range(table.shape[0]):
        full = jnp.broadcast_to(rows[h : h + 1], (BLOCK, ROLL))
        tiles.append(jnp.transpose(pltpu.roll(full, 0, 1, stride=1, stride_axis=0)[:, :BAND]))
    return tiles, onehot


def head_masks(heads):
    lane = iota((1, heads * HEAD), 1)
    return [((lane >= h * HEAD) & (lane < (h + 1) * HEAD)).astype(f32).astype(bf16) for h in range(heads)]


def padded_segments(seg):
    edge = jnp.full((1, BLOCK), -1.0, f32)
    return column_of(jnp.concatenate([edge, seg, edge], 1))


def first_norm(tok, gain):
    scale = lax.rsqrt(jnp.mean(tok * tok, -1, keepdims=True) + norm_eps)
    return (tok * scale * gain).astype(bf16), scale


def probabilities(scores, bias, same):
    scores = jnp.where(same, scores + bias, masked_score)
    weights = jnp.exp(scores - jnp.max(scores, 0, keepdims=True))
    return weights * (1.0 / jnp.sum(weights, 0, keepdims=True))


def stack_heads(rows, masks):
    return jnp.concatenate([rows * mask for mask in masks], 0)


def own_blocks(product, heads):
    return jnp.concatenate(
        [product[h * HEAD : (h + 1) * HEAD, h * BLOCK : (h + 1) * BLOCK] for h in range(heads)], 0
    )


def fill_rows(ref, value):
    rows = value.shape[0]
    edge = jnp.zeros((BLOCK, value.shape[1]), bf16)
    ref[pl.ds(0, BLOCK), :] = edge
    ref[pl.ds(rows + BLOCK, BLOCK), :] = edge
    ref[pl.ds(BLOCK, rows), :] = value


def fill_columns(ref, value):
    rows = value.shape[1]
    edge = jnp.zeros((value.shape[0], BLOCK), bf16)
    ref[:, pl.ds(0, BLOCK)] = edge
    ref[:, pl.ds(rows + BLOCK, BLOCK)] = edge
    ref[:, pl.ds(BLOCK, rows)] = value


def forward_kernel(
    tok_ref, gain_ref, iw_ref, bt_ref, seg_ref, cot_ref, choice_ref, slot_ref,
    att_ref, normed_ref, cot_slots_ref, keys, values,
):
    rows = tok_ref.shape[0]
    fill = slot_onehot(flat(choice_ref), flat(slot_ref), cot_slots_ref.shape[0])
    cot_slots_ref[...] = dot(fill, cot_ref[...]).astype(bf16)
    normed, _ = first_norm(tok_ref[...].astype(f32), flat(gain_ref))
    normed_ref[...] = normed
    queries = dot(normed, iw_ref[0], NT).astype(bf16)
    fill_rows(keys, dot(normed, iw_ref[1], NT).astype(bf16))
    fill_columns(values, dot(iw_ref[2], normed, NT).astype(bf16))
    seg = seg_ref[...].astype(f32)
    seg_keys = padded_segments(seg)
    tiles, _ = bias_tiles(bt_ref[...])
    heads = len(tiles)
    masks = head_masks(heads)
    for block in range(rows // BLOCK):
        at = block * BLOCK
        same = seg_keys[at : at + BAND] == seg[:, at : at + BLOCK]
        scores = dot(keys[pl.ds(at, BAND), :], stack_heads(queries[at : at + BLOCK], masks), NT)
        weights = [
            probabilities(scores[:, h * BLOCK : (h + 1) * BLOCK], tiles[h], same).astype(bf16) for h in range(heads)
        ]
        product = dot(values[:, pl.ds(at, BAND)], jnp.concatenate(weights, 1))
        att_ref[:, pl.ds(at, BLOCK)] = own_blocks(product, heads).astype(bf16)


def group_backward(normed, weight, out_weight, table, seg, grad_low, scratch, bias_grads):
    keys, values, keys_across, grad_keys, grad_values, grad_queries = scratch
    rows = normed.shape[0]
    queries = dot(normed, weight[0], NT).astype(bf16)
    fill_rows(keys, dot(normed, weight[1], NT).astype(bf16))
    fill_columns(keys_across, dot(weight[1], normed, NT).astype(bf16))
    fill_rows(values, dot(normed, weight[2], NT).astype(bf16))
    grad_att = dot(grad_low, out_weight, NT).astype(bf16)
    grad_keys[...] = jnp.zeros(grad_keys.shape, f32)
    grad_values[...] = jnp.zeros(grad_values.shape, f32)
    seg_keys = padded_segments(seg)
    tiles, onehot = bias_tiles(table)
    heads = len(tiles)
    masks = head_masks(heads)
    sums = [None] * heads
    for block in range(rows // BLOCK):
        at = block * BLOCK
        same = seg_keys[at : at + BAND] == seg[:, at : at + BLOCK]
        head_queries = stack_heads(queries[at : at + BLOCK], masks)
        head_grads = stack_heads(grad_att[at : at + BLOCK], masks)
        scores = dot(keys[pl.ds(at, BAND), :], head_queries, NT)
        grad_probs = dot(values[pl.ds(at, BAND), :], head_grads, NT)
        all_weights, all_grads = [], []
        for h in range(heads):
            columns = slice(h * BLOCK, (h + 1) * BLOCK)
            weights = probabilities(scores[:, columns], tiles[h], same)
            scaled = weights * grad_probs[:, columns]
            grad_scores = scaled - weights * jnp.sum(scaled, 0, keepdims=True)
            all_weights.append(weights.astype(bf16))
            all_grads.append(grad_scores.astype(bf16))
            if bias_grads:
                sums[h] = grad_scores if sums[h] is None else sums[h] + grad_scores
        low = jnp.concatenate(all_grads, 1)
        grad_queries[:, pl.ds(at, BLOCK)] = own_blocks(dot(keys_across[:, pl.ds(at, BAND)], low), heads)
        grad_keys[pl.ds(at, BAND), :] += dot(low, head_queries)
        grad_values[pl.ds(at, BAND), :] += dot(jnp.concatenate(all_weights, 1), head_grads)
    parts = (
        jnp.transpose(grad_queries[...]).astype(bf16),
        grad_keys[pl.ds(BLOCK, rows), :].astype(bf16),
        grad_values[pl.ds(BLOCK, rows), :].astype(bf16),
    )
    if not bias_grads:
        return parts, None
    diagonals = []
    row_index = iota((BLOCK, ROLL), 0)
    for h in range(heads):
        moved = jnp.concatenate([jnp.transpose(sums[h]), jnp.zeros((BLOCK, ROLL - BAND), f32)], 1)
        step = 1
        while step < BLOCK:
            moved = jnp.where((row_index & step) != 0, pltpu.roll(moved, ROLL - step, 1), moved)
            step *= 2
        diagonals.append(jnp.sum(moved, 0, keepdims=True))
    onehot = jnp.concatenate([onehot, jnp.zeros((128 - onehot.shape[0], ROLL), f32)], 0)
    by_head = dot(jnp.concatenate(diagonals, 0), onehot, NT, precision=highest)
    return parts, jnp.concatenate([by_head[h : h + 1] for h in range(heads)], 1)


def own_backward_kernel(normed_ref, iw_ref, ow_ref, bt_ref, seg_ref, low_ref, grad_iw_ref, parts_ref, table_ref, *scratch):
    normed = normed_ref[...]
    parts, table_grad = group_backward(
        normed, iw_ref, ow_ref[...], bt_ref[...], seg_ref[...].astype(f32), low_ref[...], scratch, True
    )
    table_ref[...] = jnp.concatenate(
        [table_grad, jnp.zeros((1, table_ref.shape[1] - table_grad.shape[1]), f32)], 1
    )
    width = ow_ref.shape[0]
    for j in range(3):
        parts_ref[j] = parts[j]
        grad_iw_ref[pl.ds(j * width, width), :] = dot(parts[j], normed, TN).astype(bf16)


def rest_backward_kernel(
    normed_ref, own_iw_ref, iw_ref, ow_ref, bt_ref, seg_ref, low_ref, parts_ref, tok_ref, gain_ref, grad_hidden_ref,
    table_ref, grad_tok_ref, tail_ref, total, *scratch,
):
    width = ow_ref.shape[1]
    total[...] = sum(dot(parts_ref[j], own_iw_ref[j]) for j in range(3))

    def step(group, carry):
        weight = [iw_ref[group, pl.ds(j * width, width), :] for j in range(3)]
        parts, _ = group_backward(
            normed_ref[...], weight, ow_ref[group], bt_ref[group], seg_ref[...].astype(f32), low_ref[...], scratch, False
        )
        total[...] += sum(dot(parts[j], weight[j]) for j in range(3))
        return carry

    lax.fori_loop(0, ow_ref.shape[0], step, 0)
    tok = tok_ref[...].astype(f32)
    gain = flat(gain_ref)
    scale = lax.rsqrt(jnp.mean(tok * tok, -1, keepdims=True) + norm_eps)
    grad_normed = total[...]
    tail_ref[...] = rows3([jnp.sum(grad_normed * tok * scale, 0, keepdims=True), table_ref[...]], tail_ref.shape[0])
    scaled = grad_normed * gain
    grad_tok_ref[...] = (
        grad_hidden_ref[...]
        + scale * scaled
        - tok * (scale * scale * scale) * jnp.mean(scaled * tok, -1, keepdims=True)
    )


def rows3(values, count):
    parts = [part for value in values for part in split3(value)]
    row = iota((count, values[0].shape[1]), 0)
    total = jnp.zeros(row.shape, f32)
    for index, part in enumerate(parts):
        total = jnp.where(row == index, part, total)
    return total.astype(bf16)


def finish_kernel(late_ref, early_ref, hidden_ref, prob_ref, choice_ref, result_ref, *refs):
    out_ref, grad_iw_ref, grad_ow_ref, grad_rw_ref, second_ref, first_ref, table_ref = refs
    output_kernel(hidden_ref, prob_ref, choice_ref, result_ref, out_ref)
    devices = late_ref.shape[0]
    late_rows = grad_iw_ref.shape[0] // devices
    tail = jnp.zeros((late_ref.shape[1] - late_rows, late_ref.shape[2]), f32)
    for device in range(devices):
        block = late_ref[device].astype(f32)
        grad_iw_ref[pl.ds(device * late_rows, late_rows), :] = block[:late_rows]
        tail = tail + block[late_rows:]
    first_ref[...] = jnp.sum(tail[:3], 0)
    table = jnp.sum(tail[3:6], 0, keepdims=True)
    heads, buckets = table_ref.shape
    table_ref[...] = jnp.concatenate([table[:, h * 128 : h * 128 + buckets] for h in range(heads)], 0)
    at, experts = grad_ow_ref.shape[0], grad_rw_ref.shape[0]
    early_rows = early_ref.shape[1] - 8
    early = jnp.concatenate([early_ref[device][:early_rows] for device in range(devices)], 0)
    grad_ow_ref[...] = early[:at]
    grad_rw_ref[...] = early[at : at + experts]
    second_ref[...] = jnp.sum(early[at + experts : at + experts + 8], 0)


def slot_onehot(choice, slot, slots):
    dest = jnp.where(slot >= 0, choice * CAP + slot, slots)
    return (iota((slots, dest.shape[1]), 0) == dest).astype(f32).astype(bf16)


def slot_order(slots, group, across):
    index = iota((1, slots), 1)
    big, small = slots // across, slots // group
    outer, rest = lax.div(index, big), lax.rem(index, big)
    target = lax.div(rest, CAP) * small + outer * CAP + lax.rem(rest, CAP)
    return (iota((slots, slots), 0) == target).astype(f32).astype(bf16)


def chosen_of(choice, experts):
    column = column_of(choice)[:, :experts]
    return (column == iota(column.shape, 1).astype(f32)).astype(f32)


def middle_kernel(tok_ref, own_ow_ref, ow_ref, gain_ref, rw_ref, choice_ref, slot_ref, *refs):
    att_refs, (hidden_ref, prob_ref, send_ref) = refs[:-3], refs[-3:]
    hidden = tok_ref[...].astype(f32)
    for shift, att_ref in enumerate(att_refs):
        hidden = hidden + dot(att_ref[...], ow_ref[shift - 1] if shift else own_ow_ref[...], TN)
    hidden_ref[...] = hidden
    scale = lax.rsqrt(jnp.mean(hidden * hidden, -1, keepdims=True) + norm_eps)
    normed = hidden * scale * flat(gain_ref)
    logits = dot3(normed, rw_ref[...], NT)
    raised = jnp.exp(logits - jnp.max(logits, -1, keepdims=True))
    prob = raised * (1.0 / jnp.sum(raised, -1, keepdims=True))
    prob_ref[...] = prob
    gate = jnp.sum(prob * chosen_of(flat(choice_ref), prob.shape[1]), -1, keepdims=True)
    width = normed.shape[1]
    fill = slot_onehot(flat(choice_ref), flat(slot_ref), send_ref.shape[0])
    send_ref[:, :width] = dot(fill, normed.astype(bf16)).astype(bf16)
    send_ref[:, width:] = dot(fill, columns3(gate, 128)).astype(bf16)


def expert_kernel(
    tensor_size, sources, local,
    recv_ref, cot_ref, win_ref, wout_ref,
    rows_ref, grads_ref, act_ref, grad_act_ref, dots_ref, result_ref, *refs,
):
    chunks = refs[:tensor_size]
    c_all, r_all, y_all, x_all, g_all, h_all, s_all, d_all, turned, win_slots, wout_slots, arrived, left = refs[tensor_size:]
    leaving = []

    def leave(source, target):
        leaving.append(pltpu.make_async_copy(source, target, left.at[len(leaving)]))
        leaving[-1].start()

    slots, width = cot_ref.shape
    per = slots // local
    depth = win_slots.shape[0]

    def fetch(expert):
        slot = expert % depth
        copies = [
            pltpu.make_async_copy(win_ref.at[expert], win_slots.at[slot], arrived.at[0, slot]),
            pltpu.make_async_copy(wout_ref.at[expert], wout_slots.at[slot], arrived.at[1, slot]),
        ]
        for copy in copies:
            copy.start()
        return copies

    coming = [fetch(expert) for expert in range(min(depth, local))]
    order = slot_order(slots, local, sources)
    x_all[...] = dot(order, recv_ref[:, :width]).astype(bf16)
    gate = jnp.sum(dot(order, recv_ref[:, width:]), -1, keepdims=True)
    cot = dot(order, cot_ref[...])
    c_all[...] = cot.astype(bf16)
    g_all[...] = (gate * cot).astype(bf16)
    leave(x_all, rows_ref)
    leave(g_all, grads_ref)

    for expert in range(local):
        at = pl.ds(expert * per, per)
        for copy in coming[expert]:
            copy.wait()
        x = x_all[at, :]
        g = g_all[at, :]
        weight_in = win_slots[expert % depth]
        weight_out = wout_slots[expert % depth]
        pre = dot(x, weight_in)
        grad_act = dot(g, weight_out, NT)
        inner = jnp.tanh(gelu_const * (pre + gelu_cubic * pre * pre * pre))
        act = (0.5 * pre * (1.0 + inner)).astype(bf16)
        slope = 0.5 * (1.0 + inner) + 0.5 * pre * (1.0 - inner * inner) * gelu_const * (
            1.0 + 3.0 * gelu_cubic * pre * pre
        )
        grad_act = (grad_act * slope).astype(bf16)
        r_all[at, :] = dot(grad_act, weight_in, NT).astype(bf16)
        result = dot(act, weight_out)
        y_all[at, :] = result.astype(bf16)
        d_all[at, :] = columns3(jnp.sum(result * c_all[at, :].astype(f32), -1, keepdims=True), 128)
        h_all[at, :] = act
        s_all[at, :] = grad_act
        leave(h_all.at[at], act_ref.at[at])
        leave(s_all.at[at], grad_act_ref.at[at])
        if expert + depth < local:
            coming.append(fetch(expert + depth))

    dots_ref[...] = dot(d_all[...], order, TN)[:EXTRA].astype(bf16)
    turn_chunks(tensor_size, dot(r_all[...], order, TN).astype(bf16), turned, chunks)
    result_ref[...] = dot(slot_order(slots, sources, local), y_all[...]).astype(bf16)
    for copy in leaving:
        copy.wait()


def turn_chunks(tensor_size, rows, turned, chunks):
    turned[...] = rows
    quarter = rows.shape[0] // tensor_size
    me = lax.axis_index("tensor")
    for shift in range(tensor_size):
        first = lax.rem(me + shift, tensor_size) * quarter
        chunks[shift][...] = turned[pl.ds(pl.multiple_of(first, 64), quarter), :]


def result_back_kernel(recv_ref, choice_ref, slot_ref, out_ref):
    fill = slot_onehot(flat(choice_ref), flat(slot_ref), recv_ref.shape[0])
    out_ref[...] = dot(fill, recv_ref[...], TN).astype(bf16)


def sum_kernel(*refs):
    *parts, dots_ref, out_ref = refs
    total = sum(ref[...].astype(f32) for ref in parts)
    blank = jnp.zeros((out_ref.shape[1] - total.shape[0] - EXTRA, total.shape[1]), f32)
    out_ref[...] = jnp.transpose(jnp.concatenate([total, dots_ref[...].astype(f32), blank], 0)).astype(bf16)


def back_kernel(recv_ref, choice_ref, slot_ref, out_ref):
    fill = slot_onehot(flat(choice_ref), flat(slot_ref), recv_ref.shape[0])
    out_ref[...] = dot(recv_ref[...], fill, TN)[: out_ref.shape[0]].astype(bf16)


def spread(refs, quarter, turned):
    size = len(refs)
    me = lax.axis_index("tensor")
    for shift, ref in enumerate(refs):
        first = lax.rem(me + size - shift, size) * quarter
        turned[pl.ds(pl.multiple_of(first, 64), quarter), :] = ref[pl.ds(0, quarter), :].astype(f32)
    return jnp.transpose(turned[...])


def hidden_backward_kernel(
    hidden_ref, prob_ref, cot_ref, gain_ref, rw_ref, choice_ref, att_ref, *refs,
):
    parts = refs[:-4]
    grad_hidden_ref, low_ref, sums_ref, turned = refs[-4:]
    hidden = hidden_ref[...]
    rows, width = hidden.shape
    quarter = width // len(parts)
    grad_routed = spread(parts, quarter, turned)
    dots = sum(jnp.sum(ref[pl.ds(quarter, EXTRA), :].astype(f32), 0, keepdims=True) for ref in parts)
    prob = prob_ref[...]
    chosen = chosen_of(flat(choice_ref), prob.shape[1])
    gate = jnp.sum(prob * chosen, -1, keepdims=True)
    grad_gate = column_of(dots)[:, :1]
    grad_logits = (grad_gate * gate) * (chosen - prob)
    grad_normed = grad_routed + dot3(grad_logits, rw_ref[...])
    gain = flat(gain_ref)
    scale = lax.rsqrt(jnp.mean(hidden * hidden, -1, keepdims=True) + norm_eps)
    scaled = grad_normed * gain
    grad_hidden = (
        cot_ref[...].astype(f32)
        + scale * scaled
        - hidden * (scale * scale * scale) * jnp.mean(scaled * hidden, -1, keepdims=True)
    )
    grad_hidden_ref[...] = grad_hidden
    low = grad_hidden.astype(bf16)
    low_ref[...] = low
    at, experts = att_ref.shape[0], prob.shape[1]
    sums_ref[pl.ds(0, at), :] = dot(att_ref[...], low).astype(bf16)
    sums_ref[pl.ds(at, experts), :] = dot3(grad_logits, hidden * scale * gain, TN).astype(bf16)
    tail = sums_ref.shape[0] - at - experts
    sums_ref[pl.ds(at + experts, tail), :] = rows3([jnp.sum(grad_normed * hidden * scale, 0, keepdims=True)], tail)


def output_kernel(hidden_ref, prob_ref, choice_ref, result_ref, out_ref):
    prob = prob_ref[...]
    gate = jnp.sum(prob * chosen_of(flat(choice_ref), prob.shape[1]), -1, keepdims=True)
    share = hidden_ref.shape[0] // result_ref.shape[0]
    result = jnp.concatenate([result_ref[part][:share] for part in range(result_ref.shape[0])], 0)
    out_ref[...] = (hidden_ref[...] + gate * result.astype(f32)).astype(bf16)


def make(mesh):
    tensor_size = mesh.shape["tensor"]
    expert_size = mesh.shape["expert"]

    def shards(
        tokens,
        segment_ids,
        expert_choice,
        slot_index,
        first_gain,
        input_weight,
        bias_table,
        output_weight,
        second_gain,
        router_weight,
        expert_in,
        expert_out,
        cotangent,
    ):
        token_count, width = tokens.shape
        sequences, length = segment_ids.shape
        quarter = output_weight.shape[0]
        experts = router_weight.shape[1]
        local = expert_in.shape[0]
        hidden_units = expert_in.shape[2]
        slots = experts * CAP
        per = slots // local
        chunk = slots // expert_size
        buckets, heads = bias_table.shape
        expert_index = lax.axis_index("expert")
        seg = (segment_ids + 8 * jnp.arange(sequences, dtype=i32)[:, None]).reshape(1, token_count)
        choice, slot = expert_choice, slot_index
        gain_first, gain_second = first_gain, second_gain
        iw_own = jnp.swapaxes(input_weight, 1, 2)
        table = bias_table.T
        rw = router_weight.T
        after = lax.optimization_barrier

        shifts = [[(i, (i + s) % tensor_size) for i in range(tensor_size)] for s in range(1, tensor_size)]

        def from_others(array):
            return [lax.ppermute(array, "tensor", pairs) for pairs in shifts]

        def gather_tensor(array):
            return [array] + from_others(array)

        def joined(planes, rows):
            got = lax.all_gather(planes, "expert", axis=0)
            return jnp.swapaxes(got[:, :, :rows], 0, 1).reshape(tensor_size - 1, -1, got.shape[-1])

        def exchange(array):
            rows = array.shape[0] // expert_size
            got = lax.all_to_all(array.reshape(expert_size, rows, array.shape[1]), "expert", 0, 0)
            return got.reshape(array.shape)

        ow_rows = quarter // expert_size
        ow_part = lax.dynamic_slice_in_dim(output_weight, expert_index * ow_rows, ow_rows, 0)
        ow_all = joined(jnp.stack(from_others(ow_part)), ow_rows)

        attended, first_normed, cot_slots = call(
            forward_kernel,
            [((quarter, token_count), bf16), ((token_count, width), bf16), ((slots, width), bf16)],
            (tokens, gain_first, iw_own, table, seg, cotangent, choice, slot),
            [
                pltpu.VMEM((token_count + 2 * BLOCK, quarter), bf16),
                pltpu.VMEM((quarter, token_count + 2 * BLOCK), bf16),
            ],
        )
        attended_parts = gather_tensor(attended)
        cot_recv = exchange(cot_slots)
        attended_parts, cot_recv = after((attended_parts, cot_recv))

        hidden, prob, send = call(
            middle_kernel,
            [((token_count, width), f32), ((token_count, experts), f32), ((slots, width + 128), bf16)],
            (tokens, output_weight, ow_all, gain_second, rw, choice, slot, *attended_parts),
        )
        recv = exchange(send)

        iw_rows = 3 * quarter // expert_size
        iw_part = lax.dynamic_slice_in_dim(iw_own.reshape(3 * quarter, width), expert_index * iw_rows, iw_rows, 0)
        bias_parts = jnp.stack(split3(table)).astype(bf16).reshape(-1)
        bias_parts = jnp.pad(bias_parts, (0, 8 * width - bias_parts.shape[0])).reshape(8, width)
        iw_part, _ = after((jnp.concatenate([iw_part, bias_parts], 0), send))
        iw_planes = from_others(iw_part)

        iw_planes, recv = after((iw_planes, recv))
        iw_planes = jnp.stack(iw_planes)
        iw_all = joined(iw_planes, iw_rows)

        vmem = pl.BlockSpec(memory_space=pltpu.VMEM)
        left = pl.BlockSpec(memory_space=pl.ANY)
        shapes = [(slots, width)] * 2 + [(slots, hidden_units)] * 2 + [(EXTRA, slots), (slots, width)]
        shapes = shapes + [(quarter, slots)] * tensor_size
        depth = min(4, local)
        outs = pl.pallas_call(
            lambda *refs: expert_kernel(tensor_size, expert_size, local, *refs),
            in_specs=[vmem, vmem, left, left],
            out_specs=[left] * 4 + [vmem] * (len(shapes) - 4),
            out_shape=[jax.ShapeDtypeStruct(shape, bf16) for shape in shapes],
            scratch_shapes=[pltpu.VMEM((slots, width), bf16)] * 5
            + [pltpu.VMEM((slots, hidden_units), bf16)] * 2
            + [
                pltpu.VMEM((slots, 128), bf16),
                pltpu.VMEM((width, slots), bf16),
                pltpu.VMEM((depth, width, hidden_units), bf16),
                pltpu.VMEM((depth, hidden_units, width), bf16),
                pltpu.SemaphoreType.DMA((2, depth)),
                pltpu.SemaphoreType.DMA((2 + 2 * local,)),
            ],
            compiler_params=pltpu.CompilerParams(vmem_limit_bytes=56 * 2**20),
        )(recv, cot_recv, expert_in, expert_out)
        expert_rows, grad_slots, expert_act, grad_act, dots, result_rows = outs[:6]
        grad_chunks = outs[6:]

        def trade_chunks(chunks):
            return [chunks[0]] + [lax.ppermute(c, "tensor", pairs) for c, pairs in zip(chunks[1:], shifts)]

        def sum_rows(parts):
            columns = -(-(quarter + EXTRA) // 128) * 128
            return call(sum_kernel, [((slots, columns), bf16)], parts)[0]

        def own_tokens(rows, kept):
            return call(back_kernel, [((kept, token_count), bf16)], (rows, choice, slot))[0]

        by = lambda array: array.reshape(local, per, array.shape[1])
        grad_expert_out = jnp.einsum("erf,erd->efd", by(expert_act), by(grad_slots), preferred_element_type=f32)

        (result_part,) = call(
            result_back_kernel, [((token_count, width), bf16)], (exchange(result_rows), choice, slot)
        )
        traded, grad_expert_out, result_part = after((trade_chunks(grad_chunks), grad_expert_out, result_part))
        summed = sum_rows(traded + [dots])
        expert_rows, _ = after((expert_rows, summed))
        grad_expert_in = jnp.einsum("erd,erf->edf", by(expert_rows), by(grad_act), preferred_element_type=f32)
        returned = own_tokens(exchange(summed), quarter + EXTRA)
        returned, grad_expert_in = after((returned, grad_expert_in))
        result_share = lax.psum_scatter(result_part, "tensor", scatter_dimension=0, tiled=True)
        grad_parts = gather_tensor(returned)
        bias_planes, _ = after((iw_planes, returned))
        bias_all = jnp.sum(
            bias_planes[:, iw_rows:]
            .reshape(tensor_size - 1, -1)[:, : 3 * buckets * heads]
            .reshape(tensor_size - 1, 3, heads, buckets)
            .astype(f32),
            1,
        )
        result_share = jnp.pad(result_share, ((0, 48), (0, 0)))
        grad_parts, iw_all, bias_all, result_share = after((grad_parts, iw_all, bias_all, result_share))
        result = lax.all_gather(result_share, "tensor", axis=0)

        early_rows = quarter + experts + 64
        grad_hidden, grad_low, early_sums = call(
            hidden_backward_kernel,
            [((token_count, width), f32), ((token_count, width), bf16), ((early_rows, width), bf16)],
            (hidden, prob, cotangent, gain_second, rw, choice, attended, *grad_parts),
            [pltpu.VMEM((width, token_count), f32)],
        )
        def sum_chunks(array):
            return jnp.sum(array.reshape(expert_size, -1, array.shape[1]).astype(f32), 0)

        padded = token_count + 2 * BLOCK
        scratch = [pltpu.VMEM((padded, quarter), bf16)] * 2 + [pltpu.VMEM((quarter, padded), bf16)]
        scratch = scratch + [pltpu.VMEM((padded, quarter), f32)] * 2 + [pltpu.VMEM((quarter, token_count), f32)]
        grad_iw, own_parts, table_grad = call(
            own_backward_kernel,
            [((3 * quarter, width), bf16), ((3, token_count, quarter), bf16), ((1, width), f32)],
            (first_normed, iw_own, output_weight, table, seg, grad_low),
            scratch,
        )
        grad_tokens, tail = call(
            rest_backward_kernel,
            [((token_count, width), f32), ((8, width), bf16)],
            (
                first_normed, iw_own, iw_all, ow_all, bias_all, seg, grad_low, own_parts, tokens, gain_first,
                grad_hidden, table_grad,
            ),
            [pltpu.VMEM((token_count, width), f32)] + scratch,
        )
        early_got, grad_iw = after((exchange(early_sums), grad_iw))
        early_sum = sum_chunks(early_got)
        early = lax.all_gather(jnp.pad(early_sum, ((0, 8), (0, 0))), "expert", axis=0)
        late = lax.all_gather(jnp.concatenate([sum_chunks(exchange(grad_iw)).astype(bf16), tail], 0), "expert", axis=0)
        block_output, grad_iw, grad_ow, grad_rw, grad_second, grad_first, grad_table = call(
            finish_kernel,
            [
                ((token_count, width), bf16),
                ((3 * quarter, width), f32),
                ((quarter, width), f32),
                ((experts, width), f32),
                ((width,), f32),
                ((width,), f32),
                ((heads, buckets), f32),
            ],
            (late, early, hidden, prob, choice, result),
        )
        return (
            block_output,
            grad_tokens,
            grad_first,
            jnp.swapaxes(grad_iw.reshape(3, quarter, width), 1, 2),
            grad_table.T,
            grad_ow,
            grad_second,
            grad_rw.T,
            grad_expert_in,
            grad_expert_out,
        )

    return shards


def solution(mesh):
    placed = (
        P("expert", None),
        P("expert", None),
        P("expert"),
        P("expert"),
        P(),
        P(None, None, "tensor"),
        P(None, "tensor"),
        P("tensor", None),
        P(),
        P(),
        P("expert", None, "tensor"),
        P("expert", "tensor", None),
        P("expert", None),
    )
    return jax.shard_map(
        make(mesh),
        mesh=mesh,
        in_specs=placed,
        out_specs=(
            P("expert", None),
            P("expert", None),
            P(),
            P(None, None, "tensor"),
            P(None, "tensor"),
            P("tensor", None),
            P(),
            P(),
            P("expert", None, "tensor"),
            P("expert", "tensor", None),
        ),
        check_vma=False,
    )
```

```python
import math

import jax
import jax.numpy as jnp
from jax import lax
from jax.experimental import pallas as pl
from jax.experimental.pallas import tpu as pltpu
from jax.sharding import PartitionSpec as P

CAP = 10

bucket_edges = (12, 16, 23, 32, 46, 64, 91)
norm_eps = 1e-06
masked_score = -1e30
gelu_const = math.sqrt(2.0 / math.pi)
gelu_cubic = 0.044715

BLOCK = 128
BAND = 3 * BLOCK
ROLL = 4 * BLOCK
HEAD = 64
EXTRA = 16

bf16 = jnp.bfloat16
f32 = jnp.float32
i32 = jnp.int32
highest = lax.Precision.HIGHEST

NN = (((1,), (0,)), ((), ()))
NT = (((1,), (1,)), ((), ()))
TN = (((0,), (0,)), ((), ()))


def dot(left, right, dims=NN, precision=None):
    return lax.dot_general(left, right, dims, precision=precision, preferred_element_type=f32)


def dot3(left, right, dims=NN):
    left_high, right_high = left.astype(bf16), right.astype(bf16)
    left_low = (left - left_high.astype(f32)).astype(bf16)
    right_low = (right - right_high.astype(f32)).astype(bf16)
    return dot(left_high, right_high, dims) + (dot(left_high, right_low, dims) + dot(left_low, right_high, dims))


def flat(ref):
    return ref[...].reshape(1, -1)


def iota(shape, axis):
    return lax.broadcasted_iota(i32, shape, axis)


def call(kernel, outs, args, scratch=(), room=56):
    vmem = pl.BlockSpec(memory_space=pltpu.VMEM)
    return pl.pallas_call(
        kernel,
        out_shape=[jax.ShapeDtypeStruct(shape, dtype) for shape, dtype in outs],
        in_specs=[vmem] * len(args),
        out_specs=[vmem] * len(outs),
        scratch_shapes=list(scratch),
        compiler_params=pltpu.CompilerParams(vmem_limit_bytes=room * 2**20),
    )(*args)


def split3(value):
    high = value.astype(bf16).astype(f32)
    rest = value - high
    middle = rest.astype(bf16).astype(f32)
    return high, middle, rest - middle


def columns3(value, width):
    high, middle, low = split3(value)
    lane = iota((value.shape[0], width), 1)
    picked = jnp.where(lane == 0, high, jnp.where(lane == 1, middle, jnp.where(lane == 2, low, 0.0)))
    return picked.astype(bf16)


def column_of(row):
    return jnp.transpose(jnp.broadcast_to(row.astype(f32), (128, row.shape[1])))


def wide(column, width):
    return jnp.concatenate([column] * (width // 128), 1)


def bucket_of(relative):
    distance = jnp.abs(relative)
    beyond = jnp.zeros_like(distance)
    for threshold in bucket_edges:
        beyond = beyond + (distance >= threshold).astype(i32)
    magnitude = jnp.where(distance < 8, distance, 8 + beyond)
    return magnitude + 16 * (relative > 0).astype(i32)


def band_rows(table):
    buckets = table.shape[1]
    offset = iota((buckets, ROLL), 1)
    relative = jnp.where(offset < BAND, offset, offset - ROLL) - BLOCK
    onehot = (bucket_of(relative) == iota((buckets, ROLL), 0)).astype(f32)
    return dot(table, onehot, precision=highest), onehot


def bias_tiles(table):
    rows, onehot = band_rows(table)
    tiles = []
    for h in range(table.shape[0]):
        full = jnp.broadcast_to(rows[h : h + 1], (BLOCK, ROLL))
        tiles.append(jnp.transpose(pltpu.roll(full, 0, 1, stride=1, stride_axis=0)[:, :BAND]))
    return tiles, onehot


def head_masks(heads):
    lane = iota((1, heads * HEAD), 1)
    return [((lane >= h * HEAD) & (lane < (h + 1) * HEAD)).astype(f32).astype(bf16) for h in range(heads)]


def padded_segments(seg):
    edge = jnp.full((1, BLOCK), -1.0, f32)
    return column_of(jnp.concatenate([edge, seg, edge], 1))


def first_norm(tok, gain):
    scale = lax.rsqrt(jnp.mean(tok * tok, -1, keepdims=True) + norm_eps)
    return (tok * scale * gain).astype(bf16), scale


def probabilities(scores, bias, same):
    scores = jnp.where(same, scores + bias, masked_score)
    weights = jnp.exp(scores - jnp.max(scores, 0, keepdims=True))
    return weights * (1.0 / jnp.sum(weights, 0, keepdims=True))


def stack_heads(rows, masks):
    return jnp.concatenate([rows * mask for mask in masks], 0)


def own_blocks(product, heads):
    return jnp.concatenate(
        [product[h * HEAD : (h + 1) * HEAD, h * BLOCK : (h + 1) * BLOCK] for h in range(heads)], 0
    )


def fill_rows(ref, value):
    rows = value.shape[0]
    edge = jnp.zeros((BLOCK, value.shape[1]), bf16)
    ref[pl.ds(0, BLOCK), :] = edge
    ref[pl.ds(rows + BLOCK, BLOCK), :] = edge
    ref[pl.ds(BLOCK, rows), :] = value


def fill_columns(ref, value):
    rows = value.shape[1]
    edge = jnp.zeros((value.shape[0], BLOCK), bf16)
    ref[:, pl.ds(0, BLOCK)] = edge
    ref[:, pl.ds(rows + BLOCK, BLOCK)] = edge
    ref[:, pl.ds(BLOCK, rows)] = value


def forward_kernel(
    tok_ref, gain_ref, iw_ref, bt_ref, seg_ref, cot_ref, choice_ref, slot_ref,
    att_ref, normed_ref, cot_slots_ref, keys, values,
):
    rows = tok_ref.shape[0]
    fill = slot_onehot(flat(choice_ref), flat(slot_ref), cot_slots_ref.shape[0])
    cot_slots_ref[...] = dot(fill, cot_ref[...]).astype(bf16)
    normed, _ = first_norm(tok_ref[...].astype(f32), flat(gain_ref))
    normed_ref[...] = normed
    queries = dot(normed, iw_ref[0], NT).astype(bf16)
    fill_rows(keys, dot(normed, iw_ref[1], NT).astype(bf16))
    fill_columns(values, dot(iw_ref[2], normed, NT).astype(bf16))
    seg = seg_ref[...].astype(f32)
    seg_keys = padded_segments(seg)
    tiles, _ = bias_tiles(bt_ref[...])
    heads = len(tiles)
    masks = head_masks(heads)
    for block in range(rows // BLOCK):
        at = block * BLOCK
        same = seg_keys[at : at + BAND] == seg[:, at : at + BLOCK]
        scores = dot(keys[pl.ds(at, BAND), :], stack_heads(queries[at : at + BLOCK], masks), NT)
        weights = [
            probabilities(scores[:, h * BLOCK : (h + 1) * BLOCK], tiles[h], same).astype(bf16) for h in range(heads)
        ]
        product = dot(values[:, pl.ds(at, BAND)], jnp.concatenate(weights, 1))
        att_ref[:, pl.ds(at, BLOCK)] = own_blocks(product, heads).astype(bf16)


def group_backward(normed, weight, out_weight, table, seg, grad_low, scratch, bias_grads):
    keys, values, keys_across, grad_keys, grad_values, grad_queries = scratch
    rows = normed.shape[0]
    queries = dot(normed, weight[0], NT).astype(bf16)
    fill_rows(keys, dot(normed, weight[1], NT).astype(bf16))
    fill_columns(keys_across, dot(weight[1], normed, NT).astype(bf16))
    fill_rows(values, dot(normed, weight[2], NT).astype(bf16))
    grad_att = dot(grad_low, out_weight, NT).astype(bf16)
    grad_keys[...] = jnp.zeros(grad_keys.shape, f32)
    grad_values[...] = jnp.zeros(grad_values.shape, f32)
    seg_keys = padded_segments(seg)
    tiles, onehot = bias_tiles(table)
    heads = len(tiles)
    masks = head_masks(heads)
    sums = [None] * heads
    for block in range(rows // BLOCK):
        at = block * BLOCK
        same = seg_keys[at : at + BAND] == seg[:, at : at + BLOCK]
        head_queries = stack_heads(queries[at : at + BLOCK], masks)
        head_grads = stack_heads(grad_att[at : at + BLOCK], masks)
        scores = dot(keys[pl.ds(at, BAND), :], head_queries, NT)
        grad_probs = dot(values[pl.ds(at, BAND), :], head_grads, NT)
        all_weights, all_grads = [], []
        for h in range(heads):
            columns = slice(h * BLOCK, (h + 1) * BLOCK)
            weights = probabilities(scores[:, columns], tiles[h], same)
            scaled = weights * grad_probs[:, columns]
            grad_scores = scaled - weights * jnp.sum(scaled, 0, keepdims=True)
            all_weights.append(weights.astype(bf16))
            all_grads.append(grad_scores.astype(bf16))
            if bias_grads:
                sums[h] = grad_scores if sums[h] is None else sums[h] + grad_scores
        low = jnp.concatenate(all_grads, 1)
        grad_queries[:, pl.ds(at, BLOCK)] = own_blocks(dot(keys_across[:, pl.ds(at, BAND)], low), heads)
        grad_keys[pl.ds(at, BAND), :] += dot(low, head_queries)
        grad_values[pl.ds(at, BAND), :] += dot(jnp.concatenate(all_weights, 1), head_grads)
    parts = (
        jnp.transpose(grad_queries[...]).astype(bf16),
        grad_keys[pl.ds(BLOCK, rows), :].astype(bf16),
        grad_values[pl.ds(BLOCK, rows), :].astype(bf16),
    )
    if not bias_grads:
        return parts, None
    diagonals = []
    row_index = iota((BLOCK, ROLL), 0)
    for h in range(heads):
        moved = jnp.concatenate([jnp.transpose(sums[h]), jnp.zeros((BLOCK, ROLL - BAND), f32)], 1)
        step = 1
        while step < BLOCK:
            moved = jnp.where((row_index & step) != 0, pltpu.roll(moved, ROLL - step, 1), moved)
            step *= 2
        diagonals.append(jnp.sum(moved, 0, keepdims=True))
    onehot = jnp.concatenate([onehot, jnp.zeros((128 - onehot.shape[0], ROLL), f32)], 0)
    by_head = dot(jnp.concatenate(diagonals, 0), onehot, NT, precision=highest)
    return parts, jnp.concatenate([by_head[h : h + 1] for h in range(heads)], 1)


def own_backward_kernel(normed_ref, iw_ref, ow_ref, bt_ref, seg_ref, low_ref, grad_iw_ref, parts_ref, table_ref, *scratch):
    normed = normed_ref[...]
    parts, table_grad = group_backward(
        normed, iw_ref, ow_ref[...], bt_ref[...], seg_ref[...].astype(f32), low_ref[...], scratch, True
    )
    table_ref[...] = jnp.concatenate(
        [table_grad, jnp.zeros((1, table_ref.shape[1] - table_grad.shape[1]), f32)], 1
    )
    width = ow_ref.shape[0]
    for j in range(3):
        parts_ref[j] = parts[j]
        grad_iw_ref[pl.ds(j * width, width), :] = dot(parts[j], normed, TN).astype(bf16)


def rest_backward_kernel(
    normed_ref, own_iw_ref, iw_ref, ow_ref, bt_ref, seg_ref, low_ref, parts_ref, tok_ref, gain_ref, grad_hidden_ref,
    table_ref, grad_tok_ref, tail_ref, total, *scratch,
):
    width = ow_ref.shape[1]
    total[...] = sum(dot(parts_ref[j], own_iw_ref[j]) for j in range(3))

    def step(group, carry):
        weight = [iw_ref[group, pl.ds(j * width, width), :] for j in range(3)]
        parts, _ = group_backward(
            normed_ref[...], weight, ow_ref[group], bt_ref[group], seg_ref[...].astype(f32), low_ref[...], scratch, False
        )
        total[...] += sum(dot(parts[j], weight[j]) for j in range(3))
        return carry

    lax.fori_loop(0, ow_ref.shape[0], step, 0)
    tok = tok_ref[...].astype(f32)
    gain = flat(gain_ref)
    scale = lax.rsqrt(jnp.mean(tok * tok, -1, keepdims=True) + norm_eps)
    grad_normed = total[...]
    tail_ref[...] = rows3([jnp.sum(grad_normed * tok * scale, 0, keepdims=True), table_ref[...]], tail_ref.shape[0])
    scaled = grad_normed * gain
    grad_tok_ref[...] = (
        grad_hidden_ref[...]
        + scale * scaled
        - tok * (scale * scale * scale) * jnp.mean(scaled * tok, -1, keepdims=True)
    )


def rows3(values, count):
    parts = [part for value in values for part in split3(value)]
    row = iota((count, values[0].shape[1]), 0)
    total = jnp.zeros(row.shape, f32)
    for index, part in enumerate(parts):
        total = jnp.where(row == index, part, total)
    return total.astype(bf16)


def finish_kernel(late_ref, early_ref, hidden_ref, prob_ref, choice_ref, result_ref, *refs):
    out_ref, grad_iw_ref, grad_ow_ref, grad_rw_ref, second_ref, first_ref, table_ref = refs
    output_kernel(hidden_ref, prob_ref, choice_ref, result_ref, out_ref)
    devices = late_ref.shape[0]
    late_rows = grad_iw_ref.shape[0] // devices
    tail = jnp.zeros((late_ref.shape[1] - late_rows, late_ref.shape[2]), f32)
    for device in range(devices):
        block = late_ref[device].astype(f32)
        grad_iw_ref[pl.ds(device * late_rows, late_rows), :] = block[:late_rows]
        tail = tail + block[late_rows:]
    first_ref[...] = jnp.sum(tail[:3], 0)
    table = jnp.sum(tail[3:6], 0, keepdims=True)
    heads, buckets = table_ref.shape
    table_ref[...] = jnp.concatenate([table[:, h * 128 : h * 128 + buckets] for h in range(heads)], 0)
    at, experts = grad_ow_ref.shape[0], grad_rw_ref.shape[0]
    early = jnp.concatenate([early_ref[device] for device in range(devices)], 0)
    grad_ow_ref[...] = early[:at]
    grad_rw_ref[...] = early[at : at + experts]
    second_ref[...] = jnp.sum(early[at + experts : at + experts + 8], 0)


def slot_onehot(choice, slot, slots):
    dest = jnp.where(slot >= 0, choice * CAP + slot, slots)
    return (iota((slots, dest.shape[1]), 0) == dest).astype(f32).astype(bf16)


def slot_order(slots, group, across):
    index = iota((1, slots), 1)
    big, small = slots // across, slots // group
    outer, rest = lax.div(index, big), lax.rem(index, big)
    target = lax.div(rest, CAP) * small + outer * CAP + lax.rem(rest, CAP)
    return (iota((slots, slots), 0) == target).astype(f32).astype(bf16)


def chosen_of(choice, experts):
    column = column_of(choice)[:, :experts]
    return (column == iota(column.shape, 1).astype(f32)).astype(f32)


def middle_kernel(tok_ref, own_ow_ref, ow_ref, gain_ref, rw_ref, choice_ref, slot_ref, *refs):
    att_refs, (hidden_ref, prob_ref, send_ref) = refs[:-3], refs[-3:]
    hidden = tok_ref[...].astype(f32)
    for shift, att_ref in enumerate(att_refs):
        hidden = hidden + dot(att_ref[...], ow_ref[shift - 1] if shift else own_ow_ref[...], TN)
    hidden_ref[...] = hidden
    scale = lax.rsqrt(jnp.mean(hidden * hidden, -1, keepdims=True) + norm_eps)
    normed = hidden * scale * flat(gain_ref)
    logits = dot3(normed, rw_ref[...], NT)
    raised = jnp.exp(logits - jnp.max(logits, -1, keepdims=True))
    prob = raised * (1.0 / jnp.sum(raised, -1, keepdims=True))
    prob_ref[...] = prob
    gate = jnp.sum(prob * chosen_of(flat(choice_ref), prob.shape[1]), -1, keepdims=True)
    width = normed.shape[1]
    fill = slot_onehot(flat(choice_ref), flat(slot_ref), send_ref.shape[0])
    send_ref[:, :width] = dot(fill, normed.astype(bf16)).astype(bf16)
    send_ref[:, width:] = dot(fill, columns3(gate, 128)).astype(bf16)


def expert_kernel(
    tensor_size, sources, local,
    recv_ref, cot_ref, win_ref, wout_ref,
    rows_ref, grads_ref, act_ref, grad_act_ref, dots_ref, result_ref, *refs,
):
    chunks = refs[:tensor_size]
    c_all, r_all, y_all, x_all, g_all, h_all, s_all, d_all, turned, win_slots, wout_slots, arrived, left = refs[tensor_size:]
    leaving = []

    def leave(source, target):
        leaving.append(pltpu.make_async_copy(source, target, left.at[len(leaving)]))
        leaving[-1].start()

    slots, width = cot_ref.shape
    per = slots // local
    depth = win_slots.shape[0]

    def fetch(expert):
        slot = expert % depth
        copies = [
            pltpu.make_async_copy(win_ref.at[expert], win_slots.at[slot], arrived.at[0, slot]),
            pltpu.make_async_copy(wout_ref.at[expert], wout_slots.at[slot], arrived.at[1, slot]),
        ]
        for copy in copies:
            copy.start()
        return copies

    coming = [fetch(expert) for expert in range(min(depth, local))]
    order = slot_order(slots, local, sources)
    x_all[...] = dot(order, recv_ref[:, :width]).astype(bf16)
    gate = jnp.sum(dot(order, recv_ref[:, width:]), -1, keepdims=True)
    cot = dot(order, cot_ref[...])
    c_all[...] = cot.astype(bf16)
    g_all[...] = (gate * cot).astype(bf16)
    leave(x_all, rows_ref)
    leave(g_all, grads_ref)

    for expert in range(local):
        at = pl.ds(expert * per, per)
        for copy in coming[expert]:
            copy.wait()
        x = x_all[at, :]
        g = g_all[at, :]
        weight_in = win_slots[expert % depth]
        weight_out = wout_slots[expert % depth]
        pre = dot(x, weight_in)
        grad_act = dot(g, weight_out, NT)
        inner = jnp.tanh(gelu_const * (pre + gelu_cubic * pre * pre * pre))
        act = (0.5 * pre * (1.0 + inner)).astype(bf16)
        slope = 0.5 * (1.0 + inner) + 0.5 * pre * (1.0 - inner * inner) * gelu_const * (
            1.0 + 3.0 * gelu_cubic * pre * pre
        )
        grad_act = (grad_act * slope).astype(bf16)
        r_all[at, :] = dot(grad_act, weight_in, NT).astype(bf16)
        result = dot(act, weight_out)
        y_all[at, :] = result.astype(bf16)
        d_all[at, :] = columns3(jnp.sum(result * c_all[at, :].astype(f32), -1, keepdims=True), 128)
        h_all[at, :] = act
        s_all[at, :] = grad_act
        leave(h_all.at[at], act_ref.at[at])
        leave(s_all.at[at], grad_act_ref.at[at])
        if expert + depth < local:
            coming.append(fetch(expert + depth))

    dots_ref[...] = dot(d_all[...], order, TN)[:EXTRA].astype(bf16)
    turn_chunks(tensor_size, dot(r_all[...], order, TN).astype(bf16), turned, chunks)
    result_ref[...] = dot(slot_order(slots, sources, local), y_all[...]).astype(bf16)
    for copy in leaving:
        copy.wait()


def turn_chunks(tensor_size, rows, turned, chunks):
    turned[...] = rows
    quarter = rows.shape[0] // tensor_size
    me = lax.axis_index("tensor")
    for shift in range(tensor_size):
        first = lax.rem(me + shift, tensor_size) * quarter
        chunks[shift][...] = turned[pl.ds(pl.multiple_of(first, 64), quarter), :]


def result_back_kernel(recv_ref, choice_ref, slot_ref, out_ref):
    fill = slot_onehot(flat(choice_ref), flat(slot_ref), recv_ref.shape[0])
    out_ref[...] = dot(fill, recv_ref[...], TN).astype(bf16)


def sum_kernel(*refs):
    *parts, dots_ref, out_ref = refs
    total = sum(ref[...].astype(f32) for ref in parts)
    blank = jnp.zeros((out_ref.shape[1] - total.shape[0] - EXTRA, total.shape[1]), f32)
    out_ref[...] = jnp.transpose(jnp.concatenate([total, dots_ref[...].astype(f32), blank], 0)).astype(bf16)


def back_kernel(recv_ref, choice_ref, slot_ref, out_ref):
    fill = slot_onehot(flat(choice_ref), flat(slot_ref), recv_ref.shape[0])
    out_ref[...] = dot(recv_ref[...], fill, TN)[: out_ref.shape[0]].astype(bf16)


def spread(refs, quarter, turned):
    size = len(refs)
    me = lax.axis_index("tensor")
    for shift, ref in enumerate(refs):
        first = lax.rem(me + size - shift, size) * quarter
        turned[pl.ds(pl.multiple_of(first, 64), quarter), :] = ref[pl.ds(0, quarter), :].astype(f32)
    return jnp.transpose(turned[...])


def hidden_backward_kernel(
    hidden_ref, prob_ref, cot_ref, gain_ref, rw_ref, choice_ref, att_ref, *refs,
):
    parts = refs[:-4]
    grad_hidden_ref, low_ref, sums_ref, turned = refs[-4:]
    hidden = hidden_ref[...]
    rows, width = hidden.shape
    quarter = width // len(parts)
    grad_routed = spread(parts, quarter, turned)
    dots = sum(jnp.sum(ref[pl.ds(quarter, EXTRA), :].astype(f32), 0, keepdims=True) for ref in parts)
    prob = prob_ref[...]
    chosen = chosen_of(flat(choice_ref), prob.shape[1])
    gate = jnp.sum(prob * chosen, -1, keepdims=True)
    grad_gate = column_of(dots)[:, :1]
    grad_logits = (grad_gate * gate) * (chosen - prob)
    grad_normed = grad_routed + dot3(grad_logits, rw_ref[...])
    gain = flat(gain_ref)
    scale = lax.rsqrt(jnp.mean(hidden * hidden, -1, keepdims=True) + norm_eps)
    scaled = grad_normed * gain
    grad_hidden = (
        cot_ref[...].astype(f32)
        + scale * scaled
        - hidden * (scale * scale * scale) * jnp.mean(scaled * hidden, -1, keepdims=True)
    )
    grad_hidden_ref[...] = grad_hidden
    low = grad_hidden.astype(bf16)
    low_ref[...] = low
    at, experts = att_ref.shape[0], prob.shape[1]
    sums_ref[pl.ds(0, at), :] = dot(att_ref[...], low).astype(bf16)
    sums_ref[pl.ds(at, experts), :] = dot3(grad_logits, hidden * scale * gain, TN).astype(bf16)
    tail = sums_ref.shape[0] - at - experts
    sums_ref[pl.ds(at + experts, tail), :] = rows3([jnp.sum(grad_normed * hidden * scale, 0, keepdims=True)], tail)


def output_kernel(hidden_ref, prob_ref, choice_ref, result_ref, out_ref):
    prob = prob_ref[...]
    gate = jnp.sum(prob * chosen_of(flat(choice_ref), prob.shape[1]), -1, keepdims=True)
    share = hidden_ref.shape[0] // result_ref.shape[0]
    result = jnp.concatenate([result_ref[part][:share] for part in range(result_ref.shape[0])], 0)
    out_ref[...] = (hidden_ref[...] + gate * result.astype(f32)).astype(bf16)


def make(mesh):
    tensor_size = mesh.shape["tensor"]
    expert_size = mesh.shape["expert"]

    def shards(
        tokens,
        segment_ids,
        expert_choice,
        slot_index,
        first_gain,
        input_weight,
        bias_table,
        output_weight,
        second_gain,
        router_weight,
        expert_in,
        expert_out,
        cotangent,
    ):
        token_count, width = tokens.shape
        sequences, length = segment_ids.shape
        quarter = output_weight.shape[0]
        experts = router_weight.shape[1]
        local = expert_in.shape[0]
        hidden_units = expert_in.shape[2]
        slots = experts * CAP
        per = slots // local
        chunk = slots // expert_size
        buckets, heads = bias_table.shape
        expert_index = lax.axis_index("expert")
        seg = (segment_ids + 8 * jnp.arange(sequences, dtype=i32)[:, None]).reshape(1, token_count)
        choice, slot = expert_choice, slot_index
        gain_first, gain_second = first_gain, second_gain
        iw_own = jnp.swapaxes(input_weight, 1, 2)
        table = bias_table.T
        rw = router_weight.T
        after = lax.optimization_barrier

        shifts = [[(i, (i + s) % tensor_size) for i in range(tensor_size)] for s in range(1, tensor_size)]

        def from_others(array):
            return [lax.ppermute(array, "tensor", pairs) for pairs in shifts]

        def gather_tensor(array):
            return [array] + from_others(array)

        def joined(planes, rows):
            got = lax.all_gather(planes, "expert", axis=0)
            return jnp.swapaxes(got[:, :, :rows], 0, 1).reshape(tensor_size - 1, -1, got.shape[-1])

        def exchange(array):
            rows = array.shape[0] // expert_size
            got = lax.all_to_all(array.reshape(expert_size, rows, array.shape[1]), "expert", 0, 0)
            return got.reshape(array.shape)

        ow_rows = quarter // expert_size
        ow_part = lax.dynamic_slice_in_dim(output_weight, expert_index * ow_rows, ow_rows, 0)
        ow_all = joined(jnp.stack(from_others(ow_part)), ow_rows)

        attended, first_normed, cot_slots = call(
            forward_kernel,
            [((quarter, token_count), bf16), ((token_count, width), bf16), ((slots, width), bf16)],
            (tokens, gain_first, iw_own, table, seg, cotangent, choice, slot),
            [
                pltpu.VMEM((token_count + 2 * BLOCK, quarter), bf16),
                pltpu.VMEM((quarter, token_count + 2 * BLOCK), bf16),
            ],
        )
        attended_parts = gather_tensor(attended)
        cot_recv = exchange(cot_slots)
        attended_parts, cot_recv = after((attended_parts, cot_recv))

        hidden, prob, send = call(
            middle_kernel,
            [((token_count, width), f32), ((token_count, experts), f32), ((slots, width + 128), bf16)],
            (tokens, output_weight, ow_all, gain_second, rw, choice, slot, *attended_parts),
        )
        recv = exchange(send)

        iw_rows = 3 * quarter // expert_size
        iw_part = lax.dynamic_slice_in_dim(iw_own.reshape(3 * quarter, width), expert_index * iw_rows, iw_rows, 0)
        bias_parts = jnp.stack(split3(table)).astype(bf16).reshape(-1)
        bias_parts = jnp.pad(bias_parts, (0, 8 * width - bias_parts.shape[0])).reshape(8, width)
        iw_part, _ = after((jnp.concatenate([iw_part, bias_parts], 0), send))
        iw_planes = from_others(iw_part)

        iw_planes, recv = after((iw_planes, recv))
        iw_planes = jnp.stack(iw_planes)
        iw_all = joined(iw_planes, iw_rows)

        vmem = pl.BlockSpec(memory_space=pltpu.VMEM)
        left = pl.BlockSpec(memory_space=pl.ANY)
        shapes = [(slots, width)] * 2 + [(slots, hidden_units)] * 2 + [(EXTRA, slots), (slots, width)]
        shapes = shapes + [(quarter, slots)] * tensor_size
        depth = min(4, local)
        outs = pl.pallas_call(
            lambda *refs: expert_kernel(tensor_size, expert_size, local, *refs),
            in_specs=[vmem, vmem, left, left],
            out_specs=[left] * 4 + [vmem] * (len(shapes) - 4),
            out_shape=[jax.ShapeDtypeStruct(shape, bf16) for shape in shapes],
            scratch_shapes=[pltpu.VMEM((slots, width), bf16)] * 5
            + [pltpu.VMEM((slots, hidden_units), bf16)] * 2
            + [
                pltpu.VMEM((slots, 128), bf16),
                pltpu.VMEM((width, slots), bf16),
                pltpu.VMEM((depth, width, hidden_units), bf16),
                pltpu.VMEM((depth, hidden_units, width), bf16),
                pltpu.SemaphoreType.DMA((2, depth)),
                pltpu.SemaphoreType.DMA((2 + 2 * local,)),
            ],
            compiler_params=pltpu.CompilerParams(vmem_limit_bytes=56 * 2**20),
        )(recv, cot_recv, expert_in, expert_out)
        expert_rows, grad_slots, expert_act, grad_act, dots, result_rows = outs[:6]
        grad_chunks = outs[6:]

        def trade_chunks(chunks):
            return [chunks[0]] + [lax.ppermute(c, "tensor", pairs) for c, pairs in zip(chunks[1:], shifts)]

        def sum_rows(parts):
            columns = -(-(quarter + EXTRA) // 128) * 128
            return call(sum_kernel, [((slots, columns), bf16)], parts)[0]

        def own_tokens(rows, kept):
            return call(back_kernel, [((kept, token_count), bf16)], (rows, choice, slot))[0]

        by = lambda array: array.reshape(local, per, array.shape[1])
        grad_expert_out = jnp.einsum("erf,erd->efd", by(expert_act), by(grad_slots), preferred_element_type=f32)

        (result_part,) = call(
            result_back_kernel, [((token_count, width), bf16)], (exchange(result_rows), choice, slot)
        )
        traded, grad_expert_out, result_part = after((trade_chunks(grad_chunks), grad_expert_out, result_part))
        summed = sum_rows(traded + [dots])
        expert_rows, _ = after((expert_rows, summed))
        grad_expert_in = jnp.einsum("erd,erf->edf", by(expert_rows), by(grad_act), preferred_element_type=f32)
        returned = own_tokens(exchange(summed), quarter + EXTRA)
        returned, grad_expert_in = after((returned, grad_expert_in))
        result_share = lax.psum_scatter(result_part, "tensor", scatter_dimension=0, tiled=True)
        grad_parts = gather_tensor(returned)
        bias_planes, _ = after((iw_planes, returned))
        bias_all = jnp.sum(
            bias_planes[:, iw_rows:]
            .reshape(tensor_size - 1, -1)[:, : 3 * buckets * heads]
            .reshape(tensor_size - 1, 3, heads, buckets)
            .astype(f32),
            1,
        )
        result_share = jnp.pad(result_share, ((0, 48), (0, 0)))
        grad_parts, iw_all, bias_all, result_share = after((grad_parts, iw_all, bias_all, result_share))
        result = lax.all_gather(result_share, "tensor", axis=0)

        early_rows = quarter + experts + 128
        grad_hidden, grad_low, early_sums = call(
            hidden_backward_kernel,
            [((token_count, width), f32), ((token_count, width), bf16), ((early_rows, width), bf16)],
            (hidden, prob, cotangent, gain_second, rw, choice, attended, *grad_parts),
            [pltpu.VMEM((width, token_count), f32)],
        )
        def sum_chunks(array):
            return jnp.sum(array.reshape(expert_size, -1, array.shape[1]).astype(f32), 0)

        padded = token_count + 2 * BLOCK
        scratch = [pltpu.VMEM((padded, quarter), bf16)] * 2 + [pltpu.VMEM((quarter, padded), bf16)]
        scratch = scratch + [pltpu.VMEM((padded, quarter), f32)] * 2 + [pltpu.VMEM((quarter, token_count), f32)]
        grad_iw, own_parts, table_grad = call(
            own_backward_kernel,
            [((3 * quarter, width), bf16), ((3, token_count, quarter), bf16), ((1, width), f32)],
            (first_normed, iw_own, output_weight, table, seg, grad_low),
            scratch,
        )
        grad_tokens, tail = call(
            rest_backward_kernel,
            [((token_count, width), f32), ((8, width), bf16)],
            (
                first_normed, iw_own, iw_all, ow_all, bias_all, seg, grad_low, own_parts, tokens, gain_first,
                grad_hidden, table_grad,
            ),
            [pltpu.VMEM((token_count, width), f32)] + scratch,
        )
        early_got, grad_iw = after((exchange(early_sums), grad_iw))
        early_sum = sum_chunks(early_got)
        early = lax.all_gather(early_sum, "expert", axis=0)
        late = lax.all_gather(jnp.concatenate([sum_chunks(exchange(grad_iw)).astype(bf16), tail], 0), "expert", axis=0)
        block_output, grad_iw, grad_ow, grad_rw, grad_second, grad_first, grad_table = call(
            finish_kernel,
            [
                ((token_count, width), bf16),
                ((3 * quarter, width), f32),
                ((quarter, width), f32),
                ((experts, width), f32),
                ((width,), f32),
                ((width,), f32),
                ((heads, buckets), f32),
            ],
            (late, early, hidden, prob, choice, result),
            room=24,
        )
        return (
            block_output,
            grad_tokens,
            grad_first,
            jnp.swapaxes(grad_iw.reshape(3, quarter, width), 1, 2),
            grad_table.T,
            grad_ow,
            grad_second,
            grad_rw.T,
            grad_expert_in,
            grad_expert_out,
        )

    return shards


def solution(mesh):
    placed = (
        P("expert", None),
        P("expert", None),
        P("expert"),
        P("expert"),
        P(),
        P(None, None, "tensor"),
        P(None, "tensor"),
        P("tensor", None),
        P(),
        P(),
        P("expert", None, "tensor"),
        P("expert", "tensor", None),
        P("expert", None),
    )
    return jax.shard_map(
        make(mesh),
        mesh=mesh,
        in_specs=placed,
        out_specs=(
            P("expert", None),
            P("expert", None),
            P(),
            P(None, None, "tensor"),
            P(None, "tensor"),
            P("tensor", None),
            P(),
            P(),
            P("expert", None, "tensor"),
            P("expert", "tensor", None),
        ),
        check_vma=False,
    )
```
